32 devices in a mesh: parts: 2 (over x), genome: 8 (over z, y), reads: 2 (over core).
Axes of the slice: x: 2, y: 2, z: 4, core: 2. Of those that a mesh axis runs over, the one named last changes fastest.
Arguments:
- likelihood: bfloat16 [32, 64, 256, 128], P(('parts', 'reads'), 'genome'), parts along dimension 0, may hold values from 0.0099487305 to 1
- block_ids: int32 [32, 64], P(('parts', 'reads'), 'genome'), parts along dimension 0, may hold values from 0 to 191, as said below
- slot_valid: int32 [32, 64], P(('parts', 'reads'), 'genome'), parts along dimension 0, may hold values from 0 to 1, as said below
- start_weights: float32 [49152], P(('parts', 'genome', 'reads')), parts along dimension 0, may hold values from 0.5 to 2
Outputs:
- abundance: float32 [49152], P(('parts', 'genome', 'reads')), parts along dimension 0
The draws below stay inside these ranges and needn't reach their ends.
There are 2 independent parts, one for each index of `parts`. The reference program is written for one: setup_inputs(seed, part) draws one part's arguments, and reference() takes and returns one part's arrays. A program takes and returns all parts, laid end to end along the dimension named above; each array names one. Nothing has to cross between parts.
Inputs may be any that keep to these rules, and one draw needn't show every extreme that they name: `block_ids`: the 64 genome blocks of one read block are distinct. `slot_valid`: within each read block, the valid slots among the 8 slots held by one index of genome come first; slot 0 of every read block is valid.
All inputs are finite; a program needn't handle non-finite values.
Results may differ from the reference program's by a relative error of at most 0.0003.
Values sent between devices are 32-bit elements; how exact they have to be, the bound alone decides.
No kernel may reach another device: no remote copies, remote signals or barrier semaphores. Data moves between devices by JAX's collectives and lax.ppermute only.
A program may use at most 64 MiB of HBM per device.

```python
import math
import jax
import jax.numpy as jnp
from jax import lax

BLOCK_READS = 256
BLOCK_COLS = 128
KD = 8
ITERS = 2
READ_BLOCKS = 16
SLOTS = 64
GB = 192
GENOMES = 24576
READS = 4096


def draw_block_ids(key, part):
    key = jax.random.fold_in(key, 11)
    keys = jax.random.split(key, READ_BLOCKS)
    chosen = jax.vmap(lambda k: jax.random.permutation(k, GB)[:SLOTS])(keys)
    return chosen.astype(jnp.int32)


def draw_slot_valid(key, part):
    key = jax.random.fold_in(key, 23)
    groups = SLOTS // KD
    filled = jax.random.randint(key, (READ_BLOCKS, groups), 0, KD + 1)
    filled = filled.at[:, 0].set(jnp.maximum(filled[:, 0], 1))
    valid = jnp.arange(KD)[None, None, :] < filled[:, :, None]
    return valid.astype(jnp.int32).reshape(READ_BLOCKS, SLOTS)


def levels(own_key, shape, shards, smallest, high):
    def one(dim, parts):
        heights = jax.random.uniform(jax.random.fold_in(jax.random.fold_in(own_key, 6), dim), (parts,), jnp.float32, smallest / len(shards), high / len(shards))
        return jnp.repeat(jnp.exp(heights), shape[dim] // parts).reshape((-1,) + (1,) * (len(shape) - dim - 1))

    gain = one(*shards[0])
    for cut in shards[1:]:
        gain = gain * one(*cut)
    return gain


def setup_inputs(seed: int = 0, part: int = 0) -> dict:
    streams_of = jax.random.split(jax.random.key(seed), 5)
    own_keys = jax.random.split(jax.random.fold_in(streams_of[4], part), 5)
    likelihood = jnp.clip(jnp.exp(math.log(1.0) - 4.61031033 * jax.random.uniform(own_keys[0], (READ_BLOCKS, SLOTS, BLOCK_READS, BLOCK_COLS), jnp.float32) ** levels(own_keys[0], (READ_BLOCKS, SLOTS, BLOCK_READS, BLOCK_COLS), ((0, 2), (1, 8)), -0.2, 0.2)), 0.0099487305, 1.0).astype(jnp.bfloat16)
    block_ids = draw_block_ids(jax.random.fold_in(jax.random.fold_in(streams_of[4], part), 71), part)
    slot_valid = draw_slot_valid(jax.random.fold_in(jax.random.fold_in(streams_of[4], part), 71), part)
    start_weights = jnp.clip(jnp.exp(math.log(2.0) - 1.3862944 * jax.random.uniform(own_keys[3], (GENOMES,), jnp.float32) ** levels(own_keys[3], (GENOMES,), ((0, 16),), -0.2, 0.2)), 0.5, 2.0)
    return dict(likelihood=likelihood, block_ids=block_ids, slot_valid=slot_valid, start_weights=start_weights)


def reference(likelihood, block_ids, slot_valid, start_weights):
    weights = start_weights.astype(jnp.float32)
    scale = GENOMES / READS
    for step in range(ITERS):
        table = weights.reshape(GB, BLOCK_COLS)

        def one_block(counts, items):
            lik_block, ids_block, valid_block = items
            picked = table[ids_block] * valid_block.astype(jnp.float32)[:, None]
            lik_float = lik_block.astype(jnp.float32)
            row_total = jnp.sum(lik_float * picked[:, None, :], axis=(0, 2))
            inverse = 1.0 / row_total
            contrib = picked * jnp.sum(lik_float * inverse[None, :, None], axis=1)
            counts = counts.at[ids_block].add(contrib)
            return counts, None

        counts0 = jnp.zeros((GB, BLOCK_COLS), jnp.float32)
        counts, unused = lax.scan(one_block, counts0, (likelihood, block_ids, slot_valid))
        weights = counts.reshape(GENOMES) * scale
    return weights
```

```python
import jax
import jax.numpy as jnp
from jax import lax
from jax.sharding import PartitionSpec as P

ITERS = 2
ALL = ("genome", "reads")


def spread(x, axes):
    n = lax.axis_size(axes)
    sent = jnp.broadcast_to(x[None], (n,) + x.shape)
    return lax.all_to_all(sent, axes, 0, 0, tiled=True)


def sum_genome_steps(x):
    n = lax.axis_size("genome")
    hop = 1
    while hop < n:
        pairs = [(i, i ^ hop) for i in range(n)]
        x = x + lax.ppermute(x, "genome", pairs)
        hop *= 2
    return x


def sum_genome_direct(x):
    return jnp.sum(spread(x, "genome"), axis=0)


def local_counts(table, likelihood, block_ids, slot_valid, sum_genome):
    blocks, cols = table.shape
    picked = table[block_ids] * slot_valid.astype(jnp.float32)[:, :, None]
    lik_float = likelihood.astype(jnp.float32)
    row_part = jnp.sum(lik_float * picked[:, :, None, :], axis=(1, 3))
    row_total = sum_genome(row_part)
    inverse = 1.0 / row_total
    contrib = picked * jnp.sum(lik_float * inverse[:, None, :, None], axis=2)
    flat_ids = block_ids.reshape(-1)
    one_hot = (flat_ids[None, :] == jnp.arange(blocks, dtype=jnp.int32)[:, None]).astype(
        jnp.float32
    )
    return jnp.dot(
        one_hot,
        contrib.reshape(-1, cols),
        preferred_element_type=jnp.float32,
        precision=lax.Precision.HIGHEST,
    )


def local(likelihood, block_ids, slot_valid, start_weights):
    cols = likelihood.shape[3]
    n = lax.axis_size(ALL)
    owned = start_weights.reshape(-1, cols)
    own_blocks = owned.shape[0]
    blocks = own_blocks * n
    total_reads = likelihood.shape[0] * lax.axis_size("reads") * likelihood.shape[2]
    scale = blocks * cols / total_reads
    for step in range(ITERS):
        table = spread(owned, ALL).reshape(blocks, cols)
        summer = sum_genome_steps if step == 0 else sum_genome_direct
        counts = local_counts(table, likelihood, block_ids, slot_valid, summer)
        parts = lax.all_to_all(counts.reshape(n, own_blocks, cols), ALL, 0, 0, tiled=True)
        owned = jnp.sum(parts, axis=0) * scale
    return owned.reshape(-1)


def solution(mesh):
    placed = (
        P(("parts", "reads"), "genome", None, None),
        P(("parts", "reads"), "genome"),
        P(("parts", "reads"), "genome"),
        P(("parts", "genome", "reads")),
    )
    return jax.shard_map(
        local,
        mesh=mesh,
        in_specs=placed,
        out_specs=P(("parts", "genome", "reads")),
        check_vma=False,
    )
```

```python
import jax
import jax.numpy as jnp
from jax import lax
from jax.sharding import PartitionSpec as P

ITERS = 2
ALL = ("genome", "reads")


def radices(n):
    out = []
    while n > 1:
        r = 4 if n % 4 == 0 else 2
        out.append(r)
        n //= r
    return out


def swap(x, axes, k):
    n = lax.axis_size(axes)
    return lax.ppermute(x, axes, [(i, i ^ k) for i in range(n)])


def tree_sum(parts):
    while len(parts) > 1:
        parts = [a + b for a, b in zip(parts[::2], parts[1::2])] + (
            [parts[-1]] if len(parts) % 2 else []
        )
    return parts[0]


def position(k, n):
    place = 0
    for r in radices(n):
        n //= r
        place = place + (k % r) * n
        k = k // r
    return place


def scatter_sum(x, axes):
    stride = 1
    for r in radices(lax.axis_size(axes)):
        rows = x.shape[0] // r
        parts = [x[j * rows : (j + 1) * rows] for j in range(r)]
        x = tree_sum([parts[0]] + [swap(parts[j], axes, j * stride) for j in range(1, r)])
        stride *= r
    return x


def gather(x, axes):
    stride = lax.axis_size(axes)
    for r in radices(stride)[::-1]:
        stride //= r
        x = jnp.concatenate([x] + [swap(x, axes, j * stride) for j in range(1, r)], axis=0)
    return x


def sum_all(x, axes):
    n = lax.axis_size(axes)
    stride = 1
    for r in radices(n)[::-1]:
        x = tree_sum([x] + [swap(x, axes, j * stride) for j in range(1, r)])
        stride *= r
    return x


def local(likelihood, block_ids, slot_valid, start_weights):
    cols = likelihood.shape[3]
    n = lax.axis_size(ALL)
    me = lax.axis_index(ALL)
    owned = start_weights.reshape(-1, cols)
    own_blocks = owned.shape[0]
    blocks = own_blocks * n
    total_reads = likelihood.shape[0] * lax.axis_size("reads") * likelihood.shape[2]
    scale = blocks * cols / total_reads
    place = position((block_ids // own_blocks) ^ me, n) * own_blocks + block_ids % own_blocks
    valid = slot_valid.astype(jnp.float32)[:, :, None]
    one_hot = (
        place.reshape(-1)[None, :] == jnp.arange(blocks, dtype=jnp.int32)[:, None]
    ).astype(jnp.float32)
    lik_float = likelihood.astype(jnp.float32)
    for step in range(ITERS):
        table = gather(owned, ALL)
        picked = table[place] * valid
        row_part = jnp.sum(lik_float * picked[:, :, None, :], axis=(1, 3))
        inverse = 1.0 / sum_all(row_part, "genome")
        contrib = picked * jnp.sum(lik_float * inverse[:, None, :, None], axis=2)
        counts = jnp.dot(
            one_hot,
            contrib.reshape(-1, cols),
            preferred_element_type=jnp.float32,
            precision=lax.Precision.HIGHEST,
        )
        owned = scatter_sum(counts, ALL) * scale
    return owned.reshape(-1)


def solution(mesh):
    placed = (
        P(("parts", "reads"), "genome", None, None),
        P(("parts", "reads"), "genome"),
        P(("parts", "reads"), "genome"),
        P(("parts", "genome", "reads")),
    )
    return jax.shard_map(
        local,
        mesh=mesh,
        in_specs=placed,
        out_specs=P(("parts", "genome", "reads")),
        check_vma=False,
    )
```

```python
import jax
import jax.numpy as jnp
from jax import lax
from jax.experimental import pallas as pl
from jax.experimental.pallas import tpu as pltpu
from jax.sharding import PartitionSpec as P

ITERS = 2
ALL = ("genome", "reads")
TERMS = 16


def radices(n):
    out = []
    while n > 1:
        r = 4 if n % 4 == 0 else 2
        out.append(r)
        n //= r
    return out


def swap(x, axes, k):
    n = lax.axis_size(axes)
    return lax.ppermute(x, axes, [(i, i ^ k) for i in range(n)])


def tree_sum(parts):
    while len(parts) > 1:
        parts = [a + b for a, b in zip(parts[::2], parts[1::2])] + (
            [parts[-1]] if len(parts) % 2 else []
        )
    return parts[0]


def position(k, n):
    place = 0
    for r in radices(n):
        n //= r
        place = place + (k % r) * n
        k = k // r
    return place


def scatter_sum(x, axes):
    stride = 1
    for r in radices(lax.axis_size(axes)):
        rows = x.shape[0] // r
        parts = [x[j * rows : (j + 1) * rows] for j in range(r)]
        x = tree_sum([parts[0]] + [swap(parts[j], axes, j * stride) for j in range(1, r)])
        stride *= r
    return x


def gather_high(x, axes):
    stride = lax.axis_size(axes)
    for r in radices(stride)[:0:-1]:
        stride //= r
        x = jnp.concatenate([x] + [swap(x, axes, j * stride) for j in range(1, r)], axis=0)
    return x


def spread(x, axes):
    n = lax.axis_size(axes)
    sent = jnp.broadcast_to(x[None], (n,) + x.shape)
    return lax.all_to_all(sent, axes, 0, 0, tiled=True)


def dot_exact(a, b):
    return jnp.dot(
        a, b, preferred_element_type=jnp.float32, precision=lax.Precision.HIGHEST
    )


def split(row):
    x = jnp.broadcast_to(row, (TERMS, row.shape[1]))
    hi = x.astype(jnp.bfloat16).astype(jnp.float32)
    rest = x - hi
    mid = rest.astype(jnp.bfloat16).astype(jnp.float32)
    low = rest - mid
    at = lax.broadcasted_iota(jnp.int32, x.shape, 0)
    out = jnp.where(at == 0, hi, jnp.where(at == 1, mid, jnp.where(at == 2, low, 0.0)))
    return out.astype(jnp.bfloat16)


def row_kernel(picked_ref, lik_ref, out_ref):
    read_blocks, slots, reads, cols = lik_ref.shape
    for b in range(read_blocks):
        total = None
        for s in range(0, slots, 2):
            at = b * slots + s
            left = jnp.concatenate(
                [split(picked_ref[at : at + 1, :]), split(picked_ref[at + 1 : at + 2, :])], axis=1
            )
            right = jnp.concatenate([lik_ref[b, s], lik_ref[b, s + 1]], axis=1)
            part = lax.dot_general(
                left, right, (((1,), (1,)), ((), ())), preferred_element_type=jnp.float32
            )
            total = part if total is None else total + part
        out_ref[b : b + 1, :] = jnp.sum(total, axis=0, keepdims=True)


def col_kernel(parts_ref, picked_ref, lik_ref, out_ref, inverse_ref):
    read_blocks, slots, reads, cols = lik_ref.shape
    total = parts_ref[0]
    for i in range(1, parts_ref.shape[0]):
        total = total + parts_ref[i]
    inverse_ref[...] = 1.0 / total
    for b in range(read_blocks):
        left = split(inverse_ref[b : b + 1, :])
        for s in range(0, slots, 2):
            at = b * slots + s
            right = jnp.concatenate([lik_ref[b, s], lik_ref[b, s + 1]], axis=1)
            part = jnp.dot(left, right, preferred_element_type=jnp.float32)
            summed = jnp.sum(part, axis=0, keepdims=True)
            out_ref[at : at + 1, :] = picked_ref[at : at + 1, :] * summed[:, :cols]
            out_ref[at + 1 : at + 2, :] = picked_ref[at + 1 : at + 2, :] * summed[:, cols:]


def call(kernel, shape, scratch, *operands):
    vmem = pl.BlockSpec(memory_space=pltpu.VMEM)
    return pl.pallas_call(
        kernel,
        out_shape=jax.ShapeDtypeStruct(shape, jnp.float32),
        in_specs=[vmem] * len(operands),
        out_specs=vmem,
        scratch_shapes=scratch,
        compiler_params=pltpu.CompilerParams(vmem_limit_bytes=40 * 2**20),
    )(*operands)


def local(likelihood, block_ids, slot_valid, start_weights):
    read_blocks, slots, reads, cols = likelihood.shape
    n = lax.axis_size(ALL)
    me = lax.axis_index(ALL)
    near = radices(n)[0]
    own_weights = start_weights.reshape(-1, cols)
    own_blocks = own_weights.shape[0]
    blocks = own_blocks * n
    all_slots = read_blocks * slots
    total_reads = read_blocks * lax.axis_size("reads") * reads
    scale = blocks * cols / total_reads
    likelihood = pltpu.with_memory_space_constraint(likelihood, pltpu.VMEM)

    ids = block_ids.reshape(-1)
    valid = slot_valid.reshape(-1)
    owner = position((ids // own_blocks) ^ me, n)

    id_rows = -(-all_slots // cols)
    rows = -(-(own_blocks + id_rows) // 8) * 8
    coded = jnp.where(valid > 0, ids, -1).astype(jnp.float32)
    coded = jnp.pad(coded, (0, id_rows * cols - all_slots)).reshape(id_rows, cols)
    sent = jnp.pad(
        jnp.concatenate([own_weights, coded], axis=0), ((0, rows - own_blocks - id_rows), (0, 0))
    )
    far = gather_high(sent, ALL)
    full = jnp.concatenate([far] + [swap(far, ALL, j) for j in range(1, near)], axis=0)
    every = full.reshape(near, n // near, rows, cols)
    known = every[:, :, own_blocks : own_blocks + id_rows].reshape(near, n // near, -1)
    known = known[:, :, :all_slots]
    wanted = known[:, 0].reshape(-1)
    given = known[0].reshape(-1)
    match = ((wanted[:, None] == given[None, :]) & (wanted[:, None] >= 0)).astype(jnp.float32)

    place = jnp.where(valid > 0, owner * rows + ids % own_blocks, -1)
    pick = (place[:, None] == jnp.arange(n * rows, dtype=jnp.int32)[None, :]).astype(jnp.float32)
    picked = dot_exact(pick, full)

    for step in range(ITERS):
        row_part = call(row_kernel, (read_blocks, reads), [], picked, likelihood)
        row_parts = spread(row_part, "genome")
        contrib = call(
            col_kernel,
            (all_slots, cols),
            [pltpu.VMEM((read_blocks, reads), jnp.float32)],
            row_parts,
            picked,
            likelihood,
        )
        if step + 1 < ITERS:
            sums = dot_exact(match, gather_high(contrib, ALL))
            parts = [sums[j * all_slots : (j + 1) * all_slots] for j in range(near)]
            picked = scale * tree_sum(
                [parts[0]] + [swap(parts[j], ALL, j) for j in range(1, near)]
            )

    place = owner * own_blocks + ids % own_blocks
    count = (jnp.arange(blocks, dtype=jnp.int32)[:, None] == place[None, :]).astype(jnp.float32)
    return (scatter_sum(dot_exact(count, contrib), ALL) * scale).reshape(-1)


def solution(mesh):
    placed = (
        P(("parts", "reads"), "genome", None, None),
        P(("parts", "reads"), "genome"),
        P(("parts", "reads"), "genome"),
        P(("parts", "genome", "reads")),
    )
    return jax.shard_map(
        local,
        mesh=mesh,
        in_specs=placed,
        out_specs=P(("parts", "genome", "reads")),
        check_vma=False,
    )
```

```python
import jax
import jax.numpy as jnp
from jax import lax
from jax.experimental import pallas as pl
from jax.experimental.pallas import tpu as pltpu
from jax.sharding import PartitionSpec as P

ITERS = 2
ALL = ("genome", "reads")
TERMS = 16


def radices(n):
    out = []
    while n > 1:
        r = 4 if n % 4 == 0 else 2
        out.append(r)
        n //= r
    return out


def swap(x, axes, k):
    n = lax.axis_size(axes)
    return lax.ppermute(x, axes, [(i, i ^ k) for i in range(n)])


def tree_sum(parts):
    while len(parts) > 1:
        parts = [a + b for a, b in zip(parts[::2], parts[1::2])] + (
            [parts[-1]] if len(parts) % 2 else []
        )
    return parts[0]


def far_groups(axes, near):
    n = lax.axis_size(axes)
    return [list(range(i, n, near)) for i in range(near)]


def spread(x, axes, near):
    count = lax.axis_size(axes) // near
    sent = jnp.broadcast_to(x[None], (count,) + x.shape)
    return lax.all_to_all(
        sent, axes, 0, 0, tiled=True, axis_index_groups=far_groups(axes, near)
    )


def dot_exact(a, b):
    return jnp.dot(
        a, b, preferred_element_type=jnp.float32, precision=lax.Precision.HIGHEST
    )


def split(row):
    x = jnp.broadcast_to(row, (TERMS, row.shape[1]))
    hi = x.astype(jnp.bfloat16).astype(jnp.float32)
    rest = x - hi
    mid = rest.astype(jnp.bfloat16).astype(jnp.float32)
    low = rest - mid
    at = lax.broadcasted_iota(jnp.int32, x.shape, 0)
    out = jnp.where(at == 0, hi, jnp.where(at == 1, mid, jnp.where(at == 2, low, 0.0)))
    return out.astype(jnp.bfloat16)


def row_kernel(picked_ref, lik_ref, out_ref):
    read_blocks, slots, reads, cols = lik_ref.shape
    for b in range(read_blocks):
        total = None
        for s in range(0, slots, 2):
            at = b * slots + s
            left = jnp.concatenate(
                [split(picked_ref[at : at + 1, :]), split(picked_ref[at + 1 : at + 2, :])], axis=1
            )
            right = jnp.concatenate([lik_ref[b, s], lik_ref[b, s + 1]], axis=1)
            part = lax.dot_general(
                left, right, (((1,), (1,)), ((), ())), preferred_element_type=jnp.float32
            )
            total = part if total is None else total + part
        out_ref[b : b + 1, :] = jnp.sum(total, axis=0, keepdims=True)


def col_kernel(parts_ref, picked_ref, lik_ref, out_ref, inverse_ref):
    read_blocks, slots, reads, cols = lik_ref.shape
    total = parts_ref[0]
    for i in range(1, parts_ref.shape[0]):
        total = total + parts_ref[i]
    inverse_ref[...] = 1.0 / total
    for b in range(read_blocks):
        left = split(inverse_ref[b : b + 1, :])
        for s in range(0, slots, 2):
            at = b * slots + s
            right = jnp.concatenate([lik_ref[b, s], lik_ref[b, s + 1]], axis=1)
            part = jnp.dot(left, right, preferred_element_type=jnp.float32)
            summed = jnp.sum(part, axis=0, keepdims=True)
            out_ref[at : at + 1, :] = picked_ref[at : at + 1, :] * summed[:, :cols]
            out_ref[at + 1 : at + 2, :] = picked_ref[at + 1 : at + 2, :] * summed[:, cols:]


def pack_kernel(weights_ref, ids_ref, valid_ref, out_ref, wide_ref):
    own_blocks = weights_ref.shape[0]
    read_blocks, slots = ids_ref.shape
    wide_ref[...] = jnp.zeros_like(wide_ref)
    coded = jnp.where(valid_ref[...] > 0, ids_ref[...], -1)
    wide_ref[:, :slots] = coded.astype(jnp.float32)
    rolled = pltpu.roll(wide_ref[...], 0, 1, stride=slots, stride_axis=0)
    out_ref[...] = jnp.zeros_like(out_ref)
    out_ref[:own_blocks, :] = weights_ref[...]
    out_ref[own_blocks : own_blocks + 1, :] = jnp.sum(rolled, axis=0, keepdims=True)


def load_kernel(source_ref, out_ref, sems):
    copies = [
        pltpu.make_async_copy(source_ref.at[b], out_ref.at[b], sems.at[b])
        for b in range(out_ref.shape[0])
    ]
    for copy in copies:
        copy.start()
    for copy in copies:
        copy.wait()


def load(x):
    return pl.pallas_call(
        load_kernel,
        out_shape=pltpu.VMEM(x.shape, x.dtype),
        in_specs=[pl.BlockSpec(memory_space=pl.ANY)],
        out_specs=pl.BlockSpec(memory_space=pltpu.VMEM),
        scratch_shapes=[pltpu.SemaphoreType.DMA((x.shape[0],))],
        compiler_params=pltpu.CompilerParams(vmem_limit_bytes=16 * 2**20),
    )(x)


def call(kernel, shape, scratch, *operands):
    vmem = pl.BlockSpec(memory_space=pltpu.VMEM)
    return pl.pallas_call(
        kernel,
        out_shape=jax.ShapeDtypeStruct(shape, jnp.float32),
        in_specs=[vmem] * len(operands),
        out_specs=vmem,
        scratch_shapes=scratch,
        compiler_params=pltpu.CompilerParams(vmem_limit_bytes=16 * 2**20),
    )(*operands)


def local(likelihood, block_ids, slot_valid, start_weights):
    read_blocks, slots, reads, cols = likelihood.shape
    n = lax.axis_size(ALL)
    me = lax.axis_index(ALL)
    near = radices(n)[0]
    far = n // near
    own_weights = start_weights.reshape(-1, cols)
    own_blocks = own_weights.shape[0]
    blocks = own_blocks * n
    all_slots = read_blocks * slots
    total_reads = read_blocks * lax.axis_size("reads") * reads
    scale = blocks * cols / total_reads
    held = load(pltpu.with_memory_space_constraint(likelihood, pltpu.HBM))

    rows = -(-(own_blocks + 1) // 8) * 8
    sent = call(
        pack_kernel,
        (rows, cols),
        [pltpu.VMEM((read_blocks, cols), jnp.float32)],
        own_weights,
        block_ids,
        slot_valid,
    )
    column = spread(sent, ALL, near).reshape(far * rows, cols)
    full = jnp.concatenate([column] + [swap(column, ALL, j) for j in range(1, near)], axis=0)

    ids = block_ids.reshape(-1)
    valid = slot_valid.reshape(-1)
    owner = ids // own_blocks
    owner = ((owner % near) ^ (me % near)) * far + owner // near
    place = jnp.where(valid > 0, owner * rows + ids % own_blocks, -1)
    pick = (place[:, None] == jnp.arange(n * rows, dtype=jnp.int32)[None, :]).astype(jnp.float32)
    picked = dot_exact(pick, full)

    known = full.reshape(near, far, rows, cols)[:, :, own_blocks, :all_slots]
    wanted = lax.dynamic_index_in_dim(known, me // near, 1, keepdims=False).reshape(-1)
    given = known[0].reshape(-1)
    match = ((wanted[:, None] == given[None, :]) & (wanted[:, None] >= 0)).astype(jnp.float32)

    for step in range(ITERS):
        row_part = call(row_kernel, (read_blocks, reads), [], picked, held)
        row_part = row_part + swap(row_part, "genome", 1)
        row_parts = spread(row_part, "genome", 2)
        contrib = call(
            col_kernel,
            (all_slots, cols),
            [pltpu.VMEM((read_blocks, reads), jnp.float32)],
            row_parts,
            picked,
            held,
        )
        if step + 1 < ITERS:
            column = spread(contrib, ALL, near).reshape(far * all_slots, cols)
            sums = dot_exact(match, column)
            parts = [sums[j * all_slots : (j + 1) * all_slots] for j in range(near)]
            picked = scale * tree_sum(
                [parts[0]] + [swap(parts[j], ALL, j) for j in range(1, near)]
            )

    place = owner * own_blocks + ids % own_blocks
    count = (jnp.arange(blocks, dtype=jnp.int32)[:, None] == place[None, :]).astype(jnp.float32)
    counts = dot_exact(count, contrib)
    share = far * own_blocks
    parts = [counts[j * share : (j + 1) * share] for j in range(near)]
    counts = tree_sum([parts[0]] + [swap(parts[j], ALL, j) for j in range(1, near)])
    counts = lax.all_to_all(
        counts.reshape(far, own_blocks, cols),
        ALL,
        0,
        0,
        tiled=True,
        axis_index_groups=far_groups(ALL, near),
    )
    return (jnp.sum(counts, axis=0) * scale).reshape(-1)


def solution(mesh):
    placed = (
        P(("parts", "reads"), "genome", None, None),
        P(("parts", "reads"), "genome"),
        P(("parts", "reads"), "genome"),
        P(("parts", "genome", "reads")),
    )
    return jax.shard_map(
        local,
        mesh=mesh,
        in_specs=placed,
        out_specs=P(("parts", "genome", "reads")),
        check_vma=False,
    )
```

```python
import jax
import jax.numpy as jnp
from jax import lax
from jax.experimental import pallas as pl
from jax.experimental.pallas import tpu as pltpu
from jax.sharding import PartitionSpec as P

ITERS = 2
ALL = ("genome", "reads")
TERMS = 16
ID_ROWS = 8
LANES = 128
VMEM = pl.BlockSpec(memory_space=pltpu.VMEM)
ANY = pl.BlockSpec(memory_space=pl.ANY)


def radices(n):
    out = []
    while n > 1:
        r = 4 if n % 4 == 0 else 2
        out.append(r)
        n //= r
    return out


def swap(x, axes, k):
    n = lax.axis_size(axes)
    return lax.ppermute(x, axes, [(i, i ^ k) for i in range(n)])


def position(k, n):
    place = 0
    for r in radices(n):
        n //= r
        place = place + (k % r) * n
        k = k // r
    return place


def gather_far(x, axes):
    parts = [x]
    stride = lax.axis_size(axes)
    for r in radices(stride)[:0:-1]:
        stride //= r
        sent = parts[0] if len(parts) == 1 else jnp.concatenate(parts, axis=0)
        parts = [sent] + [swap(sent, axes, j * stride) for j in range(1, r)]
    return parts


def dot(a, b, dims=(((1,), (0,)), ((), ()))):
    return lax.dot_general(a, b, dims, preferred_element_type=jnp.float32)


def terms(x):
    hi = x.astype(jnp.bfloat16)
    rest = x - hi.astype(jnp.float32)
    mid = rest.astype(jnp.bfloat16)
    return hi, mid, (rest - mid.astype(jnp.float32)).astype(jnp.bfloat16)


def select_rows(hot, x):
    hi, mid, low = terms(x)
    hot = hot.astype(jnp.bfloat16)
    return dot(hot, hi) + dot(hot, mid) + dot(hot, low)


def split(row):
    x = jnp.broadcast_to(row, (TERMS, row.shape[1]))
    hi = x.astype(jnp.bfloat16).astype(jnp.float32)
    rest = x - hi
    mid = rest.astype(jnp.bfloat16).astype(jnp.float32)
    low = rest - mid
    at = lax.broadcasted_iota(jnp.int32, x.shape, 0)
    out = jnp.where(at == 0, hi, jnp.where(at == 1, mid, jnp.where(at == 2, low, 0.0)))
    return out.astype(jnp.bfloat16)


def down(row):
    return jnp.transpose(jnp.broadcast_to(row, (LANES, LANES)))


def hot_rows(values, count):
    column = down(values)
    blocks = []
    for start in range(0, count, LANES):
        width = min(LANES, count - start)
        lane = lax.broadcasted_iota(jnp.int32, (LANES, width), 1).astype(jnp.float32) + start
        blocks.append((column[:, :width] == lane).astype(jnp.float32))
    return blocks[0] if len(blocks) == 1 else jnp.concatenate(blocks, axis=1)


def prepare_kernel(own_blocks, lik_ref, ids_ref, valid_ref, held_ref, info_ref, ids, valid, wide, sems):
    read_blocks, slots = ids.shape
    copies = [
        pltpu.make_async_copy(ids_ref, ids, sems.at[0]),
        pltpu.make_async_copy(valid_ref, valid, sems.at[1]),
    ]
    held = [
        pltpu.make_async_copy(lik_ref.at[b], held_ref.at[b], sems.at[2 + b])
        for b in range(held_ref.shape[0])
    ]
    for copy in copies + held:
        copy.start()
    for copy in copies:
        copy.wait()
    n = lax.axis_size(ALL)
    near = radices(n)[0]
    far = n // near
    me = lax.axis_index("genome") * lax.axis_size("reads") + lax.axis_index("reads")
    lane = lax.broadcasted_iota(jnp.int32, wide.shape, 1)
    wide[...] = jnp.zeros_like(wide)
    wide[:, :slots] = jnp.where(valid[...] > 0, ids[...], -1).astype(jnp.float32)
    flat = jnp.sum(
        pltpu.roll(wide[...], 0, 1, stride=slots, stride_axis=0), axis=0, keepdims=True
    )
    flat = jnp.where(lane[:1] < read_blocks * slots, flat, -1.0)
    owner = ((flat + 0.5) * (1.0 / own_blocks)).astype(jnp.int32)
    inside = flat.astype(jnp.int32) - owner * own_blocks
    away = owner ^ me
    place = position(away, n)
    place = (place // far) * near_rows(far, own_blocks) + (place % far) * own_blocks + inside
    place = jnp.where(flat < 0, -1, place).astype(jnp.float32)
    row = lax.broadcasted_iota(jnp.int32, info_ref.shape, 0)
    info_ref[...] = jnp.where(row == 0, flat, jnp.where(row == 1, place, 0.0))
    for copy in held:
        copy.wait()


def join_kernel(*refs):
    out_ref = refs[-1]
    at = 0
    for ref in refs[:-1]:
        out_ref[at : at + ref.shape[0], :] = ref[...]
        at += ref.shape[0]
    if at < out_ref.shape[0]:
        out_ref[at:, :] = jnp.zeros((out_ref.shape[0] - at, out_ref.shape[1]), jnp.float32)


def near_rows(far, own_blocks):
    return -(-(far * own_blocks + ID_ROWS) // 16) * 16


def row_sums(picked_ref, lik_ref, out_ref):
    read_blocks, slots, reads, cols = lik_ref.shape
    for b in range(read_blocks):
        total = None
        for s in range(0, slots, 2):
            at = b * slots + s
            left = jnp.concatenate(
                [split(picked_ref[at : at + 1, :]), split(picked_ref[at + 1 : at + 2, :])], axis=1
            )
            right = jnp.concatenate([lik_ref[b, s], lik_ref[b, s + 1]], axis=1)
            part = dot(left, right, (((1,), (1,)), ((), ())))
            total = part if total is None else total + part
        row = jnp.sum(total, axis=0, keepdims=True)
        for i in range(out_ref.shape[0]):
            out_ref[i, b : b + 1, :] = row


def first_row_kernel(near, info_ref, *refs):
    pieces, (lik_ref, out_ref, picked_ref) = refs[:near], refs[near:]
    table = jnp.concatenate([piece[...] for piece in pieces], axis=0)
    hot = hot_rows(info_ref[1:2, :], table.shape[0])
    picked_ref[...] = select_rows(hot[: picked_ref.shape[0]], table)
    row_sums(picked_ref, lik_ref, out_ref)


def next_row_kernel(near, scale, *refs):
    parts, (lik_ref, out_ref, picked_ref) = refs[:near], refs[near:]
    total = parts[0][...]
    for part in parts[1:]:
        total = total + part[...]
    picked_ref[...] = total * scale
    row_sums(picked_ref, lik_ref, out_ref)


def column_sums(parts_ref, picked_ref, lik_ref, contrib_ref, inverse_ref):
    read_blocks, slots, reads, cols = lik_ref.shape
    total = parts_ref[0]
    for i in range(1, parts_ref.shape[0]):
        total = total + parts_ref[i]
    inverse_ref[...] = 1.0 / total
    for b in range(read_blocks):
        left = split(inverse_ref[b : b + 1, :])
        for s in range(0, slots, 2):
            at = b * slots + s
            right = jnp.concatenate([lik_ref[b, s], lik_ref[b, s + 1]], axis=1)
            summed = jnp.sum(dot(left, right), axis=0, keepdims=True)
            contrib_ref[at : at + 1, :] = picked_ref[at : at + 1, :] * summed[:, :cols]
            contrib_ref[at + 1 : at + 2, :] = picked_ref[at + 1 : at + 2, :] * summed[:, cols:]


def column_kernel(info_ref, parts_ref, picked_ref, lik_ref, out_ref, inverse_ref):
    column_sums(parts_ref, picked_ref, lik_ref, out_ref, inverse_ref)
    out_ref[picked_ref.shape[0] :, :] = info_ref[...]


def last_column_kernel(info_ref, parts_ref, picked_ref, lik_ref, out_ref, inverse_ref, contrib_ref):
    column_sums(parts_ref, picked_ref, lik_ref, contrib_ref, inverse_ref)
    owners, own_blocks, cols = out_ref.shape
    all_slots = contrib_ref.shape[0]
    block = lax.broadcasted_iota(jnp.int32, (owners * own_blocks, all_slots), 0)
    hot = (block.astype(jnp.float32) == info_ref[0:1, :all_slots]).astype(jnp.float32)
    counts = select_rows(hot, contrib_ref[...])
    for i in range(owners):
        out_ref[i] = counts[i * own_blocks : (i + 1) * own_blocks, :]


def wanted_kernel(near, all_slots, pieces, *refs):
    given_refs, wanted, outs = refs[:pieces], refs[pieces : pieces + near], refs[pieces + near :]
    rows = all_slots + ID_ROWS
    half = LANES // 2
    lane = lax.broadcasted_iota(jnp.int32, (1, LANES), 1)
    ids, values = [], []
    for ref in given_refs:
        for at in range(0, ref.shape[0], rows):
            ids.append(ref[at + all_slots : at + all_slots + 1, :])
            values.append(ref[at : at + all_slots, :])
    pairs = [
        jnp.where(lane < half, a, pltpu.roll(b, half, 1)) for a, b in zip(ids[::2], ids[1::2])
    ]
    given = terms(jnp.concatenate(values, axis=0))
    for ids_ref, out_ref in zip(wanted, outs):
        column = down(ids_ref[0:1, :])[:all_slots]
        hot = jnp.concatenate([(column == pair).astype(jnp.float32) for pair in pairs], axis=1)
        hot = hot.astype(jnp.bfloat16)
        out_ref[...] = dot(hot, given[0]) + dot(hot, given[1]) + dot(hot, given[2])


def call(kernel, outs, scratch, *operands):
    return pl.pallas_call(
        kernel,
        out_shape=[jax.ShapeDtypeStruct(shape, jnp.float32) for shape in outs],
        in_specs=[VMEM] * len(operands),
        out_specs=[VMEM] * len(outs),
        scratch_shapes=[pltpu.VMEM(shape, jnp.float32) for shape in scratch],
        compiler_params=pltpu.CompilerParams(vmem_limit_bytes=16 * 2**20),
    )(*operands)


def prepare(own_blocks, likelihood, block_ids, slot_valid):
    read_blocks, slots = block_ids.shape
    return pl.pallas_call(
        lambda *refs: prepare_kernel(own_blocks, *refs),
        out_shape=[
            pltpu.VMEM(likelihood.shape, likelihood.dtype),
            jax.ShapeDtypeStruct((ID_ROWS, LANES), jnp.float32),
        ],
        in_specs=[ANY] * 3,
        out_specs=[VMEM] * 2,
        scratch_shapes=[
            pltpu.VMEM((read_blocks, slots), jnp.int32),
            pltpu.VMEM((read_blocks, slots), jnp.int32),
            pltpu.VMEM((read_blocks, LANES), jnp.float32),
            pltpu.SemaphoreType.DMA((2 + read_blocks,)),
        ],
        compiler_params=pltpu.CompilerParams(vmem_limit_bytes=16 * 2**20),
    )(*[pltpu.with_memory_space_constraint(x, pltpu.HBM) for x in (likelihood, block_ids, slot_valid)])


def local(likelihood, block_ids, slot_valid, start_weights):
    read_blocks, slots, reads, cols = likelihood.shape
    n = lax.axis_size(ALL)
    chips = lax.axis_size("genome")
    near = radices(n)[0]
    far = n // near
    own_weights = start_weights.reshape(-1, cols)
    own_blocks = own_weights.shape[0]
    all_slots = read_blocks * slots
    total_reads = read_blocks * lax.axis_size("reads") * reads
    scale = n * own_blocks * cols / total_reads

    column = gather_far(own_weights, ALL)
    held, info = prepare(own_blocks, likelihood, block_ids, slot_valid)
    (sent,) = call(join_kernel, [(near_rows(far, own_blocks), cols)], [], *column, info)
    pieces = [sent] + [swap(sent, ALL, j) for j in range(1, near)]
    at = far * own_blocks
    wanted = [info] + [piece[at : at + ID_ROWS] for piece in pieces[1:]]

    row_shapes = [(chips, read_blocks, reads), (all_slots, cols)]
    inverse = (read_blocks, reads)
    for step in range(ITERS):
        if step == 0:
            row_parts, picked = call(
                lambda *refs: first_row_kernel(near, *refs), row_shapes, [], info, *pieces, held
            )
        else:
            row_parts, picked = call(
                lambda *refs: next_row_kernel(near, scale, *refs), row_shapes, [], *parts, held
            )
        row_parts = lax.all_to_all(row_parts, "genome", 0, 0, tiled=True)
        if step + 1 < ITERS:
            (contrib,) = call(
                column_kernel,
                [(all_slots + ID_ROWS, cols)],
                [inverse],
                info,
                row_parts,
                picked,
                held,
            )
            given = gather_far(contrib, ALL)
            sums = call(
                lambda *refs: wanted_kernel(near, all_slots, len(given), *refs),
                [(all_slots, cols)] * near,
                [],
                *given,
                *wanted,
            )
            parts = [sums[0]] + [swap(sums[j], ALL, j) for j in range(1, near)]
    (counts,) = call(
        last_column_kernel,
        [(n, own_blocks, cols)],
        [inverse, (all_slots, cols)],
        info,
        row_parts,
        picked,
        held,
    )
    counts = lax.all_to_all(counts, ALL, 0, 0, tiled=True)
    return (jnp.sum(counts, axis=0) * scale).reshape(-1)


def solution(mesh):
    placed = (
        P(("parts", "reads"), "genome", None, None),
        P(("parts", "reads"), "genome"),
        P(("parts", "reads"), "genome"),
        P(("parts", "genome", "reads")),
    )
    return jax.shard_map(
        local,
        mesh=mesh,
        in_specs=placed,
        out_specs=P(("parts", "genome", "reads")),
        check_vma=False,
    )
```

```python
import jax
import jax.numpy as jnp
from jax import lax
from jax.experimental import pallas as pl
from jax.experimental.pallas import tpu as pltpu
from jax.sharding import PartitionSpec as P

ITERS = 2
ALL = ("genome", "reads")
TERMS = 16
ID_ROWS = 8
NEAR = 4
LANES = 128
VMEM = pl.BlockSpec(memory_space=pltpu.VMEM)
ANY = pl.BlockSpec(memory_space=pl.ANY)


def radices(n):
    out = []
    while n > 1:
        r = 4 if n % 4 == 0 else 2
        out.append(r)
        n //= r
    return out


def swap(x, k):
    return lax.ppermute(x, ALL, [(i, i ^ k) for i in range(lax.axis_size(ALL))])


def near_swaps(parts):
    return [parts[0]] + [swap(parts[j], j) for j in range(1, len(parts))]


def far_radices():
    return radices(lax.axis_size(ALL) // NEAR)


def far_swaps(first, second, r, stride):
    everyone = range(lax.axis_size(ALL))
    if r == 2:
        got = lax.ppermute(first, ALL, [(i, i ^ stride) for i in everyone if i % 2])
        return [got]
    pairs = [(i, i ^ (2 * stride if i % 2 else stride)) for i in everyone]
    got = lax.ppermute(first, ALL, pairs)
    pairs = [(i, i ^ (3 * stride)) for i in everyone if i % 2]
    return [got, lax.ppermute(second, ALL, pairs)]


def dot(a, b, dims=(((1,), (0,)), ((), ()))):
    return lax.dot_general(a, b, dims, preferred_element_type=jnp.float32)


def terms(x):
    hi = x.astype(jnp.bfloat16)
    rest = x - hi.astype(jnp.float32)
    mid = rest.astype(jnp.bfloat16)
    return hi, mid, (rest - mid.astype(jnp.float32)).astype(jnp.bfloat16)


def select_rows(hot, x):
    hi, mid, low = terms(x)
    hot = hot.astype(jnp.bfloat16)
    return dot(hot, hi) + dot(hot, mid) + dot(hot, low)


def split(row):
    x = jnp.broadcast_to(row, (TERMS, row.shape[1]))
    hi = x.astype(jnp.bfloat16).astype(jnp.float32)
    rest = x - hi
    mid = rest.astype(jnp.bfloat16).astype(jnp.float32)
    low = rest - mid
    at = lax.broadcasted_iota(jnp.int32, x.shape, 0)
    out = jnp.where(at == 0, hi, jnp.where(at == 1, mid, jnp.where(at == 2, low, 0.0)))
    return out.astype(jnp.bfloat16)


def down(row):
    return jnp.transpose(jnp.broadcast_to(row, (LANES, LANES)))


def hot_rows(values, count):
    column = down(values)
    blocks = []
    for start in range(0, count, LANES):
        width = min(LANES, count - start)
        lane = lax.broadcasted_iota(jnp.int32, (LANES, width), 1).astype(jnp.float32) + start
        blocks.append((column[:, :width] == lane).astype(jnp.float32))
    return blocks[0] if len(blocks) == 1 else jnp.concatenate(blocks, axis=1)


def on_core_0():
    return lax.axis_index("reads") == 0


def far_place(owner, own_blocks):
    k = owner ^ (lax.axis_index("genome") * 2 + lax.axis_index("reads"))
    row = (owner % 2) * own_blocks
    size = 2 * own_blocks
    rest = k // NEAR
    half = 0 * rest
    radix = far_radices()
    for i, r in enumerate(radix):
        digit = rest % r
        rest = rest // r
        if i + 1 == len(radix):
            half = digit // (r // 2)
            digit = digit % (r // 2)
        row = row + digit * size
        size *= r
    return (k // 2) % 2 * 2 + (half ^ lax.axis_index("reads")), row


def near_rows(own_rows):
    return -(-(own_rows + ID_ROWS) // 16) * 16


def prepare_kernel(own_blocks, lik_ref, ids_ref, valid_ref, held_ref, info_ref, ids, valid, wide, sems):
    read_blocks, slots = ids.shape
    copies = [
        pltpu.make_async_copy(ids_ref, ids, sems.at[0]),
        pltpu.make_async_copy(valid_ref, valid, sems.at[1]),
    ]
    held = [
        pltpu.make_async_copy(lik_ref.at[b], held_ref.at[b], sems.at[2 + b])
        for b in range(held_ref.shape[0])
    ]
    for copy in copies + held:
        copy.start()
    for copy in copies:
        copy.wait()
    own_rows = lax.axis_size(ALL) // NEAR * own_blocks
    lane = lax.broadcasted_iota(jnp.int32, wide.shape, 1)
    wide[...] = jnp.zeros_like(wide)
    wide[:, :slots] = jnp.where(valid[...] > 0, ids[...], -1).astype(jnp.float32)
    flat = jnp.sum(
        pltpu.roll(wide[...], 0, 1, stride=slots, stride_axis=0), axis=0, keepdims=True
    )
    flat = jnp.where(lane[:1] < read_blocks * slots, flat, -1.0)
    block = jnp.maximum(flat, 0.0)
    owner = ((block + 0.5) * (1.0 / own_blocks)).astype(jnp.int32)
    inside = block.astype(jnp.int32) - owner * own_blocks
    piece, start = far_place(owner, own_blocks)
    picked = jnp.where(flat < 0, -1, piece * near_rows(own_rows) + start + inside)
    counted = jnp.where(flat < 0, -1, piece * own_rows + start + inside)
    row = lax.broadcasted_iota(jnp.int32, info_ref.shape, 0)
    info_ref[...] = jnp.where(
        row == 0,
        flat,
        jnp.where(
            row == 1, picked.astype(jnp.float32), jnp.where(row == 2, counted.astype(jnp.float32), 0.0)
        ),
    )
    for copy in held:
        copy.wait()


def chip_kernel(mine_ref, theirs_ref, out_ref):
    first = on_core_0()
    rows = mine_ref.shape[0]
    out_ref[:rows, :] = jnp.where(first, mine_ref[...], theirs_ref[...])
    out_ref[rows:, :] = jnp.where(first, theirs_ref[...], mine_ref[...])


def half_kernel(*refs):
    refs, out_ref = refs[:-1], refs[-1]
    rows = refs[0].shape[0]
    partners = 2 if len(refs) >= 3 and refs[2].shape == refs[0].shape else 1
    first = on_core_0()
    for i in range(partners):
        out_ref[i * rows : (i + 1) * rows, :] = jnp.where(first, refs[i][...], refs[i + 1][...])
    at = partners * rows
    for ref in refs[partners + 1 :]:
        out_ref[at : at + ref.shape[0], :] = ref[...]
        at += ref.shape[0]
    if at < out_ref.shape[0]:
        out_ref[at:, :] = jnp.zeros((out_ref.shape[0] - at, out_ref.shape[1]), jnp.float32)


def far_sum(first, x, *got):
    if len(got) == 1:
        return jnp.where(first, x, got[0])
    return got[0] + jnp.where(first, x, got[1])


def near_total_kernel(mine_ref, core_ref, chip_ref, both_ref, out_ref):
    rows = mine_ref.shape[0]
    out_ref[:rows, :] = mine_ref[...] + chip_ref[...]
    out_ref[rows:, :] = core_ref[...] + both_ref[...]


def far_total_kernel(x_ref, *refs):
    got, out_ref = refs[:-1], refs[-1]
    out_ref[...] = far_sum(on_core_0(), x_ref[...], *[ref[...] for ref in got])


def cross_kernel(mine_ref, theirs_ref, out_ref):
    rows = mine_ref.shape[0] // 2
    out_ref[:rows, :] = mine_ref[:rows, :] + theirs_ref[rows:, :]
    out_ref[rows:, :] = mine_ref[rows:, :] + theirs_ref[:rows, :]


def far_last_total_kernel(x_ref, *refs):
    got, (mine_ref, theirs_ref) = refs[:-2], refs[-2:]
    total = far_sum(on_core_0(), x_ref[...], *[ref[...] for ref in got])
    rows = mine_ref.shape[0]
    mine_ref[...] = total[:rows]
    theirs_ref[...] = total[rows:]


def near_counts_kernel(r, a_ref, b_ref, c_ref, d_ref, keep_ref, *outs):
    total = (a_ref[...] + b_ref[...]) + (c_ref[...] + d_ref[...])
    send_counts(r, total, keep_ref, *outs)


def send_counts(r, total, keep_ref, *outs):
    rows = keep_ref.shape[0]
    keep_ref[...] = total[:rows]
    if r == 4:
        outs[0][...] = jnp.where(on_core_0(), total[rows:], total[:rows])
        outs[1][...] = total[rows:]


def far_counts_kernel(x_ref, *refs):
    got, (mine_ref, theirs_ref) = refs[:-2], refs[-2:]
    first = on_core_0()
    total = far_sum(first, x_ref[...], *[ref[...] for ref in got])
    rows = mine_ref.shape[0]
    mine_ref[...] = jnp.where(first, total[:rows], total[rows:])
    theirs_ref[...] = jnp.where(first, total[rows:], total[:rows])


def next_counts_kernel(r, mine_ref, theirs_ref, keep_ref, *outs):
    send_counts(r, mine_ref[...] + theirs_ref[...], keep_ref, *outs)


def row_sums(picked_ref, lik_ref, out_ref):
    read_blocks, slots, reads, cols = lik_ref.shape
    for b in range(read_blocks):
        total = None
        for s in range(0, slots, 2):
            at = b * slots + s
            left = jnp.concatenate(
                [split(picked_ref[at : at + 1, :]), split(picked_ref[at + 1 : at + 2, :])], axis=1
            )
            right = jnp.concatenate([lik_ref[b, s], lik_ref[b, s + 1]], axis=1)
            part = dot(left, right, (((1,), (1,)), ((), ())))
            total = part if total is None else total + part
        out_ref[b : b + 1, :] = jnp.sum(total, axis=0, keepdims=True)


def first_row_kernel(info_ref, *refs):
    pieces, (lik_ref, out_ref, picked_ref) = refs[:NEAR], refs[NEAR:]
    table = jnp.concatenate([piece[...] for piece in pieces], axis=0)
    hot = hot_rows(info_ref[1:2, :], table.shape[0])
    picked_ref[...] = select_rows(hot[: picked_ref.shape[0]], table)
    row_sums(picked_ref, lik_ref, out_ref)


def next_row_kernel(scale, *refs):
    parts, (lik_ref, out_ref, picked_ref) = refs[:NEAR], refs[NEAR:]
    total = parts[0][...]
    for part in parts[1:]:
        total = total + part[...]
    picked_ref[...] = total * scale
    row_sums(picked_ref, lik_ref, out_ref)


def column_sums(mine_ref, theirs_ref, picked_ref, lik_ref, contrib_ref, inverse_ref):
    read_blocks, slots, reads, cols = lik_ref.shape
    inverse_ref[...] = 1.0 / (mine_ref[...] + theirs_ref[...])
    for b in range(read_blocks):
        left = split(inverse_ref[b : b + 1, :])
        for s in range(0, slots, 2):
            at = b * slots + s
            right = jnp.concatenate([lik_ref[b, s], lik_ref[b, s + 1]], axis=1)
            summed = jnp.sum(dot(left, right), axis=0, keepdims=True)
            contrib_ref[at : at + 1, :] = picked_ref[at : at + 1, :] * summed[:, :cols]
            contrib_ref[at + 1 : at + 2, :] = picked_ref[at + 1 : at + 2, :] * summed[:, cols:]


def column_kernel(info_ref, mine_ref, theirs_ref, picked_ref, lik_ref, out_ref, inverse_ref):
    column_sums(mine_ref, theirs_ref, picked_ref, lik_ref, out_ref, inverse_ref)
    out_ref[picked_ref.shape[0] :, :] = info_ref[...]


def last_column_kernel(info_ref, mine_ref, theirs_ref, picked_ref, lik_ref, *refs):
    outs, (inverse_ref, contrib_ref) = refs[:NEAR], refs[NEAR:]
    column_sums(mine_ref, theirs_ref, picked_ref, lik_ref, contrib_ref, inverse_ref)
    rows = outs[0].shape[0]
    all_slots = contrib_ref.shape[0]
    block = lax.broadcasted_iota(jnp.int32, (NEAR * rows, all_slots), 0)
    hot = (block.astype(jnp.float32) == info_ref[2:3, :all_slots]).astype(jnp.float32)
    counts = select_rows(hot, contrib_ref[...])
    for i in range(NEAR):
        outs[i][...] = counts[i * rows : (i + 1) * rows, :]


def wanted_kernel(all_slots, r, *refs):
    given, refs = refs[: r // 2 + 1], refs[r // 2 + 1 :]
    wanted, outs = refs[:NEAR], refs[NEAR:]
    rows = all_slots + ID_ROWS
    half = LANES // 2
    first = on_core_0()
    lane = lax.broadcasted_iota(jnp.int32, (1, LANES), 1)
    ids, values = [], []
    for i in range(r // 2):
        x = jnp.where(first, given[i][...], given[i + 1][...])
        for at in range(0, x.shape[0], rows):
            ids.append(x[at + all_slots : at + all_slots + 1, :])
            values.append(x[at : at + all_slots, :])
    pairs = [
        jnp.where(lane < half, a, pltpu.roll(b, half, 1)) for a, b in zip(ids[::2], ids[1::2])
    ]
    given = terms(jnp.concatenate(values, axis=0))
    for ids_ref, out_ref in zip(wanted, outs):
        column = down(ids_ref[0:1, :])[:all_slots]
        hot = jnp.concatenate([(column == pair).astype(jnp.float32) for pair in pairs], axis=1)
        hot = hot.astype(jnp.bfloat16)
        out_ref[...] = dot(hot, given[0]) + dot(hot, given[1]) + dot(hot, given[2])


def call(kernel, outs, scratch, *operands):
    return pl.pallas_call(
        kernel,
        out_shape=[jax.ShapeDtypeStruct(shape, jnp.float32) for shape in outs],
        in_specs=[VMEM] * len(operands),
        out_specs=[VMEM] * len(outs),
        scratch_shapes=[pltpu.VMEM(shape, jnp.float32) for shape in scratch],
        compiler_params=pltpu.CompilerParams(vmem_limit_bytes=16 * 2**20),
    )(*operands)


def prepare(own_blocks, likelihood, block_ids, slot_valid):
    read_blocks, slots = block_ids.shape
    return pl.pallas_call(
        lambda *refs: prepare_kernel(own_blocks, *refs),
        out_shape=[
            pltpu.VMEM(likelihood.shape, likelihood.dtype),
            jax.ShapeDtypeStruct((ID_ROWS, LANES), jnp.float32),
        ],
        in_specs=[ANY] * 3,
        out_specs=[VMEM] * 2,
        scratch_shapes=[
            pltpu.VMEM((read_blocks, slots), jnp.int32),
            pltpu.VMEM((read_blocks, slots), jnp.int32),
            pltpu.VMEM((read_blocks, LANES), jnp.float32),
            pltpu.SemaphoreType.DMA((2 + read_blocks,)),
        ],
        compiler_params=pltpu.CompilerParams(vmem_limit_bytes=16 * 2**20),
    )(*[pltpu.with_memory_space_constraint(x, pltpu.HBM) for x in (likelihood, block_ids, slot_valid)])


def far_gather(x):
    radix = far_radices()
    stride = NEAR
    for i, r in enumerate(radix):
        (x,) = call(chip_kernel, [(2 * x.shape[0], x.shape[1])], [], x, swap(x, 1))
        got = far_swaps(x, x, r, stride)
        stride *= r
        if i + 1 < len(radix):
            (x,) = call(half_kernel, [(r // 2 * x.shape[0], x.shape[1])], [], x, *got)
    return [x] + got


def total_rows(x):
    (x,) = call(near_total_kernel, [(2 * x.shape[0], x.shape[1])], [], *near_swaps([x] * NEAR))
    radix = far_radices()
    stride = NEAR
    for i, r in enumerate(radix):
        got = far_swaps(x, x, r, stride)
        stride *= r
        if i + 1 < len(radix):
            (x,) = call(far_total_kernel, [x.shape], [], x, *got)
            (x,) = call(cross_kernel, [x.shape], [], x, swap(x, 1))
    half = (x.shape[0] // 2, x.shape[1])
    mine, theirs = call(far_last_total_kernel, [half, half], [], x, *got)
    return mine, swap(theirs, 1)


def scatter_counts(parts):
    radix = far_radices()
    stride = NEAR
    for r in radix[:-1]:
        stride *= r
    rows, cols = parts[0].shape
    operands, kernel = near_swaps(parts), near_counts_kernel
    for r, before in zip(radix[::-1], radix[-2::-1] + [0]):
        rows = rows // (r // 2)
        outs = [(rows, cols)] * (3 if r == 4 else 1)
        kept, *sent = call(lambda *refs: kernel(r, *refs), outs, [], *operands)
        sent = sent or [kept, kept]
        got = far_swaps(*sent, r, stride)
        stride //= max(before, 1)
        rows //= 2
        mine, theirs = call(far_counts_kernel, [(rows, cols)] * 2, [], kept, *got)
        operands, kernel = [mine, swap(theirs, 1)], next_counts_kernel
    return operands


def local(likelihood, block_ids, slot_valid, start_weights):
    read_blocks, slots, reads, cols = likelihood.shape
    own_weights = start_weights.reshape(-1, cols)
    own_blocks = own_weights.shape[0]
    own_rows = lax.axis_size(ALL) // NEAR * own_blocks
    all_slots = read_blocks * slots
    total_reads = read_blocks * lax.axis_size("reads") * reads
    scale = lax.axis_size(ALL) * own_blocks * cols / total_reads

    column = far_gather(own_weights)
    held, info = prepare(own_blocks, likelihood, block_ids, slot_valid)
    (sent,) = call(half_kernel, [(near_rows(own_rows), cols)], [], *column, info)
    pieces = near_swaps([sent] * NEAR)
    wanted = [info] + [piece[own_rows : own_rows + ID_ROWS] for piece in pieces[1:]]

    outs = [(read_blocks, reads), (all_slots, cols)]
    inverse = (read_blocks, reads)
    row_part, picked = call(first_row_kernel, outs, [], info, *pieces, held)
    for step in range(ITERS - 1):
        totals = total_rows(row_part)
        (contrib,) = call(
            column_kernel, [(all_slots + ID_ROWS, cols)], [inverse], info, *totals, picked, held
        )
        given = far_gather(contrib)
        sums = call(
            lambda *refs: wanted_kernel(all_slots, far_radices()[-1], *refs),
            [(all_slots, cols)] * NEAR,
            [],
            *given,
            *wanted,
        )
        row_part, picked = call(
            lambda *refs: next_row_kernel(scale, *refs), outs, [], *near_swaps(sums), held
        )
    totals = total_rows(row_part)
    counts = call(
        last_column_kernel,
        [(own_rows, cols)] * NEAR,
        [inverse, (all_slots, cols)],
        info,
        *totals,
        picked,
        held,
    )
    mine, theirs = scatter_counts(counts)
    return ((mine + theirs) * scale).reshape(-1)


def solution(mesh):
    placed = (
        P(("parts", "reads"), "genome", None, None),
        P(("parts", "reads"), "genome"),
        P(("parts", "reads"), "genome"),
        P(("parts", "genome", "reads")),
    )
    return jax.shard_map(
        local,
        mesh=mesh,
        in_specs=placed,
        out_specs=P(("parts", "genome", "reads")),
        check_vma=False,
    )
```

```python
import jax
import jax.numpy as jnp
from jax import lax
from jax.experimental import pallas as pl
from jax.experimental.pallas import tpu as pltpu
from jax.sharding import PartitionSpec as P

ITERS = 2
ALL = ("genome", "reads")
TERMS = 16
ID_ROWS = 8
LANES = 128
VMEM = pl.BlockSpec(memory_space=pltpu.VMEM)
ANY = pl.BlockSpec(memory_space=pl.ANY)


def radices(n):
    out = []
    while n > 1:
        r = 4 if n % 4 == 0 else 2
        out.append(r)
        n //= r
    return out


def swap(x, axes, k):
    n = lax.axis_size(axes)
    return lax.ppermute(x, axes, [(i, i ^ k) for i in range(n)])


def middle_first(n, k):
    return [i ^ k for i in range(n)]


def position(k, n):
    place = 0
    for r in radices(n):
        n //= r
        place = place + (k % r) * n
        k = k // r
    return place


def gather_far(x, axes):
    parts = [x]
    stride = lax.axis_size(axes)
    for r in radices(stride)[:0:-1]:
        stride //= r
        sent = parts[0] if len(parts) == 1 else jnp.concatenate(parts, axis=0)
        parts = [sent] + [swap(sent, axes, j * stride) for j in range(1, r)]
    return parts


def dot(a, b, dims=(((1,), (0,)), ((), ()))):
    return lax.dot_general(a, b, dims, preferred_element_type=jnp.float32)


def terms(x):
    hi = x.astype(jnp.bfloat16)
    rest = x - hi.astype(jnp.float32)
    mid = rest.astype(jnp.bfloat16)
    return hi, mid, (rest - mid.astype(jnp.float32)).astype(jnp.bfloat16)


def select_rows(hot, x):
    hi, mid, low = terms(x)
    hot = hot.astype(jnp.bfloat16)
    return dot(hot, hi) + dot(hot, mid) + dot(hot, low)


def split(row):
    x = jnp.broadcast_to(row, (TERMS, row.shape[1]))
    hi = x.astype(jnp.bfloat16).astype(jnp.float32)
    rest = x - hi
    mid = rest.astype(jnp.bfloat16).astype(jnp.float32)
    low = rest - mid
    at = lax.broadcasted_iota(jnp.int32, x.shape, 0)
    out = jnp.where(at == 0, hi, jnp.where(at == 1, mid, jnp.where(at == 2, low, 0.0)))
    return out.astype(jnp.bfloat16)


def down(row):
    return jnp.transpose(jnp.broadcast_to(row, (LANES, LANES)))


def hot_rows(values, count):
    column = down(values)
    blocks = []
    for start in range(0, count, LANES):
        width = min(LANES, count - start)
        lane = lax.broadcasted_iota(jnp.int32, (LANES, width), 1).astype(jnp.float32) + start
        blocks.append((column[:, :width] == lane).astype(jnp.float32))
    return blocks[0] if len(blocks) == 1 else jnp.concatenate(blocks, axis=1)


def prepare_kernel(own_blocks, lik_ref, ids_ref, valid_ref, held_ref, info_ref, ids, valid, wide, sems):
    read_blocks, slots = ids.shape
    copies = [
        pltpu.make_async_copy(ids_ref, ids, sems.at[0]),
        pltpu.make_async_copy(valid_ref, valid, sems.at[1]),
    ]
    held = [
        pltpu.make_async_copy(lik_ref.at[b], held_ref.at[b], sems.at[2 + b])
        for b in range(held_ref.shape[0])
    ]
    for copy in copies + held:
        copy.start()
    for copy in copies:
        copy.wait()
    n = lax.axis_size(ALL)
    near = radices(n)[0]
    far = n // near
    me = lax.axis_index("genome") * lax.axis_size("reads") + lax.axis_index("reads")
    lane = lax.broadcasted_iota(jnp.int32, wide.shape, 1)
    wide[...] = jnp.zeros_like(wide)
    wide[:, :slots] = jnp.where(valid[...] > 0, ids[...], -1).astype(jnp.float32)
    flat = jnp.sum(
        pltpu.roll(wide[...], 0, 1, stride=slots, stride_axis=0), axis=0, keepdims=True
    )
    flat = jnp.where(lane[:1] < read_blocks * slots, flat, -1.0)
    owner = ((flat + 0.5) * (1.0 / own_blocks)).astype(jnp.int32)
    inside = flat.astype(jnp.int32) - owner * own_blocks
    away = owner ^ me
    place = position(away, n)
    place = (place // far) * near_rows(far, own_blocks) + (place % far) * own_blocks + inside
    place = jnp.where(flat < 0, -1, place).astype(jnp.float32)
    row = lax.broadcasted_iota(jnp.int32, info_ref.shape, 0)
    info_ref[...] = jnp.where(row == 0, flat, jnp.where(row == 1, place, 0.0))
    for copy in held:
        copy.wait()


def join_kernel(*refs):
    out_ref = refs[-1]
    at = 0
    for ref in refs[:-1]:
        out_ref[at : at + ref.shape[0], :] = ref[...]
        at += ref.shape[0]
    if at < out_ref.shape[0]:
        out_ref[at:, :] = jnp.zeros((out_ref.shape[0] - at, out_ref.shape[1]), jnp.float32)


def near_rows(far, own_blocks):
    return -(-(far * own_blocks + ID_ROWS) // 16) * 16


def row_sums(picked_ref, lik_ref, out_ref):
    read_blocks, slots, reads, cols = lik_ref.shape
    for b in range(read_blocks):
        total = None
        for s in range(0, slots, 2):
            at = b * slots + s
            left = jnp.concatenate(
                [split(picked_ref[at : at + 1, :]), split(picked_ref[at + 1 : at + 2, :])], axis=1
            )
            right = jnp.concatenate([lik_ref[b, s], lik_ref[b, s + 1]], axis=1)
            part = dot(left, right, (((1,), (1,)), ((), ())))
            total = part if total is None else total + part
        row = jnp.sum(total, axis=0, keepdims=True)
        for i in range(out_ref.shape[0]):
            out_ref[i, b : b + 1, :] = row


def first_row_kernel(near, info_ref, *refs):
    pieces, (lik_ref, out_ref, picked_ref) = refs[:near], refs[near:]
    table = jnp.concatenate([piece[...] for piece in pieces], axis=0)
    hot = hot_rows(info_ref[1:2, :], table.shape[0])
    picked_ref[...] = select_rows(hot[: picked_ref.shape[0]], table)
    row_sums(picked_ref, lik_ref, out_ref)


def next_row_kernel(near, scale, *refs):
    parts, (lik_ref, out_ref, picked_ref) = refs[:near], refs[near:]
    total = parts[0][...]
    for part in parts[1:]:
        total = total + part[...]
    picked_ref[...] = total * scale
    row_sums(picked_ref, lik_ref, out_ref)


def column_sums(parts_ref, picked_ref, lik_ref, contrib_ref, inverse_ref):
    read_blocks, slots, reads, cols = lik_ref.shape
    total = parts_ref[0]
    for i in range(1, parts_ref.shape[0]):
        total = total + parts_ref[i]
    inverse_ref[...] = 1.0 / total
    for b in range(read_blocks):
        left = split(inverse_ref[b : b + 1, :])
        for s in range(0, slots, 2):
            at = b * slots + s
            right = jnp.concatenate([lik_ref[b, s], lik_ref[b, s + 1]], axis=1)
            summed = jnp.sum(dot(left, right), axis=0, keepdims=True)
            contrib_ref[at : at + 1, :] = picked_ref[at : at + 1, :] * summed[:, :cols]
            contrib_ref[at + 1 : at + 2, :] = picked_ref[at + 1 : at + 2, :] * summed[:, cols:]


def column_kernel(info_ref, parts_ref, picked_ref, lik_ref, out_ref, inverse_ref):
    column_sums(parts_ref, picked_ref, lik_ref, out_ref, inverse_ref)
    out_ref[picked_ref.shape[0] :, :] = info_ref[...]


def last_column_kernel(order, info_ref, parts_ref, picked_ref, lik_ref, out_ref, inverse_ref, contrib_ref):
    column_sums(parts_ref, picked_ref, lik_ref, contrib_ref, inverse_ref)
    owners, own_blocks, cols = out_ref.shape
    all_slots = contrib_ref.shape[0]
    block = lax.broadcasted_iota(jnp.int32, (owners * own_blocks, all_slots), 0)
    hot = (block.astype(jnp.float32) == info_ref[0:1, :all_slots]).astype(jnp.float32)
    counts = select_rows(hot, contrib_ref[...])
    for i, owner in enumerate(order):
        out_ref[i] = counts[owner * own_blocks : (owner + 1) * own_blocks, :]


def wanted_kernel(near, all_slots, pieces, *refs):
    given_refs, wanted, outs = refs[:pieces], refs[pieces : pieces + near], refs[pieces + near :]
    rows = all_slots + ID_ROWS
    half = LANES // 2
    lane = lax.broadcasted_iota(jnp.int32, (1, LANES), 1)
    ids, values = [], []
    for ref in given_refs:
        for at in range(0, ref.shape[0], rows):
            ids.append(ref[at + all_slots : at + all_slots + 1, :])
            values.append(ref[at : at + all_slots, :])
    pairs = [
        jnp.where(lane < half, a, pltpu.roll(b, half, 1)) for a, b in zip(ids[::2], ids[1::2])
    ]
    given = terms(jnp.concatenate(values, axis=0))
    for ids_ref, out_ref in zip(wanted, outs):
        column = down(ids_ref[0:1, :])[:all_slots]
        hot = jnp.concatenate([(column == pair).astype(jnp.float32) for pair in pairs], axis=1)
        hot = hot.astype(jnp.bfloat16)
        out_ref[...] = dot(hot, given[0]) + dot(hot, given[1]) + dot(hot, given[2])


def call(kernel, outs, scratch, *operands):
    return pl.pallas_call(
        kernel,
        out_shape=[jax.ShapeDtypeStruct(shape, jnp.float32) for shape in outs],
        in_specs=[VMEM] * len(operands),
        out_specs=[VMEM] * len(outs),
        scratch_shapes=[pltpu.VMEM(shape, jnp.float32) for shape in scratch],
        compiler_params=pltpu.CompilerParams(vmem_limit_bytes=16 * 2**20),
    )(*operands)


def prepare(own_blocks, likelihood, block_ids, slot_valid):
    read_blocks, slots = block_ids.shape
    return pl.pallas_call(
        lambda *refs: prepare_kernel(own_blocks, *refs),
        out_shape=[
            pltpu.VMEM(likelihood.shape, likelihood.dtype),
            jax.ShapeDtypeStruct((ID_ROWS, LANES), jnp.float32),
        ],
        in_specs=[ANY] * 3,
        out_specs=[VMEM] * 2,
        scratch_shapes=[
            pltpu.VMEM((read_blocks, slots), jnp.int32),
            pltpu.VMEM((read_blocks, slots), jnp.int32),
            pltpu.VMEM((read_blocks, LANES), jnp.float32),
            pltpu.SemaphoreType.DMA((2 + read_blocks,)),
        ],
        compiler_params=pltpu.CompilerParams(vmem_limit_bytes=16 * 2**20),
    )(*[pltpu.with_memory_space_constraint(x, pltpu.HBM) for x in (likelihood, block_ids, slot_valid)])


def local(likelihood, block_ids, slot_valid, start_weights):
    read_blocks, slots, reads, cols = likelihood.shape
    n = lax.axis_size(ALL)
    chips = lax.axis_size("genome")
    near = radices(n)[0]
    far = n // near
    own_weights = start_weights.reshape(-1, cols)
    own_blocks = own_weights.shape[0]
    all_slots = read_blocks * slots
    total_reads = read_blocks * lax.axis_size("reads") * reads
    scale = n * own_blocks * cols / total_reads

    column = gather_far(own_weights, ALL)
    held, info = prepare(own_blocks, likelihood, block_ids, slot_valid)
    (sent,) = call(join_kernel, [(near_rows(far, own_blocks), cols)], [], *column, info)
    pieces = [sent] + [swap(sent, ALL, j) for j in range(1, near)]
    at = far * own_blocks
    wanted = [info] + [piece[at : at + ID_ROWS] for piece in pieces[1:]]

    row_shapes = [(chips, read_blocks, reads), (all_slots, cols)]
    inverse = (read_blocks, reads)
    for step in range(ITERS):
        if step == 0:
            row_parts, picked = call(
                lambda *refs: first_row_kernel(near, *refs), row_shapes, [], info, *pieces, held
            )
        else:
            row_parts, picked = call(
                lambda *refs: next_row_kernel(near, scale, *refs), row_shapes, [], *parts, held
            )
        row_parts = lax.all_to_all(
            row_parts,
            "genome",
            0,
            0,
            tiled=True,
            axis_index_groups=[middle_first(chips, chips // 2)],
        )
        if step + 1 < ITERS:
            (contrib,) = call(
                column_kernel,
                [(all_slots + ID_ROWS, cols)],
                [inverse],
                info,
                row_parts,
                picked,
                held,
            )
            given = gather_far(contrib, ALL)
            sums = call(
                lambda *refs: wanted_kernel(near, all_slots, len(given), *refs),
                [(all_slots, cols)] * near,
                [],
                *given,
                *wanted,
            )
            parts = [sums[0]] + [swap(sums[j], ALL, j) for j in range(1, near)]
    order = middle_first(n, n // 2 + 1)
    (counts,) = call(
        lambda *refs: last_column_kernel(order, *refs),
        [(n, own_blocks, cols)],
        [inverse, (all_slots, cols)],
        info,
        row_parts,
        picked,
        held,
    )
    counts = lax.all_to_all(counts, ALL, 0, 0, tiled=True, axis_index_groups=[order])
    return (jnp.sum(counts, axis=0) * scale).reshape(-1)


def solution(mesh):
    placed = (
        P(("parts", "reads"), "genome", None, None),
        P(("parts", "reads"), "genome"),
        P(("parts", "reads"), "genome"),
        P(("parts", "genome", "reads")),
    )
    return jax.shard_map(
        local,
        mesh=mesh,
        in_specs=placed,
        out_specs=P(("parts", "genome", "reads")),
        check_vma=False,
    )
```

```python
import jax
import jax.numpy as jnp
from jax import lax
from jax.experimental import pallas as pl
from jax.experimental.pallas import tpu as pltpu
from jax.sharding import PartitionSpec as P

ITERS = 2
ALL = ("genome", "reads")
TERMS = 16
ID_ROWS = 8
LANES = 128
VMEM = pl.BlockSpec(memory_space=pltpu.VMEM)
ANY = pl.BlockSpec(memory_space=pl.ANY)


def radices(n):
    out = []
    while n > 1:
        r = 4 if n % 4 == 0 else 2
        out.append(r)
        n //= r
    return out


def swap(x, axes, k):
    n = lax.axis_size(axes)
    return lax.ppermute(x, axes, [(i, i ^ k) for i in range(n)])


def middle_first(n, k):
    return [i ^ k for i in range(n)]


def position(k, n):
    place = 0
    for r in radices(n):
        n //= r
        place = place + (k % r) * n
        k = k // r
    return place


def gather_far(x, axes):
    parts = [x]
    stride = lax.axis_size(axes)
    for r in radices(stride)[:0:-1]:
        stride //= r
        sent = parts[0] if len(parts) == 1 else jnp.concatenate(parts, axis=0)
        parts = [sent] + [swap(sent, axes, j * stride) for j in range(1, r)]
    return parts


def dot(a, b, dims=(((1,), (0,)), ((), ()))):
    return lax.dot_general(a, b, dims, preferred_element_type=jnp.float32)


def terms(x):
    hi = x.astype(jnp.bfloat16)
    rest = x - hi.astype(jnp.float32)
    mid = rest.astype(jnp.bfloat16)
    return hi, mid, (rest - mid.astype(jnp.float32)).astype(jnp.bfloat16)


def select_rows(hot, x):
    hi, mid, low = terms(x)
    hot = hot.astype(jnp.bfloat16)
    return dot(hot, hi) + dot(hot, mid) + dot(hot, low)


def split(row):
    x = jnp.broadcast_to(row, (TERMS, row.shape[1]))
    hi = x.astype(jnp.bfloat16).astype(jnp.float32)
    rest = x - hi
    mid = rest.astype(jnp.bfloat16).astype(jnp.float32)
    low = rest - mid
    at = lax.broadcasted_iota(jnp.int32, x.shape, 0)
    out = jnp.where(at == 0, hi, jnp.where(at == 1, mid, jnp.where(at == 2, low, 0.0)))
    return out.astype(jnp.bfloat16)


def down(row):
    return jnp.transpose(jnp.broadcast_to(row, (LANES, LANES)))


def hot_rows(values, count):
    column = down(values)
    blocks = []
    for start in range(0, count, LANES):
        width = min(LANES, count - start)
        lane = lax.broadcasted_iota(jnp.int32, (LANES, width), 1).astype(jnp.float32) + start
        blocks.append((column[:, :width] == lane).astype(jnp.float32))
    return blocks[0] if len(blocks) == 1 else jnp.concatenate(blocks, axis=1)


def prepare_kernel(own_blocks, lik_ref, ids_ref, valid_ref, held_ref, info_ref, ids, valid, wide, sems):
    read_blocks, slots = ids.shape
    copies = [
        pltpu.make_async_copy(ids_ref, ids, sems.at[0]),
        pltpu.make_async_copy(valid_ref, valid, sems.at[1]),
    ]
    held = [
        pltpu.make_async_copy(lik_ref.at[b], held_ref.at[b], sems.at[2 + b])
        for b in range(held_ref.shape[0])
    ]
    for copy in copies + held:
        copy.start()
    for copy in copies:
        copy.wait()
    n = lax.axis_size(ALL)
    near = radices(n)[0]
    far = n // near
    me = lax.axis_index("genome") * lax.axis_size("reads") + lax.axis_index("reads")
    lane = lax.broadcasted_iota(jnp.int32, wide.shape, 1)
    wide[...] = jnp.zeros_like(wide)
    wide[:, :slots] = jnp.where(valid[...] > 0, ids[...], -1).astype(jnp.float32)
    flat = jnp.sum(
        pltpu.roll(wide[...], 0, 1, stride=slots, stride_axis=0), axis=0, keepdims=True
    )
    flat = jnp.where(lane[:1] < read_blocks * slots, flat, -1.0)
    owner = ((flat + 0.5) * (1.0 / own_blocks)).astype(jnp.int32)
    inside = flat.astype(jnp.int32) - owner * own_blocks
    away = owner ^ me
    place = position(away, n)
    place = (place // far) * near_rows(far, own_blocks) + (place % far) * own_blocks + inside
    place = jnp.where(flat < 0, -1, place).astype(jnp.float32)
    row = lax.broadcasted_iota(jnp.int32, info_ref.shape, 0)
    info_ref[...] = jnp.where(row == 0, flat, jnp.where(row == 1, place, 0.0))
    for copy in held:
        copy.wait()


def join_kernel(*refs):
    out_ref = refs[-1]
    at = 0
    for ref in refs[:-1]:
        out_ref[at : at + ref.shape[0], :] = ref[...]
        at += ref.shape[0]
    if at < out_ref.shape[0]:
        out_ref[at:, :] = jnp.zeros((out_ref.shape[0] - at, out_ref.shape[1]), jnp.float32)


def near_rows(far, own_blocks):
    return -(-(far * own_blocks + ID_ROWS) // 16) * 16


def row_sums(picked_ref, lik_ref, out_ref):
    read_blocks, slots, reads, cols = lik_ref.shape
    for b in range(read_blocks):
        total = None
        for s in range(0, slots, 2):
            at = b * slots + s
            left = jnp.concatenate(
                [split(picked_ref[at : at + 1, :]), split(picked_ref[at + 1 : at + 2, :])], axis=1
            )
            right = jnp.concatenate([lik_ref[b, s], lik_ref[b, s + 1]], axis=1)
            part = dot(left, right, (((1,), (1,)), ((), ())))
            total = part if total is None else total + part
        row = jnp.sum(total, axis=0, keepdims=True)
        for i in range(out_ref.shape[0]):
            out_ref[i, b : b + 1, :] = row


def first_row_kernel(near, info_ref, *refs):
    pieces, (lik_ref, out_ref, picked_ref) = refs[:near], refs[near:]
    table = jnp.concatenate([piece[...] for piece in pieces], axis=0)
    hot = hot_rows(info_ref[1:2, :], table.shape[0])
    picked_ref[...] = select_rows(hot[: picked_ref.shape[0]], table)
    row_sums(picked_ref, lik_ref, out_ref)


def next_row_kernel(near, scale, *refs):
    parts, (lik_ref, out_ref, picked_ref) = refs[:near], refs[near:]
    total = parts[0][...]
    for part in parts[1:]:
        total = total + part[...]
    picked_ref[...] = total * scale
    row_sums(picked_ref, lik_ref, out_ref)


def column_sums(parts_ref, picked_ref, lik_ref, contrib_ref, inverse_ref):
    read_blocks, slots, reads, cols = lik_ref.shape
    total = parts_ref[0]
    for i in range(1, parts_ref.shape[0]):
        total = total + parts_ref[i]
    inverse_ref[...] = 1.0 / total
    for b in range(read_blocks):
        left = split(inverse_ref[b : b + 1, :])
        for s in range(0, slots, 2):
            at = b * slots + s
            right = jnp.concatenate([lik_ref[b, s], lik_ref[b, s + 1]], axis=1)
            summed = jnp.sum(dot(left, right), axis=0, keepdims=True)
            contrib_ref[at : at + 1, :] = picked_ref[at : at + 1, :] * summed[:, :cols]
            contrib_ref[at + 1 : at + 2, :] = picked_ref[at + 1 : at + 2, :] * summed[:, cols:]


def column_kernel(info_ref, parts_ref, picked_ref, lik_ref, out_ref, inverse_ref):
    column_sums(parts_ref, picked_ref, lik_ref, out_ref, inverse_ref)
    out_ref[picked_ref.shape[0] :, :] = info_ref[...]


def last_column_kernel(order, info_ref, parts_ref, picked_ref, lik_ref, out_ref, inverse_ref, contrib_ref):
    column_sums(parts_ref, picked_ref, lik_ref, contrib_ref, inverse_ref)
    owners, own_blocks, cols = out_ref.shape
    all_slots = contrib_ref.shape[0]
    block = lax.broadcasted_iota(jnp.int32, (owners * own_blocks, all_slots), 0)
    hot = (block.astype(jnp.float32) == info_ref[0:1, :all_slots]).astype(jnp.float32)
    counts = select_rows(hot, contrib_ref[...])
    for i, owner in enumerate(order):
        out_ref[i] = counts[owner * own_blocks : (owner + 1) * own_blocks, :]


def wanted_kernel(near, all_slots, pieces, *refs):
    given_refs, wanted, outs = refs[:pieces], refs[pieces : pieces + near], refs[pieces + near :]
    rows = all_slots + ID_ROWS
    half = LANES // 2
    lane = lax.broadcasted_iota(jnp.int32, (1, LANES), 1)
    ids, values = [], []
    for ref in given_refs:
        for at in range(0, ref.shape[0], rows):
            ids.append(ref[at + all_slots : at + all_slots + 1, :])
            values.append(ref[at : at + all_slots, :])
    pairs = [
        jnp.where(lane < half, a, pltpu.roll(b, half, 1)) for a, b in zip(ids[::2], ids[1::2])
    ]
    given = terms(jnp.concatenate(values, axis=0))
    for ids_ref, out_ref in zip(wanted, outs):
        column = down(ids_ref[0:1, :])[:all_slots]
        hot = jnp.concatenate([(column == pair).astype(jnp.float32) for pair in pairs], axis=1)
        hot = hot.astype(jnp.bfloat16)
        out_ref[...] = dot(hot, given[0]) + dot(hot, given[1]) + dot(hot, given[2])


def call(kernel, outs, scratch, *operands):
    return pl.pallas_call(
        kernel,
        out_shape=[jax.ShapeDtypeStruct(shape, jnp.float32) for shape in outs],
        in_specs=[VMEM] * len(operands),
        out_specs=[VMEM] * len(outs),
        scratch_shapes=[pltpu.VMEM(shape, jnp.float32) for shape in scratch],
        compiler_params=pltpu.CompilerParams(vmem_limit_bytes=16 * 2**20),
    )(*operands)


def prepare(own_blocks, likelihood, block_ids, slot_valid):
    read_blocks, slots = block_ids.shape
    return pl.pallas_call(
        lambda *refs: prepare_kernel(own_blocks, *refs),
        out_shape=[
            pltpu.VMEM(likelihood.shape, likelihood.dtype),
            jax.ShapeDtypeStruct((ID_ROWS, LANES), jnp.float32),
        ],
        in_specs=[ANY] * 3,
        out_specs=[VMEM] * 2,
        scratch_shapes=[
            pltpu.VMEM((read_blocks, slots), jnp.int32),
            pltpu.VMEM((read_blocks, slots), jnp.int32),
            pltpu.VMEM((read_blocks, LANES), jnp.float32),
            pltpu.SemaphoreType.DMA((2 + read_blocks,)),
        ],
        compiler_params=pltpu.CompilerParams(vmem_limit_bytes=16 * 2**20),
    )(*[pltpu.with_memory_space_constraint(x, pltpu.HBM) for x in (likelihood, block_ids, slot_valid)])


def local(likelihood, block_ids, slot_valid, start_weights):
    read_blocks, slots, reads, cols = likelihood.shape
    n = lax.axis_size(ALL)
    chips = lax.axis_size("genome")
    near = radices(n)[0]
    far = n // near
    own_weights = start_weights.reshape(-1, cols)
    own_blocks = own_weights.shape[0]
    all_slots = read_blocks * slots
    total_reads = read_blocks * lax.axis_size("reads") * reads
    scale = n * own_blocks * cols / total_reads

    column = gather_far(own_weights, ALL)
    held, info = prepare(own_blocks, likelihood, block_ids, slot_valid)
    (sent,) = call(join_kernel, [(near_rows(far, own_blocks), cols)], [], *column, info)
    pieces = [sent] + [swap(sent, ALL, j) for j in range(1, near)]
    at = far * own_blocks
    wanted = [info] + [piece[at : at + ID_ROWS] for piece in pieces[1:]]

    row_shapes = [(chips, read_blocks, reads), (all_slots, cols)]
    inverse = (read_blocks, reads)
    for step in range(ITERS):
        if step == 0:
            row_parts, picked = call(
                lambda *refs: first_row_kernel(near, *refs), row_shapes, [], info, *pieces, held
            )
        else:
            row_parts, picked = call(
                lambda *refs: next_row_kernel(near, scale, *refs), row_shapes, [], *parts, held
            )
        row_parts = lax.all_to_all(
            row_parts,
            "genome",
            0,
            0,
            tiled=True,
            axis_index_groups=[middle_first(chips, chips // 2 + 1)],
        )
        if step + 1 < ITERS:
            (contrib,) = call(
                column_kernel,
                [(all_slots + ID_ROWS, cols)],
                [inverse],
                info,
                row_parts,
                picked,
                held,
            )
            given = gather_far(contrib, ALL)
            sums = call(
                lambda *refs: wanted_kernel(near, all_slots, len(given), *refs),
                [(all_slots, cols)] * near,
                [],
                *given,
                *wanted,
            )
            parts = [sums[0]] + [swap(sums[j], ALL, j) for j in range(1, near)]
    order = middle_first(n, n // 2 + 3)
    (counts,) = call(
        lambda *refs: last_column_kernel(order, *refs),
        [(n, own_blocks, cols)],
        [inverse, (all_slots, cols)],
        info,
        row_parts,
        picked,
        held,
    )
    counts = lax.all_to_all(counts, ALL, 0, 0, tiled=True, axis_index_groups=[order])
    return (jnp.sum(counts, axis=0) * scale).reshape(-1)


def solution(mesh):
    placed = (
        P(("parts", "reads"), "genome", None, None),
        P(("parts", "reads"), "genome"),
        P(("parts", "reads"), "genome"),
        P(("parts", "genome", "reads")),
    )
    return jax.shard_map(
        local,
        mesh=mesh,
        in_specs=placed,
        out_specs=P(("parts", "genome", "reads")),
        check_vma=False,
    )
```

```python
import jax
import jax.numpy as jnp
from jax import lax
from jax.experimental import pallas as pl
from jax.experimental.pallas import tpu as pltpu
from jax.sharding import PartitionSpec as P

ITERS = 2
ALL = ("genome", "reads")
TERMS = 16
LANES = 128
VMEM = pl.BlockSpec(memory_space=pltpu.VMEM)
ANY = pl.BlockSpec(memory_space=pl.ANY)


def radices(n):
    out = []
    while n > 1:
        r = 4 if n % 4 == 0 else 2
        out.append(r)
        n //= r
    return out


def swap(x, axes, k):
    n = lax.axis_size(axes)
    return lax.ppermute(x, axes, [(i, i ^ k) for i in range(n)])


def middle_first(n, k):
    return [i ^ k for i in range(n)]


def gather_far(x, axes):
    parts = [x]
    stride = lax.axis_size(axes)
    for r in radices(stride)[:0:-1]:
        stride //= r
        sent = parts[0] if len(parts) == 1 else jnp.concatenate(parts, axis=0)
        parts = [sent] + [swap(sent, axes, j * stride) for j in range(1, r)]
    return parts


def far_order(n):
    order = [0]
    stride = n
    for r in radices(n)[:0:-1]:
        stride //= r
        order = [o ^ (j * stride) for j in range(r) for o in order]
    return order


def dot(a, b, dims=(((1,), (0,)), ((), ()))):
    return lax.dot_general(a, b, dims, preferred_element_type=jnp.float32)


def terms(x):
    hi = x.astype(jnp.bfloat16)
    rest = x - hi.astype(jnp.float32)
    mid = rest.astype(jnp.bfloat16)
    return hi, mid, (rest - mid.astype(jnp.float32)).astype(jnp.bfloat16)


def select_rows(hot, x):
    hi, mid, low = terms(x)
    hot = hot.astype(jnp.bfloat16)
    return dot(hot, hi) + dot(hot, mid) + dot(hot, low)


def split(row):
    x = jnp.broadcast_to(row, (TERMS, row.shape[1]))
    hi = x.astype(jnp.bfloat16).astype(jnp.float32)
    rest = x - hi
    mid = rest.astype(jnp.bfloat16).astype(jnp.float32)
    low = rest - mid
    at = lax.broadcasted_iota(jnp.int32, x.shape, 0)
    out = jnp.where(at == 0, hi, jnp.where(at == 1, mid, jnp.where(at == 2, low, 0.0)))
    return out.astype(jnp.bfloat16)


def down(row):
    return jnp.transpose(jnp.broadcast_to(row, (LANES, LANES)))


def hot_rows(values, count):
    column = down(values)
    blocks = []
    for start in range(0, count, LANES):
        width = min(LANES, count - start)
        lane = lax.broadcasted_iota(jnp.int32, (LANES, width), 1).astype(jnp.float32) + start
        blocks.append((column[:, :width] == lane).astype(jnp.float32))
    return blocks[0] if len(blocks) == 1 else jnp.concatenate(blocks, axis=1)


def prepare_kernel(
    first,
    weights_ref,
    ids_ref,
    valid_ref,
    lik_ref,
    out_ref,
    info_ref,
    held_ref,
    weights,
    ids,
    valid,
    wide,
    sems,
    held_sems,
):
    copies = [
        pltpu.make_async_copy(source, target, sems.at[i])
        for i, (source, target) in enumerate(
            [(ids_ref, ids), (valid_ref, valid), (weights_ref, weights)]
        )
    ]
    held = block_copies(lik_ref, held_ref, held_sems, 0)
    for copy in copies + held:
        copy.start()
    wide[...] = jnp.zeros_like(wide)
    for copy in copies:
        copy.wait()
    read_blocks, slots = ids.shape
    count, rows, cols = out_ref.shape
    own_blocks = weights.shape[0]
    lane = lax.broadcasted_iota(jnp.int32, (1, cols), 1)
    wide[:, :slots] = jnp.where(valid[...] > 0, ids[...], -1).astype(jnp.float32)
    flat = jnp.sum(
        pltpu.roll(wide[...], 0, 1, stride=slots, stride_axis=0), axis=0, keepdims=True
    )
    flat = jnp.where(lane < read_blocks * slots, flat, -1.0)
    for i in range(count):
        out_ref[i, :own_blocks, :] = weights[...]
        out_ref[i, own_blocks:, :] = jnp.broadcast_to(flat, (rows - own_blocks, cols))
    block = jnp.maximum(flat, 0.0)
    owner = ((block + 0.5) * (1.0 / own_blocks)).astype(jnp.int32)
    inside = block.astype(jnp.int32) - owner * own_blocks
    place = jnp.where(flat < 0, -1, (owner ^ first) * rows + inside).astype(jnp.float32)
    row = lax.broadcasted_iota(jnp.int32, info_ref.shape, 0)
    info_ref[...] = jnp.where(row == 0, flat, jnp.where(row == 1, place, 0.0))
    for copy in held:
        copy.wait()


def block_copies(lik_ref, held_ref, sems, start):
    return [
        pltpu.make_async_copy(lik_ref.at[start + b], held_ref.at[b], sems.at[b])
        for b in range(held_ref.shape[0])
    ]


def block_of(held_refs, b):
    first, second = held_refs
    return first.at[b] if b < first.shape[0] else second.at[b - first.shape[0]]


def row_sums(picked_ref, held_refs, out_ref, copies=()):
    slots = held_refs[0].shape[1]
    early = out_ref.shape[1] - len(copies)
    for b in range(out_ref.shape[1]):
        if copies and b >= early:
            copies[b - early].wait()
        lik_ref = block_of(held_refs, b)
        total = None
        for s in range(0, slots, 2):
            at = b * slots + s
            left = jnp.concatenate(
                [split(picked_ref[at : at + 1, :]), split(picked_ref[at + 1 : at + 2, :])], axis=1
            )
            right = jnp.concatenate([lik_ref[s], lik_ref[s + 1]], axis=1)
            part = dot(left, right, (((1,), (1,)), ((), ())))
            total = part if total is None else total + part
        row = jnp.sum(total, axis=0, keepdims=True)
        for i in range(out_ref.shape[0]):
            out_ref[i, b : b + 1, :] = row


def first_row_kernel(
    info_ref, table_ref, early_ref, lik_ref, out_ref, picked_ref, late_ref, sems
):
    copies = block_copies(lik_ref, late_ref, sems, early_ref.shape[0])
    for copy in copies:
        copy.start()
    count, rows, cols = table_ref.shape
    hot = hot_rows(info_ref[1:2, :], count * rows)
    table = table_ref[...].reshape(count * rows, cols)
    picked_ref[...] = select_rows(hot[: picked_ref.shape[0]], table)
    row_sums(picked_ref, (early_ref, late_ref), out_ref, copies)


def next_row_kernel(near, scale, *refs):
    parts, (early_ref, late_ref, out_ref, picked_ref) = refs[:near], refs[near:]
    total = parts[0][...]
    for part in parts[1:]:
        total = total + part[...]
    picked_ref[...] = total * scale
    row_sums(picked_ref, (early_ref, late_ref), out_ref)


def column_sums(parts_ref, picked_ref, held_refs, contrib_ref, inverse_ref):
    slots, cols = held_refs[0].shape[1], held_refs[0].shape[3]
    total = parts_ref[0]
    for i in range(1, parts_ref.shape[0]):
        total = total + parts_ref[i]
    inverse_ref[...] = 1.0 / total
    for b in range(inverse_ref.shape[0]):
        lik_ref = block_of(held_refs, b)
        left = split(inverse_ref[b : b + 1, :])
        for s in range(0, slots, 2):
            at = b * slots + s
            right = jnp.concatenate([lik_ref[s], lik_ref[s + 1]], axis=1)
            summed = jnp.sum(dot(left, right), axis=0, keepdims=True)
            contrib_ref[at : at + 1, :] = picked_ref[at : at + 1, :] * summed[:, :cols]
            contrib_ref[at + 1 : at + 2, :] = picked_ref[at + 1 : at + 2, :] * summed[:, cols:]


def column_kernel(parts_ref, picked_ref, early_ref, late_ref, out_ref, inverse_ref):
    column_sums(parts_ref, picked_ref, (early_ref, late_ref), out_ref, inverse_ref)


def last_column_kernel(
    order, info_ref, parts_ref, picked_ref, early_ref, late_ref, out_ref, inverse_ref, contrib_ref
):
    column_sums(parts_ref, picked_ref, (early_ref, late_ref), contrib_ref, inverse_ref)
    owners, own_blocks, cols = out_ref.shape
    all_slots = contrib_ref.shape[0]
    block = lax.broadcasted_iota(jnp.int32, (owners * own_blocks, all_slots), 0)
    hot = (block.astype(jnp.float32) == info_ref[0:1, :all_slots]).astype(jnp.float32)
    counts = select_rows(hot, contrib_ref[...])
    for i, owner in enumerate(order):
        out_ref[i] = counts[owner * own_blocks : (owner + 1) * own_blocks, :]


def wanted_kernel(first, own_blocks, table_ref, *refs):
    n = lax.axis_size(ALL)
    me = lax.axis_index("genome") * 2 + lax.axis_index("reads")
    near = radices(n)[0]
    given_refs, outs = refs[:-near], refs[-near:]
    all_slots = outs[0].shape[0]
    half = LANES // 2
    lane = lax.broadcasted_iota(jnp.int32, (1, LANES), 1)

    def ids_of(k):
        return table_ref[me ^ k ^ first, own_blocks : own_blocks + 1, :]

    ids = [ids_of(k) for k in far_order(n)]
    pairs = [
        jnp.where(lane < half, a, pltpu.roll(b, half, 1)) for a, b in zip(ids[::2], ids[1::2])
    ]
    given = terms(jnp.concatenate([ref[...] for ref in given_refs], axis=0))
    for j, out_ref in enumerate(outs):
        column = down(ids_of(j))[:all_slots]
        hot = jnp.concatenate([(column == pair).astype(jnp.float32) for pair in pairs], axis=1)
        hot = hot.astype(jnp.bfloat16)
        out_ref[...] = dot(hot, given[0]) + dot(hot, given[1]) + dot(hot, given[2])


PARAMS = pltpu.CompilerParams(vmem_limit_bytes=16 * 2**20)


def call(kernel, outs, scratch, *operands):
    return pl.pallas_call(
        kernel,
        out_shape=[jax.ShapeDtypeStruct(shape, jnp.float32) for shape in outs],
        in_specs=[VMEM] * len(operands),
        out_specs=[VMEM] * len(outs),
        scratch_shapes=[pltpu.VMEM(shape, jnp.float32) for shape in scratch],
        compiler_params=PARAMS,
    )(*operands)


def in_hbm(*arrays):
    return [pltpu.with_memory_space_constraint(x, pltpu.HBM) for x in arrays]


def prepare(shape, first, early, weights, block_ids, slot_valid, likelihood):
    return pl.pallas_call(
        lambda *refs: prepare_kernel(first, *refs),
        out_shape=[
            jax.ShapeDtypeStruct(shape, jnp.float32),
            jax.ShapeDtypeStruct((8, LANES), jnp.float32),
            pltpu.VMEM((early,) + likelihood.shape[1:], likelihood.dtype),
        ],
        in_specs=[ANY] * 4,
        out_specs=[VMEM] * 3,
        scratch_shapes=[
            pltpu.VMEM(weights.shape, jnp.float32),
            pltpu.VMEM(block_ids.shape, jnp.int32),
            pltpu.VMEM(block_ids.shape, jnp.int32),
            pltpu.VMEM((block_ids.shape[0], LANES), jnp.float32),
            pltpu.SemaphoreType.DMA((3,)),
            pltpu.SemaphoreType.DMA((early,)),
        ],
        compiler_params=PARAMS,
    )(*in_hbm(weights, block_ids, slot_valid, likelihood))


def first_rows(outs, info, table, held, likelihood):
    late = likelihood.shape[0] - held.shape[0]
    return pl.pallas_call(
        first_row_kernel,
        out_shape=[jax.ShapeDtypeStruct(shape, jnp.float32) for shape in outs]
        + [pltpu.VMEM((late,) + likelihood.shape[1:], likelihood.dtype)],
        in_specs=[VMEM] * 3 + [ANY],
        out_specs=[VMEM] * 3,
        scratch_shapes=[pltpu.SemaphoreType.DMA((late,))],
        compiler_params=PARAMS,
    )(info, table, held, *in_hbm(likelihood))


def local(likelihood, block_ids, slot_valid, start_weights):
    read_blocks, slots, reads, cols = likelihood.shape
    n = lax.axis_size(ALL)
    chips = lax.axis_size("genome")
    near = radices(n)[0]
    own_weights = start_weights.reshape(-1, cols)
    own_blocks = own_weights.shape[0]
    all_slots = read_blocks * slots
    total_reads = read_blocks * lax.axis_size("reads") * reads
    scale = n * own_blocks * cols / total_reads
    first_chip = chips // 2 + 1
    first = first_chip * 2 + 1
    order = middle_first(n, first)

    rows = -(-(own_blocks + 1) // 8) * 8
    early = read_blocks * 3 // 8
    sent, info, held = prepare(
        (n, rows, cols), first, early, own_weights, block_ids, slot_valid, likelihood
    )
    table = lax.all_to_all(sent, ALL, 0, 0, tiled=True, axis_index_groups=[order])

    outs = [(chips, read_blocks, reads), (all_slots, cols)]
    inverse = (read_blocks, reads)
    for step in range(ITERS):
        if step == 0:
            row_parts, picked, rest = first_rows(outs, info, table, held, likelihood)
            held = [held, rest]
        else:
            row_parts, picked = call(
                lambda *refs: next_row_kernel(near, scale, *refs), outs, [], *parts, *held
            )
        row_parts = lax.all_to_all(
            row_parts,
            "genome",
            0,
            0,
            tiled=True,
            axis_index_groups=[middle_first(chips, first_chip)],
        )
        if step + 1 < ITERS:
            (contrib,) = call(
                column_kernel, [(all_slots, cols)], [inverse], row_parts, picked, *held
            )
            sums = call(
                lambda *refs: wanted_kernel(first, own_blocks, *refs),
                [(all_slots, cols)] * near,
                [],
                table,
                *gather_far(contrib, ALL),
            )
            parts = [sums[0]] + [swap(sums[j], ALL, j) for j in range(1, near)]
    (counts,) = call(
        lambda *refs: last_column_kernel(order, *refs),
        [(n, own_blocks, cols)],
        [inverse, (all_slots, cols)],
        info,
        row_parts,
        picked,
        *held,
    )
    counts = lax.all_to_all(counts, ALL, 0, 0, tiled=True, axis_index_groups=[order])
    return (jnp.sum(counts, axis=0) * scale).reshape(-1)


def solution(mesh):
    placed = (
        P(("parts", "reads"), "genome", None, None),
        P(("parts", "reads"), "genome"),
        P(("parts", "reads"), "genome"),
        P(("parts", "genome", "reads")),
    )
    return jax.shard_map(
        local,
        mesh=mesh,
        in_specs=placed,
        out_specs=P(("parts", "genome", "reads")),
        check_vma=False,
    )
```

```python
import jax
import jax.numpy as jnp
from jax import lax
from jax.experimental import pallas as pl
from jax.experimental.pallas import tpu as pltpu
from jax.sharding import PartitionSpec as P

ITERS = 2
ALL = ("genome", "reads")
TERMS = 16
ID_ROWS = 8
LANES = 128
VMEM = pl.BlockSpec(memory_space=pltpu.VMEM)
ANY = pl.BlockSpec(memory_space=pl.ANY)


def radices(n):
    out = []
    while n > 1:
        r = 4 if n % 4 == 0 else 2
        out.append(r)
        n //= r
    return out


def swap(x, axes, k):
    n = lax.axis_size(axes)
    return lax.ppermute(x, axes, [(i, i ^ k) for i in range(n)])


def middle_first(n, k):
    return [i ^ k for i in range(n)]


def position(k, n):
    place = 0
    for r in radices(n):
        n //= r
        place = place + (k % r) * n
        k = k // r
    return place


def gather_far(x, axes):
    parts = [x]
    stride = lax.axis_size(axes)
    for r in radices(stride)[:0:-1]:
        stride //= r
        sent = parts[0] if len(parts) == 1 else jnp.concatenate(parts, axis=0)
        parts = [sent] + [swap(sent, axes, j * stride) for j in range(1, r)]
    return parts


def dot(a, b, dims=(((1,), (0,)), ((), ()))):
    return lax.dot_general(a, b, dims, preferred_element_type=jnp.float32)


def terms(x):
    hi = x.astype(jnp.bfloat16)
    rest = x - hi.astype(jnp.float32)
    mid = rest.astype(jnp.bfloat16)
    return hi, mid, (rest - mid.astype(jnp.float32)).astype(jnp.bfloat16)


def select_rows(hot, x):
    hi, mid, low = terms(x)
    hot = hot.astype(jnp.bfloat16)
    return dot(hot, hi) + dot(hot, mid) + dot(hot, low)


def split(row):
    x = jnp.broadcast_to(row, (TERMS, row.shape[1]))
    hi = x.astype(jnp.bfloat16).astype(jnp.float32)
    rest = x - hi
    mid = rest.astype(jnp.bfloat16).astype(jnp.float32)
    low = rest - mid
    at = lax.broadcasted_iota(jnp.int32, x.shape, 0)
    out = jnp.where(at == 0, hi, jnp.where(at == 1, mid, jnp.where(at == 2, low, 0.0)))
    return out.astype(jnp.bfloat16)


def down(row):
    return jnp.transpose(jnp.broadcast_to(row, (LANES, LANES)))


def hot_rows(values, count):
    column = down(values)
    blocks = []
    for start in range(0, count, LANES):
        width = min(LANES, count - start)
        lane = lax.broadcasted_iota(jnp.int32, (LANES, width), 1).astype(jnp.float32) + start
        blocks.append((column[:, :width] == lane).astype(jnp.float32))
    return blocks[0] if len(blocks) == 1 else jnp.concatenate(blocks, axis=1)


def prepare_kernel(own_blocks, lik_ref, ids_ref, valid_ref, held_ref, info_ref, ids, valid, wide, sems):
    read_blocks, slots = ids.shape
    copies = [
        pltpu.make_async_copy(ids_ref, ids, sems.at[0]),
        pltpu.make_async_copy(valid_ref, valid, sems.at[1]),
    ]
    held = [
        pltpu.make_async_copy(lik_ref.at[b], held_ref.at[b], sems.at[2 + b])
        for b in range(held_ref.shape[0])
    ]
    for copy in copies + held:
        copy.start()
    for copy in copies:
        copy.wait()
    n = lax.axis_size(ALL)
    near = radices(n)[0]
    far = n // near
    me = lax.axis_index("genome") * lax.axis_size("reads") + lax.axis_index("reads")
    lane = lax.broadcasted_iota(jnp.int32, wide.shape, 1)
    wide[...] = jnp.zeros_like(wide)
    wide[:, :slots] = jnp.where(valid[...] > 0, ids[...], -1).astype(jnp.float32)
    flat = jnp.sum(
        pltpu.roll(wide[...], 0, 1, stride=slots, stride_axis=0), axis=0, keepdims=True
    )
    flat = jnp.where(lane[:1] < read_blocks * slots, flat, -1.0)
    owner = ((flat + 0.5) * (1.0 / own_blocks)).astype(jnp.int32)
    inside = flat.astype(jnp.int32) - owner * own_blocks
    away = owner ^ me
    place = position(away, n)
    place = (place // far) * near_rows(far, own_blocks) + (place % far) * own_blocks + inside
    place = jnp.where(flat < 0, -1, place).astype(jnp.float32)
    row = lax.broadcasted_iota(jnp.int32, info_ref.shape, 0)
    info_ref[...] = jnp.where(row == 0, flat, jnp.where(row == 1, place, 0.0))
    for copy in held:
        copy.wait()


def join_kernel(*refs):
    out_ref = refs[-1]
    at = 0
    for ref in refs[:-1]:
        out_ref[at : at + ref.shape[0], :] = ref[...]
        at += ref.shape[0]
    if at < out_ref.shape[0]:
        out_ref[at:, :] = jnp.zeros((out_ref.shape[0] - at, out_ref.shape[1]), jnp.float32)


def near_rows(far, own_blocks):
    return -(-(far * own_blocks + ID_ROWS) // 16) * 16


def flip_kernel(after_ref, lik_ref, out_ref):
    read_blocks, slots, reads, cols = lik_ref.shape
    for b in range(read_blocks):
        for s in range(slots):
            start = s % 2 * cols
            out_ref[b, s // 2, start : start + cols, :] = jnp.transpose(lik_ref[b, s])


def row_sums(picked_ref, flip_ref, out_ref):
    read_blocks, pairs = flip_ref.shape[:2]
    for b in range(read_blocks):
        total = None
        for s in range(pairs):
            at = (b * pairs + s) * 2
            left = jnp.concatenate(
                [split(picked_ref[at : at + 1, :]), split(picked_ref[at + 1 : at + 2, :])], axis=1
            )
            part = dot(left, flip_ref[b, s])
            total = part if total is None else total + part
        row = jnp.sum(total, axis=0, keepdims=True)
        for i in range(out_ref.shape[0]):
            out_ref[i, b : b + 1, :] = row


def first_row_kernel(near, info_ref, *refs):
    pieces, (flip_ref, out_ref, picked_ref) = refs[:near], refs[near:]
    table = jnp.concatenate([piece[...] for piece in pieces], axis=0)
    hot = hot_rows(info_ref[1:2, :], table.shape[0])
    picked_ref[...] = select_rows(hot[: picked_ref.shape[0]], table)
    row_sums(picked_ref, flip_ref, out_ref)


def next_row_kernel(near, scale, *refs):
    parts, (flip_ref, out_ref, picked_ref) = refs[:near], refs[near:]
    total = parts[0][...]
    for part in parts[1:]:
        total = total + part[...]
    picked_ref[...] = total * scale
    row_sums(picked_ref, flip_ref, out_ref)


def column_sums(parts_ref, picked_ref, lik_ref, contrib_ref, inverse_ref):
    read_blocks, slots, reads, cols = lik_ref.shape
    total = parts_ref[0]
    for i in range(1, parts_ref.shape[0]):
        total = total + parts_ref[i]
    inverse_ref[...] = 1.0 / total
    for b in range(read_blocks):
        left = split(inverse_ref[b : b + 1, :])
        for s in range(0, slots, 2):
            at = b * slots + s
            right = jnp.concatenate([lik_ref[b, s], lik_ref[b, s + 1]], axis=1)
            summed = jnp.sum(dot(left, right), axis=0, keepdims=True)
            contrib_ref[at : at + 1, :] = picked_ref[at : at + 1, :] * summed[:, :cols]
            contrib_ref[at + 1 : at + 2, :] = picked_ref[at + 1 : at + 2, :] * summed[:, cols:]


def column_kernel(info_ref, parts_ref, picked_ref, lik_ref, out_ref, inverse_ref):
    column_sums(parts_ref, picked_ref, lik_ref, out_ref, inverse_ref)
    out_ref[picked_ref.shape[0] :, :] = info_ref[...]


def last_column_kernel(order, info_ref, parts_ref, picked_ref, lik_ref, out_ref, inverse_ref, contrib_ref):
    column_sums(parts_ref, picked_ref, lik_ref, contrib_ref, inverse_ref)
    owners, own_blocks, cols = out_ref.shape
    all_slots = contrib_ref.shape[0]
    block = lax.broadcasted_iota(jnp.int32, (owners * own_blocks, all_slots), 0)
    hot = (block.astype(jnp.float32) == info_ref[0:1, :all_slots]).astype(jnp.float32)
    counts = select_rows(hot, contrib_ref[...])
    for i, owner in enumerate(order):
        out_ref[i] = counts[owner * own_blocks : (owner + 1) * own_blocks, :]


def wanted_kernel(near, all_slots, pieces, *refs):
    given_refs, wanted, outs = refs[:pieces], refs[pieces : pieces + near], refs[pieces + near :]
    rows = all_slots + ID_ROWS
    half = LANES // 2
    lane = lax.broadcasted_iota(jnp.int32, (1, LANES), 1)
    ids, values = [], []
    for ref in given_refs:
        for at in range(0, ref.shape[0], rows):
            ids.append(ref[at + all_slots : at + all_slots + 1, :])
            values.append(ref[at : at + all_slots, :])
    pairs = [
        jnp.where(lane < half, a, pltpu.roll(b, half, 1)) for a, b in zip(ids[::2], ids[1::2])
    ]
    given = terms(jnp.concatenate(values, axis=0))
    for ids_ref, out_ref in zip(wanted, outs):
        column = down(ids_ref[0:1, :])[:all_slots]
        hot = jnp.concatenate([(column == pair).astype(jnp.float32) for pair in pairs], axis=1)
        hot = hot.astype(jnp.bfloat16)
        out_ref[...] = dot(hot, given[0]) + dot(hot, given[1]) + dot(hot, given[2])


def call(kernel, outs, scratch, *operands):
    return pl.pallas_call(
        kernel,
        out_shape=[jax.ShapeDtypeStruct(shape, jnp.float32) for shape in outs],
        in_specs=[VMEM] * len(operands),
        out_specs=[VMEM] * len(outs),
        scratch_shapes=[pltpu.VMEM(shape, jnp.float32) for shape in scratch],
        compiler_params=pltpu.CompilerParams(vmem_limit_bytes=16 * 2**20),
    )(*operands)


def prepare(own_blocks, likelihood, block_ids, slot_valid):
    read_blocks, slots = block_ids.shape
    return pl.pallas_call(
        lambda *refs: prepare_kernel(own_blocks, *refs),
        out_shape=[
            pltpu.VMEM(likelihood.shape, likelihood.dtype),
            jax.ShapeDtypeStruct((ID_ROWS, LANES), jnp.float32),
        ],
        in_specs=[ANY] * 3,
        out_specs=[VMEM] * 2,
        scratch_shapes=[
            pltpu.VMEM((read_blocks, slots), jnp.int32),
            pltpu.VMEM((read_blocks, slots), jnp.int32),
            pltpu.VMEM((read_blocks, LANES), jnp.float32),
            pltpu.SemaphoreType.DMA((2 + read_blocks,)),
        ],
        compiler_params=pltpu.CompilerParams(vmem_limit_bytes=16 * 2**20),
    )(*[pltpu.with_memory_space_constraint(x, pltpu.HBM) for x in (likelihood, block_ids, slot_valid)])


def flip(after, likelihood):
    read_blocks, slots, reads, cols = likelihood.shape
    return pl.pallas_call(
        flip_kernel,
        out_shape=pltpu.VMEM((read_blocks, slots // 2, 2 * cols, reads), likelihood.dtype),
        in_specs=[ANY, VMEM],
        out_specs=VMEM,
        compiler_params=pltpu.CompilerParams(vmem_limit_bytes=16 * 2**20),
    )(after, likelihood)


def local(likelihood, block_ids, slot_valid, start_weights):
    read_blocks, slots, reads, cols = likelihood.shape
    n = lax.axis_size(ALL)
    chips = lax.axis_size("genome")
    near = radices(n)[0]
    far = n // near
    own_weights = start_weights.reshape(-1, cols)
    own_blocks = own_weights.shape[0]
    all_slots = read_blocks * slots
    total_reads = read_blocks * lax.axis_size("reads") * reads
    scale = n * own_blocks * cols / total_reads

    column = gather_far(own_weights, ALL)
    held, info = prepare(own_blocks, likelihood, block_ids, slot_valid)
    (sent,) = call(join_kernel, [(near_rows(far, own_blocks), cols)], [], *column, info)
    flipped = flip(sent, held)
    pieces = [sent] + [swap(sent, ALL, j) for j in range(1, near)]
    at = far * own_blocks
    wanted = [info] + [piece[at : at + ID_ROWS] for piece in pieces[1:]]

    row_shapes = [(chips, read_blocks, reads), (all_slots, cols)]
    inverse = (read_blocks, reads)
    for step in range(ITERS):
        if step == 0:
            row_parts, picked = call(
                lambda *refs: first_row_kernel(near, *refs), row_shapes, [], info, *pieces, flipped
            )
        else:
            row_parts, picked = call(
                lambda *refs: next_row_kernel(near, scale, *refs), row_shapes, [], *parts, flipped
            )
        row_parts = lax.all_to_all(
            row_parts,
            "genome",
            0,
            0,
            tiled=True,
            axis_index_groups=[middle_first(chips, chips // 2 + 1)],
        )
        if step + 1 < ITERS:
            (contrib,) = call(
                column_kernel,
                [(all_slots + ID_ROWS, cols)],
                [inverse],
                info,
                row_parts,
                picked,
                held,
            )
            given = gather_far(contrib, ALL)
            sums = call(
                lambda *refs: wanted_kernel(near, all_slots, len(given), *refs),
                [(all_slots, cols)] * near,
                [],
                *given,
                *wanted,
            )
            parts = [sums[0]] + [swap(sums[j], ALL, j) for j in range(1, near)]
    order = middle_first(n, n // 2 + 3)
    (counts,) = call(
        lambda *refs: last_column_kernel(order, *refs),
        [(n, own_blocks, cols)],
        [inverse, (all_slots, cols)],
        info,
        row_parts,
        picked,
        held,
    )
    counts = lax.all_to_all(counts, ALL, 0, 0, tiled=True, axis_index_groups=[order])
    return (jnp.sum(counts, axis=0) * scale).reshape(-1)


def solution(mesh):
    placed = (
        P(("parts", "reads"), "genome", None, None),
        P(("parts", "reads"), "genome"),
        P(("parts", "reads"), "genome"),
        P(("parts", "genome", "reads")),
    )
    return jax.shard_map(
        local,
        mesh=mesh,
        in_specs=placed,
        out_specs=P(("parts", "genome", "reads")),
        check_vma=False,
    )
```

```python
import jax
import jax.numpy as jnp
from jax import lax
from jax.experimental import pallas as pl
from jax.experimental.pallas import tpu as pltpu
from jax.sharding import PartitionSpec as P

ITERS = 2
ALL = ("genome", "reads")
TERMS = 16
ID_ROWS = 8
LANES = 128
VMEM = pl.BlockSpec(memory_space=pltpu.VMEM)
ANY = pl.BlockSpec(memory_space=pl.ANY)


def radices(n):
    out = []
    while n > 1:
        r = 4 if n % 4 == 0 else 2
        out.append(r)
        n //= r
    return out


def swap(x, axes, k):
    n = lax.axis_size(axes)
    return lax.ppermute(x, axes, [(i, i ^ k) for i in range(n)])


def middle_first(n, k):
    return [i ^ k for i in range(n)]


def position(k, n):
    place = 0
    for r in radices(n):
        n //= r
        place = place + (k % r) * n
        k = k // r
    return place


def gather_far(x, axes):
    parts = [x]
    stride = lax.axis_size(axes)
    for r in radices(stride)[:0:-1]:
        stride //= r
        sent = parts[0] if len(parts) == 1 else jnp.concatenate(parts, axis=0)
        parts = [sent] + [swap(sent, axes, j * stride) for j in range(1, r)]
    return parts


def gather_shared(x, axes):
    n = lax.axis_size(axes)
    radix = radices(n)[1:]
    if radix[-1] != 4:
        return gather_far(x, axes)
    stride = n // 4
    parts = [x]
    step = radices(n)[0]
    for r in radix[:-1]:
        sent = parts[0] if len(parts) == 1 else jnp.concatenate(parts, axis=0)
        parts = [sent] + [swap(sent, axes, j * step) for j in range(1, r)]
        step *= r
    x = parts[0] if len(parts) == 1 else jnp.concatenate(parts, axis=0)
    other = lax.ppermute(x, axes, [(i, i ^ 1) for i in range(0, n, 2)])

    def to(x, first, second):
        pairs = [(i, i ^ (j * stride)) for i in range(n) if (j := (first, second)[i % 2])]
        return lax.ppermute(x, axes, pairs)

    return [x, to(x, 0, 1), to(x, 1, 2), to(x, 2, 3), to(other, 0, 3)]


def dot(a, b, dims=(((1,), (0,)), ((), ()))):
    return lax.dot_general(a, b, dims, preferred_element_type=jnp.float32)


def terms(x):
    hi = x.astype(jnp.bfloat16)
    rest = x - hi.astype(jnp.float32)
    mid = rest.astype(jnp.bfloat16)
    return hi, mid, (rest - mid.astype(jnp.float32)).astype(jnp.bfloat16)


def select_rows(hot, x):
    hi, mid, low = terms(x)
    hot = hot.astype(jnp.bfloat16)
    return dot(hot, hi) + dot(hot, mid) + dot(hot, low)


def split(row):
    x = jnp.broadcast_to(row, (TERMS, row.shape[1]))
    hi = x.astype(jnp.bfloat16).astype(jnp.float32)
    rest = x - hi
    mid = rest.astype(jnp.bfloat16).astype(jnp.float32)
    low = rest - mid
    at = lax.broadcasted_iota(jnp.int32, x.shape, 0)
    out = jnp.where(at == 0, hi, jnp.where(at == 1, mid, jnp.where(at == 2, low, 0.0)))
    return out.astype(jnp.bfloat16)


def down(row):
    return jnp.transpose(jnp.broadcast_to(row, (LANES, LANES)))


def hot_rows(values, count):
    column = down(values)
    blocks = []
    for start in range(0, count, LANES):
        width = min(LANES, count - start)
        lane = lax.broadcasted_iota(jnp.int32, (LANES, width), 1).astype(jnp.float32) + start
        blocks.append((column[:, :width] == lane).astype(jnp.float32))
    return blocks[0] if len(blocks) == 1 else jnp.concatenate(blocks, axis=1)


def prepare_kernel(own_blocks, lik_ref, ids_ref, valid_ref, held_ref, info_ref, ids, valid, wide, sems):
    read_blocks, slots = ids.shape
    copies = [
        pltpu.make_async_copy(ids_ref, ids, sems.at[0]),
        pltpu.make_async_copy(valid_ref, valid, sems.at[1]),
    ]
    held = [
        pltpu.make_async_copy(lik_ref.at[b], held_ref.at[b], sems.at[2 + b])
        for b in range(held_ref.shape[0])
    ]
    for copy in copies + held:
        copy.start()
    for copy in copies:
        copy.wait()
    n = lax.axis_size(ALL)
    near = radices(n)[0]
    far = n // near
    me = lax.axis_index("genome") * lax.axis_size("reads") + lax.axis_index("reads")
    lane = lax.broadcasted_iota(jnp.int32, wide.shape, 1)
    wide[...] = jnp.zeros_like(wide)
    wide[:, :slots] = jnp.where(valid[...] > 0, ids[...], -1).astype(jnp.float32)
    flat = jnp.sum(
        pltpu.roll(wide[...], 0, 1, stride=slots, stride_axis=0), axis=0, keepdims=True
    )
    flat = jnp.where(lane[:1] < read_blocks * slots, flat, -1.0)
    owner = ((flat + 0.5) * (1.0 / own_blocks)).astype(jnp.int32)
    inside = flat.astype(jnp.int32) - owner * own_blocks
    away = owner ^ me
    place = position(away, n)
    place = (place // far) * near_rows(far, own_blocks) + (place % far) * own_blocks + inside
    place = jnp.where(flat < 0, -1, place).astype(jnp.float32)
    row = lax.broadcasted_iota(jnp.int32, info_ref.shape, 0)
    info_ref[...] = jnp.where(row == 0, flat, jnp.where(row == 1, place, 0.0))
    for copy in held:
        copy.wait()


def join_kernel(*refs):
    out_ref = refs[-1]
    at = 0
    for ref in refs[:-1]:
        out_ref[at : at + ref.shape[0], :] = ref[...]
        at += ref.shape[0]
    if at < out_ref.shape[0]:
        out_ref[at:, :] = jnp.zeros((out_ref.shape[0] - at, out_ref.shape[1]), jnp.float32)


def near_rows(far, own_blocks):
    return -(-(far * own_blocks + ID_ROWS) // 16) * 16


def flip_kernel(after_ref, lik_ref, out_ref):
    read_blocks, slots, reads, cols = lik_ref.shape
    for b in range(read_blocks):
        for s in range(slots):
            start = s % 2 * cols
            out_ref[b, s // 2, start : start + cols, :] = jnp.transpose(lik_ref[b, s])


def row_sums(picked_ref, flip_ref, out_ref):
    read_blocks, pairs = flip_ref.shape[:2]
    for b in range(read_blocks):
        total = None
        for s in range(pairs):
            at = (b * pairs + s) * 2
            left = jnp.concatenate(
                [split(picked_ref[at : at + 1, :]), split(picked_ref[at + 1 : at + 2, :])], axis=1
            )
            part = dot(left, flip_ref[b, s])
            total = part if total is None else total + part
        row = jnp.sum(total, axis=0, keepdims=True)
        for i in range(out_ref.shape[0]):
            out_ref[i, b : b + 1, :] = row


def first_row_kernel(near, info_ref, *refs):
    pieces, (flip_ref, out_ref, picked_ref) = refs[:near], refs[near:]
    table = jnp.concatenate([piece[...] for piece in pieces], axis=0)
    hot = hot_rows(info_ref[1:2, :], table.shape[0])
    picked_ref[...] = select_rows(hot[: picked_ref.shape[0]], table)
    row_sums(picked_ref, flip_ref, out_ref)


def next_row_kernel(near, scale, *refs):
    parts, (flip_ref, out_ref, picked_ref) = refs[:near], refs[near:]
    total = parts[0][...]
    for part in parts[1:]:
        total = total + part[...]
    picked_ref[...] = total * scale
    row_sums(picked_ref, flip_ref, out_ref)


def column_sums(parts_ref, picked_ref, lik_ref, contrib_ref, inverse_ref):
    read_blocks, slots, reads, cols = lik_ref.shape
    total = parts_ref[0]
    for i in range(1, parts_ref.shape[0]):
        total = total + parts_ref[i]
    inverse_ref[...] = 1.0 / total
    for b in range(read_blocks):
        left = split(inverse_ref[b : b + 1, :])
        for s in range(0, slots, 2):
            at = b * slots + s
            right = jnp.concatenate([lik_ref[b, s], lik_ref[b, s + 1]], axis=1)
            summed = jnp.sum(dot(left, right), axis=0, keepdims=True)
            contrib_ref[at : at + 1, :] = picked_ref[at : at + 1, :] * summed[:, :cols]
            contrib_ref[at + 1 : at + 2, :] = picked_ref[at + 1 : at + 2, :] * summed[:, cols:]


def column_kernel(info_ref, parts_ref, picked_ref, lik_ref, out_ref, inverse_ref):
    column_sums(parts_ref, picked_ref, lik_ref, out_ref, inverse_ref)
    out_ref[picked_ref.shape[0] :, :] = info_ref[...]


def last_column_kernel(order, info_ref, parts_ref, picked_ref, lik_ref, out_ref, inverse_ref, contrib_ref):
    column_sums(parts_ref, picked_ref, lik_ref, contrib_ref, inverse_ref)
    owners, own_blocks, cols = out_ref.shape
    all_slots = contrib_ref.shape[0]
    block = lax.broadcasted_iota(jnp.int32, (owners * own_blocks, all_slots), 0)
    hot = (block.astype(jnp.float32) == info_ref[0:1, :all_slots]).astype(jnp.float32)
    counts = select_rows(hot, contrib_ref[...])
    for i, owner in enumerate(order):
        out_ref[i] = counts[owner * own_blocks : (owner + 1) * own_blocks, :]


def wanted_kernel(near, all_slots, pieces, *refs):
    given_refs, wanted, outs = refs[:pieces], refs[pieces : pieces + near], refs[pieces + near :]
    rows = all_slots + ID_ROWS
    half = LANES // 2
    lane = lax.broadcasted_iota(jnp.int32, (1, LANES), 1)
    ids, values = [], []
    for ref in given_refs:
        for at in range(0, ref.shape[0], rows):
            ids.append(ref[at + all_slots : at + all_slots + 1, :])
            values.append(ref[at : at + all_slots, :])
    if len(ids) % 2:
        ids.append(jnp.full_like(ids[0], -2.0))
        values.append(jnp.zeros_like(values[0]))
    pairs = [
        jnp.where(lane < half, a, pltpu.roll(b, half, 1)) for a, b in zip(ids[::2], ids[1::2])
    ]
    given = terms(jnp.concatenate(values, axis=0))
    for ids_ref, out_ref in zip(wanted, outs):
        column = down(ids_ref[0:1, :])[:all_slots]
        hot = jnp.concatenate([(column == pair).astype(jnp.float32) for pair in pairs], axis=1)
        hot = hot.astype(jnp.bfloat16)
        out_ref[...] = dot(hot, given[0]) + dot(hot, given[1]) + dot(hot, given[2])


def call(kernel, outs, scratch, *operands):
    return pl.pallas_call(
        kernel,
        out_shape=[jax.ShapeDtypeStruct(shape, jnp.float32) for shape in outs],
        in_specs=[VMEM] * len(operands),
        out_specs=[VMEM] * len(outs),
        scratch_shapes=[pltpu.VMEM(shape, jnp.float32) for shape in scratch],
        compiler_params=pltpu.CompilerParams(vmem_limit_bytes=16 * 2**20),
    )(*operands)


def prepare(own_blocks, likelihood, block_ids, slot_valid):
    read_blocks, slots = block_ids.shape
    return pl.pallas_call(
        lambda *refs: prepare_kernel(own_blocks, *refs),
        out_shape=[
            pltpu.VMEM(likelihood.shape, likelihood.dtype),
            jax.ShapeDtypeStruct((ID_ROWS, LANES), jnp.float32),
        ],
        in_specs=[ANY] * 3,
        out_specs=[VMEM] * 2,
        scratch_shapes=[
            pltpu.VMEM((read_blocks, slots), jnp.int32),
            pltpu.VMEM((read_blocks, slots), jnp.int32),
            pltpu.VMEM((read_blocks, LANES), jnp.float32),
            pltpu.SemaphoreType.DMA((2 + read_blocks,)),
        ],
        compiler_params=pltpu.CompilerParams(vmem_limit_bytes=16 * 2**20),
    )(*[pltpu.with_memory_space_constraint(x, pltpu.HBM) for x in (likelihood, block_ids, slot_valid)])


def flip(after, likelihood):
    read_blocks, slots, reads, cols = likelihood.shape
    return pl.pallas_call(
        flip_kernel,
        out_shape=pltpu.VMEM((read_blocks, slots // 2, 2 * cols, reads), likelihood.dtype),
        in_specs=[ANY, VMEM],
        out_specs=VMEM,
        compiler_params=pltpu.CompilerParams(vmem_limit_bytes=16 * 2**20),
    )(after, likelihood)


def local(likelihood, block_ids, slot_valid, start_weights):
    read_blocks, slots, reads, cols = likelihood.shape
    n = lax.axis_size(ALL)
    chips = lax.axis_size("genome")
    near = radices(n)[0]
    far = n // near
    own_weights = start_weights.reshape(-1, cols)
    own_blocks = own_weights.shape[0]
    all_slots = read_blocks * slots
    total_reads = read_blocks * lax.axis_size("reads") * reads
    scale = n * own_blocks * cols / total_reads

    column = gather_far(own_weights, ALL)
    held, info = prepare(own_blocks, likelihood, block_ids, slot_valid)
    (sent,) = call(join_kernel, [(near_rows(far, own_blocks), cols)], [], *column, info)
    flipped = flip(sent, held)
    pieces = [sent] + [swap(sent, ALL, j) for j in range(1, near)]
    at = far * own_blocks
    wanted = [info] + [piece[at : at + ID_ROWS] for piece in pieces[1:]]

    row_shapes = [(chips, read_blocks, reads), (all_slots, cols)]
    inverse = (read_blocks, reads)
    for step in range(ITERS):
        if step == 0:
            row_parts, picked = call(
                lambda *refs: first_row_kernel(near, *refs), row_shapes, [], info, *pieces, flipped
            )
        else:
            row_parts, picked = call(
                lambda *refs: next_row_kernel(near, scale, *refs), row_shapes, [], *parts, flipped
            )
        row_parts = lax.all_to_all(
            row_parts,
            "genome",
            0,
            0,
            tiled=True,
            axis_index_groups=[middle_first(chips, chips // 2 + 1)],
        )
        if step + 1 < ITERS:
            (contrib,) = call(
                column_kernel,
                [(all_slots + ID_ROWS, cols)],
                [inverse],
                info,
                row_parts,
                picked,
                held,
            )
            given = gather_shared(contrib, ALL)
            sums = call(
                lambda *refs: wanted_kernel(near, all_slots, len(given), *refs),
                [(all_slots, cols)] * near,
                [],
                *given,
                *wanted,
            )
            parts = [sums[0]] + [swap(sums[j], ALL, j) for j in range(1, near)]
    order = middle_first(n, n // 2 + 3)
    (counts,) = call(
        lambda *refs: last_column_kernel(order, *refs),
        [(n, own_blocks, cols)],
        [inverse, (all_slots, cols)],
        info,
        row_parts,
        picked,
        held,
    )
    counts = lax.all_to_all(counts, ALL, 0, 0, tiled=True, axis_index_groups=[order])
    return (jnp.sum(counts, axis=0) * scale).reshape(-1)


def solution(mesh):
    placed = (
        P(("parts", "reads"), "genome", None, None),
        P(("parts", "reads"), "genome"),
        P(("parts", "reads"), "genome"),
        P(("parts", "genome", "reads")),
    )
    return jax.shard_map(
        local,
        mesh=mesh,
        in_specs=placed,
        out_specs=P(("parts", "genome", "reads")),
        check_vma=False,
    )
```

```python
import jax
import jax.numpy as jnp
from jax import lax
from jax.experimental import pallas as pl
from jax.experimental.pallas import tpu as pltpu
from jax.sharding import PartitionSpec as P

ITERS = 2
ALL = ("genome", "reads")
TERMS = 16
ID_ROWS = 8
LANES = 128
VMEM = pl.BlockSpec(memory_space=pltpu.VMEM)
ANY = pl.BlockSpec(memory_space=pl.ANY)


def radices(n):
    out = []
    while n > 1:
        r = 4 if n % 4 == 0 else 2
        out.append(r)
        n //= r
    return out


def swap(x, axes, k):
    n = lax.axis_size(axes)
    return lax.ppermute(x, axes, [(i, i ^ k) for i in range(n)])


def middle_first(n, k):
    return [i ^ k for i in range(n)]


def position(k, n):
    place = 0
    for r in radices(n):
        n //= r
        place = place + (k % r) * n
        k = k // r
    return place


def gather_far(x, axes):
    parts = [x]
    stride = lax.axis_size(axes)
    for r in radices(stride)[:0:-1]:
        stride //= r
        sent = parts[0] if len(parts) == 1 else jnp.concatenate(parts, axis=0)
        parts = [sent] + [swap(sent, axes, j * stride + 1) for j in range(1, r)]
    return parts


def dot(a, b, dims=(((1,), (0,)), ((), ()))):
    return lax.dot_general(a, b, dims, preferred_element_type=jnp.float32)


def terms(x):
    hi = x.astype(jnp.bfloat16)
    rest = x - hi.astype(jnp.float32)
    mid = rest.astype(jnp.bfloat16)
    return hi, mid, (rest - mid.astype(jnp.float32)).astype(jnp.bfloat16)


def select_rows(hot, x):
    hi, mid, low = terms(x)
    hot = hot.astype(jnp.bfloat16)
    return dot(hot, hi) + dot(hot, mid) + dot(hot, low)


def split(row):
    x = jnp.broadcast_to(row, (TERMS, row.shape[1]))
    hi = x.astype(jnp.bfloat16).astype(jnp.float32)
    rest = x - hi
    mid = rest.astype(jnp.bfloat16).astype(jnp.float32)
    low = rest - mid
    at = lax.broadcasted_iota(jnp.int32, x.shape, 0)
    out = jnp.where(at == 0, hi, jnp.where(at == 1, mid, jnp.where(at == 2, low, 0.0)))
    return out.astype(jnp.bfloat16)


def down(row):
    return jnp.transpose(jnp.broadcast_to(row, (LANES, LANES)))


def hot_rows(values, count):
    column = down(values)
    blocks = []
    for start in range(0, count, LANES):
        width = min(LANES, count - start)
        lane = lax.broadcasted_iota(jnp.int32, (LANES, width), 1).astype(jnp.float32) + start
        blocks.append((column[:, :width] == lane).astype(jnp.float32))
    return blocks[0] if len(blocks) == 1 else jnp.concatenate(blocks, axis=1)


def prepare_kernel(own_blocks, lik_ref, ids_ref, valid_ref, held_ref, info_ref, ids, valid, wide, sems):
    read_blocks, slots = ids.shape
    copies = [
        pltpu.make_async_copy(ids_ref, ids, sems.at[0]),
        pltpu.make_async_copy(valid_ref, valid, sems.at[1]),
    ]
    held = [
        pltpu.make_async_copy(lik_ref.at[b], held_ref.at[b], sems.at[2 + b])
        for b in range(held_ref.shape[0])
    ]
    for copy in copies + held:
        copy.start()
    for copy in copies:
        copy.wait()
    n = lax.axis_size(ALL)
    near = radices(n)[0]
    far = n // near
    me = lax.axis_index("genome") * lax.axis_size("reads") + lax.axis_index("reads")
    lane = lax.broadcasted_iota(jnp.int32, wide.shape, 1)
    wide[...] = jnp.zeros_like(wide)
    wide[:, :slots] = jnp.where(valid[...] > 0, ids[...], -1).astype(jnp.float32)
    flat = jnp.sum(
        pltpu.roll(wide[...], 0, 1, stride=slots, stride_axis=0), axis=0, keepdims=True
    )
    flat = jnp.where(lane[:1] < read_blocks * slots, flat, -1.0)
    owner = ((flat + 0.5) * (1.0 / own_blocks)).astype(jnp.int32)
    inside = flat.astype(jnp.int32) - owner * own_blocks
    away = owner ^ me
    rest = away // near
    for r in radices(n)[1:]:
        away = away ^ jnp.where(rest % r > 0, 1, 0)
        rest = rest // r
    place = position(away, n)
    place = (place // far) * near_rows(far, own_blocks) + (place % far) * own_blocks + inside
    place = jnp.where(flat < 0, -1, place).astype(jnp.float32)
    row = lax.broadcasted_iota(jnp.int32, info_ref.shape, 0)
    info_ref[...] = jnp.where(row == 0, flat, jnp.where(row == 1, place, 0.0))
    for copy in held:
        copy.wait()


def join_kernel(*refs):
    out_ref = refs[-1]
    at = 0
    for ref in refs[:-1]:
        out_ref[at : at + ref.shape[0], :] = ref[...]
        at += ref.shape[0]
    if at < out_ref.shape[0]:
        out_ref[at:, :] = jnp.zeros((out_ref.shape[0] - at, out_ref.shape[1]), jnp.float32)


def near_rows(far, own_blocks):
    return -(-(far * own_blocks + ID_ROWS) // 16) * 16


def flip_kernel(after_ref, lik_ref, out_ref):
    read_blocks, slots, reads, cols = lik_ref.shape
    for b in range(read_blocks):
        for s in range(slots):
            start = s % 2 * cols
            out_ref[b, s // 2, start : start + cols, :] = jnp.transpose(lik_ref[b, s])


def row_sums(picked_ref, flip_ref, out_ref):
    read_blocks, pairs = flip_ref.shape[:2]
    for b in range(read_blocks):
        total = None
        for s in range(pairs):
            at = (b * pairs + s) * 2
            left = jnp.concatenate(
                [split(picked_ref[at : at + 1, :]), split(picked_ref[at + 1 : at + 2, :])], axis=1
            )
            part = dot(left, flip_ref[b, s])
            total = part if total is None else total + part
        row = jnp.sum(total, axis=0, keepdims=True)
        for i in range(out_ref.shape[0]):
            out_ref[i, b : b + 1, :] = row


def first_row_kernel(near, info_ref, *refs):
    pieces, (flip_ref, out_ref, picked_ref) = refs[:near], refs[near:]
    table = jnp.concatenate([piece[...] for piece in pieces], axis=0)
    hot = hot_rows(info_ref[1:2, :], table.shape[0])
    picked_ref[...] = select_rows(hot[: picked_ref.shape[0]], table)
    row_sums(picked_ref, flip_ref, out_ref)


def next_row_kernel(near, scale, *refs):
    parts, (flip_ref, out_ref, picked_ref) = refs[:near], refs[near:]
    total = parts[0][...]
    for part in parts[1:]:
        total = total + part[...]
    picked_ref[...] = total * scale
    row_sums(picked_ref, flip_ref, out_ref)


def column_sums(parts_ref, picked_ref, lik_ref, contrib_ref, inverse_ref):
    read_blocks, slots, reads, cols = lik_ref.shape
    total = parts_ref[0]
    for i in range(1, parts_ref.shape[0]):
        total = total + parts_ref[i]
    inverse_ref[...] = 1.0 / total
    for b in range(read_blocks):
        left = split(inverse_ref[b : b + 1, :])
        for s in range(0, slots, 2):
            at = b * slots + s
            right = jnp.concatenate([lik_ref[b, s], lik_ref[b, s + 1]], axis=1)
            summed = jnp.sum(dot(left, right), axis=0, keepdims=True)
            contrib_ref[at : at + 1, :] = picked_ref[at : at + 1, :] * summed[:, :cols]
            contrib_ref[at + 1 : at + 2, :] = picked_ref[at + 1 : at + 2, :] * summed[:, cols:]


def column_kernel(info_ref, parts_ref, picked_ref, lik_ref, out_ref, inverse_ref):
    column_sums(parts_ref, picked_ref, lik_ref, out_ref, inverse_ref)
    out_ref[picked_ref.shape[0] :, :] = info_ref[...]


def last_column_kernel(order, info_ref, parts_ref, picked_ref, lik_ref, out_ref, inverse_ref, contrib_ref):
    column_sums(parts_ref, picked_ref, lik_ref, contrib_ref, inverse_ref)
    owners, own_blocks, cols = out_ref.shape
    all_slots = contrib_ref.shape[0]
    block = lax.broadcasted_iota(jnp.int32, (owners * own_blocks, all_slots), 0)
    hot = (block.astype(jnp.float32) == info_ref[0:1, :all_slots]).astype(jnp.float32)
    counts = select_rows(hot, contrib_ref[...])
    for i, owner in enumerate(order):
        out_ref[i] = counts[owner * own_blocks : (owner + 1) * own_blocks, :]


def wanted_kernel(near, all_slots, pieces, *refs):
    given_refs, wanted, outs = refs[:pieces], refs[pieces : pieces + near], refs[pieces + near :]
    rows = all_slots + ID_ROWS
    half = LANES // 2
    lane = lax.broadcasted_iota(jnp.int32, (1, LANES), 1)
    ids, values = [], []
    for ref in given_refs:
        for at in range(0, ref.shape[0], rows):
            ids.append(ref[at + all_slots : at + all_slots + 1, :])
            values.append(ref[at : at + all_slots, :])
    pairs = [
        jnp.where(lane < half, a, pltpu.roll(b, half, 1)) for a, b in zip(ids[::2], ids[1::2])
    ]
    given = terms(jnp.concatenate(values, axis=0))
    for ids_ref, out_ref in zip(wanted, outs):
        column = down(ids_ref[0:1, :])[:all_slots]
        hot = jnp.concatenate([(column == pair).astype(jnp.float32) for pair in pairs], axis=1)
        hot = hot.astype(jnp.bfloat16)
        out_ref[...] = dot(hot, given[0]) + dot(hot, given[1]) + dot(hot, given[2])


def call(kernel, outs, scratch, *operands):
    return pl.pallas_call(
        kernel,
        out_shape=[jax.ShapeDtypeStruct(shape, jnp.float32) for shape in outs],
        in_specs=[VMEM] * len(operands),
        out_specs=[VMEM] * len(outs),
        scratch_shapes=[pltpu.VMEM(shape, jnp.float32) for shape in scratch],
        compiler_params=pltpu.CompilerParams(vmem_limit_bytes=16 * 2**20),
    )(*operands)


def prepare(own_blocks, likelihood, block_ids, slot_valid):
    read_blocks, slots = block_ids.shape
    return pl.pallas_call(
        lambda *refs: prepare_kernel(own_blocks, *refs),
        out_shape=[
            pltpu.VMEM(likelihood.shape, likelihood.dtype),
            jax.ShapeDtypeStruct((ID_ROWS, LANES), jnp.float32),
        ],
        in_specs=[ANY] * 3,
        out_specs=[VMEM] * 2,
        scratch_shapes=[
            pltpu.VMEM((read_blocks, slots), jnp.int32),
            pltpu.VMEM((read_blocks, slots), jnp.int32),
            pltpu.VMEM((read_blocks, LANES), jnp.float32),
            pltpu.SemaphoreType.DMA((2 + read_blocks,)),
        ],
        compiler_params=pltpu.CompilerParams(vmem_limit_bytes=16 * 2**20),
    )(*[pltpu.with_memory_space_constraint(x, pltpu.HBM) for x in (likelihood, block_ids, slot_valid)])


def flip(after, likelihood):
    read_blocks, slots, reads, cols = likelihood.shape
    return pl.pallas_call(
        flip_kernel,
        out_shape=pltpu.VMEM((read_blocks, slots // 2, 2 * cols, reads), likelihood.dtype),
        in_specs=[ANY, VMEM],
        out_specs=VMEM,
        compiler_params=pltpu.CompilerParams(vmem_limit_bytes=16 * 2**20),
    )(after, likelihood)


def local(likelihood, block_ids, slot_valid, start_weights):
    read_blocks, slots, reads, cols = likelihood.shape
    n = lax.axis_size(ALL)
    chips = lax.axis_size("genome")
    near = radices(n)[0]
    far = n // near
    own_weights = start_weights.reshape(-1, cols)
    own_blocks = own_weights.shape[0]
    all_slots = read_blocks * slots
    total_reads = read_blocks * lax.axis_size("reads") * reads
    scale = n * own_blocks * cols / total_reads

    column = gather_far(own_weights, ALL)
    held, info = prepare(own_blocks, likelihood, block_ids, slot_valid)
    (sent,) = call(join_kernel, [(near_rows(far, own_blocks), cols)], [], *column, info)
    flipped = flip(sent, held)
    pieces = [sent] + [swap(sent, ALL, j) for j in range(1, near)]
    at = far * own_blocks
    wanted = [info] + [piece[at : at + ID_ROWS] for piece in pieces[1:]]

    row_shapes = [(chips, read_blocks, reads), (all_slots, cols)]
    inverse = (read_blocks, reads)
    for step in range(ITERS):
        if step == 0:
            row_parts, picked = call(
                lambda *refs: first_row_kernel(near, *refs), row_shapes, [], info, *pieces, flipped
            )
        else:
            row_parts, picked = call(
                lambda *refs: next_row_kernel(near, scale, *refs), row_shapes, [], *parts, flipped
            )
        row_parts = lax.all_to_all(
            row_parts,
            "genome",
            0,
            0,
            tiled=True,
            axis_index_groups=[middle_first(chips, chips // 2 + 1)],
        )
        if step + 1 < ITERS:
            (contrib,) = call(
                column_kernel,
                [(all_slots + ID_ROWS, cols)],
                [inverse],
                info,
                row_parts,
                picked,
                held,
            )
            given = gather_far(contrib, ALL)
            sums = call(
                lambda *refs: wanted_kernel(near, all_slots, len(given), *refs),
                [(all_slots, cols)] * near,
                [],
                *given,
                *wanted,
            )
            parts = [sums[0]] + [swap(sums[j], ALL, j) for j in range(1, near)]
    order = middle_first(n, n // 2 + 3)
    (counts,) = call(
        lambda *refs: last_column_kernel(order, *refs),
        [(n, own_blocks, cols)],
        [inverse, (all_slots, cols)],
        info,
        row_parts,
        picked,
        held,
    )
    counts = lax.all_to_all(counts, ALL, 0, 0, tiled=True, axis_index_groups=[order])
    return (jnp.sum(counts, axis=0) * scale).reshape(-1)


def solution(mesh):
    placed = (
        P(("parts", "reads"), "genome", None, None),
        P(("parts", "reads"), "genome"),
        P(("parts", "reads"), "genome"),
        P(("parts", "genome", "reads")),
    )
    return jax.shard_map(
        local,
        mesh=mesh,
        in_specs=placed,
        out_specs=P(("parts", "genome", "reads")),
        check_vma=False,
    )
```

```python
import jax
import jax.numpy as jnp
from jax import lax
from jax.experimental import pallas as pl
from jax.experimental.pallas import tpu as pltpu
from jax.sharding import PartitionSpec as P

ITERS = 2
ALL = ("genome", "reads")
TERMS = 16
ID_ROWS = 8
LANES = 128
VMEM = pl.BlockSpec(memory_space=pltpu.VMEM)
ANY = pl.BlockSpec(memory_space=pl.ANY)


def radices(n):
    out = []
    while n > 1:
        r = 4 if n % 4 == 0 else 2
        out.append(r)
        n //= r
    return out


def swap(x, axes, k):
    n = lax.axis_size(axes)
    return lax.ppermute(x, axes, [(i, i ^ k) for i in range(n)])


def middle_first(n, k):
    return [i ^ k for i in range(n)]


def position(k, n):
    place = 0
    for r in radices(n):
        n //= r
        place = place + (k % r) * n
        k = k // r
    return place


def gather_far(x, axes):
    parts = [x]
    stride = lax.axis_size(axes)
    for r in radices(stride)[:0:-1]:
        stride //= r
        sent = parts[0] if len(parts) == 1 else jnp.concatenate(parts, axis=0)
        parts = [sent] + [swap(sent, axes, j * stride + 1) for j in range(1, r)]
    return parts


def dot(a, b, dims=(((1,), (0,)), ((), ()))):
    return lax.dot_general(a, b, dims, preferred_element_type=jnp.float32)


def terms(x):
    hi = x.astype(jnp.bfloat16)
    rest = x - hi.astype(jnp.float32)
    mid = rest.astype(jnp.bfloat16)
    return hi, mid, (rest - mid.astype(jnp.float32)).astype(jnp.bfloat16)


def select_rows(hot, x):
    hi, mid, low = terms(x)
    hot = hot.astype(jnp.bfloat16)
    return dot(hot, hi) + dot(hot, mid) + dot(hot, low)


def split(row):
    x = jnp.broadcast_to(row, (TERMS, row.shape[1]))
    hi = x.astype(jnp.bfloat16).astype(jnp.float32)
    rest = x - hi
    mid = rest.astype(jnp.bfloat16).astype(jnp.float32)
    low = rest - mid
    at = lax.broadcasted_iota(jnp.int32, x.shape, 0)
    out = jnp.where(at == 0, hi, jnp.where(at == 1, mid, jnp.where(at == 2, low, 0.0)))
    return out.astype(jnp.bfloat16)


def down(row):
    return jnp.transpose(jnp.broadcast_to(row, (LANES, LANES)))


def hot_rows(values, count):
    column = down(values)
    blocks = []
    for start in range(0, count, LANES):
        width = min(LANES, count - start)
        lane = lax.broadcasted_iota(jnp.int32, (LANES, width), 1).astype(jnp.float32) + start
        blocks.append((column[:, :width] == lane).astype(jnp.float32))
    return blocks[0] if len(blocks) == 1 else jnp.concatenate(blocks, axis=1)


def prepare_kernel(
    own_blocks,
    lik_ref,
    ids_ref,
    valid_ref,
    held_ref,
    info_ref,
    ids,
    valid,
    wide,
    sems,
    held_sems,
):
    read_blocks, slots = ids.shape
    copies = [
        pltpu.make_async_copy(ids_ref, ids, sems.at[0]),
        pltpu.make_async_copy(valid_ref, valid, sems.at[1]),
    ]
    held = block_copies(lik_ref, held_ref, held_sems, 0)
    for copy in copies + held:
        copy.start()
    for copy in copies:
        copy.wait()
    n = lax.axis_size(ALL)
    near = radices(n)[0]
    far = n // near
    me = lax.axis_index("genome") * lax.axis_size("reads") + lax.axis_index("reads")
    lane = lax.broadcasted_iota(jnp.int32, wide.shape, 1)
    wide[...] = jnp.zeros_like(wide)
    wide[:, :slots] = jnp.where(valid[...] > 0, ids[...], -1).astype(jnp.float32)
    flat = jnp.sum(
        pltpu.roll(wide[...], 0, 1, stride=slots, stride_axis=0), axis=0, keepdims=True
    )
    flat = jnp.where(lane[:1] < read_blocks * slots, flat, -1.0)
    owner = ((flat + 0.5) * (1.0 / own_blocks)).astype(jnp.int32)
    inside = flat.astype(jnp.int32) - owner * own_blocks
    away = owner ^ me
    rest = away // near
    for r in radices(n)[1:]:
        away = away ^ jnp.where(rest % r > 0, 1, 0)
        rest = rest // r
    place = position(away, n)
    place = (place // far) * near_rows(far, own_blocks) + (place % far) * own_blocks + inside
    place = jnp.where(flat < 0, -1, place).astype(jnp.float32)
    row = lax.broadcasted_iota(jnp.int32, info_ref.shape, 0)
    info_ref[...] = jnp.where(row == 0, flat, jnp.where(row == 1, place, 0.0))
    for copy in held:
        copy.wait()


def join_kernel(*refs):
    out_ref = refs[-1]
    at = 0
    for ref in refs[:-1]:
        out_ref[at : at + ref.shape[0], :] = ref[...]
        at += ref.shape[0]
    if at < out_ref.shape[0]:
        out_ref[at:, :] = jnp.zeros((out_ref.shape[0] - at, out_ref.shape[1]), jnp.float32)


def near_rows(far, own_blocks):
    return -(-(far * own_blocks + ID_ROWS) // 16) * 16


def flip_kernel(after_ref, early_ref, lik_ref, late_ref, out_ref, sems):
    early = early_ref.shape[0]
    copies = block_copies(lik_ref, late_ref, sems, early)
    for copy in copies:
        copy.start()
    for b in range(out_ref.shape[0]):
        if b >= early:
            copies[b - early].wait()
        held_ref = block_of((early_ref, late_ref), b)
        slots, reads, cols = held_ref.shape
        for s in range(slots):
            start = s % 2 * cols
            out_ref[b, s // 2, start : start + cols, :] = jnp.transpose(held_ref[s])


def block_copies(lik_ref, held_ref, sems, start):
    return [
        pltpu.make_async_copy(lik_ref.at[start + b], held_ref.at[b], sems.at[b])
        for b in range(held_ref.shape[0])
    ]


def block_of(held_refs, b):
    early_ref, late_ref = held_refs
    early = early_ref.shape[0]
    return early_ref.at[b] if b < early else late_ref.at[b - early]


def row_sums(picked_ref, flip_ref, out_ref):
    read_blocks, pairs = flip_ref.shape[:2]
    for b in range(read_blocks):
        total = None
        for s in range(pairs):
            at = (b * pairs + s) * 2
            left = jnp.concatenate(
                [split(picked_ref[at : at + 1, :]), split(picked_ref[at + 1 : at + 2, :])], axis=1
            )
            part = dot(left, flip_ref[b, s])
            total = part if total is None else total + part
        row = jnp.sum(total, axis=0, keepdims=True)
        for i in range(out_ref.shape[0]):
            out_ref[i, b : b + 1, :] = row


def first_row_kernel(near, info_ref, *refs):
    pieces, (flip_ref, out_ref, picked_ref) = refs[:near], refs[near:]
    table = jnp.concatenate([piece[...] for piece in pieces], axis=0)
    hot = hot_rows(info_ref[1:2, :], table.shape[0])
    picked_ref[...] = select_rows(hot[: picked_ref.shape[0]], table)
    row_sums(picked_ref, flip_ref, out_ref)


def next_row_kernel(near, scale, *refs):
    parts, (flip_ref, out_ref, picked_ref) = refs[:near], refs[near:]
    total = parts[0][...]
    for part in parts[1:]:
        total = total + part[...]
    picked_ref[...] = total * scale
    row_sums(picked_ref, flip_ref, out_ref)


def column_sums(parts_ref, picked_ref, held_refs, contrib_ref, inverse_ref):
    slots, reads, cols = held_refs[0].shape[1:]
    total = parts_ref[0]
    for i in range(1, parts_ref.shape[0]):
        total = total + parts_ref[i]
    inverse_ref[...] = 1.0 / total
    for b in range(inverse_ref.shape[0]):
        held_ref = block_of(held_refs, b)
        left = split(inverse_ref[b : b + 1, :])
        for s in range(0, slots, 2):
            at = b * slots + s
            right = jnp.concatenate([held_ref[s], held_ref[s + 1]], axis=1)
            summed = jnp.sum(dot(left, right), axis=0, keepdims=True)
            contrib_ref[at : at + 1, :] = picked_ref[at : at + 1, :] * summed[:, :cols]
            contrib_ref[at + 1 : at + 2, :] = picked_ref[at + 1 : at + 2, :] * summed[:, cols:]


def column_kernel(info_ref, parts_ref, picked_ref, early_ref, late_ref, out_ref, inverse_ref):
    column_sums(parts_ref, picked_ref, (early_ref, late_ref), out_ref, inverse_ref)
    out_ref[picked_ref.shape[0] :, :] = info_ref[...]


def last_column_kernel(
    order, info_ref, parts_ref, picked_ref, early_ref, late_ref, out_ref, inverse_ref, contrib_ref
):
    column_sums(parts_ref, picked_ref, (early_ref, late_ref), contrib_ref, inverse_ref)
    owners, own_blocks, cols = out_ref.shape
    all_slots = contrib_ref.shape[0]
    block = lax.broadcasted_iota(jnp.int32, (owners * own_blocks, all_slots), 0)
    hot = (block.astype(jnp.float32) == info_ref[0:1, :all_slots]).astype(jnp.float32)
    counts = select_rows(hot, contrib_ref[...])
    for i, owner in enumerate(order):
        out_ref[i] = counts[owner * own_blocks : (owner + 1) * own_blocks, :]


def wanted_kernel(near, all_slots, pieces, *refs):
    given_refs, wanted, outs = refs[:pieces], refs[pieces : pieces + near], refs[pieces + near :]
    rows = all_slots + ID_ROWS
    half = LANES // 2
    lane = lax.broadcasted_iota(jnp.int32, (1, LANES), 1)
    ids, values = [], []
    for ref in given_refs:
        for at in range(0, ref.shape[0], rows):
            ids.append(ref[at + all_slots : at + all_slots + 1, :])
            values.append(ref[at : at + all_slots, :])
    pairs = [
        jnp.where(lane < half, a, pltpu.roll(b, half, 1)) for a, b in zip(ids[::2], ids[1::2])
    ]
    given = terms(jnp.concatenate(values, axis=0))
    for ids_ref, out_ref in zip(wanted, outs):
        column = down(ids_ref[0:1, :])[:all_slots]
        hot = jnp.concatenate([(column == pair).astype(jnp.float32) for pair in pairs], axis=1)
        hot = hot.astype(jnp.bfloat16)
        out_ref[...] = dot(hot, given[0]) + dot(hot, given[1]) + dot(hot, given[2])


def call(kernel, outs, scratch, *operands):
    return pl.pallas_call(
        kernel,
        out_shape=[jax.ShapeDtypeStruct(shape, jnp.float32) for shape in outs],
        in_specs=[VMEM] * len(operands),
        out_specs=[VMEM] * len(outs),
        scratch_shapes=[pltpu.VMEM(shape, jnp.float32) for shape in scratch],
        compiler_params=PARAMS,
    )(*operands)


PARAMS = pltpu.CompilerParams(vmem_limit_bytes=16 * 2**20)


def in_hbm(*arrays):
    return [pltpu.with_memory_space_constraint(x, pltpu.HBM) for x in arrays]


def prepare(own_blocks, early, likelihood, block_ids, slot_valid):
    read_blocks, slots = block_ids.shape
    return pl.pallas_call(
        lambda *refs: prepare_kernel(own_blocks, *refs),
        out_shape=[
            pltpu.VMEM((early,) + likelihood.shape[1:], likelihood.dtype),
            jax.ShapeDtypeStruct((ID_ROWS, LANES), jnp.float32),
        ],
        in_specs=[ANY] * 3,
        out_specs=[VMEM] * 2,
        scratch_shapes=[
            pltpu.VMEM((read_blocks, slots), jnp.int32),
            pltpu.VMEM((read_blocks, slots), jnp.int32),
            pltpu.VMEM((read_blocks, LANES), jnp.float32),
            pltpu.SemaphoreType.DMA((2,)),
            pltpu.SemaphoreType.DMA((early,)),
        ],
        compiler_params=PARAMS,
    )(*in_hbm(likelihood, block_ids, slot_valid))


def flip(after, held, likelihood):
    read_blocks, slots, reads, cols = likelihood.shape
    late = read_blocks - held.shape[0]
    return pl.pallas_call(
        flip_kernel,
        out_shape=[
            pltpu.VMEM((late,) + likelihood.shape[1:], likelihood.dtype),
            pltpu.VMEM((read_blocks, slots // 2, 2 * cols, reads), likelihood.dtype),
        ],
        in_specs=[ANY, VMEM, ANY],
        out_specs=[VMEM] * 2,
        scratch_shapes=[pltpu.SemaphoreType.DMA((late,))],
        compiler_params=PARAMS,
    )(after, held, *in_hbm(likelihood))


def local(likelihood, block_ids, slot_valid, start_weights):
    read_blocks, slots, reads, cols = likelihood.shape
    n = lax.axis_size(ALL)
    chips = lax.axis_size("genome")
    near = radices(n)[0]
    far = n // near
    own_weights = start_weights.reshape(-1, cols)
    own_blocks = own_weights.shape[0]
    all_slots = read_blocks * slots
    total_reads = read_blocks * lax.axis_size("reads") * reads
    scale = n * own_blocks * cols / total_reads

    column = gather_far(own_weights, ALL)
    held, info = prepare(own_blocks, read_blocks // 2, likelihood, block_ids, slot_valid)
    (sent,) = call(join_kernel, [(near_rows(far, own_blocks), cols)], [], *column, info)
    rest, flipped = flip(sent, held, likelihood)
    pieces = [sent] + [swap(sent, ALL, j) for j in range(1, near)]
    at = far * own_blocks
    wanted = [info] + [piece[at : at + ID_ROWS] for piece in pieces[1:]]

    row_shapes = [(chips, read_blocks, reads), (all_slots, cols)]
    inverse = (read_blocks, reads)
    for step in range(ITERS):
        if step == 0:
            row_parts, picked = call(
                lambda *refs: first_row_kernel(near, *refs), row_shapes, [], info, *pieces, flipped
            )
        else:
            row_parts, picked = call(
                lambda *refs: next_row_kernel(near, scale, *refs), row_shapes, [], *parts, flipped
            )
        row_parts = lax.all_to_all(
            row_parts,
            "genome",
            0,
            0,
            tiled=True,
            axis_index_groups=[middle_first(chips, chips // 2 + 1)],
        )
        if step + 1 < ITERS:
            (contrib,) = call(
                column_kernel,
                [(all_slots + ID_ROWS, cols)],
                [inverse],
                info,
                row_parts,
                picked,
                held,
                rest,
            )
            given = gather_far(contrib, ALL)
            sums = call(
                lambda *refs: wanted_kernel(near, all_slots, len(given), *refs),
                [(all_slots, cols)] * near,
                [],
                *given,
                *wanted,
            )
            parts = [sums[0]] + [swap(sums[j], ALL, j) for j in range(1, near)]
    order = middle_first(n, n // 2 + 3)
    (counts,) = call(
        lambda *refs: last_column_kernel(order, *refs),
        [(n, own_blocks, cols)],
        [inverse, (all_slots, cols)],
        info,
        row_parts,
        picked,
        held,
        rest,
    )
    counts = lax.all_to_all(counts, ALL, 0, 0, tiled=True, axis_index_groups=[order])
    return (jnp.sum(counts, axis=0) * scale).reshape(-1)


def solution(mesh):
    placed = (
        P(("parts", "reads"), "genome", None, None),
        P(("parts", "reads"), "genome"),
        P(("parts", "reads"), "genome"),
        P(("parts", "genome", "reads")),
    )
    return jax.shard_map(
        local,
        mesh=mesh,
        in_specs=placed,
        out_specs=P(("parts", "genome", "reads")),
        check_vma=False,
    )
```

```python
import jax
import jax.numpy as jnp
from jax import lax
from jax.experimental import pallas as pl
from jax.experimental.pallas import tpu as pltpu
from jax.sharding import PartitionSpec as P

ITERS = 2
ALL = ("genome", "reads")
TERMS = 16
ID_ROWS = 8
LANES = 128
VMEM = pl.BlockSpec(memory_space=pltpu.VMEM)
ANY = pl.BlockSpec(memory_space=pl.ANY)


def radices(n):
    out = []
    while n > 1:
        r = 4 if n % 4 == 0 else 2
        out.append(r)
        n //= r
    return out


def swap(x, axes, k):
    n = lax.axis_size(axes)
    return lax.ppermute(x, axes, [(i, i ^ k) for i in range(n)])


def middle_first(n, k):
    return [i ^ k for i in range(n)]


def position(k, n):
    place = 0
    for r in radices(n):
        n //= r
        place = place + (k % r) * n
        k = k // r
    return place


def gather_far(x, axes):
    parts = [x]
    stride = lax.axis_size(axes)
    for r in radices(stride)[:0:-1]:
        stride //= r
        sent = parts[0] if len(parts) == 1 else jnp.concatenate(parts, axis=0)
        parts = [sent] + [swap(sent, axes, j * stride + 1) for j in range(1, r)]
    return parts


def dot(a, b, dims=(((1,), (0,)), ((), ()))):
    return lax.dot_general(a, b, dims, preferred_element_type=jnp.float32)


def terms(x):
    hi = x.astype(jnp.bfloat16)
    rest = x - hi.astype(jnp.float32)
    mid = rest.astype(jnp.bfloat16)
    return hi, mid, (rest - mid.astype(jnp.float32)).astype(jnp.bfloat16)


def select_rows(hot, x):
    hi, mid, low = terms(x)
    hot = hot.astype(jnp.bfloat16)
    return dot(hot, hi) + dot(hot, mid) + dot(hot, low)


def split(row):
    x = jnp.broadcast_to(row, (TERMS, row.shape[1]))
    hi = x.astype(jnp.bfloat16).astype(jnp.float32)
    rest = x - hi
    mid = rest.astype(jnp.bfloat16).astype(jnp.float32)
    low = rest - mid
    at = lax.broadcasted_iota(jnp.int32, x.shape, 0)
    out = jnp.where(at == 0, hi, jnp.where(at == 1, mid, jnp.where(at == 2, low, 0.0)))
    return out.astype(jnp.bfloat16)


def down(row):
    return jnp.transpose(jnp.broadcast_to(row, (LANES, LANES)))


def hot_rows(values, count):
    column = down(values)
    blocks = []
    for start in range(0, count, LANES):
        width = min(LANES, count - start)
        lane = lax.broadcasted_iota(jnp.int32, (LANES, width), 1).astype(jnp.float32) + start
        blocks.append((column[:, :width] == lane).astype(jnp.float32))
    return blocks[0] if len(blocks) == 1 else jnp.concatenate(blocks, axis=1)


def prepare_kernel(
    own_blocks,
    lik_ref,
    ids_ref,
    valid_ref,
    held_ref,
    info_ref,
    ids,
    valid,
    wide,
    sems,
    held_sems,
):
    read_blocks, slots = ids.shape
    copies = [
        pltpu.make_async_copy(ids_ref, ids, sems.at[0]),
        pltpu.make_async_copy(valid_ref, valid, sems.at[1]),
    ]
    held = block_copies(lik_ref, held_ref, held_sems, 0)
    for copy in copies + held:
        copy.start()
    for copy in copies:
        copy.wait()
    n = lax.axis_size(ALL)
    near = radices(n)[0]
    far = n // near
    me = lax.axis_index("genome") * lax.axis_size("reads") + lax.axis_index("reads")
    lane = lax.broadcasted_iota(jnp.int32, wide.shape, 1)
    wide[...] = jnp.zeros_like(wide)
    wide[:, :slots] = jnp.where(valid[...] > 0, ids[...], -1).astype(jnp.float32)
    flat = jnp.sum(
        pltpu.roll(wide[...], 0, 1, stride=slots, stride_axis=0), axis=0, keepdims=True
    )
    flat = jnp.where(lane[:1] < read_blocks * slots, flat, -1.0)
    owner = ((flat + 0.5) * (1.0 / own_blocks)).astype(jnp.int32)
    inside = flat.astype(jnp.int32) - owner * own_blocks
    away = owner ^ me
    rest = away // near
    for r in radices(n)[1:]:
        away = away ^ jnp.where(rest % r > 0, 1, 0)
        rest = rest // r
    place = position(away, n)
    place = (place // far) * near_rows(far, own_blocks) + (place % far) * own_blocks + inside
    place = jnp.where(flat < 0, -1, place).astype(jnp.float32)
    row = lax.broadcasted_iota(jnp.int32, info_ref.shape, 0)
    info_ref[...] = jnp.where(row == 0, flat, jnp.where(row == 1, place, 0.0))
    for copy in held:
        copy.wait()


def join_kernel(*refs):
    out_ref = refs[-1]
    at = 0
    for ref in refs[:-1]:
        out_ref[at : at + ref.shape[0], :] = ref[...]
        at += ref.shape[0]
    if at < out_ref.shape[0]:
        out_ref[at:, :] = jnp.zeros((out_ref.shape[0] - at, out_ref.shape[1]), jnp.float32)


def near_rows(far, own_blocks):
    return -(-(far * own_blocks + ID_ROWS) // 16) * 16


def flip_kernel(after_ref, early_ref, lik_ref, late_ref, out_ref, sems):
    early = early_ref.shape[0]
    copies = block_copies(lik_ref, late_ref, sems, early)
    for copy in copies:
        copy.start()
    for b in range(out_ref.shape[0]):
        if b >= early:
            copies[b - early].wait()
        held_ref = block_of((early_ref, late_ref), b)
        slots, reads, cols = held_ref.shape
        for s in range(slots):
            start = s % 2 * cols
            out_ref[b, s // 2, start : start + cols, :] = jnp.transpose(held_ref[s])


def block_copies(lik_ref, held_ref, sems, start):
    return [
        pltpu.make_async_copy(lik_ref.at[start + b], held_ref.at[b], sems.at[b])
        for b in range(held_ref.shape[0])
    ]


def block_of(held_refs, b):
    early_ref, late_ref = held_refs
    early = early_ref.shape[0]
    return early_ref.at[b] if b < early else late_ref.at[b - early]


def row_sums(picked_ref, flip_ref, out_ref):
    read_blocks, pairs = flip_ref.shape[:2]
    for b in range(read_blocks):
        total = None
        for s in range(pairs):
            at = (b * pairs + s) * 2
            left = jnp.concatenate(
                [split(picked_ref[at : at + 1, :]), split(picked_ref[at + 1 : at + 2, :])], axis=1
            )
            part = dot(left, flip_ref[b, s])
            total = part if total is None else total + part
        row = jnp.sum(total, axis=0, keepdims=True)
        for i in range(out_ref.shape[0]):
            out_ref[i, b : b + 1, :] = row


def first_row_kernel(near, info_ref, *refs):
    pieces, (flip_ref, out_ref, picked_ref) = refs[:near], refs[near:]
    table = jnp.concatenate([piece[...] for piece in pieces], axis=0)
    hot = hot_rows(info_ref[1:2, :], table.shape[0])
    picked_ref[...] = select_rows(hot[: picked_ref.shape[0]], table)
    row_sums(picked_ref, flip_ref, out_ref)


def next_row_kernel(near, scale, *refs):
    parts, (flip_ref, out_ref, picked_ref) = refs[:near], refs[near:]
    total = parts[0][...]
    for part in parts[1:]:
        total = total + part[...]
    picked_ref[...] = total * scale
    row_sums(picked_ref, flip_ref, out_ref)


def column_sums(parts_ref, picked_ref, held_refs, contrib_ref, inverse_ref):
    slots, reads, cols = held_refs[0].shape[1:]
    total = parts_ref[0]
    for i in range(1, parts_ref.shape[0]):
        total = total + parts_ref[i]
    inverse_ref[...] = 1.0 / total
    for b in range(inverse_ref.shape[0]):
        held_ref = block_of(held_refs, b)
        left = split(inverse_ref[b : b + 1, :])
        for s in range(0, slots, 2):
            at = b * slots + s
            right = jnp.concatenate([held_ref[s], held_ref[s + 1]], axis=1)
            summed = jnp.sum(dot(left, right), axis=0, keepdims=True)
            contrib_ref[at : at + 1, :] = picked_ref[at : at + 1, :] * summed[:, :cols]
            contrib_ref[at + 1 : at + 2, :] = picked_ref[at + 1 : at + 2, :] * summed[:, cols:]


def column_kernel(info_ref, parts_ref, picked_ref, early_ref, late_ref, out_ref, inverse_ref):
    column_sums(parts_ref, picked_ref, (early_ref, late_ref), out_ref, inverse_ref)
    out_ref[picked_ref.shape[0] :, :] = info_ref[...]


def last_column_kernel(
    order, info_ref, parts_ref, picked_ref, early_ref, late_ref, out_ref, inverse_ref, contrib_ref
):
    column_sums(parts_ref, picked_ref, (early_ref, late_ref), contrib_ref, inverse_ref)
    owners, own_blocks, cols = out_ref.shape
    all_slots = contrib_ref.shape[0]
    block = lax.broadcasted_iota(jnp.int32, (owners * own_blocks, all_slots), 0)
    hot = (block.astype(jnp.float32) == info_ref[0:1, :all_slots]).astype(jnp.float32)
    counts = select_rows(hot, contrib_ref[...])
    for i, owner in enumerate(order):
        out_ref[i] = counts[owner * own_blocks : (owner + 1) * own_blocks, :]


def wanted_kernel(near, all_slots, pieces, *refs):
    given_refs, wanted, outs = refs[:pieces], refs[pieces : pieces + near], refs[pieces + near :]
    rows = all_slots + ID_ROWS
    half = LANES // 2
    lane = lax.broadcasted_iota(jnp.int32, (1, LANES), 1)
    ids, values = [], []
    for ref in given_refs:
        for at in range(0, ref.shape[0], rows):
            ids.append(ref[at + all_slots : at + all_slots + 1, :])
            values.append(ref[at : at + all_slots, :])
    pairs = [
        jnp.where(lane < half, a, pltpu.roll(b, half, 1)) for a, b in zip(ids[::2], ids[1::2])
    ]
    given = terms(jnp.concatenate(values, axis=0))
    for ids_ref, out_ref in zip(wanted, outs):
        column = down(ids_ref[0:1, :])[:all_slots]
        hot = jnp.concatenate([(column == pair).astype(jnp.float32) for pair in pairs], axis=1)
        hot = hot.astype(jnp.bfloat16)
        out_ref[...] = dot(hot, given[0]) + dot(hot, given[1]) + dot(hot, given[2])


def call(kernel, outs, scratch, *operands):
    return pl.pallas_call(
        kernel,
        out_shape=[jax.ShapeDtypeStruct(shape, jnp.float32) for shape in outs],
        in_specs=[VMEM] * len(operands),
        out_specs=[VMEM] * len(outs),
        scratch_shapes=[pltpu.VMEM(shape, jnp.float32) for shape in scratch],
        compiler_params=PARAMS,
    )(*operands)


PARAMS = pltpu.CompilerParams(vmem_limit_bytes=16 * 2**20)


def in_hbm(*arrays):
    return [pltpu.with_memory_space_constraint(x, pltpu.HBM) for x in arrays]


def prepare(own_blocks, early, likelihood, block_ids, slot_valid):
    read_blocks, slots = block_ids.shape
    return pl.pallas_call(
        lambda *refs: prepare_kernel(own_blocks, *refs),
        out_shape=[
            pltpu.VMEM((early,) + likelihood.shape[1:], likelihood.dtype),
            jax.ShapeDtypeStruct((ID_ROWS, LANES), jnp.float32),
        ],
        in_specs=[ANY] * 3,
        out_specs=[VMEM] * 2,
        scratch_shapes=[
            pltpu.VMEM((read_blocks, slots), jnp.int32),
            pltpu.VMEM((read_blocks, slots), jnp.int32),
            pltpu.VMEM((read_blocks, LANES), jnp.float32),
            pltpu.SemaphoreType.DMA((2,)),
            pltpu.SemaphoreType.DMA((early,)),
        ],
        compiler_params=PARAMS,
    )(*in_hbm(likelihood, block_ids, slot_valid))


def flip(after, held, likelihood):
    read_blocks, slots, reads, cols = likelihood.shape
    late = read_blocks - held.shape[0]
    return pl.pallas_call(
        flip_kernel,
        out_shape=[
            pltpu.VMEM((late,) + likelihood.shape[1:], likelihood.dtype),
            pltpu.VMEM((read_blocks, slots // 2, 2 * cols, reads), likelihood.dtype),
        ],
        in_specs=[ANY, VMEM, ANY],
        out_specs=[VMEM] * 2,
        scratch_shapes=[pltpu.SemaphoreType.DMA((late,))],
        compiler_params=PARAMS,
    )(after, held, *in_hbm(likelihood))


def local(likelihood, block_ids, slot_valid, start_weights):
    read_blocks, slots, reads, cols = likelihood.shape
    n = lax.axis_size(ALL)
    chips = lax.axis_size("genome")
    near = radices(n)[0]
    far = n // near
    own_weights = start_weights.reshape(-1, cols)
    own_blocks = own_weights.shape[0]
    all_slots = read_blocks * slots
    total_reads = read_blocks * lax.axis_size("reads") * reads
    scale = n * own_blocks * cols / total_reads

    column = gather_far(own_weights, ALL)
    held, info = prepare(own_blocks, read_blocks // 2, likelihood, block_ids, slot_valid)
    (sent,) = call(join_kernel, [(near_rows(far, own_blocks), cols)], [], *column, info)
    rest, flipped = flip(sent, held, likelihood)
    pieces = [sent] + [swap(sent, ALL, j) for j in range(1, near)]
    at = far * own_blocks
    wanted = [info] + [piece[at : at + ID_ROWS] for piece in pieces[1:]]

    row_shapes = [(chips, read_blocks, reads), (all_slots, cols)]
    inverse = (read_blocks, reads)
    for step in range(ITERS):
        if step == 0:
            row_parts, picked = call(
                lambda *refs: first_row_kernel(near, *refs), row_shapes, [], info, *pieces, flipped
            )
        else:
            row_parts, picked = call(
                lambda *refs: next_row_kernel(near, scale, *refs), row_shapes, [], *parts, flipped
            )
        row_parts = lax.all_to_all(
            row_parts,
            "genome",
            0,
            0,
            tiled=True,
            axis_index_groups=[middle_first(chips, chips // 2 + step)],
        )
        if step + 1 < ITERS:
            (contrib,) = call(
                column_kernel,
                [(all_slots + ID_ROWS, cols)],
                [inverse],
                info,
                row_parts,
                picked,
                held,
                rest,
            )
            given = gather_far(contrib, ALL)
            sums = call(
                lambda *refs: wanted_kernel(near, all_slots, len(given), *refs),
                [(all_slots, cols)] * near,
                [],
                *given,
                *wanted,
            )
            parts = [sums[0]] + [swap(sums[j], ALL, j) for j in range(1, near)]
    order = middle_first(n, n // 2 + 3)
    (counts,) = call(
        lambda *refs: last_column_kernel(order, *refs),
        [(n, own_blocks, cols)],
        [inverse, (all_slots, cols)],
        info,
        row_parts,
        picked,
        held,
        rest,
    )
    counts = lax.all_to_all(counts, ALL, 0, 0, tiled=True, axis_index_groups=[order])
    return (jnp.sum(counts, axis=0) * scale).reshape(-1)


def solution(mesh):
    placed = (
        P(("parts", "reads"), "genome", None, None),
        P(("parts", "reads"), "genome"),
        P(("parts", "reads"), "genome"),
        P(("parts", "genome", "reads")),
    )
    return jax.shard_map(
        local,
        mesh=mesh,
        in_specs=placed,
        out_specs=P(("parts", "genome", "reads")),
        check_vma=False,
    )
```

```python
import jax
import jax.numpy as jnp
from jax import lax
from jax.experimental import pallas as pl
from jax.experimental.pallas import tpu as pltpu
from jax.sharding import PartitionSpec as P

ITERS = 2
ALL = ("genome", "reads")
TERMS = 16
ID_ROWS = 8
CROSSED = (1,)
LANES = 128
VMEM = pl.BlockSpec(memory_space=pltpu.VMEM)
ANY = pl.BlockSpec(memory_space=pl.ANY)


def radices(n):
    out = []
    while n > 1:
        r = 4 if n % 4 == 0 else 2
        out.append(r)
        n //= r
    return out


def swap(x, axes, k):
    n = lax.axis_size(axes)
    return lax.ppermute(x, axes, [(i, i ^ k) for i in range(n)])


def middle_first(n, k):
    return [i ^ k for i in range(n)]


def position(k, n):
    place = 0
    for r in radices(n):
        n //= r
        place = place + (k % r) * n
        k = k // r
    return place


def gather_far(x, axes, crossed):
    parts = [x]
    stride = lax.axis_size(axes)
    for r in radices(stride)[:0:-1]:
        stride //= r
        sent = parts[0] if len(parts) == 1 else jnp.concatenate(parts, axis=0)
        parts = [sent] + [swap(sent, axes, j * stride + (j in crossed)) for j in range(1, r)]
    return parts


def dot(a, b, dims=(((1,), (0,)), ((), ()))):
    return lax.dot_general(a, b, dims, preferred_element_type=jnp.float32)


def terms(x):
    hi = x.astype(jnp.bfloat16)
    rest = x - hi.astype(jnp.float32)
    mid = rest.astype(jnp.bfloat16)
    return hi, mid, (rest - mid.astype(jnp.float32)).astype(jnp.bfloat16)


def select_rows(hot, x):
    hi, mid, low = terms(x)
    hot = hot.astype(jnp.bfloat16)
    return dot(hot, hi) + dot(hot, mid) + dot(hot, low)


def split(row):
    x = jnp.broadcast_to(row, (TERMS, row.shape[1]))
    hi = x.astype(jnp.bfloat16).astype(jnp.float32)
    rest = x - hi
    mid = rest.astype(jnp.bfloat16).astype(jnp.float32)
    low = rest - mid
    at = lax.broadcasted_iota(jnp.int32, x.shape, 0)
    out = jnp.where(at == 0, hi, jnp.where(at == 1, mid, jnp.where(at == 2, low, 0.0)))
    return out.astype(jnp.bfloat16)


def down(row):
    return jnp.transpose(jnp.broadcast_to(row, (LANES, LANES)))


def hot_rows(values, count):
    column = down(values)
    blocks = []
    for start in range(0, count, LANES):
        width = min(LANES, count - start)
        lane = lax.broadcasted_iota(jnp.int32, (LANES, width), 1).astype(jnp.float32) + start
        blocks.append((column[:, :width] == lane).astype(jnp.float32))
    return blocks[0] if len(blocks) == 1 else jnp.concatenate(blocks, axis=1)


def prepare_kernel(
    own_blocks,
    lik_ref,
    ids_ref,
    valid_ref,
    held_ref,
    info_ref,
    ids,
    valid,
    wide,
    sems,
    held_sems,
):
    read_blocks, slots = ids.shape
    copies = [
        pltpu.make_async_copy(ids_ref, ids, sems.at[0]),
        pltpu.make_async_copy(valid_ref, valid, sems.at[1]),
    ]
    held = block_copies(lik_ref, held_ref, held_sems, 0)
    for copy in copies + held:
        copy.start()
    for copy in copies:
        copy.wait()
    n = lax.axis_size(ALL)
    near = radices(n)[0]
    far = n // near
    me = lax.axis_index("genome") * lax.axis_size("reads") + lax.axis_index("reads")
    lane = lax.broadcasted_iota(jnp.int32, wide.shape, 1)
    wide[...] = jnp.zeros_like(wide)
    wide[:, :slots] = jnp.where(valid[...] > 0, ids[...], -1).astype(jnp.float32)
    flat = jnp.sum(
        pltpu.roll(wide[...], 0, 1, stride=slots, stride_axis=0), axis=0, keepdims=True
    )
    flat = jnp.where(lane[:1] < read_blocks * slots, flat, -1.0)
    owner = ((flat + 0.5) * (1.0 / own_blocks)).astype(jnp.int32)
    inside = flat.astype(jnp.int32) - owner * own_blocks
    away = owner ^ me
    rest = away // near
    for r in radices(n)[1:]:
        for j in CROSSED:
            away = away ^ jnp.where(rest % r == j, 1, 0)
        rest = rest // r
    place = position(away, n)
    place = (place // far) * near_rows(far, own_blocks) + (place % far) * own_blocks + inside
    place = jnp.where(flat < 0, -1, place).astype(jnp.float32)
    row = lax.broadcasted_iota(jnp.int32, info_ref.shape, 0)
    info_ref[...] = jnp.where(row == 0, flat, jnp.where(row == 1, place, 0.0))
    for copy in held:
        copy.wait()


def join_kernel(*refs):
    out_ref = refs[-1]
    at = 0
    for ref in refs[:-1]:
        out_ref[at : at + ref.shape[0], :] = ref[...]
        at += ref.shape[0]
    if at < out_ref.shape[0]:
        out_ref[at:, :] = jnp.zeros((out_ref.shape[0] - at, out_ref.shape[1]), jnp.float32)


def near_rows(far, own_blocks):
    return -(-(far * own_blocks + ID_ROWS) // 16) * 16


def flip_kernel(after_ref, early_ref, lik_ref, late_ref, out_ref, sems):
    early = early_ref.shape[0]
    copies = block_copies(lik_ref, late_ref, sems, early)
    for copy in copies:
        copy.start()
    for b in range(out_ref.shape[0]):
        if b >= early:
            copies[b - early].wait()
        held_ref = block_of((early_ref, late_ref), b)
        slots, reads, cols = held_ref.shape
        for s in range(slots):
            start = s % 2 * cols
            out_ref[b, s // 2, start : start + cols, :] = jnp.transpose(held_ref[s])


def block_copies(lik_ref, held_ref, sems, start):
    return [
        pltpu.make_async_copy(lik_ref.at[start + b], held_ref.at[b], sems.at[b])
        for b in range(held_ref.shape[0])
    ]


def block_of(held_refs, b):
    early_ref, late_ref = held_refs
    early = early_ref.shape[0]
    return early_ref.at[b] if b < early else late_ref.at[b - early]


def row_sums(picked_ref, flip_ref, out_ref):
    read_blocks, pairs = flip_ref.shape[:2]
    for b in range(read_blocks):
        total = None
        for s in range(pairs):
            at = (b * pairs + s) * 2
            left = jnp.concatenate(
                [split(picked_ref[at : at + 1, :]), split(picked_ref[at + 1 : at + 2, :])], axis=1
            )
            part = dot(left, flip_ref[b, s])
            total = part if total is None else total + part
        row = jnp.sum(total, axis=0, keepdims=True)
        for i in range(out_ref.shape[0]):
            out_ref[i, b : b + 1, :] = row


def first_row_kernel(near, info_ref, *refs):
    pieces, (flip_ref, out_ref, picked_ref) = refs[:near], refs[near:]
    table = jnp.concatenate([piece[...] for piece in pieces], axis=0)
    hot = hot_rows(info_ref[1:2, :], table.shape[0])
    picked_ref[...] = select_rows(hot[: picked_ref.shape[0]], table)
    row_sums(picked_ref, flip_ref, out_ref)


def next_row_kernel(near, scale, *refs):
    parts, (flip_ref, out_ref, picked_ref) = refs[:near], refs[near:]
    total = parts[0][...]
    for part in parts[1:]:
        total = total + part[...]
    picked_ref[...] = total * scale
    row_sums(picked_ref, flip_ref, out_ref)


def column_sums(parts_ref, picked_ref, held_refs, contrib_ref, inverse_ref):
    slots, reads, cols = held_refs[0].shape[1:]
    total = parts_ref[0]
    for i in range(1, parts_ref.shape[0]):
        total = total + parts_ref[i]
    inverse_ref[...] = 1.0 / total
    for b in range(inverse_ref.shape[0]):
        held_ref = block_of(held_refs, b)
        left = split(inverse_ref[b : b + 1, :])
        for s in range(0, slots, 2):
            at = b * slots + s
            right = jnp.concatenate([held_ref[s], held_ref[s + 1]], axis=1)
            summed = jnp.sum(dot(left, right), axis=0, keepdims=True)
            contrib_ref[at : at + 1, :] = picked_ref[at : at + 1, :] * summed[:, :cols]
            contrib_ref[at + 1 : at + 2, :] = picked_ref[at + 1 : at + 2, :] * summed[:, cols:]


def column_kernel(info_ref, parts_ref, picked_ref, early_ref, late_ref, out_ref, inverse_ref):
    column_sums(parts_ref, picked_ref, (early_ref, late_ref), out_ref, inverse_ref)
    out_ref[picked_ref.shape[0] :, :] = info_ref[...]


def last_column_kernel(
    order, info_ref, parts_ref, picked_ref, early_ref, late_ref, out_ref, inverse_ref, contrib_ref
):
    column_sums(parts_ref, picked_ref, (early_ref, late_ref), contrib_ref, inverse_ref)
    owners, own_blocks, cols = out_ref.shape
    all_slots = contrib_ref.shape[0]
    block = lax.broadcasted_iota(jnp.int32, (owners * own_blocks, all_slots), 0)
    hot = (block.astype(jnp.float32) == info_ref[0:1, :all_slots]).astype(jnp.float32)
    counts = select_rows(hot, contrib_ref[...])
    for i, owner in enumerate(order):
        out_ref[i] = counts[owner * own_blocks : (owner + 1) * own_blocks, :]


def wanted_kernel(near, all_slots, pieces, *refs):
    given_refs, wanted, outs = refs[:pieces], refs[pieces : pieces + near], refs[pieces + near :]
    rows = all_slots + ID_ROWS
    half = LANES // 2
    lane = lax.broadcasted_iota(jnp.int32, (1, LANES), 1)
    ids, values = [], []
    for ref in given_refs:
        for at in range(0, ref.shape[0], rows):
            ids.append(ref[at + all_slots : at + all_slots + 1, :])
            values.append(ref[at : at + all_slots, :])
    pairs = [
        jnp.where(lane < half, a, pltpu.roll(b, half, 1)) for a, b in zip(ids[::2], ids[1::2])
    ]
    given = terms(jnp.concatenate(values, axis=0))
    for ids_ref, out_ref in zip(wanted, outs):
        column = down(ids_ref[0:1, :])[:all_slots]
        hot = jnp.concatenate([(column == pair).astype(jnp.float32) for pair in pairs], axis=1)
        hot = hot.astype(jnp.bfloat16)
        out_ref[...] = dot(hot, given[0]) + dot(hot, given[1]) + dot(hot, given[2])


def call(kernel, outs, scratch, *operands):
    return pl.pallas_call(
        kernel,
        out_shape=[jax.ShapeDtypeStruct(shape, jnp.float32) for shape in outs],
        in_specs=[VMEM] * len(operands),
        out_specs=[VMEM] * len(outs),
        scratch_shapes=[pltpu.VMEM(shape, jnp.float32) for shape in scratch],
        compiler_params=PARAMS,
    )(*operands)


PARAMS = pltpu.CompilerParams(vmem_limit_bytes=16 * 2**20)


def in_hbm(*arrays):
    return [pltpu.with_memory_space_constraint(x, pltpu.HBM) for x in arrays]


def prepare(own_blocks, early, likelihood, block_ids, slot_valid):
    read_blocks, slots = block_ids.shape
    return pl.pallas_call(
        lambda *refs: prepare_kernel(own_blocks, *refs),
        out_shape=[
            pltpu.VMEM((early,) + likelihood.shape[1:], likelihood.dtype),
            jax.ShapeDtypeStruct((ID_ROWS, LANES), jnp.float32),
        ],
        in_specs=[ANY] * 3,
        out_specs=[VMEM] * 2,
        scratch_shapes=[
            pltpu.VMEM((read_blocks, slots), jnp.int32),
            pltpu.VMEM((read_blocks, slots), jnp.int32),
            pltpu.VMEM((read_blocks, LANES), jnp.float32),
            pltpu.SemaphoreType.DMA((2,)),
            pltpu.SemaphoreType.DMA((early,)),
        ],
        compiler_params=PARAMS,
    )(*in_hbm(likelihood, block_ids, slot_valid))


def flip(after, held, likelihood):
    read_blocks, slots, reads, cols = likelihood.shape
    late = read_blocks - held.shape[0]
    return pl.pallas_call(
        flip_kernel,
        out_shape=[
            pltpu.VMEM((late,) + likelihood.shape[1:], likelihood.dtype),
            pltpu.VMEM((read_blocks, slots // 2, 2 * cols, reads), likelihood.dtype),
        ],
        in_specs=[ANY, VMEM, ANY],
        out_specs=[VMEM] * 2,
        scratch_shapes=[pltpu.SemaphoreType.DMA((late,))],
        compiler_params=PARAMS,
    )(after, held, *in_hbm(likelihood))


def local(likelihood, block_ids, slot_valid, start_weights):
    read_blocks, slots, reads, cols = likelihood.shape
    n = lax.axis_size(ALL)
    chips = lax.axis_size("genome")
    near = radices(n)[0]
    far = n // near
    own_weights = start_weights.reshape(-1, cols)
    own_blocks = own_weights.shape[0]
    all_slots = read_blocks * slots
    total_reads = read_blocks * lax.axis_size("reads") * reads
    scale = n * own_blocks * cols / total_reads

    column = gather_far(own_weights, ALL, CROSSED)
    held, info = prepare(own_blocks, read_blocks // 2, likelihood, block_ids, slot_valid)
    (sent,) = call(join_kernel, [(near_rows(far, own_blocks), cols)], [], *column, info)
    rest, flipped = flip(sent, held, likelihood)
    pieces = [sent] + [swap(sent, ALL, j) for j in range(1, near)]
    at = far * own_blocks
    wanted = [info] + [piece[at : at + ID_ROWS] for piece in pieces[1:]]

    row_shapes = [(chips, read_blocks, reads), (all_slots, cols)]
    inverse = (read_blocks, reads)
    for step in range(ITERS):
        if step == 0:
            row_parts, picked = call(
                lambda *refs: first_row_kernel(near, *refs), row_shapes, [], info, *pieces, flipped
            )
        else:
            row_parts, picked = call(
                lambda *refs: next_row_kernel(near, scale, *refs), row_shapes, [], *parts, flipped
            )
        row_parts = lax.all_to_all(
            row_parts,
            "genome",
            0,
            0,
            tiled=True,
            axis_index_groups=[middle_first(chips, chips // 2 + step)],
        )
        if step + 1 < ITERS:
            (contrib,) = call(
                column_kernel,
                [(all_slots + ID_ROWS, cols)],
                [inverse],
                info,
                row_parts,
                picked,
                held,
                rest,
            )
            given = gather_far(contrib, ALL, (1, 2, 3))
            sums = call(
                lambda *refs: wanted_kernel(near, all_slots, len(given), *refs),
                [(all_slots, cols)] * near,
                [],
                *given,
                *wanted,
            )
            parts = [sums[0]] + [swap(sums[j], ALL, j) for j in range(near - 1, 0, -1)]
    order = middle_first(n, n // 2 + 3)
    (counts,) = call(
        lambda *refs: last_column_kernel(order, *refs),
        [(n, own_blocks, cols)],
        [inverse, (all_slots, cols)],
        info,
        row_parts,
        picked,
        held,
        rest,
    )
    counts = lax.all_to_all(counts, ALL, 0, 0, tiled=True, axis_index_groups=[order])
    return (jnp.sum(counts, axis=0) * scale).reshape(-1)


def solution(mesh):
    placed = (
        P(("parts", "reads"), "genome", None, None),
        P(("parts", "reads"), "genome"),
        P(("parts", "reads"), "genome"),
        P(("parts", "genome", "reads")),
    )
    return jax.shard_map(
        local,
        mesh=mesh,
        in_specs=placed,
        out_specs=P(("parts", "genome", "reads")),
        check_vma=False,
    )
```

```python
import jax
import jax.numpy as jnp
from jax import lax
from jax.experimental import pallas as pl
from jax.experimental.pallas import tpu as pltpu
from jax.sharding import PartitionSpec as P

ITERS = 2
ALL = ("genome", "reads")
TERMS = 16
ID_ROWS = 8
CROSSED = (1,)
LANES = 128
VMEM = pl.BlockSpec(memory_space=pltpu.VMEM)
ANY = pl.BlockSpec(memory_space=pl.ANY)


def radices(n):
    out = []
    while n > 1:
        r = 4 if n % 4 == 0 else 2
        out.append(r)
        n //= r
    return out


def swap(x, axes, k):
    n = lax.axis_size(axes)
    return lax.ppermute(x, axes, [(i, i ^ k) for i in range(n)])


def middle_first(n, k):
    return [i ^ k for i in range(n)]


def position(k, n):
    place = 0
    for r in radices(n):
        n //= r
        place = place + (k % r) * n
        k = k // r
    return place


def gather_far(x, axes, crossed):
    parts = [x]
    stride = lax.axis_size(axes)
    for r in radices(stride)[:0:-1]:
        stride //= r
        sent = parts[0] if len(parts) == 1 else jnp.concatenate(parts, axis=0)
        parts = [sent] + [swap(sent, axes, j * stride + (j in crossed)) for j in range(1, r)]
    return parts


def dot(a, b, dims=(((1,), (0,)), ((), ()))):
    return lax.dot_general(a, b, dims, preferred_element_type=jnp.float32)


def terms(x):
    hi = x.astype(jnp.bfloat16)
    rest = x - hi.astype(jnp.float32)
    mid = rest.astype(jnp.bfloat16)
    return hi, mid, (rest - mid.astype(jnp.float32)).astype(jnp.bfloat16)


def select_rows(hot, x):
    hi, mid, low = terms(x)
    hot = hot.astype(jnp.bfloat16)
    return dot(hot, hi) + dot(hot, mid) + dot(hot, low)


def split(row):
    x = jnp.broadcast_to(row, (TERMS, row.shape[1]))
    hi = x.astype(jnp.bfloat16).astype(jnp.float32)
    rest = x - hi
    mid = rest.astype(jnp.bfloat16).astype(jnp.float32)
    low = rest - mid
    at = lax.broadcasted_iota(jnp.int32, x.shape, 0)
    out = jnp.where(at == 0, hi, jnp.where(at == 1, mid, jnp.where(at == 2, low, 0.0)))
    return out.astype(jnp.bfloat16)


def down(row):
    return jnp.transpose(jnp.broadcast_to(row, (LANES, LANES)))


def hot_rows(values, count):
    column = down(values)
    blocks = []
    for start in range(0, count, LANES):
        width = min(LANES, count - start)
        lane = lax.broadcasted_iota(jnp.int32, (LANES, width), 1).astype(jnp.float32) + start
        blocks.append((column[:, :width] == lane).astype(jnp.float32))
    return blocks[0] if len(blocks) == 1 else jnp.concatenate(blocks, axis=1)


def prepare_kernel(
    own_blocks,
    lik_ref,
    ids_ref,
    valid_ref,
    held_ref,
    info_ref,
    ids,
    valid,
    wide,
    sems,
    held_sems,
):
    read_blocks, slots = ids.shape
    copies = [
        pltpu.make_async_copy(ids_ref, ids, sems.at[0]),
        pltpu.make_async_copy(valid_ref, valid, sems.at[1]),
    ]
    held = block_copies(lik_ref, held_ref, held_sems, 0)
    for copy in copies + held:
        copy.start()
    for copy in copies:
        copy.wait()
    n = lax.axis_size(ALL)
    near = radices(n)[0]
    far = n // near
    me = lax.axis_index("genome") * lax.axis_size("reads") + lax.axis_index("reads")
    lane = lax.broadcasted_iota(jnp.int32, wide.shape, 1)
    wide[...] = jnp.zeros_like(wide)
    wide[:, :slots] = jnp.where(valid[...] > 0, ids[...], -1).astype(jnp.float32)
    flat = jnp.sum(
        pltpu.roll(wide[...], 0, 1, stride=slots, stride_axis=0), axis=0, keepdims=True
    )
    flat = jnp.where(lane[:1] < read_blocks * slots, flat, -1.0)
    owner = ((flat + 0.5) * (1.0 / own_blocks)).astype(jnp.int32)
    inside = flat.astype(jnp.int32) - owner * own_blocks
    away = owner ^ me
    rest = away // near
    for r in radices(n)[1:]:
        for j in CROSSED:
            away = away ^ jnp.where(rest % r == j, 1, 0)
        rest = rest // r
    place = position(away, n)
    place = (place // far) * near_rows(far, own_blocks) + (place % far) * own_blocks + inside
    place = jnp.where(flat < 0, -1, place).astype(jnp.float32)
    row = lax.broadcasted_iota(jnp.int32, info_ref.shape, 0)
    info_ref[...] = jnp.where(row == 0, flat, jnp.where(row == 1, place, 0.0))
    for copy in held:
        copy.wait()


def join_kernel(*refs):
    out_ref = refs[-1]
    at = 0
    for ref in refs[:-1]:
        out_ref[at : at + ref.shape[0], :] = ref[...]
        at += ref.shape[0]
    if at < out_ref.shape[0]:
        out_ref[at:, :] = jnp.zeros((out_ref.shape[0] - at, out_ref.shape[1]), jnp.float32)


def near_rows(far, own_blocks):
    return -(-(far * own_blocks + ID_ROWS) // 16) * 16


def flip_kernel(after_ref, early_ref, lik_ref, late_ref, out_ref, sems):
    early = early_ref.shape[0]
    copies = block_copies(lik_ref, late_ref, sems, early)
    for copy in copies:
        copy.start()
    for b in range(out_ref.shape[0]):
        if b >= early:
            copies[b - early].wait()
        held_ref = block_of((early_ref, late_ref), b)
        slots, reads, cols = held_ref.shape
        for s in range(slots):
            start = s % 2 * cols
            out_ref[b, s // 2, start : start + cols, :] = jnp.transpose(held_ref[s])


def block_copies(lik_ref, held_ref, sems, start):
    return [
        pltpu.make_async_copy(lik_ref.at[start + b], held_ref.at[b], sems.at[b])
        for b in range(held_ref.shape[0])
    ]


def block_of(held_refs, b):
    early_ref, late_ref = held_refs
    early = early_ref.shape[0]
    return early_ref.at[b] if b < early else late_ref.at[b - early]


def row_sums(picked_ref, flip_ref, out_ref):
    read_blocks, pairs = flip_ref.shape[:2]
    for b in range(read_blocks):
        total = None
        for s in range(pairs):
            at = (b * pairs + s) * 2
            left = jnp.concatenate(
                [split(picked_ref[at : at + 1, :]), split(picked_ref[at + 1 : at + 2, :])], axis=1
            )
            part = dot(left, flip_ref[b, s])
            total = part if total is None else total + part
        row = jnp.sum(total, axis=0, keepdims=True)
        for i in range(out_ref.shape[0]):
            out_ref[i, b : b + 1, :] = row


def first_row_kernel(near, info_ref, *refs):
    pieces, (flip_ref, out_ref, picked_ref) = refs[:near], refs[near:]
    table = jnp.concatenate([piece[...] for piece in pieces], axis=0)
    hot = hot_rows(info_ref[1:2, :], table.shape[0])
    picked_ref[...] = select_rows(hot[: picked_ref.shape[0]], table)
    row_sums(picked_ref, flip_ref, out_ref)


def next_row_kernel(near, scale, *refs):
    parts, (flip_ref, out_ref, picked_ref) = refs[:near], refs[near:]
    total = parts[0][...]
    for part in parts[1:]:
        total = total + part[...]
    picked_ref[...] = total * scale
    row_sums(picked_ref, flip_ref, out_ref)


def column_sums(parts_ref, picked_ref, held_refs, contrib_ref, inverse_ref):
    slots, reads, cols = held_refs[0].shape[1:]
    total = parts_ref[0]
    for i in range(1, parts_ref.shape[0]):
        total = total + parts_ref[i]
    inverse_ref[...] = 1.0 / total
    for b in range(inverse_ref.shape[0]):
        held_ref = block_of(held_refs, b)
        left = split(inverse_ref[b : b + 1, :])
        for s in range(0, slots, 2):
            at = b * slots + s
            right = jnp.concatenate([held_ref[s], held_ref[s + 1]], axis=1)
            summed = jnp.sum(dot(left, right), axis=0, keepdims=True)
            contrib_ref[at : at + 1, :] = picked_ref[at : at + 1, :] * summed[:, :cols]
            contrib_ref[at + 1 : at + 2, :] = picked_ref[at + 1 : at + 2, :] * summed[:, cols:]


def column_kernel(info_ref, parts_ref, picked_ref, early_ref, late_ref, out_ref, inverse_ref):
    column_sums(parts_ref, picked_ref, (early_ref, late_ref), out_ref, inverse_ref)
    out_ref[picked_ref.shape[0] :, :] = info_ref[...]


def last_column_kernel(
    order, info_ref, parts_ref, picked_ref, early_ref, late_ref, out_ref, inverse_ref, contrib_ref
):
    column_sums(parts_ref, picked_ref, (early_ref, late_ref), contrib_ref, inverse_ref)
    owners, own_blocks, cols = out_ref.shape
    all_slots = contrib_ref.shape[0]
    block = lax.broadcasted_iota(jnp.int32, (owners * own_blocks, all_slots), 0)
    hot = (block.astype(jnp.float32) == info_ref[0:1, :all_slots]).astype(jnp.float32)
    counts = select_rows(hot, contrib_ref[...])
    for i, owner in enumerate(order):
        out_ref[i] = counts[owner * own_blocks : (owner + 1) * own_blocks, :]


def wanted_kernel(near, all_slots, pieces, *refs):
    given_refs, wanted, outs = refs[:pieces], refs[pieces : pieces + near], refs[pieces + near :]
    rows = all_slots + ID_ROWS
    half = LANES // 2
    lane = lax.broadcasted_iota(jnp.int32, (1, LANES), 1)
    ids, values = [], []
    for ref in given_refs:
        for at in range(0, ref.shape[0], rows):
            ids.append(ref[at + all_slots : at + all_slots + 1, :])
            values.append(ref[at : at + all_slots, :])
    pairs = [
        jnp.where(lane < half, a, pltpu.roll(b, half, 1)) for a, b in zip(ids[::2], ids[1::2])
    ]
    given = terms(jnp.concatenate(values, axis=0))
    for ids_ref, out_ref in zip(wanted, outs):
        column = down(ids_ref[0:1, :])[:all_slots]
        hot = jnp.concatenate([(column == pair).astype(jnp.float32) for pair in pairs], axis=1)
        hot = hot.astype(jnp.bfloat16)
        out_ref[...] = dot(hot, given[0]) + dot(hot, given[1]) + dot(hot, given[2])


def call(kernel, outs, scratch, *operands):
    return pl.pallas_call(
        kernel,
        out_shape=[jax.ShapeDtypeStruct(shape, jnp.float32) for shape in outs],
        in_specs=[VMEM] * len(operands),
        out_specs=[VMEM] * len(outs),
        scratch_shapes=[pltpu.VMEM(shape, jnp.float32) for shape in scratch],
        compiler_params=PARAMS,
    )(*operands)


PARAMS = pltpu.CompilerParams(vmem_limit_bytes=16 * 2**20)


def in_hbm(*arrays):
    return [pltpu.with_memory_space_constraint(x, pltpu.HBM) for x in arrays]


def prepare(own_blocks, early, likelihood, block_ids, slot_valid):
    read_blocks, slots = block_ids.shape
    return pl.pallas_call(
        lambda *refs: prepare_kernel(own_blocks, *refs),
        out_shape=[
            pltpu.VMEM((early,) + likelihood.shape[1:], likelihood.dtype),
            jax.ShapeDtypeStruct((ID_ROWS, LANES), jnp.float32),
        ],
        in_specs=[ANY] * 3,
        out_specs=[VMEM] * 2,
        scratch_shapes=[
            pltpu.VMEM((read_blocks, slots), jnp.int32),
            pltpu.VMEM((read_blocks, slots), jnp.int32),
            pltpu.VMEM((read_blocks, LANES), jnp.float32),
            pltpu.SemaphoreType.DMA((2,)),
            pltpu.SemaphoreType.DMA((early,)),
        ],
        compiler_params=PARAMS,
    )(*in_hbm(likelihood, block_ids, slot_valid))


def flip(after, held, likelihood):
    read_blocks, slots, reads, cols = likelihood.shape
    late = read_blocks - held.shape[0]
    return pl.pallas_call(
        flip_kernel,
        out_shape=[
            pltpu.VMEM((late,) + likelihood.shape[1:], likelihood.dtype),
            pltpu.VMEM((read_blocks, slots // 2, 2 * cols, reads), likelihood.dtype),
        ],
        in_specs=[ANY, VMEM, ANY],
        out_specs=[VMEM] * 2,
        scratch_shapes=[pltpu.SemaphoreType.DMA((late,))],
        compiler_params=PARAMS,
    )(after, held, *in_hbm(likelihood))


def local(likelihood, block_ids, slot_valid, start_weights):
    read_blocks, slots, reads, cols = likelihood.shape
    n = lax.axis_size(ALL)
    chips = lax.axis_size("genome")
    near = radices(n)[0]
    far = n // near
    own_weights = start_weights.reshape(-1, cols)
    own_blocks = own_weights.shape[0]
    all_slots = read_blocks * slots
    total_reads = read_blocks * lax.axis_size("reads") * reads
    scale = n * own_blocks * cols / total_reads

    column = gather_far(own_weights, ALL, CROSSED)
    held, info = prepare(own_blocks, read_blocks // 2, likelihood, block_ids, slot_valid)
    (sent,) = call(join_kernel, [(near_rows(far, own_blocks), cols)], [], *column, info)
    rest, flipped = flip(sent, held, likelihood)
    pieces = [sent] + [swap(sent, ALL, j) for j in range(1, near)]
    at = far * own_blocks
    wanted = [info] + [piece[at : at + ID_ROWS] for piece in pieces[1:]]

    row_shapes = [(chips, read_blocks, reads), (all_slots, cols)]
    inverse = (read_blocks, reads)
    for step in range(ITERS):
        if step == 0:
            row_parts, picked = call(
                lambda *refs: first_row_kernel(near, *refs), row_shapes, [], info, *pieces, flipped
            )
        else:
            row_parts, picked = call(
                lambda *refs: next_row_kernel(near, scale, *refs), row_shapes, [], *parts, flipped
            )
        row_parts = lax.all_to_all(
            row_parts,
            "genome",
            0,
            0,
            tiled=True,
            axis_index_groups=[middle_first(chips, chips // 2 + step)],
        )
        if step + 1 < ITERS:
            (contrib,) = call(
                column_kernel,
                [(all_slots + ID_ROWS, cols)],
                [inverse],
                info,
                row_parts,
                picked,
                held,
                rest,
            )
            given = gather_far(contrib, ALL, (3,))
            sums = call(
                lambda *refs: wanted_kernel(near, all_slots, len(given), *refs),
                [(all_slots, cols)] * near,
                [],
                *given,
                *wanted,
            )
            parts = [sums[0]] + [swap(sums[j], ALL, j) for j in list(range(2, near)) + [1]]
    order = middle_first(n, n // 2 + 3)
    (counts,) = call(
        lambda *refs: last_column_kernel(order, *refs),
        [(n, own_blocks, cols)],
        [inverse, (all_slots, cols)],
        info,
        row_parts,
        picked,
        held,
        rest,
    )
    counts = lax.all_to_all(counts, ALL, 0, 0, tiled=True, axis_index_groups=[order])
    return (jnp.sum(counts, axis=0) * scale).reshape(-1)


def solution(mesh):
    placed = (
        P(("parts", "reads"), "genome", None, None),
        P(("parts", "reads"), "genome"),
        P(("parts", "reads"), "genome"),
        P(("parts", "genome", "reads")),
    )
    return jax.shard_map(
        local,
        mesh=mesh,
        in_specs=placed,
        out_specs=P(("parts", "genome", "reads")),
        check_vma=False,
    )
```

```python
import jax
import jax.numpy as jnp
from jax import lax
from jax.experimental import pallas as pl
from jax.experimental.pallas import tpu as pltpu
from jax.sharding import PartitionSpec as P

ITERS = 2
ALL = ("genome", "reads")
TERMS = 8
ID_ROWS = 8
CROSSED = (1,)
LANES = 128
VMEM = pl.BlockSpec(memory_space=pltpu.VMEM)
ANY = pl.BlockSpec(memory_space=pl.ANY)


def radices(n):
    out = []
    while n > 1:
        r = 4 if n % 4 == 0 else 2
        out.append(r)
        n //= r
    return out


def swap(x, axes, k):
    n = lax.axis_size(axes)
    return lax.ppermute(x, axes, [(i, i ^ k) for i in range(n)])


def middle_first(n, k):
    return [i ^ k for i in range(n)]


def position(k, n):
    place = 0
    for r in radices(n):
        n //= r
        place = place + (k % r) * n
        k = k // r
    return place


def gather_far(x, axes, crossed):
    parts = [x]
    stride = lax.axis_size(axes)
    for r in radices(stride)[:0:-1]:
        stride //= r
        sent = parts[0] if len(parts) == 1 else jnp.concatenate(parts, axis=0)
        parts = [sent] + [swap(sent, axes, j * stride + (j in crossed)) for j in range(1, r)]
    return parts


def dot(a, b, dims=(((1,), (0,)), ((), ()))):
    return lax.dot_general(a, b, dims, preferred_element_type=jnp.float32)


def terms(x):
    hi = x.astype(jnp.bfloat16)
    rest = x - hi.astype(jnp.float32)
    mid = rest.astype(jnp.bfloat16)
    return hi, mid, (rest - mid.astype(jnp.float32)).astype(jnp.bfloat16)


def select_rows(hot, x):
    hi, mid, low = terms(x)
    hot = hot.astype(jnp.bfloat16)
    return dot(hot, hi) + dot(hot, mid) + dot(hot, low)


def split(row):
    x = jnp.broadcast_to(row, (TERMS, row.shape[1]))
    hi = x.astype(jnp.bfloat16).astype(jnp.float32)
    rest = x - hi
    mid = rest.astype(jnp.bfloat16).astype(jnp.float32)
    low = rest - mid
    at = lax.broadcasted_iota(jnp.int32, x.shape, 0)
    out = jnp.where(at == 0, hi, jnp.where(at == 1, mid, jnp.where(at == 2, low, 0.0)))
    return out.astype(jnp.bfloat16)


def down(row):
    return jnp.transpose(jnp.broadcast_to(row, (LANES, LANES)))


def hot_rows(values, count):
    column = down(values)
    blocks = []
    for start in range(0, count, LANES):
        width = min(LANES, count - start)
        lane = lax.broadcasted_iota(jnp.int32, (LANES, width), 1).astype(jnp.float32) + start
        blocks.append((column[:, :width] == lane).astype(jnp.float32))
    return blocks[0] if len(blocks) == 1 else jnp.concatenate(blocks, axis=1)


def prepare_kernel(
    own_blocks,
    lik_ref,
    ids_ref,
    valid_ref,
    held_ref,
    info_ref,
    ids,
    valid,
    wide,
    sems,
    held_sems,
):
    read_blocks, slots = ids.shape
    copies = [
        pltpu.make_async_copy(ids_ref, ids, sems.at[0]),
        pltpu.make_async_copy(valid_ref, valid, sems.at[1]),
    ]
    held = block_copies(lik_ref, held_ref, held_sems, 0)
    for copy in copies + held:
        copy.start()
    for copy in copies:
        copy.wait()
    n = lax.axis_size(ALL)
    near = radices(n)[0]
    far = n // near
    me = lax.axis_index("genome") * lax.axis_size("reads") + lax.axis_index("reads")
    lane = lax.broadcasted_iota(jnp.int32, wide.shape, 1)
    wide[...] = jnp.zeros_like(wide)
    wide[:, :slots] = jnp.where(valid[...] > 0, ids[...], -1).astype(jnp.float32)
    flat = jnp.sum(
        pltpu.roll(wide[...], 0, 1, stride=slots, stride_axis=0), axis=0, keepdims=True
    )
    flat = jnp.where(lane[:1] < read_blocks * slots, flat, -1.0)
    owner = ((flat + 0.5) * (1.0 / own_blocks)).astype(jnp.int32)
    inside = flat.astype(jnp.int32) - owner * own_blocks
    away = owner ^ me
    rest = away // near
    for r in radices(n)[1:]:
        for j in CROSSED:
            away = away ^ jnp.where(rest % r == j, 1, 0)
        rest = rest // r
    place = position(away, n)
    place = (place // far) * near_rows(far, own_blocks) + (place % far) * own_blocks + inside
    place = jnp.where(flat < 0, -1, place).astype(jnp.float32)
    row = lax.broadcasted_iota(jnp.int32, info_ref.shape, 0)
    info_ref[...] = jnp.where(row == 0, flat, jnp.where(row == 1, place, 0.0))
    for copy in held:
        copy.wait()


def join_kernel(*refs):
    out_ref = refs[-1]
    at = 0
    for ref in refs[:-1]:
        out_ref[at : at + ref.shape[0], :] = ref[...]
        at += ref.shape[0]
    if at < out_ref.shape[0]:
        out_ref[at:, :] = jnp.zeros((out_ref.shape[0] - at, out_ref.shape[1]), jnp.float32)


def near_rows(far, own_blocks):
    return -(-(far * own_blocks + ID_ROWS) // 16) * 16


def flip_kernel(after_ref, info_ref, early_ref, lik_ref, late_ref, out_ref, pick_ref, count_ref, sems):
    early = early_ref.shape[0]
    copies = block_copies(lik_ref, late_ref, sems, early)
    for copy in copies:
        copy.start()
    for b in range(out_ref.shape[0]):
        if b >= early:
            copies[b - early].wait()
        held_ref = block_of((early_ref, late_ref), b)
        slots, reads, cols = held_ref.shape
        for s in range(slots):
            start = s % 2 * cols
            out_ref[b, s // 2, start : start + cols, :] = jnp.transpose(held_ref[s])
    all_slots, picks = pick_ref.shape
    pick_ref[...] = hot_rows(info_ref[1:2, :], picks)[:all_slots].astype(jnp.bfloat16)
    block = lax.broadcasted_iota(jnp.int32, count_ref.shape, 0).astype(jnp.float32)
    count_ref[...] = (block == info_ref[0:1, : count_ref.shape[1]]).astype(jnp.bfloat16)


def block_copies(lik_ref, held_ref, sems, start):
    return [
        pltpu.make_async_copy(lik_ref.at[start + b], held_ref.at[b], sems.at[b])
        for b in range(held_ref.shape[0])
    ]


def block_of(held_refs, b):
    early_ref, late_ref = held_refs
    early = early_ref.shape[0]
    return early_ref.at[b] if b < early else late_ref.at[b - early]


def row_sums(picked_ref, flip_ref, out_ref):
    read_blocks, pairs = flip_ref.shape[:2]
    for b in range(read_blocks):
        total = None
        for s in range(pairs):
            at = (b * pairs + s) * 2
            left = jnp.concatenate(
                [split(picked_ref[at : at + 1, :]), split(picked_ref[at + 1 : at + 2, :])], axis=1
            )
            part = dot(left, flip_ref[b, s])
            total = part if total is None else total + part
        row = jnp.sum(total, axis=0, keepdims=True)
        for i in range(out_ref.shape[0]):
            out_ref[i, b : b + 1, :] = row


def first_row_kernel(near, pick_ref, *refs):
    pieces, (flip_ref, out_ref, picked_ref) = refs[:near], refs[near:]
    table = jnp.concatenate([piece[...] for piece in pieces], axis=0)
    picked_ref[...] = select_rows(pick_ref[...], table)
    row_sums(picked_ref, flip_ref, out_ref)


def next_row_kernel(near, scale, *refs):
    parts, (flip_ref, out_ref, picked_ref) = refs[:near], refs[near:]
    total = parts[0][...]
    for part in parts[1:]:
        total = total + part[...]
    picked_ref[...] = total * scale
    row_sums(picked_ref, flip_ref, out_ref)


def column_sums(parts_ref, picked_ref, held_refs, contrib_ref, inverse_ref):
    slots, reads, cols = held_refs[0].shape[1:]
    total = parts_ref[0]
    for i in range(1, parts_ref.shape[0]):
        total = total + parts_ref[i]
    inverse_ref[...] = 1.0 / total
    for b in range(inverse_ref.shape[0]):
        held_ref = block_of(held_refs, b)
        left = split(inverse_ref[b : b + 1, :])
        for s in range(0, slots, 2):
            at = b * slots + s
            right = jnp.concatenate([held_ref[s], held_ref[s + 1]], axis=1)
            summed = jnp.sum(dot(left, right), axis=0, keepdims=True)
            contrib_ref[at : at + 1, :] = picked_ref[at : at + 1, :] * summed[:, :cols]
            contrib_ref[at + 1 : at + 2, :] = picked_ref[at + 1 : at + 2, :] * summed[:, cols:]


def column_kernel(info_ref, parts_ref, picked_ref, early_ref, late_ref, out_ref, inverse_ref):
    column_sums(parts_ref, picked_ref, (early_ref, late_ref), out_ref, inverse_ref)
    out_ref[picked_ref.shape[0] :, :] = info_ref[...]


def last_column_kernel(
    order, count_ref, parts_ref, picked_ref, early_ref, late_ref, out_ref, inverse_ref, contrib_ref
):
    column_sums(parts_ref, picked_ref, (early_ref, late_ref), contrib_ref, inverse_ref)
    owners, own_blocks, cols = out_ref.shape
    counts = select_rows(count_ref[...], contrib_ref[...])
    for i, owner in enumerate(order):
        out_ref[i] = counts[owner * own_blocks : (owner + 1) * own_blocks, :]


def wanted_kernel(near, all_slots, pieces, *refs):
    given_refs, wanted, outs = refs[:pieces], refs[pieces : pieces + near], refs[pieces + near :]
    rows = all_slots + ID_ROWS
    half = LANES // 2
    lane = lax.broadcasted_iota(jnp.int32, (1, LANES), 1)
    ids, values = [], []
    for ref in given_refs:
        for at in range(0, ref.shape[0], rows):
            ids.append(ref[at + all_slots : at + all_slots + 1, :])
            values.append(ref[at : at + all_slots, :])
    pairs = [
        jnp.where(lane < half, a, pltpu.roll(b, half, 1)) for a, b in zip(ids[::2], ids[1::2])
    ]
    given = terms(jnp.concatenate(values, axis=0))
    for ids_ref, out_ref in zip(wanted, outs):
        column = down(ids_ref[0:1, :])[:all_slots]
        hot = jnp.concatenate([(column == pair).astype(jnp.float32) for pair in pairs], axis=1)
        hot = hot.astype(jnp.bfloat16)
        out_ref[...] = dot(hot, given[0]) + dot(hot, given[1]) + dot(hot, given[2])


def call(kernel, outs, scratch, *operands):
    return pl.pallas_call(
        kernel,
        out_shape=[jax.ShapeDtypeStruct(shape, jnp.float32) for shape in outs],
        in_specs=[VMEM] * len(operands),
        out_specs=[VMEM] * len(outs),
        scratch_shapes=[pltpu.VMEM(shape, jnp.float32) for shape in scratch],
        compiler_params=PARAMS,
    )(*operands)


PARAMS = pltpu.CompilerParams(vmem_limit_bytes=16 * 2**20)


def in_hbm(*arrays):
    return [pltpu.with_memory_space_constraint(x, pltpu.HBM) for x in arrays]


def prepare(own_blocks, early, likelihood, block_ids, slot_valid):
    read_blocks, slots = block_ids.shape
    return pl.pallas_call(
        lambda *refs: prepare_kernel(own_blocks, *refs),
        out_shape=[
            pltpu.VMEM((early,) + likelihood.shape[1:], likelihood.dtype),
            jax.ShapeDtypeStruct((ID_ROWS, LANES), jnp.float32),
        ],
        in_specs=[ANY] * 3,
        out_specs=[VMEM] * 2,
        scratch_shapes=[
            pltpu.VMEM((read_blocks, slots), jnp.int32),
            pltpu.VMEM((read_blocks, slots), jnp.int32),
            pltpu.VMEM((read_blocks, LANES), jnp.float32),
            pltpu.SemaphoreType.DMA((2,)),
            pltpu.SemaphoreType.DMA((early,)),
        ],
        compiler_params=PARAMS,
    )(*in_hbm(likelihood, block_ids, slot_valid))


def flip(picks, blocks, after, info, held, likelihood):
    read_blocks, slots, reads, cols = likelihood.shape
    late = read_blocks - held.shape[0]
    return pl.pallas_call(
        flip_kernel,
        out_shape=[
            pltpu.VMEM((late,) + likelihood.shape[1:], likelihood.dtype),
            pltpu.VMEM((read_blocks, slots // 2, 2 * cols, reads), likelihood.dtype),
            pltpu.VMEM((read_blocks * slots, picks), jnp.bfloat16),
            pltpu.VMEM((blocks, read_blocks * slots), jnp.bfloat16),
        ],
        in_specs=[ANY, VMEM, VMEM, ANY],
        out_specs=[VMEM] * 4,
        scratch_shapes=[pltpu.SemaphoreType.DMA((late,))],
        compiler_params=PARAMS,
    )(after, info, held, *in_hbm(likelihood))


def local(likelihood, block_ids, slot_valid, start_weights):
    read_blocks, slots, reads, cols = likelihood.shape
    n = lax.axis_size(ALL)
    chips = lax.axis_size("genome")
    near = radices(n)[0]
    far = n // near
    own_weights = start_weights.reshape(-1, cols)
    own_blocks = own_weights.shape[0]
    all_slots = read_blocks * slots
    total_reads = read_blocks * lax.axis_size("reads") * reads
    scale = n * own_blocks * cols / total_reads

    column = gather_far(own_weights, ALL, CROSSED)
    held, info = prepare(own_blocks, read_blocks // 2, likelihood, block_ids, slot_valid)
    (sent,) = call(join_kernel, [(near_rows(far, own_blocks), cols)], [], *column, info)
    rest, flipped, pick, count = flip(
        near * sent.shape[0], n * own_blocks, sent, info, held, likelihood
    )
    pieces = [sent] + [swap(sent, ALL, j) for j in range(1, near)]
    at = far * own_blocks
    wanted = [info] + [piece[at : at + ID_ROWS] for piece in pieces[1:]]

    row_shapes = [(chips, read_blocks, reads), (all_slots, cols)]
    inverse = (read_blocks, reads)
    for step in range(ITERS):
        if step == 0:
            row_parts, picked = call(
                lambda *refs: first_row_kernel(near, *refs), row_shapes, [], pick, *pieces, flipped
            )
        else:
            row_parts, picked = call(
                lambda *refs: next_row_kernel(near, scale, *refs), row_shapes, [], *parts, flipped
            )
        row_parts = lax.all_to_all(
            row_parts,
            "genome",
            0,
            0,
            tiled=True,
            axis_index_groups=[middle_first(chips, chips // 2 + step)],
        )
        if step + 1 < ITERS:
            (contrib,) = call(
                column_kernel,
                [(all_slots + ID_ROWS, cols)],
                [inverse],
                info,
                row_parts,
                picked,
                held,
                rest,
            )
            given = gather_far(contrib, ALL, (1, 2, 3))
            sums = call(
                lambda *refs: wanted_kernel(near, all_slots, len(given), *refs),
                [(all_slots, cols)] * near,
                [],
                *given,
                *wanted,
            )
            parts = [sums[0]] + [swap(sums[j], ALL, j) for j in range(near - 1, 0, -1)]
    order = middle_first(n, n // 2 + 3)
    (counts,) = call(
        lambda *refs: last_column_kernel(order, *refs),
        [(n, own_blocks, cols)],
        [inverse, (all_slots, cols)],
        count,
        row_parts,
        picked,
        held,
        rest,
    )
    counts = lax.all_to_all(counts, ALL, 0, 0, tiled=True, axis_index_groups=[order])
    return (jnp.sum(counts, axis=0) * scale).reshape(-1)


def solution(mesh):
    placed = (
        P(("parts", "reads"), "genome", None, None),
        P(("parts", "reads"), "genome"),
        P(("parts", "reads"), "genome"),
        P(("parts", "genome", "reads")),
    )
    return jax.shard_map(
        local,
        mesh=mesh,
        in_specs=placed,
        out_specs=P(("parts", "genome", "reads")),
        check_vma=False,
    )
```

```python
import jax
import jax.numpy as jnp
from jax import lax
from jax.experimental import pallas as pl
from jax.experimental.pallas import tpu as pltpu
from jax.sharding import PartitionSpec as P

ITERS = 2
ALL = ("genome", "reads")
TERMS = 16
ID_ROWS = 8
CROSSED = (1,)
LANES = 128
VMEM = pl.BlockSpec(memory_space=pltpu.VMEM)
ANY = pl.BlockSpec(memory_space=pl.ANY)


def radices(n):
    out = []
    while n > 1:
        r = 4 if n % 4 == 0 else 2
        out.append(r)
        n //= r
    return out


def swap(x, axes, k):
    n = lax.axis_size(axes)
    return lax.ppermute(x, axes, [(i, i ^ k) for i in range(n)])


def middle_first(n, k):
    return [k] + sorted((i for i in range(n) if i != k), key=lambda i: (-abs(i - k), i))


def position(k, n):
    place = 0
    for r in radices(n):
        n //= r
        place = place + (k % r) * n
        k = k // r
    return place


def gather_far(x, axes, crossed):
    parts = [x]
    stride = lax.axis_size(axes)
    for r in radices(stride)[:0:-1]:
        stride //= r
        sent = parts[0] if len(parts) == 1 else jnp.concatenate(parts, axis=0)
        parts = [sent] + [swap(sent, axes, j * stride + (j in crossed)) for j in range(1, r)]
    return parts


def dot(a, b, dims=(((1,), (0,)), ((), ()))):
    return lax.dot_general(a, b, dims, preferred_element_type=jnp.float32)


def terms(x):
    hi = x.astype(jnp.bfloat16)
    rest = x - hi.astype(jnp.float32)
    mid = rest.astype(jnp.bfloat16)
    return hi, mid, (rest - mid.astype(jnp.float32)).astype(jnp.bfloat16)


def select_rows(hot, x):
    hi, mid, low = terms(x)
    hot = hot.astype(jnp.bfloat16)
    return dot(hot, hi) + dot(hot, mid) + dot(hot, low)


def split(row):
    x = jnp.broadcast_to(row, (TERMS, row.shape[1]))
    hi = x.astype(jnp.bfloat16).astype(jnp.float32)
    rest = x - hi
    mid = rest.astype(jnp.bfloat16).astype(jnp.float32)
    low = rest - mid
    at = lax.broadcasted_iota(jnp.int32, x.shape, 0)
    out = jnp.where(at == 0, hi, jnp.where(at == 1, mid, jnp.where(at == 2, low, 0.0)))
    return out.astype(jnp.bfloat16)


def down(row):
    return jnp.transpose(jnp.broadcast_to(row, (LANES, LANES)))


def hot_rows(values, count):
    column = down(values)
    blocks = []
    for start in range(0, count, LANES):
        width = min(LANES, count - start)
        lane = lax.broadcasted_iota(jnp.int32, (LANES, width), 1).astype(jnp.float32) + start
        blocks.append((column[:, :width] == lane).astype(jnp.float32))
    return blocks[0] if len(blocks) == 1 else jnp.concatenate(blocks, axis=1)


def prepare_kernel(
    own_blocks,
    lik_ref,
    ids_ref,
    valid_ref,
    held_ref,
    info_ref,
    ids,
    valid,
    wide,
    sems,
    held_sems,
):
    read_blocks, slots = ids.shape
    copies = [
        pltpu.make_async_copy(ids_ref, ids, sems.at[0]),
        pltpu.make_async_copy(valid_ref, valid, sems.at[1]),
    ]
    held = block_copies(lik_ref, held_ref, held_sems, 0)
    for copy in copies + held:
        copy.start()
    for copy in copies:
        copy.wait()
    n = lax.axis_size(ALL)
    near = radices(n)[0]
    far = n // near
    me = lax.axis_index("genome") * lax.axis_size("reads") + lax.axis_index("reads")
    lane = lax.broadcasted_iota(jnp.int32, wide.shape, 1)
    wide[...] = jnp.zeros_like(wide)
    wide[:, :slots] = jnp.where(valid[...] > 0, ids[...], -1).astype(jnp.float32)
    flat = jnp.sum(
        pltpu.roll(wide[...], 0, 1, stride=slots, stride_axis=0), axis=0, keepdims=True
    )
    flat = jnp.where(lane[:1] < read_blocks * slots, flat, -1.0)
    owner = ((flat + 0.5) * (1.0 / own_blocks)).astype(jnp.int32)
    inside = flat.astype(jnp.int32) - owner * own_blocks
    away = owner ^ me
    rest = away // near
    for r in radices(n)[1:]:
        for j in CROSSED:
            away = away ^ jnp.where(rest % r == j, 1, 0)
        rest = rest // r
    place = position(away, n)
    place = (place // far) * near_rows(far, own_blocks) + (place % far) * own_blocks + inside
    place = jnp.where(flat < 0, -1, place).astype(jnp.float32)
    row = lax.broadcasted_iota(jnp.int32, info_ref.shape, 0)
    info_ref[...] = jnp.where(row == 0, flat, jnp.where(row == 1, place, 0.0))
    for copy in held:
        copy.wait()


def join_kernel(*refs):
    out_ref = refs[-1]
    at = 0
    for ref in refs[:-1]:
        out_ref[at : at + ref.shape[0], :] = ref[...]
        at += ref.shape[0]
    if at < out_ref.shape[0]:
        out_ref[at:, :] = jnp.zeros((out_ref.shape[0] - at, out_ref.shape[1]), jnp.float32)


def near_rows(far, own_blocks):
    return -(-(far * own_blocks + ID_ROWS) // 16) * 16


def flip_kernel(after_ref, early_ref, lik_ref, late_ref, out_ref, sems):
    early = early_ref.shape[0]
    copies = block_copies(lik_ref, late_ref, sems, early)
    for copy in copies:
        copy.start()
    for b in range(out_ref.shape[0]):
        if b >= early:
            copies[b - early].wait()
        held_ref = block_of((early_ref, late_ref), b)
        slots, reads, cols = held_ref.shape
        for s in range(slots):
            start = s % 2 * cols
            out_ref[b, s // 2, start : start + cols, :] = jnp.transpose(held_ref[s])


def block_copies(lik_ref, held_ref, sems, start):
    return [
        pltpu.make_async_copy(lik_ref.at[start + b], held_ref.at[b], sems.at[b])
        for b in range(held_ref.shape[0])
    ]


def block_of(held_refs, b):
    early_ref, late_ref = held_refs
    early = early_ref.shape[0]
    return early_ref.at[b] if b < early else late_ref.at[b - early]


def row_sums(picked_ref, flip_ref, out_ref):
    read_blocks, pairs = flip_ref.shape[:2]
    for b in range(read_blocks):
        total = None
        for s in range(pairs):
            at = (b * pairs + s) * 2
            left = jnp.concatenate(
                [split(picked_ref[at : at + 1, :]), split(picked_ref[at + 1 : at + 2, :])], axis=1
            )
            part = dot(left, flip_ref[b, s])
            total = part if total is None else total + part
        row = jnp.sum(total, axis=0, keepdims=True)
        for i in range(out_ref.shape[0]):
            out_ref[i, b : b + 1, :] = row


def first_row_kernel(near, info_ref, *refs):
    pieces, (flip_ref, out_ref, picked_ref) = refs[:near], refs[near:]
    table = jnp.concatenate([piece[...] for piece in pieces], axis=0)
    hot = hot_rows(info_ref[1:2, :], table.shape[0])
    picked_ref[...] = select_rows(hot[: picked_ref.shape[0]], table)
    row_sums(picked_ref, flip_ref, out_ref)


def next_row_kernel(near, scale, *refs):
    parts, (flip_ref, out_ref, picked_ref) = refs[:near], refs[near:]
    total = parts[0][...]
    for part in parts[1:]:
        total = total + part[...]
    picked_ref[...] = total * scale
    row_sums(picked_ref, flip_ref, out_ref)


def column_sums(parts_ref, picked_ref, held_refs, contrib_ref, inverse_ref):
    slots, reads, cols = held_refs[0].shape[1:]
    total = parts_ref[0]
    for i in range(1, parts_ref.shape[0]):
        total = total + parts_ref[i]
    inverse_ref[...] = 1.0 / total
    for b in range(inverse_ref.shape[0]):
        held_ref = block_of(held_refs, b)
        left = split(inverse_ref[b : b + 1, :])
        for s in range(0, slots, 2):
            at = b * slots + s
            right = jnp.concatenate([held_ref[s], held_ref[s + 1]], axis=1)
            summed = jnp.sum(dot(left, right), axis=0, keepdims=True)
            contrib_ref[at : at + 1, :] = picked_ref[at : at + 1, :] * summed[:, :cols]
            contrib_ref[at + 1 : at + 2, :] = picked_ref[at + 1 : at + 2, :] * summed[:, cols:]


def column_kernel(info_ref, parts_ref, picked_ref, early_ref, late_ref, out_ref, inverse_ref):
    column_sums(parts_ref, picked_ref, (early_ref, late_ref), out_ref, inverse_ref)
    out_ref[picked_ref.shape[0] :, :] = info_ref[...]


def last_column_kernel(
    order, info_ref, parts_ref, picked_ref, early_ref, late_ref, out_ref, inverse_ref, contrib_ref
):
    column_sums(parts_ref, picked_ref, (early_ref, late_ref), contrib_ref, inverse_ref)
    owners, own_blocks, cols = out_ref.shape
    all_slots = contrib_ref.shape[0]
    block = lax.broadcasted_iota(jnp.int32, (owners * own_blocks, all_slots), 0)
    hot = (block.astype(jnp.float32) == info_ref[0:1, :all_slots]).astype(jnp.float32)
    counts = select_rows(hot, contrib_ref[...])
    for i, owner in enumerate(order):
        out_ref[i] = counts[owner * own_blocks : (owner + 1) * own_blocks, :]


def wanted_kernel(near, all_slots, pieces, *refs):
    given_refs, wanted, outs = refs[:pieces], refs[pieces : pieces + near], refs[pieces + near :]
    rows = all_slots + ID_ROWS
    half = LANES // 2
    lane = lax.broadcasted_iota(jnp.int32, (1, LANES), 1)
    ids, values = [], []
    for ref in given_refs:
        for at in range(0, ref.shape[0], rows):
            ids.append(ref[at + all_slots : at + all_slots + 1, :])
            values.append(ref[at : at + all_slots, :])
    pairs = [
        jnp.where(lane < half, a, pltpu.roll(b, half, 1)) for a, b in zip(ids[::2], ids[1::2])
    ]
    given = terms(jnp.concatenate(values, axis=0))
    for ids_ref, out_ref in zip(wanted, outs):
        column = down(ids_ref[0:1, :])[:all_slots]
        hot = jnp.concatenate([(column == pair).astype(jnp.float32) for pair in pairs], axis=1)
        hot = hot.astype(jnp.bfloat16)
        out_ref[...] = dot(hot, given[0]) + dot(hot, given[1]) + dot(hot, given[2])


def call(kernel, outs, scratch, *operands):
    return pl.pallas_call(
        kernel,
        out_shape=[jax.ShapeDtypeStruct(shape, jnp.float32) for shape in outs],
        in_specs=[VMEM] * len(operands),
        out_specs=[VMEM] * len(outs),
        scratch_shapes=[pltpu.VMEM(shape, jnp.float32) for shape in scratch],
        compiler_params=PARAMS,
    )(*operands)


PARAMS = pltpu.CompilerParams(vmem_limit_bytes=16 * 2**20)


def in_hbm(*arrays):
    return [pltpu.with_memory_space_constraint(x, pltpu.HBM) for x in arrays]


def prepare(own_blocks, early, likelihood, block_ids, slot_valid):
    read_blocks, slots = block_ids.shape
    return pl.pallas_call(
        lambda *refs: prepare_kernel(own_blocks, *refs),
        out_shape=[
            pltpu.VMEM((early,) + likelihood.shape[1:], likelihood.dtype),
            jax.ShapeDtypeStruct((ID_ROWS, LANES), jnp.float32),
        ],
        in_specs=[ANY] * 3,
        out_specs=[VMEM] * 2,
        scratch_shapes=[
            pltpu.VMEM((read_blocks, slots), jnp.int32),
            pltpu.VMEM((read_blocks, slots), jnp.int32),
            pltpu.VMEM((read_blocks, LANES), jnp.float32),
            pltpu.SemaphoreType.DMA((2,)),
            pltpu.SemaphoreType.DMA((early,)),
        ],
        compiler_params=PARAMS,
    )(*in_hbm(likelihood, block_ids, slot_valid))


def flip(after, held, likelihood):
    read_blocks, slots, reads, cols = likelihood.shape
    late = read_blocks - held.shape[0]
    return pl.pallas_call(
        flip_kernel,
        out_shape=[
            pltpu.VMEM((late,) + likelihood.shape[1:], likelihood.dtype),
            pltpu.VMEM((read_blocks, slots // 2, 2 * cols, reads), likelihood.dtype),
        ],
        in_specs=[ANY, VMEM, ANY],
        out_specs=[VMEM] * 2,
        scratch_shapes=[pltpu.SemaphoreType.DMA((late,))],
        compiler_params=PARAMS,
    )(after, held, *in_hbm(likelihood))


def local(likelihood, block_ids, slot_valid, start_weights):
    read_blocks, slots, reads, cols = likelihood.shape
    n = lax.axis_size(ALL)
    chips = lax.axis_size("genome")
    near = radices(n)[0]
    far = n // near
    own_weights = start_weights.reshape(-1, cols)
    own_blocks = own_weights.shape[0]
    all_slots = read_blocks * slots
    total_reads = read_blocks * lax.axis_size("reads") * reads
    scale = n * own_blocks * cols / total_reads

    column = gather_far(own_weights, ALL, CROSSED)
    held, info = prepare(own_blocks, read_blocks // 2, likelihood, block_ids, slot_valid)
    (sent,) = call(join_kernel, [(near_rows(far, own_blocks), cols)], [], *column, info)
    rest, flipped = flip(sent, held, likelihood)
    pieces = [sent] + [swap(sent, ALL, j) for j in range(1, near)]
    at = far * own_blocks
    wanted = [info] + [piece[at : at + ID_ROWS] for piece in pieces[1:]]

    row_shapes = [(chips, read_blocks, reads), (all_slots, cols)]
    inverse = (read_blocks, reads)
    for step in range(ITERS):
        if step == 0:
            row_parts, picked = call(
                lambda *refs: first_row_kernel(near, *refs), row_shapes, [], info, *pieces, flipped
            )
        else:
            row_parts, picked = call(
                lambda *refs: next_row_kernel(near, scale, *refs), row_shapes, [], *parts, flipped
            )
        row_parts = lax.all_to_all(
            row_parts,
            "genome",
            0,
            0,
            tiled=True,
            axis_index_groups=[middle_first(chips, chips // 2 + step)],
        )
        if step + 1 < ITERS:
            (contrib,) = call(
                column_kernel,
                [(all_slots + ID_ROWS, cols)],
                [inverse],
                info,
                row_parts,
                picked,
                held,
                rest,
            )
            given = gather_far(contrib, ALL, (1, 2, 3))
            sums = call(
                lambda *refs: wanted_kernel(near, all_slots, len(given), *refs),
                [(all_slots, cols)] * near,
                [],
                *given,
                *wanted,
            )
            parts = [sums[0]] + [swap(sums[j], ALL, j) for j in range(near - 1, 0, -1)]
    order = middle_first(n, n // 2 + 3)
    (counts,) = call(
        lambda *refs: last_column_kernel(order, *refs),
        [(n, own_blocks, cols)],
        [inverse, (all_slots, cols)],
        info,
        row_parts,
        picked,
        held,
        rest,
    )
    counts = lax.all_to_all(counts, ALL, 0, 0, tiled=True, axis_index_groups=[order])
    return (jnp.sum(counts, axis=0) * scale).reshape(-1)


def solution(mesh):
    placed = (
        P(("parts", "reads"), "genome", None, None),
        P(("parts", "reads"), "genome"),
        P(("parts", "reads"), "genome"),
        P(("parts", "genome", "reads")),
    )
    return jax.shard_map(
        local,
        mesh=mesh,
        in_specs=placed,
        out_specs=P(("parts", "genome", "reads")),
        check_vma=False,
    )
```

```python
import jax
import jax.numpy as jnp
from jax import lax
from jax.experimental import pallas as pl
from jax.experimental.pallas import tpu as pltpu
from jax.sharding import PartitionSpec as P

ITERS = 2
ALL = ("genome", "reads")
TERMS = 16
ID_ROWS = 8
CROSSED = (1,)
LANES = 128
VMEM = pl.BlockSpec(memory_space=pltpu.VMEM)
ANY = pl.BlockSpec(memory_space=pl.ANY)


def radices(n):
    out = []
    while n > 1:
        r = 4 if n % 4 == 0 else 2
        out.append(r)
        n //= r
    return out


def swap(x, axes, k):
    n = lax.axis_size(axes)
    return lax.ppermute(x, axes, [(i, i ^ k) for i in range(n)])


def middle_first(n, k):
    return [i ^ k for i in range(n)]


def middle_then_up(n, k):
    pairs = [k // 2] + [p for p in range(n // 2) if p != k // 2]
    return [2 * p + (i ^ (k % 2)) for p in pairs for i in range(2)]


def position(k, n):
    place = 0
    for r in radices(n):
        n //= r
        place = place + (k % r) * n
        k = k // r
    return place


def gather_far(x, axes, crossed):
    parts = [x]
    stride = lax.axis_size(axes)
    for r in radices(stride)[:0:-1]:
        stride //= r
        sent = parts[0] if len(parts) == 1 else jnp.concatenate(parts, axis=0)
        parts = [sent] + [swap(sent, axes, j * stride + (j in crossed)) for j in range(1, r)]
    return parts


def dot(a, b, dims=(((1,), (0,)), ((), ()))):
    return lax.dot_general(a, b, dims, preferred_element_type=jnp.float32)


def terms(x):
    hi = x.astype(jnp.bfloat16)
    rest = x - hi.astype(jnp.float32)
    mid = rest.astype(jnp.bfloat16)
    return hi, mid, (rest - mid.astype(jnp.float32)).astype(jnp.bfloat16)


def select_rows(hot, x):
    hi, mid, low = terms(x)
    hot = hot.astype(jnp.bfloat16)
    return dot(hot, hi) + dot(hot, mid) + dot(hot, low)


def split(row):
    x = jnp.broadcast_to(row, (TERMS, row.shape[1]))
    hi = x.astype(jnp.bfloat16).astype(jnp.float32)
    rest = x - hi
    mid = rest.astype(jnp.bfloat16).astype(jnp.float32)
    low = rest - mid
    at = lax.broadcasted_iota(jnp.int32, x.shape, 0)
    out = jnp.where(at == 0, hi, jnp.where(at == 1, mid, jnp.where(at == 2, low, 0.0)))
    return out.astype(jnp.bfloat16)


def down(row):
    return jnp.transpose(jnp.broadcast_to(row, (LANES, LANES)))


def hot_rows(values, count):
    column = down(values)
    blocks = []
    for start in range(0, count, LANES):
        width = min(LANES, count - start)
        lane = lax.broadcasted_iota(jnp.int32, (LANES, width), 1).astype(jnp.float32) + start
        blocks.append((column[:, :width] == lane).astype(jnp.float32))
    return blocks[0] if len(blocks) == 1 else jnp.concatenate(blocks, axis=1)


def prepare_kernel(
    own_blocks,
    lik_ref,
    ids_ref,
    valid_ref,
    held_ref,
    info_ref,
    ids,
    valid,
    wide,
    sems,
    held_sems,
):
    read_blocks, slots = ids.shape
    copies = [
        pltpu.make_async_copy(ids_ref, ids, sems.at[0]),
        pltpu.make_async_copy(valid_ref, valid, sems.at[1]),
    ]
    held = block_copies(lik_ref, held_ref, held_sems, 0)
    for copy in copies + held:
        copy.start()
    for copy in copies:
        copy.wait()
    n = lax.axis_size(ALL)
    near = radices(n)[0]
    far = n // near
    me = lax.axis_index("genome") * lax.axis_size("reads") + lax.axis_index("reads")
    lane = lax.broadcasted_iota(jnp.int32, wide.shape, 1)
    wide[...] = jnp.zeros_like(wide)
    wide[:, :slots] = jnp.where(valid[...] > 0, ids[...], -1).astype(jnp.float32)
    flat = jnp.sum(
        pltpu.roll(wide[...], 0, 1, stride=slots, stride_axis=0), axis=0, keepdims=True
    )
    flat = jnp.where(lane[:1] < read_blocks * slots, flat, -1.0)
    owner = ((flat + 0.5) * (1.0 / own_blocks)).astype(jnp.int32)
    inside = flat.astype(jnp.int32) - owner * own_blocks
    away = owner ^ me
    rest = away // near
    for r in radices(n)[1:]:
        for j in CROSSED:
            away = away ^ jnp.where(rest % r == j, 1, 0)
        rest = rest // r
    place = position(away, n)
    place = (place // far) * near_rows(far, own_blocks) + (place % far) * own_blocks + inside
    place = jnp.where(flat < 0, -1, place).astype(jnp.float32)
    row = lax.broadcasted_iota(jnp.int32, info_ref.shape, 0)
    info_ref[...] = jnp.where(row == 0, flat, jnp.where(row == 1, place, 0.0))
    for copy in held:
        copy.wait()


def join_kernel(*refs):
    out_ref = refs[-1]
    at = 0
    for ref in refs[:-1]:
        out_ref[at : at + ref.shape[0], :] = ref[...]
        at += ref.shape[0]
    if at < out_ref.shape[0]:
        out_ref[at:, :] = jnp.zeros((out_ref.shape[0] - at, out_ref.shape[1]), jnp.float32)


def near_rows(far, own_blocks):
    return -(-(far * own_blocks + ID_ROWS) // 16) * 16


def flip_kernel(after_ref, early_ref, lik_ref, late_ref, out_ref, sems):
    early = early_ref.shape[0]
    copies = block_copies(lik_ref, late_ref, sems, early)
    for copy in copies:
        copy.start()
    for b in range(out_ref.shape[0]):
        if b >= early:
            copies[b - early].wait()
        held_ref = block_of((early_ref, late_ref), b)
        slots, reads, cols = held_ref.shape
        for s in range(slots):
            start = s % 2 * cols
            out_ref[b, s // 2, start : start + cols, :] = jnp.transpose(held_ref[s])


def block_copies(lik_ref, held_ref, sems, start):
    return [
        pltpu.make_async_copy(lik_ref.at[start + b], held_ref.at[b], sems.at[b])
        for b in range(held_ref.shape[0])
    ]


def block_of(held_refs, b):
    early_ref, late_ref = held_refs
    early = early_ref.shape[0]
    return early_ref.at[b] if b < early else late_ref.at[b - early]


def row_sums(picked_ref, flip_ref, out_ref):
    read_blocks, pairs = flip_ref.shape[:2]
    for b in range(read_blocks):
        total = None
        for s in range(pairs):
            at = (b * pairs + s) * 2
            left = jnp.concatenate(
                [split(picked_ref[at : at + 1, :]), split(picked_ref[at + 1 : at + 2, :])], axis=1
            )
            part = dot(left, flip_ref[b, s])
            total = part if total is None else total + part
        row = jnp.sum(total, axis=0, keepdims=True)
        for i in range(out_ref.shape[0]):
            out_ref[i, b : b + 1, :] = row


def first_row_kernel(near, info_ref, *refs):
    pieces, (flip_ref, out_ref, picked_ref) = refs[:near], refs[near:]
    table = jnp.concatenate([piece[...] for piece in pieces], axis=0)
    hot = hot_rows(info_ref[1:2, :], table.shape[0])
    picked_ref[...] = select_rows(hot[: picked_ref.shape[0]], table)
    row_sums(picked_ref, flip_ref, out_ref)


def next_row_kernel(near, scale, *refs):
    parts, (flip_ref, out_ref, picked_ref) = refs[:near], refs[near:]
    total = parts[0][...]
    for part in parts[1:]:
        total = total + part[...]
    picked_ref[...] = total * scale
    row_sums(picked_ref, flip_ref, out_ref)


def column_sums(parts_ref, picked_ref, held_refs, contrib_ref, inverse_ref):
    slots, reads, cols = held_refs[0].shape[1:]
    total = parts_ref[0]
    for i in range(1, parts_ref.shape[0]):
        total = total + parts_ref[i]
    inverse_ref[...] = 1.0 / total
    for b in range(inverse_ref.shape[0]):
        held_ref = block_of(held_refs, b)
        left = split(inverse_ref[b : b + 1, :])
        for s in range(0, slots, 2):
            at = b * slots + s
            right = jnp.concatenate([held_ref[s], held_ref[s + 1]], axis=1)
            summed = jnp.sum(dot(left, right), axis=0, keepdims=True)
            contrib_ref[at : at + 1, :] = picked_ref[at : at + 1, :] * summed[:, :cols]
            contrib_ref[at + 1 : at + 2, :] = picked_ref[at + 1 : at + 2, :] * summed[:, cols:]


def column_kernel(info_ref, parts_ref, picked_ref, early_ref, late_ref, out_ref, inverse_ref):
    column_sums(parts_ref, picked_ref, (early_ref, late_ref), out_ref, inverse_ref)
    out_ref[picked_ref.shape[0] :, :] = info_ref[...]


def last_column_kernel(
    order, info_ref, parts_ref, picked_ref, early_ref, late_ref, out_ref, inverse_ref, contrib_ref
):
    column_sums(parts_ref, picked_ref, (early_ref, late_ref), contrib_ref, inverse_ref)
    owners, own_blocks, cols = out_ref.shape
    all_slots = contrib_ref.shape[0]
    block = lax.broadcasted_iota(jnp.int32, (owners * own_blocks, all_slots), 0)
    hot = (block.astype(jnp.float32) == info_ref[0:1, :all_slots]).astype(jnp.float32)
    counts = select_rows(hot, contrib_ref[...])
    for i, owner in enumerate(order):
        out_ref[i] = counts[owner * own_blocks : (owner + 1) * own_blocks, :]


def wanted_kernel(near, all_slots, pieces, *refs):
    given_refs, wanted, outs = refs[:pieces], refs[pieces : pieces + near], refs[pieces + near :]
    rows = all_slots + ID_ROWS
    half = LANES // 2
    lane = lax.broadcasted_iota(jnp.int32, (1, LANES), 1)
    ids, values = [], []
    for ref in given_refs:
        for at in range(0, ref.shape[0], rows):
            ids.append(ref[at + all_slots : at + all_slots + 1, :])
            values.append(ref[at : at + all_slots, :])
    pairs = [
        jnp.where(lane < half, a, pltpu.roll(b, half, 1)) for a, b in zip(ids[::2], ids[1::2])
    ]
    given = terms(jnp.concatenate(values, axis=0))
    for ids_ref, out_ref in zip(wanted, outs):
        column = down(ids_ref[0:1, :])[:all_slots]
        hot = jnp.concatenate([(column == pair).astype(jnp.float32) for pair in pairs], axis=1)
        hot = hot.astype(jnp.bfloat16)
        out_ref[...] = dot(hot, given[0]) + dot(hot, given[1]) + dot(hot, given[2])


def call(kernel, outs, scratch, *operands):
    return pl.pallas_call(
        kernel,
        out_shape=[jax.ShapeDtypeStruct(shape, jnp.float32) for shape in outs],
        in_specs=[VMEM] * len(operands),
        out_specs=[VMEM] * len(outs),
        scratch_shapes=[pltpu.VMEM(shape, jnp.float32) for shape in scratch],
        compiler_params=PARAMS,
    )(*operands)


PARAMS = pltpu.CompilerParams(vmem_limit_bytes=16 * 2**20)


def in_hbm(*arrays):
    return [pltpu.with_memory_space_constraint(x, pltpu.HBM) for x in arrays]


def prepare(own_blocks, early, likelihood, block_ids, slot_valid):
    read_blocks, slots = block_ids.shape
    return pl.pallas_call(
        lambda *refs: prepare_kernel(own_blocks, *refs),
        out_shape=[
            pltpu.VMEM((early,) + likelihood.shape[1:], likelihood.dtype),
            jax.ShapeDtypeStruct((ID_ROWS, LANES), jnp.float32),
        ],
        in_specs=[ANY] * 3,
        out_specs=[VMEM] * 2,
        scratch_shapes=[
            pltpu.VMEM((read_blocks, slots), jnp.int32),
            pltpu.VMEM((read_blocks, slots), jnp.int32),
            pltpu.VMEM((read_blocks, LANES), jnp.float32),
            pltpu.SemaphoreType.DMA((2,)),
            pltpu.SemaphoreType.DMA((early,)),
        ],
        compiler_params=PARAMS,
    )(*in_hbm(likelihood, block_ids, slot_valid))


def flip(after, held, likelihood):
    read_blocks, slots, reads, cols = likelihood.shape
    late = read_blocks - held.shape[0]
    return pl.pallas_call(
        flip_kernel,
        out_shape=[
            pltpu.VMEM((late,) + likelihood.shape[1:], likelihood.dtype),
            pltpu.VMEM((read_blocks, slots // 2, 2 * cols, reads), likelihood.dtype),
        ],
        in_specs=[ANY, VMEM, ANY],
        out_specs=[VMEM] * 2,
        scratch_shapes=[pltpu.SemaphoreType.DMA((late,))],
        compiler_params=PARAMS,
    )(after, held, *in_hbm(likelihood))


def local(likelihood, block_ids, slot_valid, start_weights):
    read_blocks, slots, reads, cols = likelihood.shape
    n = lax.axis_size(ALL)
    chips = lax.axis_size("genome")
    near = radices(n)[0]
    far = n // near
    own_weights = start_weights.reshape(-1, cols)
    own_blocks = own_weights.shape[0]
    all_slots = read_blocks * slots
    total_reads = read_blocks * lax.axis_size("reads") * reads
    scale = n * own_blocks * cols / total_reads

    column = gather_far(own_weights, ALL, CROSSED)
    held, info = prepare(own_blocks, read_blocks // 2, likelihood, block_ids, slot_valid)
    (sent,) = call(join_kernel, [(near_rows(far, own_blocks), cols)], [], *column, info)
    rest, flipped = flip(sent, held, likelihood)
    pieces = [sent] + [swap(sent, ALL, j) for j in range(1, near)]
    at = far * own_blocks
    wanted = [info] + [piece[at : at + ID_ROWS] for piece in pieces[1:]]

    row_shapes = [(chips, read_blocks, reads), (all_slots, cols)]
    inverse = (read_blocks, reads)
    for step in range(ITERS):
        if step == 0:
            row_parts, picked = call(
                lambda *refs: first_row_kernel(near, *refs), row_shapes, [], info, *pieces, flipped
            )
        else:
            row_parts, picked = call(
                lambda *refs: next_row_kernel(near, scale, *refs), row_shapes, [], *parts, flipped
            )
        row_parts = lax.all_to_all(
            row_parts,
            "genome",
            0,
            0,
            tiled=True,
            axis_index_groups=[middle_then_up(chips, chips // 2 + step)],
        )
        if step + 1 < ITERS:
            (contrib,) = call(
                column_kernel,
                [(all_slots + ID_ROWS, cols)],
                [inverse],
                info,
                row_parts,
                picked,
                held,
                rest,
            )
            given = gather_far(contrib, ALL, (1, 2, 3))
            sums = call(
                lambda *refs: wanted_kernel(near, all_slots, len(given), *refs),
                [(all_slots, cols)] * near,
                [],
                *given,
                *wanted,
            )
            parts = [sums[0]] + [swap(sums[j], ALL, j) for j in range(near - 1, 0, -1)]
    order = middle_first(n, n // 2 + 3)
    (counts,) = call(
        lambda *refs: last_column_kernel(order, *refs),
        [(n, own_blocks, cols)],
        [inverse, (all_slots, cols)],
        info,
        row_parts,
        picked,
        held,
        rest,
    )
    counts = lax.all_to_all(counts, ALL, 0, 0, tiled=True, axis_index_groups=[order])
    return (jnp.sum(counts, axis=0) * scale).reshape(-1)


def solution(mesh):
    placed = (
        P(("parts", "reads"), "genome", None, None),
        P(("parts", "reads"), "genome"),
        P(("parts", "reads"), "genome"),
        P(("parts", "genome", "reads")),
    )
    return jax.shard_map(
        local,
        mesh=mesh,
        in_specs=placed,
        out_specs=P(("parts", "genome", "reads")),
        check_vma=False,
    )
```

```python
import jax
import jax.numpy as jnp
from jax import lax
from jax.experimental import pallas as pl
from jax.experimental.pallas import tpu as pltpu
from jax.sharding import PartitionSpec as P

ITERS = 2
ALL = ("genome", "reads")
TERMS = 16
ID_ROWS = 8
CROSSED = (1,)
LANES = 128
VMEM = pl.BlockSpec(memory_space=pltpu.VMEM)
ANY = pl.BlockSpec(memory_space=pl.ANY)


def radices(n):
    out = []
    while n > 1:
        r = 4 if n % 4 == 0 else 2
        out.append(r)
        n //= r
    return out


def swap(x, axes, k):
    n = lax.axis_size(axes)
    return lax.ppermute(x, axes, [(i, i ^ k) for i in range(n)])


def middle_first(n, k):
    return [i ^ k for i in range(n)]


def position(k, n):
    place = 0
    for r in radices(n):
        n //= r
        place = place + (k % r) * n
        k = k // r
    return place


def gather_far(x, axes, crossed):
    parts = [x]
    stride = lax.axis_size(axes)
    for r in radices(stride)[:0:-1]:
        stride //= r
        sent = parts[0] if len(parts) == 1 else jnp.concatenate(parts, axis=0)
        parts = [sent] + [swap(sent, axes, j * stride + (j in crossed)) for j in range(1, r)]
    return parts


def dot(a, b, dims=(((1,), (0,)), ((), ()))):
    return lax.dot_general(a, b, dims, preferred_element_type=jnp.float32)


def terms(x):
    hi = x.astype(jnp.bfloat16)
    rest = x - hi.astype(jnp.float32)
    mid = rest.astype(jnp.bfloat16)
    return hi, mid, (rest - mid.astype(jnp.float32)).astype(jnp.bfloat16)


def select_rows(hot, x):
    hi, mid, low = terms(x)
    hot = hot.astype(jnp.bfloat16)
    return dot(hot, hi) + dot(hot, mid) + dot(hot, low)


def split(row):
    x = jnp.broadcast_to(row, (TERMS, row.shape[1]))
    hi = x.astype(jnp.bfloat16).astype(jnp.float32)
    rest = x - hi
    mid = rest.astype(jnp.bfloat16).astype(jnp.float32)
    low = rest - mid
    at = lax.broadcasted_iota(jnp.int32, x.shape, 0)
    out = jnp.where(at == 0, hi, jnp.where(at == 1, mid, jnp.where(at == 2, low, 0.0)))
    return out.astype(jnp.bfloat16)


def down(row):
    return jnp.transpose(jnp.broadcast_to(row, (LANES, LANES)))


def hot_rows(values, count):
    column = down(values)
    blocks = []
    for start in range(0, count, LANES):
        width = min(LANES, count - start)
        lane = lax.broadcasted_iota(jnp.int32, (LANES, width), 1).astype(jnp.float32) + start
        blocks.append((column[:, :width] == lane).astype(jnp.float32))
    return blocks[0] if len(blocks) == 1 else jnp.concatenate(blocks, axis=1)


def prepare_kernel(
    own_blocks,
    lik_ref,
    ids_ref,
    valid_ref,
    held_ref,
    info_ref,
    ids,
    valid,
    wide,
    sems,
    held_sems,
):
    read_blocks, slots = ids.shape
    copies = [
        pltpu.make_async_copy(ids_ref, ids, sems.at[0]),
        pltpu.make_async_copy(valid_ref, valid, sems.at[1]),
    ]
    held = block_copies(lik_ref, held_ref, held_sems, 0)
    for copy in copies + held:
        copy.start()
    for copy in copies:
        copy.wait()
    n = lax.axis_size(ALL)
    near = radices(n)[0]
    far = n // near
    me = lax.axis_index("genome") * lax.axis_size("reads") + lax.axis_index("reads")
    lane = lax.broadcasted_iota(jnp.int32, wide.shape, 1)
    wide[...] = jnp.zeros_like(wide)
    wide[:, :slots] = jnp.where(valid[...] > 0, ids[...], -1).astype(jnp.float32)
    flat = jnp.sum(
        pltpu.roll(wide[...], 0, 1, stride=slots, stride_axis=0), axis=0, keepdims=True
    )
    flat = jnp.where(lane[:1] < read_blocks * slots, flat, -1.0)
    owner = ((flat + 0.5) * (1.0 / own_blocks)).astype(jnp.int32)
    inside = flat.astype(jnp.int32) - owner * own_blocks
    away = owner ^ me
    rest = away // near
    for r in radices(n)[1:]:
        for j in CROSSED:
            away = away ^ jnp.where(rest % r == j, 1, 0)
        rest = rest // r
    place = position(away, n)
    place = (place // far) * near_rows(far, own_blocks) + (place % far) * own_blocks + inside
    place = jnp.where(flat < 0, -1, place).astype(jnp.float32)
    row = lax.broadcasted_iota(jnp.int32, info_ref.shape, 0)
    info_ref[...] = jnp.where(row == 0, flat, jnp.where(row == 1, place, 0.0))
    for copy in held:
        copy.wait()


def join_kernel(*refs):
    out_ref = refs[-1]
    at = 0
    for ref in refs[:-1]:
        out_ref[at : at + ref.shape[0], :] = ref[...]
        at += ref.shape[0]
    if at < out_ref.shape[0]:
        out_ref[at:, :] = jnp.zeros((out_ref.shape[0] - at, out_ref.shape[1]), jnp.float32)


def near_rows(far, own_blocks):
    return -(-(far * own_blocks + ID_ROWS) // 16) * 16


def flip_kernel(after_ref, early_ref, lik_ref, late_ref, out_ref, sems):
    early = early_ref.shape[0]
    copies = block_copies(lik_ref, late_ref, sems, early)
    for copy in copies:
        copy.start()
    for b in range(out_ref.shape[0]):
        if b >= early:
            copies[b - early].wait()
        held_ref = block_of((early_ref, late_ref), b)
        slots, reads, cols = held_ref.shape
        for s in range(slots):
            start = s % 2 * cols
            out_ref[b, s // 2, start : start + cols, :] = jnp.transpose(held_ref[s])


def block_copies(lik_ref, held_ref, sems, start):
    return [
        pltpu.make_async_copy(lik_ref.at[start + b], held_ref.at[b], sems.at[b])
        for b in range(held_ref.shape[0])
    ]


def block_of(held_refs, b):
    early_ref, late_ref = held_refs
    early = early_ref.shape[0]
    return early_ref.at[b] if b < early else late_ref.at[b - early]


def row_sums(picked_ref, flip_ref, out_ref):
    read_blocks, pairs = flip_ref.shape[:2]
    for b in range(read_blocks):
        total = None
        for s in range(pairs):
            at = (b * pairs + s) * 2
            left = jnp.concatenate(
                [split(picked_ref[at : at + 1, :]), split(picked_ref[at + 1 : at + 2, :])], axis=1
            )
            part = dot(left, flip_ref[b, s])
            total = part if total is None else total + part
        row = jnp.sum(total, axis=0, keepdims=True)
        for i in range(out_ref.shape[0]):
            out_ref[i, b : b + 1, :] = row


def first_row_kernel(near, info_ref, *refs):
    pieces, (flip_ref, out_ref, picked_ref) = refs[:near], refs[near:]
    table = jnp.concatenate([piece[...] for piece in pieces], axis=0)
    hot = hot_rows(info_ref[1:2, :], table.shape[0])
    picked_ref[...] = select_rows(hot[: picked_ref.shape[0]], table)
    row_sums(picked_ref, flip_ref, out_ref)


def next_row_kernel(near, scale, *refs):
    parts, (flip_ref, out_ref, picked_ref) = refs[:near], refs[near:]
    total = parts[0][...]
    for part in parts[1:]:
        total = total + part[...]
    picked_ref[...] = total * scale
    row_sums(picked_ref, flip_ref, out_ref)


def column_sums(parts_ref, picked_ref, held_refs, contrib_ref, inverse_ref):
    slots, reads, cols = held_refs[0].shape[1:]
    total = parts_ref[0]
    for i in range(1, parts_ref.shape[0]):
        total = total + parts_ref[i]
    inverse_ref[...] = 1.0 / total
    for b in range(inverse_ref.shape[0]):
        held_ref = block_of(held_refs, b)
        left = split(inverse_ref[b : b + 1, :])
        for s in range(0, slots, 2):
            at = b * slots + s
            right = jnp.concatenate([held_ref[s], held_ref[s + 1]], axis=1)
            summed = jnp.sum(dot(left, right), axis=0, keepdims=True)
            contrib_ref[at : at + 1, :] = picked_ref[at : at + 1, :] * summed[:, :cols]
            contrib_ref[at + 1 : at + 2, :] = picked_ref[at + 1 : at + 2, :] * summed[:, cols:]


def column_kernel(info_ref, parts_ref, picked_ref, early_ref, late_ref, out_ref, inverse_ref):
    column_sums(parts_ref, picked_ref, (early_ref, late_ref), out_ref, inverse_ref)
    out_ref[picked_ref.shape[0] :, :] = info_ref[...]


def last_column_kernel(
    order, info_ref, parts_ref, picked_ref, early_ref, late_ref, out_ref, inverse_ref, contrib_ref
):
    column_sums(parts_ref, picked_ref, (early_ref, late_ref), contrib_ref, inverse_ref)
    owners, own_blocks, cols = out_ref.shape
    all_slots = contrib_ref.shape[0]
    block = lax.broadcasted_iota(jnp.int32, (owners * own_blocks, all_slots), 0)
    hot = (block.astype(jnp.float32) == info_ref[0:1, :all_slots]).astype(jnp.float32)
    counts = select_rows(hot, contrib_ref[...])
    for i, owner in enumerate(order):
        out_ref[i] = counts[owner * own_blocks : (owner + 1) * own_blocks, :]


def wanted_kernel(near, all_slots, pieces, *refs):
    given_refs, wanted, outs = refs[:pieces], refs[pieces : pieces + near], refs[pieces + near :]
    rows = all_slots + ID_ROWS
    half = LANES // 2
    lane = lax.broadcasted_iota(jnp.int32, (1, LANES), 1)
    ids, values = [], []
    for ref in given_refs:
        for at in range(0, ref.shape[0], rows):
            ids.append(ref[at + all_slots : at + all_slots + 1, :])
            values.append(ref[at : at + all_slots, :])
    pairs = [
        jnp.where(lane < half, a, pltpu.roll(b, half, 1)) for a, b in zip(ids[::2], ids[1::2])
    ]
    given = terms(jnp.concatenate(values, axis=0))
    for ids_ref, out_ref in zip(wanted, outs):
        column = down(ids_ref[0:1, :])[:all_slots]
        hot = jnp.concatenate([(column == pair).astype(jnp.float32) for pair in pairs], axis=1)
        hot = hot.astype(jnp.bfloat16)
        out_ref[...] = dot(hot, given[0]) + dot(hot, given[1]) + dot(hot, given[2])


def call(kernel, outs, scratch, *operands):
    return pl.pallas_call(
        kernel,
        out_shape=[jax.ShapeDtypeStruct(shape, jnp.float32) for shape in outs],
        in_specs=[VMEM] * len(operands),
        out_specs=[VMEM] * len(outs),
        scratch_shapes=[pltpu.VMEM(shape, jnp.float32) for shape in scratch],
        compiler_params=PARAMS,
    )(*operands)


PARAMS = pltpu.CompilerParams(vmem_limit_bytes=16 * 2**20)


def in_hbm(*arrays):
    return [pltpu.with_memory_space_constraint(x, pltpu.HBM) for x in arrays]


def prepare(own_blocks, early, likelihood, block_ids, slot_valid):
    read_blocks, slots = block_ids.shape
    return pl.pallas_call(
        lambda *refs: prepare_kernel(own_blocks, *refs),
        out_shape=[
            pltpu.VMEM((early,) + likelihood.shape[1:], likelihood.dtype),
            jax.ShapeDtypeStruct((ID_ROWS, LANES), jnp.float32),
        ],
        in_specs=[ANY] * 3,
        out_specs=[VMEM] * 2,
        scratch_shapes=[
            pltpu.VMEM((read_blocks, slots), jnp.int32),
            pltpu.VMEM((read_blocks, slots), jnp.int32),
            pltpu.VMEM((read_blocks, LANES), jnp.float32),
            pltpu.SemaphoreType.DMA((2,)),
            pltpu.SemaphoreType.DMA((early,)),
        ],
        compiler_params=PARAMS,
    )(*in_hbm(likelihood, block_ids, slot_valid))


def flip(after, held, likelihood):
    read_blocks, slots, reads, cols = likelihood.shape
    late = read_blocks - held.shape[0]
    return pl.pallas_call(
        flip_kernel,
        out_shape=[
            pltpu.VMEM((late,) + likelihood.shape[1:], likelihood.dtype),
            pltpu.VMEM((read_blocks, slots // 2, 2 * cols, reads), likelihood.dtype),
        ],
        in_specs=[ANY, VMEM, ANY],
        out_specs=[VMEM] * 2,
        scratch_shapes=[pltpu.SemaphoreType.DMA((late,))],
        compiler_params=PARAMS,
    )(after, held, *in_hbm(likelihood))


def local(likelihood, block_ids, slot_valid, start_weights):
    read_blocks, slots, reads, cols = likelihood.shape
    n = lax.axis_size(ALL)
    chips = lax.axis_size("genome")
    near = radices(n)[0]
    far = n // near
    own_weights = start_weights.reshape(-1, cols)
    own_blocks = own_weights.shape[0]
    all_slots = read_blocks * slots
    total_reads = read_blocks * lax.axis_size("reads") * reads
    scale = n * own_blocks * cols / total_reads

    column = gather_far(own_weights, ALL, CROSSED)
    held, info = prepare(own_blocks, read_blocks // 4, likelihood, block_ids, slot_valid)
    (sent,) = call(join_kernel, [(near_rows(far, own_blocks), cols)], [], *column, info)
    rest, flipped = flip(sent, held, likelihood)
    pieces = [sent] + [swap(sent, ALL, j) for j in range(1, near)]
    at = far * own_blocks
    wanted = [info] + [piece[at : at + ID_ROWS] for piece in pieces[1:]]

    row_shapes = [(chips, read_blocks, reads), (all_slots, cols)]
    inverse = (read_blocks, reads)
    for step in range(ITERS):
        if step == 0:
            row_parts, picked = call(
                lambda *refs: first_row_kernel(near, *refs), row_shapes, [], info, *pieces, flipped
            )
        else:
            row_parts, picked = call(
                lambda *refs: next_row_kernel(near, scale, *refs), row_shapes, [], *parts, flipped
            )
        row_parts = lax.all_to_all(
            row_parts,
            "genome",
            0,
            0,
            tiled=True,
            axis_index_groups=[middle_first(chips, chips // 2 + step)],
        )
        if step + 1 < ITERS:
            (contrib,) = call(
                column_kernel,
                [(all_slots + ID_ROWS, cols)],
                [inverse],
                info,
                row_parts,
                picked,
                held,
                rest,
            )
            given = gather_far(contrib, ALL, (1, 2, 3))
            sums = call(
                lambda *refs: wanted_kernel(near, all_slots, len(given), *refs),
                [(all_slots, cols)] * near,
                [],
                *given,
                *wanted,
            )
            parts = [sums[0]] + [swap(sums[j], ALL, j) for j in range(near - 1, 0, -1)]
    order = middle_first(n, n // 2 + 3)
    (counts,) = call(
        lambda *refs: last_column_kernel(order, *refs),
        [(n, own_blocks, cols)],
        [inverse, (all_slots, cols)],
        info,
        row_parts,
        picked,
        held,
        rest,
    )
    counts = lax.all_to_all(counts, ALL, 0, 0, tiled=True, axis_index_groups=[order])
    return (jnp.sum(counts, axis=0) * scale).reshape(-1)


def solution(mesh):
    placed = (
        P(("parts", "reads"), "genome", None, None),
        P(("parts", "reads"), "genome"),
        P(("parts", "reads"), "genome"),
        P(("parts", "genome", "reads")),
    )
    return jax.shard_map(
        local,
        mesh=mesh,
        in_specs=placed,
        out_specs=P(("parts", "genome", "reads")),
        check_vma=False,
    )
```

```python
import jax
import jax.numpy as jnp
from jax import lax
from jax.experimental import pallas as pl
from jax.experimental.pallas import tpu as pltpu
from jax.sharding import PartitionSpec as P

ITERS = 2
ALL = ("genome", "reads")
TERMS = 16
ID_ROWS = 8
CROSSED = (1,)
LANES = 128
VMEM = pl.BlockSpec(memory_space=pltpu.VMEM)
ANY = pl.BlockSpec(memory_space=pl.ANY)


def radices(n):
    out = []
    while n > 1:
        r = 4 if n % 4 == 0 else 2
        out.append(r)
        n //= r
    return out


def swap(x, axes, k):
    n = lax.axis_size(axes)
    return lax.ppermute(x, axes, [(i, i ^ k) for i in range(n)])


def middle_first(n, k):
    return [i ^ k for i in range(n)]


def position(k, n):
    first, *rest = radices(n)
    n //= first
    place = k % first * n
    k = k // first
    for r in rest:
        n //= r
        digit = k % r
        place = place + (digit ^ (digit >> 1)) * n
        k = k // r
    return place


def gather_far(x, axes, crossed):
    parts = [x]
    stride = lax.axis_size(axes)
    for r in radices(stride)[:0:-1]:
        stride //= r
        sent = parts[0] if len(parts) == 1 else jnp.concatenate(parts, axis=0)
        parts = [sent] + [
            swap(sent, axes, j * stride + (j in crossed)) for j in (1, 3, 2) if j < r
        ]
    return parts


def dot(a, b, dims=(((1,), (0,)), ((), ()))):
    return lax.dot_general(a, b, dims, preferred_element_type=jnp.float32)


def terms(x):
    hi = x.astype(jnp.bfloat16)
    rest = x - hi.astype(jnp.float32)
    mid = rest.astype(jnp.bfloat16)
    return hi, mid, (rest - mid.astype(jnp.float32)).astype(jnp.bfloat16)


def select_rows(hot, x):
    hi, mid, low = terms(x)
    hot = hot.astype(jnp.bfloat16)
    return dot(hot, hi) + dot(hot, mid) + dot(hot, low)


def split(row):
    x = jnp.broadcast_to(row, (TERMS, row.shape[1]))
    hi = x.astype(jnp.bfloat16).astype(jnp.float32)
    rest = x - hi
    mid = rest.astype(jnp.bfloat16).astype(jnp.float32)
    low = rest - mid
    at = lax.broadcasted_iota(jnp.int32, x.shape, 0)
    out = jnp.where(at == 0, hi, jnp.where(at == 1, mid, jnp.where(at == 2, low, 0.0)))
    return out.astype(jnp.bfloat16)


def down(row):
    return jnp.transpose(jnp.broadcast_to(row, (LANES, LANES)))


def hot_rows(values, count):
    column = down(values)
    blocks = []
    for start in range(0, count, LANES):
        width = min(LANES, count - start)
        lane = lax.broadcasted_iota(jnp.int32, (LANES, width), 1).astype(jnp.float32) + start
        blocks.append((column[:, :width] == lane).astype(jnp.float32))
    return blocks[0] if len(blocks) == 1 else jnp.concatenate(blocks, axis=1)


def prepare_kernel(
    own_blocks,
    lik_ref,
    ids_ref,
    valid_ref,
    held_ref,
    info_ref,
    ids,
    valid,
    wide,
    sems,
    held_sems,
):
    read_blocks, slots = ids.shape
    copies = [
        pltpu.make_async_copy(ids_ref, ids, sems.at[0]),
        pltpu.make_async_copy(valid_ref, valid, sems.at[1]),
    ]
    held = block_copies(lik_ref, held_ref, held_sems, 0)
    for copy in copies + held:
        copy.start()
    for copy in copies:
        copy.wait()
    n = lax.axis_size(ALL)
    near = radices(n)[0]
    far = n // near
    me = lax.axis_index("genome") * lax.axis_size("reads") + lax.axis_index("reads")
    lane = lax.broadcasted_iota(jnp.int32, wide.shape, 1)
    wide[...] = jnp.zeros_like(wide)
    wide[:, :slots] = jnp.where(valid[...] > 0, ids[...], -1).astype(jnp.float32)
    flat = jnp.sum(
        pltpu.roll(wide[...], 0, 1, stride=slots, stride_axis=0), axis=0, keepdims=True
    )
    flat = jnp.where(lane[:1] < read_blocks * slots, flat, -1.0)
    owner = ((flat + 0.5) * (1.0 / own_blocks)).astype(jnp.int32)
    inside = flat.astype(jnp.int32) - owner * own_blocks
    away = owner ^ me
    rest = away // near
    for r in radices(n)[1:]:
        for j in CROSSED:
            away = away ^ jnp.where(rest % r == j, 1, 0)
        rest = rest // r
    place = position(away, n)
    place = (place // far) * near_rows(far, own_blocks) + (place % far) * own_blocks + inside
    place = jnp.where(flat < 0, -1, place).astype(jnp.float32)
    row = lax.broadcasted_iota(jnp.int32, info_ref.shape, 0)
    info_ref[...] = jnp.where(row == 0, flat, jnp.where(row == 1, place, 0.0))
    for copy in held:
        copy.wait()


def join_kernel(*refs):
    out_ref = refs[-1]
    at = 0
    for ref in refs[:-1]:
        out_ref[at : at + ref.shape[0], :] = ref[...]
        at += ref.shape[0]
    if at < out_ref.shape[0]:
        out_ref[at:, :] = jnp.zeros((out_ref.shape[0] - at, out_ref.shape[1]), jnp.float32)


def near_rows(far, own_blocks):
    return -(-(far * own_blocks + ID_ROWS) // 16) * 16


def flip_kernel(after_ref, early_ref, lik_ref, late_ref, out_ref, sems):
    early = early_ref.shape[0]
    copies = block_copies(lik_ref, late_ref, sems, early)
    for copy in copies:
        copy.start()
    for b in range(out_ref.shape[0]):
        if b >= early:
            copies[b - early].wait()
        held_ref = block_of((early_ref, late_ref), b)
        slots, reads, cols = held_ref.shape
        for s in range(slots):
            start = s % 2 * cols
            out_ref[b, s // 2, start : start + cols, :] = jnp.transpose(held_ref[s])


def block_copies(lik_ref, held_ref, sems, start):
    return [
        pltpu.make_async_copy(lik_ref.at[start + b], held_ref.at[b], sems.at[b])
        for b in range(held_ref.shape[0])
    ]


def block_of(held_refs, b):
    early_ref, late_ref = held_refs
    early = early_ref.shape[0]
    return early_ref.at[b] if b < early else late_ref.at[b - early]


def row_sums(picked_ref, flip_ref, out_ref):
    read_blocks, pairs = flip_ref.shape[:2]
    for b in range(read_blocks):
        total = None
        for s in range(pairs):
            at = (b * pairs + s) * 2
            left = jnp.concatenate(
                [split(picked_ref[at : at + 1, :]), split(picked_ref[at + 1 : at + 2, :])], axis=1
            )
            part = dot(left, flip_ref[b, s])
            total = part if total is None else total + part
        row = jnp.sum(total, axis=0, keepdims=True)
        for i in range(out_ref.shape[0]):
            out_ref[i, b : b + 1, :] = row


def first_row_kernel(near, info_ref, *refs):
    pieces, (flip_ref, out_ref, picked_ref) = refs[:near], refs[near:]
    table = jnp.concatenate([piece[...] for piece in pieces], axis=0)
    hot = hot_rows(info_ref[1:2, :], table.shape[0])
    picked_ref[...] = select_rows(hot[: picked_ref.shape[0]], table)
    row_sums(picked_ref, flip_ref, out_ref)


def next_row_kernel(near, scale, *refs):
    parts, (flip_ref, out_ref, picked_ref) = refs[:near], refs[near:]
    total = parts[0][...]
    for part in parts[1:]:
        total = total + part[...]
    picked_ref[...] = total * scale
    row_sums(picked_ref, flip_ref, out_ref)


def column_sums(parts_ref, picked_ref, held_refs, contrib_ref, inverse_ref):
    slots, reads, cols = held_refs[0].shape[1:]
    total = parts_ref[0]
    for i in range(1, parts_ref.shape[0]):
        total = total + parts_ref[i]
    inverse_ref[...] = 1.0 / total
    for b in range(inverse_ref.shape[0]):
        held_ref = block_of(held_refs, b)
        left = split(inverse_ref[b : b + 1, :])
        for s in range(0, slots, 2):
            at = b * slots + s
            right = jnp.concatenate([held_ref[s], held_ref[s + 1]], axis=1)
            summed = jnp.sum(dot(left, right), axis=0, keepdims=True)
            contrib_ref[at : at + 1, :] = picked_ref[at : at + 1, :] * summed[:, :cols]
            contrib_ref[at + 1 : at + 2, :] = picked_ref[at + 1 : at + 2, :] * summed[:, cols:]


def column_kernel(info_ref, parts_ref, picked_ref, early_ref, late_ref, out_ref, inverse_ref):
    column_sums(parts_ref, picked_ref, (early_ref, late_ref), out_ref, inverse_ref)
    out_ref[picked_ref.shape[0] :, :] = info_ref[...]


def last_column_kernel(
    order, info_ref, parts_ref, picked_ref, early_ref, late_ref, out_ref, inverse_ref, contrib_ref
):
    column_sums(parts_ref, picked_ref, (early_ref, late_ref), contrib_ref, inverse_ref)
    owners, own_blocks, cols = out_ref.shape
    all_slots = contrib_ref.shape[0]
    block = lax.broadcasted_iota(jnp.int32, (owners * own_blocks, all_slots), 0)
    hot = (block.astype(jnp.float32) == info_ref[0:1, :all_slots]).astype(jnp.float32)
    counts = select_rows(hot, contrib_ref[...])
    for i, owner in enumerate(order):
        out_ref[i] = counts[owner * own_blocks : (owner + 1) * own_blocks, :]


def wanted_kernel(near, all_slots, pieces, *refs):
    given_refs, wanted, outs = refs[:pieces], refs[pieces : pieces + near], refs[pieces + near :]
    rows = all_slots + ID_ROWS
    half = LANES // 2
    lane = lax.broadcasted_iota(jnp.int32, (1, LANES), 1)
    ids, values = [], []
    for ref in given_refs:
        for at in range(0, ref.shape[0], rows):
            ids.append(ref[at + all_slots : at + all_slots + 1, :])
            values.append(ref[at : at + all_slots, :])
    pairs = [
        jnp.where(lane < half, a, pltpu.roll(b, half, 1)) for a, b in zip(ids[::2], ids[1::2])
    ]
    given = terms(jnp.concatenate(values, axis=0))
    for ids_ref, out_ref in zip(wanted, outs):
        column = down(ids_ref[0:1, :])[:all_slots]
        hot = jnp.concatenate([(column == pair).astype(jnp.float32) for pair in pairs], axis=1)
        hot = hot.astype(jnp.bfloat16)
        out_ref[...] = dot(hot, given[0]) + dot(hot, given[1]) + dot(hot, given[2])


def call(kernel, outs, scratch, *operands):
    return pl.pallas_call(
        kernel,
        out_shape=[jax.ShapeDtypeStruct(shape, jnp.float32) for shape in outs],
        in_specs=[VMEM] * len(operands),
        out_specs=[VMEM] * len(outs),
        scratch_shapes=[pltpu.VMEM(shape, jnp.float32) for shape in scratch],
        compiler_params=PARAMS,
    )(*operands)


PARAMS = pltpu.CompilerParams(vmem_limit_bytes=16 * 2**20)


def in_hbm(*arrays):
    return [pltpu.with_memory_space_constraint(x, pltpu.HBM) for x in arrays]


def prepare(own_blocks, early, likelihood, block_ids, slot_valid):
    read_blocks, slots = block_ids.shape
    return pl.pallas_call(
        lambda *refs: prepare_kernel(own_blocks, *refs),
        out_shape=[
            pltpu.VMEM((early,) + likelihood.shape[1:], likelihood.dtype),
            jax.ShapeDtypeStruct((ID_ROWS, LANES), jnp.float32),
        ],
        in_specs=[ANY] * 3,
        out_specs=[VMEM] * 2,
        scratch_shapes=[
            pltpu.VMEM((read_blocks, slots), jnp.int32),
            pltpu.VMEM((read_blocks, slots), jnp.int32),
            pltpu.VMEM((read_blocks, LANES), jnp.float32),
            pltpu.SemaphoreType.DMA((2,)),
            pltpu.SemaphoreType.DMA((early,)),
        ],
        compiler_params=PARAMS,
    )(*in_hbm(likelihood, block_ids, slot_valid))


def flip(after, held, likelihood):
    read_blocks, slots, reads, cols = likelihood.shape
    late = read_blocks - held.shape[0]
    return pl.pallas_call(
        flip_kernel,
        out_shape=[
            pltpu.VMEM((late,) + likelihood.shape[1:], likelihood.dtype),
            pltpu.VMEM((read_blocks, slots // 2, 2 * cols, reads), likelihood.dtype),
        ],
        in_specs=[ANY, VMEM, ANY],
        out_specs=[VMEM] * 2,
        scratch_shapes=[pltpu.SemaphoreType.DMA((late,))],
        compiler_params=PARAMS,
    )(after, held, *in_hbm(likelihood))


def local(likelihood, block_ids, slot_valid, start_weights):
    read_blocks, slots, reads, cols = likelihood.shape
    n = lax.axis_size(ALL)
    chips = lax.axis_size("genome")
    near = radices(n)[0]
    far = n // near
    own_weights = start_weights.reshape(-1, cols)
    own_blocks = own_weights.shape[0]
    all_slots = read_blocks * slots
    total_reads = read_blocks * lax.axis_size("reads") * reads
    scale = n * own_blocks * cols / total_reads

    column = gather_far(own_weights, ALL, CROSSED)
    held, info = prepare(own_blocks, read_blocks * 3 // 8, likelihood, block_ids, slot_valid)
    (sent,) = call(join_kernel, [(near_rows(far, own_blocks), cols)], [], *column, info)
    rest, flipped = flip(sent, held, likelihood)
    pieces = [sent] + [swap(sent, ALL, j) for j in range(1, near)]
    at = far * own_blocks
    wanted = [info] + [piece[at : at + ID_ROWS] for piece in pieces[1:]]

    row_shapes = [(chips, read_blocks, reads), (all_slots, cols)]
    inverse = (read_blocks, reads)
    for step in range(ITERS):
        if step == 0:
            row_parts, picked = call(
                lambda *refs: first_row_kernel(near, *refs), row_shapes, [], info, *pieces, flipped
            )
        else:
            row_parts, picked = call(
                lambda *refs: next_row_kernel(near, scale, *refs), row_shapes, [], *parts, flipped
            )
        row_parts = lax.all_to_all(
            row_parts,
            "genome",
            0,
            0,
            tiled=True,
            axis_index_groups=[middle_first(chips, chips // 2 + step)],
        )
        if step + 1 < ITERS:
            (contrib,) = call(
                column_kernel,
                [(all_slots + ID_ROWS, cols)],
                [inverse],
                info,
                row_parts,
                picked,
                held,
                rest,
            )
            given = gather_far(contrib, ALL, (1, 2, 3))
            sums = call(
                lambda *refs: wanted_kernel(near, all_slots, len(given), *refs),
                [(all_slots, cols)] * near,
                [],
                *given,
                *wanted,
            )
            parts = [sums[0]] + [swap(sums[j], ALL, j) for j in range(near - 1, 0, -1)]
    order = middle_first(n, n // 2 + 3)
    (counts,) = call(
        lambda *refs: last_column_kernel(order, *refs),
        [(n, own_blocks, cols)],
        [inverse, (all_slots, cols)],
        info,
        row_parts,
        picked,
        held,
        rest,
    )
    counts = lax.all_to_all(counts, ALL, 0, 0, tiled=True, axis_index_groups=[order])
    return (jnp.sum(counts, axis=0) * scale).reshape(-1)


def solution(mesh):
    placed = (
        P(("parts", "reads"), "genome", None, None),
        P(("parts", "reads"), "genome"),
        P(("parts", "reads"), "genome"),
        P(("parts", "genome", "reads")),
    )
    return jax.shard_map(
        local,
        mesh=mesh,
        in_specs=placed,
        out_specs=P(("parts", "genome", "reads")),
        check_vma=False,
    )
```

```python
import jax
import jax.numpy as jnp
from jax import lax
from jax.experimental import pallas as pl
from jax.experimental.pallas import tpu as pltpu
from jax.sharding import PartitionSpec as P

ITERS = 2
ALL = ("genome", "reads")
TERMS = 16
ID_ROWS = 8
CROSSED = (3,)
LANES = 128
VMEM = pl.BlockSpec(memory_space=pltpu.VMEM)
ANY = pl.BlockSpec(memory_space=pl.ANY)


def radices(n):
    out = []
    while n > 1:
        r = 4 if n % 4 == 0 else 2
        out.append(r)
        n //= r
    return out


def swap(x, axes, k):
    n = lax.axis_size(axes)
    return lax.ppermute(x, axes, [(i, i ^ k) for i in range(n)])


def middle_first(n, k):
    return [i ^ k for i in range(n)]


def position(k, n):
    place = 0
    for r in radices(n):
        n //= r
        place = place + (k % r) * n
        k = k // r
    return place


def gather_far(x, axes, crossed):
    parts = [x]
    stride = lax.axis_size(axes)
    for r in radices(stride)[:0:-1]:
        stride //= r
        sent = parts[0] if len(parts) == 1 else jnp.concatenate(parts, axis=0)
        parts = [sent] + [swap(sent, axes, j * stride + (j in crossed)) for j in range(1, r)]
    return parts


def dot(a, b, dims=(((1,), (0,)), ((), ()))):
    return lax.dot_general(a, b, dims, preferred_element_type=jnp.float32)


def terms(x):
    hi = x.astype(jnp.bfloat16)
    rest = x - hi.astype(jnp.float32)
    mid = rest.astype(jnp.bfloat16)
    return hi, mid, (rest - mid.astype(jnp.float32)).astype(jnp.bfloat16)


def select_rows(hot, x):
    hi, mid, low = terms(x)
    hot = hot.astype(jnp.bfloat16)
    return dot(hot, hi) + dot(hot, mid) + dot(hot, low)


def split(row):
    x = jnp.broadcast_to(row, (TERMS, row.shape[1]))
    hi = x.astype(jnp.bfloat16).astype(jnp.float32)
    rest = x - hi
    mid = rest.astype(jnp.bfloat16).astype(jnp.float32)
    low = rest - mid
    at = lax.broadcasted_iota(jnp.int32, x.shape, 0)
    out = jnp.where(at == 0, hi, jnp.where(at == 1, mid, jnp.where(at == 2, low, 0.0)))
    return out.astype(jnp.bfloat16)


def down(row):
    return jnp.transpose(jnp.broadcast_to(row, (LANES, LANES)))


def hot_rows(values, count):
    column = down(values)
    blocks = []
    for start in range(0, count, LANES):
        width = min(LANES, count - start)
        lane = lax.broadcasted_iota(jnp.int32, (LANES, width), 1).astype(jnp.float32) + start
        blocks.append((column[:, :width] == lane).astype(jnp.float32))
    return blocks[0] if len(blocks) == 1 else jnp.concatenate(blocks, axis=1)


def prepare_kernel(
    own_blocks,
    lik_ref,
    ids_ref,
    valid_ref,
    held_ref,
    info_ref,
    ids,
    valid,
    wide,
    sems,
    held_sems,
):
    read_blocks, slots = ids.shape
    copies = [
        pltpu.make_async_copy(ids_ref, ids, sems.at[0]),
        pltpu.make_async_copy(valid_ref, valid, sems.at[1]),
    ]
    held = block_copies(lik_ref, held_ref, held_sems, 0)
    for copy in copies + held:
        copy.start()
    for copy in copies:
        copy.wait()
    n = lax.axis_size(ALL)
    near = radices(n)[0]
    far = n // near
    me = lax.axis_index("genome") * lax.axis_size("reads") + lax.axis_index("reads")
    lane = lax.broadcasted_iota(jnp.int32, wide.shape, 1)
    wide[...] = jnp.zeros_like(wide)
    wide[:, :slots] = jnp.where(valid[...] > 0, ids[...], -1).astype(jnp.float32)
    flat = jnp.sum(
        pltpu.roll(wide[...], 0, 1, stride=slots, stride_axis=0), axis=0, keepdims=True
    )
    flat = jnp.where(lane[:1] < read_blocks * slots, flat, -1.0)
    owner = ((flat + 0.5) * (1.0 / own_blocks)).astype(jnp.int32)
    inside = flat.astype(jnp.int32) - owner * own_blocks
    away = owner ^ me
    rest = away // near
    for r in radices(n)[1:]:
        for j in CROSSED:
            away = away ^ jnp.where(rest % r == j, 1, 0)
        rest = rest // r
    place = position(away, n)
    place = (place // far) * near_rows(far, own_blocks) + (place % far) * own_blocks + inside
    place = jnp.where(flat < 0, -1, place).astype(jnp.float32)
    row = lax.broadcasted_iota(jnp.int32, info_ref.shape, 0)
    info_ref[...] = jnp.where(row == 0, flat, jnp.where(row == 1, place, 0.0))
    for copy in held:
        copy.wait()


def join_kernel(*refs):
    out_ref = refs[-1]
    at = 0
    for ref in refs[:-1]:
        out_ref[at : at + ref.shape[0], :] = ref[...]
        at += ref.shape[0]
    if at < out_ref.shape[0]:
        out_ref[at:, :] = jnp.zeros((out_ref.shape[0] - at, out_ref.shape[1]), jnp.float32)


def near_rows(far, own_blocks):
    return -(-(far * own_blocks + ID_ROWS) // 16) * 16


def flip_kernel(after_ref, early_ref, lik_ref, late_ref, out_ref, sems):
    early = early_ref.shape[0]
    copies = block_copies(lik_ref, late_ref, sems, early)
    for copy in copies:
        copy.start()
    for b in range(out_ref.shape[0]):
        if b >= early:
            copies[b - early].wait()
        held_ref = block_of((early_ref, late_ref), b)
        slots, reads, cols = held_ref.shape
        for s in range(slots):
            start = s % 2 * cols
            out_ref[b, s // 2, start : start + cols, :] = jnp.transpose(held_ref[s])


def block_copies(lik_ref, held_ref, sems, start):
    return [
        pltpu.make_async_copy(lik_ref.at[start + b], held_ref.at[b], sems.at[b])
        for b in range(held_ref.shape[0])
    ]


def block_of(held_refs, b):
    early_ref, late_ref = held_refs
    early = early_ref.shape[0]
    return early_ref.at[b] if b < early else late_ref.at[b - early]


def row_sums(picked_ref, flip_ref, out_ref):
    read_blocks, pairs = flip_ref.shape[:2]
    for b in range(read_blocks):
        total = None
        for s in range(pairs):
            at = (b * pairs + s) * 2
            left = jnp.concatenate(
                [split(picked_ref[at : at + 1, :]), split(picked_ref[at + 1 : at + 2, :])], axis=1
            )
            part = dot(left, flip_ref[b, s])
            total = part if total is None else total + part
        row = jnp.sum(total, axis=0, keepdims=True)
        for i in range(out_ref.shape[0]):
            out_ref[i, b : b + 1, :] = row


def first_row_kernel(near, info_ref, *refs):
    pieces, (flip_ref, out_ref, picked_ref) = refs[:near], refs[near:]
    table = jnp.concatenate([piece[...] for piece in pieces], axis=0)
    hot = hot_rows(info_ref[1:2, :], table.shape[0])
    picked_ref[...] = select_rows(hot[: picked_ref.shape[0]], table)
    row_sums(picked_ref, flip_ref, out_ref)


def next_row_kernel(near, scale, *refs):
    parts, (flip_ref, out_ref, picked_ref) = refs[:near], refs[near:]
    total = parts[0][...]
    for part in parts[1:]:
        total = total + part[...]
    picked_ref[...] = total * scale
    row_sums(picked_ref, flip_ref, out_ref)


def column_sums(parts_ref, picked_ref, held_refs, contrib_ref, inverse_ref):
    slots, reads, cols = held_refs[0].shape[1:]
    total = parts_ref[0]
    for i in range(1, parts_ref.shape[0]):
        total = total + parts_ref[i]
    inverse_ref[...] = 1.0 / total
    for b in range(inverse_ref.shape[0]):
        held_ref = block_of(held_refs, b)
        left = split(inverse_ref[b : b + 1, :])
        for s in range(0, slots, 2):
            at = b * slots + s
            right = jnp.concatenate([held_ref[s], held_ref[s + 1]], axis=1)
            summed = jnp.sum(dot(left, right), axis=0, keepdims=True)
            contrib_ref[at : at + 1, :] = picked_ref[at : at + 1, :] * summed[:, :cols]
            contrib_ref[at + 1 : at + 2, :] = picked_ref[at + 1 : at + 2, :] * summed[:, cols:]


def column_kernel(info_ref, parts_ref, picked_ref, early_ref, late_ref, out_ref, inverse_ref):
    column_sums(parts_ref, picked_ref, (early_ref, late_ref), out_ref, inverse_ref)
    out_ref[picked_ref.shape[0] :, :] = info_ref[...]


def last_column_kernel(
    order, info_ref, parts_ref, picked_ref, early_ref, late_ref, out_ref, inverse_ref, contrib_ref
):
    column_sums(parts_ref, picked_ref, (early_ref, late_ref), contrib_ref, inverse_ref)
    owners, own_blocks, cols = out_ref.shape
    all_slots = contrib_ref.shape[0]
    block = lax.broadcasted_iota(jnp.int32, (owners * own_blocks, all_slots), 0)
    hot = (block.astype(jnp.float32) == info_ref[0:1, :all_slots]).astype(jnp.float32)
    counts = select_rows(hot, contrib_ref[...])
    for i, owner in enumerate(order):
        out_ref[i] = counts[owner * own_blocks : (owner + 1) * own_blocks, :]


def wanted_kernel(near, all_slots, pieces, *refs):
    given_refs, wanted, outs = refs[:pieces], refs[pieces : pieces + near], refs[pieces + near :]
    rows = all_slots + ID_ROWS
    half = LANES // 2
    lane = lax.broadcasted_iota(jnp.int32, (1, LANES), 1)
    ids, values = [], []
    for ref in given_refs:
        for at in range(0, ref.shape[0], rows):
            ids.append(ref[at + all_slots : at + all_slots + 1, :])
            values.append(ref[at : at + all_slots, :])
    pairs = [
        jnp.where(lane < half, a, pltpu.roll(b, half, 1)) for a, b in zip(ids[::2], ids[1::2])
    ]
    given = terms(jnp.concatenate(values, axis=0))
    for ids_ref, out_ref in zip(wanted, outs):
        column = down(ids_ref[0:1, :])[:all_slots]
        hot = jnp.concatenate([(column == pair).astype(jnp.float32) for pair in pairs], axis=1)
        hot = hot.astype(jnp.bfloat16)
        out_ref[...] = dot(hot, given[0]) + dot(hot, given[1]) + dot(hot, given[2])


def call(kernel, outs, scratch, *operands):
    return pl.pallas_call(
        kernel,
        out_shape=[jax.ShapeDtypeStruct(shape, jnp.float32) for shape in outs],
        in_specs=[VMEM] * len(operands),
        out_specs=[VMEM] * len(outs),
        scratch_shapes=[pltpu.VMEM(shape, jnp.float32) for shape in scratch],
        compiler_params=PARAMS,
    )(*operands)


PARAMS = pltpu.CompilerParams(vmem_limit_bytes=16 * 2**20)


def in_hbm(*arrays):
    return [pltpu.with_memory_space_constraint(x, pltpu.HBM) for x in arrays]


def prepare(own_blocks, early, likelihood, block_ids, slot_valid):
    read_blocks, slots = block_ids.shape
    return pl.pallas_call(
        lambda *refs: prepare_kernel(own_blocks, *refs),
        out_shape=[
            pltpu.VMEM((early,) + likelihood.shape[1:], likelihood.dtype),
            jax.ShapeDtypeStruct((ID_ROWS, LANES), jnp.float32),
        ],
        in_specs=[ANY] * 3,
        out_specs=[VMEM] * 2,
        scratch_shapes=[
            pltpu.VMEM((read_blocks, slots), jnp.int32),
            pltpu.VMEM((read_blocks, slots), jnp.int32),
            pltpu.VMEM((read_blocks, LANES), jnp.float32),
            pltpu.SemaphoreType.DMA((2,)),
            pltpu.SemaphoreType.DMA((early,)),
        ],
        compiler_params=PARAMS,
    )(*in_hbm(likelihood, block_ids, slot_valid))


def flip(after, held, likelihood):
    read_blocks, slots, reads, cols = likelihood.shape
    late = read_blocks - held.shape[0]
    return pl.pallas_call(
        flip_kernel,
        out_shape=[
            pltpu.VMEM((late,) + likelihood.shape[1:], likelihood.dtype),
            pltpu.VMEM((read_blocks, slots // 2, 2 * cols, reads), likelihood.dtype),
        ],
        in_specs=[ANY, VMEM, ANY],
        out_specs=[VMEM] * 2,
        scratch_shapes=[pltpu.SemaphoreType.DMA((late,))],
        compiler_params=PARAMS,
    )(after, held, *in_hbm(likelihood))


def local(likelihood, block_ids, slot_valid, start_weights):
    read_blocks, slots, reads, cols = likelihood.shape
    n = lax.axis_size(ALL)
    chips = lax.axis_size("genome")
    near = radices(n)[0]
    far = n // near
    own_weights = start_weights.reshape(-1, cols)
    own_blocks = own_weights.shape[0]
    all_slots = read_blocks * slots
    total_reads = read_blocks * lax.axis_size("reads") * reads
    scale = n * own_blocks * cols / total_reads

    column = gather_far(own_weights, ALL, CROSSED)
    held, info = prepare(own_blocks, read_blocks * 3 // 8, likelihood, block_ids, slot_valid)
    (sent,) = call(join_kernel, [(near_rows(far, own_blocks), cols)], [], *column, info)
    rest, flipped = flip(sent, held, likelihood)
    pieces = [sent] + [swap(sent, ALL, j) for j in range(1, near)]
    at = far * own_blocks
    wanted = [info] + [piece[at : at + ID_ROWS] for piece in pieces[1:]]

    row_shapes = [(chips, read_blocks, reads), (all_slots, cols)]
    inverse = (read_blocks, reads)
    for step in range(ITERS):
        if step == 0:
            row_parts, picked = call(
                lambda *refs: first_row_kernel(near, *refs), row_shapes, [], info, *pieces, flipped
            )
        else:
            row_parts, picked = call(
                lambda *refs: next_row_kernel(near, scale, *refs), row_shapes, [], *parts, flipped
            )
        row_parts = lax.all_to_all(
            row_parts,
            "genome",
            0,
            0,
            tiled=True,
            axis_index_groups=[middle_first(chips, chips // 2 + step)],
        )
        if step + 1 < ITERS:
            (contrib,) = call(
                column_kernel,
                [(all_slots + ID_ROWS, cols)],
                [inverse],
                info,
                row_parts,
                picked,
                held,
                rest,
            )
            given = gather_far(contrib, ALL, (1, 3))
            sums = call(
                lambda *refs: wanted_kernel(near, all_slots, len(given), *refs),
                [(all_slots, cols)] * near,
                [],
                *given,
                *wanted,
            )
            parts = [sums[0]] + [swap(sums[j], ALL, j) for j in list(range(2, near)) + [1]]
    order = middle_first(n, n // 2 + 3)
    (counts,) = call(
        lambda *refs: last_column_kernel(order, *refs),
        [(n, own_blocks, cols)],
        [inverse, (all_slots, cols)],
        info,
        row_parts,
        picked,
        held,
        rest,
    )
    counts = lax.all_to_all(counts, ALL, 0, 0, tiled=True, axis_index_groups=[order])
    return (jnp.sum(counts, axis=0) * scale).reshape(-1)


def solution(mesh):
    placed = (
        P(("parts", "reads"), "genome", None, None),
        P(("parts", "reads"), "genome"),
        P(("parts", "reads"), "genome"),
        P(("parts", "genome", "reads")),
    )
    return jax.shard_map(
        local,
        mesh=mesh,
        in_specs=placed,
        out_specs=P(("parts", "genome", "reads")),
        check_vma=False,
    )
```

```python
import jax
import jax.numpy as jnp
from jax import lax
from jax.experimental import pallas as pl
from jax.experimental.pallas import tpu as pltpu
from jax.sharding import PartitionSpec as P

ITERS = 2
ALL = ("genome", "reads")
TERMS = 16
ID_ROWS = 8
CROSSED = (1, 2, 3)
LANES = 128
VMEM = pl.BlockSpec(memory_space=pltpu.VMEM)
ANY = pl.BlockSpec(memory_space=pl.ANY)


def radices(n):
    out = []
    while n > 1:
        r = 4 if n % 4 == 0 else 2
        out.append(r)
        n //= r
    return out


def swap(x, axes, k):
    n = lax.axis_size(axes)
    return lax.ppermute(x, axes, [(i, i ^ k) for i in range(n)])


def middle_first(n, k):
    return [i ^ k for i in range(n)]


GRAY = (0, 1, 3, 2)


def position(k, n):
    place = 0
    for r in radices(n):
        n //= r
        digit = k % r
        place = place + (digit ^ (digit >> 1)) * n
        k = k // r
    return place


def gather_far(x, axes, crossed, order):
    parts = [x]
    stride = lax.axis_size(axes)
    for r in radices(stride)[:0:-1]:
        stride //= r
        sent = parts[0] if len(parts) == 1 else jnp.concatenate(parts, axis=0)
        parts = [sent] + [
            swap(sent, axes, j * stride + (j in crossed)) for j in order[1:] if j < r
        ]
    return parts


def dot(a, b, dims=(((1,), (0,)), ((), ()))):
    return lax.dot_general(a, b, dims, preferred_element_type=jnp.float32)


def terms(x):
    hi = x.astype(jnp.bfloat16)
    rest = x - hi.astype(jnp.float32)
    mid = rest.astype(jnp.bfloat16)
    return hi, mid, (rest - mid.astype(jnp.float32)).astype(jnp.bfloat16)


def select_rows(hot, x):
    hi, mid, low = terms(x)
    hot = hot.astype(jnp.bfloat16)
    return dot(hot, hi) + dot(hot, mid) + dot(hot, low)


def split(row):
    x = jnp.broadcast_to(row, (TERMS, row.shape[1]))
    hi = x.astype(jnp.bfloat16).astype(jnp.float32)
    rest = x - hi
    mid = rest.astype(jnp.bfloat16).astype(jnp.float32)
    low = rest - mid
    at = lax.broadcasted_iota(jnp.int32, x.shape, 0)
    out = jnp.where(at == 0, hi, jnp.where(at == 1, mid, jnp.where(at == 2, low, 0.0)))
    return out.astype(jnp.bfloat16)


def down(row):
    return jnp.transpose(jnp.broadcast_to(row, (LANES, LANES)))


def hot_rows(values, count):
    column = down(values)
    blocks = []
    for start in range(0, count, LANES):
        width = min(LANES, count - start)
        lane = lax.broadcasted_iota(jnp.int32, (LANES, width), 1).astype(jnp.float32) + start
        blocks.append((column[:, :width] == lane).astype(jnp.float32))
    return blocks[0] if len(blocks) == 1 else jnp.concatenate(blocks, axis=1)


def prepare_kernel(
    own_blocks,
    lik_ref,
    ids_ref,
    valid_ref,
    held_ref,
    info_ref,
    ids,
    valid,
    wide,
    sems,
    held_sems,
):
    read_blocks, slots = ids.shape
    copies = [
        pltpu.make_async_copy(ids_ref, ids, sems.at[0]),
        pltpu.make_async_copy(valid_ref, valid, sems.at[1]),
    ]
    held = block_copies(lik_ref, held_ref, held_sems, 0)
    for copy in copies + held:
        copy.start()
    for copy in copies:
        copy.wait()
    n = lax.axis_size(ALL)
    near = radices(n)[0]
    far = n // near
    me = lax.axis_index("genome") * lax.axis_size("reads") + lax.axis_index("reads")
    lane = lax.broadcasted_iota(jnp.int32, wide.shape, 1)
    wide[...] = jnp.zeros_like(wide)
    wide[:, :slots] = jnp.where(valid[...] > 0, ids[...], -1).astype(jnp.float32)
    flat = jnp.sum(
        pltpu.roll(wide[...], 0, 1, stride=slots, stride_axis=0), axis=0, keepdims=True
    )
    flat = jnp.where(lane[:1] < read_blocks * slots, flat, -1.0)
    owner = ((flat + 0.5) * (1.0 / own_blocks)).astype(jnp.int32)
    inside = flat.astype(jnp.int32) - owner * own_blocks
    away = owner ^ me
    rest = away // near
    for r in radices(n)[1:]:
        for j in CROSSED:
            away = away ^ jnp.where(rest % r == j, 1, 0)
        rest = rest // r
    place = position(away, n)
    place = (place // far) * near_rows(far, own_blocks) + (place % far) * own_blocks + inside
    place = jnp.where(flat < 0, -1, place).astype(jnp.float32)
    row = lax.broadcasted_iota(jnp.int32, info_ref.shape, 0)
    info_ref[...] = jnp.where(row == 0, flat, jnp.where(row == 1, place, 0.0))
    for copy in held:
        copy.wait()


def join_kernel(*refs):
    out_ref = refs[-1]
    at = 0
    for ref in refs[:-1]:
        out_ref[at : at + ref.shape[0], :] = ref[...]
        at += ref.shape[0]
    if at < out_ref.shape[0]:
        out_ref[at:, :] = jnp.zeros((out_ref.shape[0] - at, out_ref.shape[1]), jnp.float32)


def near_rows(far, own_blocks):
    return -(-(far * own_blocks + ID_ROWS) // 16) * 16


def flip_kernel(after_ref, early_ref, lik_ref, late_ref, out_ref, sems):
    early = early_ref.shape[0]
    copies = block_copies(lik_ref, late_ref, sems, early)
    for copy in copies:
        copy.start()
    for b in range(out_ref.shape[0]):
        if b >= early:
            copies[b - early].wait()
        held_ref = block_of((early_ref, late_ref), b)
        slots, reads, cols = held_ref.shape
        for s in range(slots):
            start = s % 2 * cols
            out_ref[b, s // 2, start : start + cols, :] = jnp.transpose(held_ref[s])


def block_copies(lik_ref, held_ref, sems, start):
    return [
        pltpu.make_async_copy(lik_ref.at[start + b], held_ref.at[b], sems.at[b])
        for b in range(held_ref.shape[0])
    ]


def block_of(held_refs, b):
    early_ref, late_ref = held_refs
    early = early_ref.shape[0]
    return early_ref.at[b] if b < early else late_ref.at[b - early]


def row_sums(picked_ref, flip_ref, out_ref):
    read_blocks, pairs = flip_ref.shape[:2]
    for b in range(read_blocks):
        total = None
        for s in range(pairs):
            at = (b * pairs + s) * 2
            left = jnp.concatenate(
                [split(picked_ref[at : at + 1, :]), split(picked_ref[at + 1 : at + 2, :])], axis=1
            )
            part = dot(left, flip_ref[b, s])
            total = part if total is None else total + part
        row = jnp.sum(total, axis=0, keepdims=True)
        for i in range(out_ref.shape[0]):
            out_ref[i, b : b + 1, :] = row


def first_row_kernel(near, info_ref, *refs):
    pieces, (flip_ref, out_ref, picked_ref) = refs[:near], refs[near:]
    table = jnp.concatenate([piece[...] for piece in pieces], axis=0)
    hot = hot_rows(info_ref[1:2, :], table.shape[0])
    picked_ref[...] = select_rows(hot[: picked_ref.shape[0]], table)
    row_sums(picked_ref, flip_ref, out_ref)


def next_row_kernel(near, scale, *refs):
    parts, (flip_ref, out_ref, picked_ref) = refs[:near], refs[near:]
    total = parts[0][...]
    for part in parts[1:]:
        total = total + part[...]
    picked_ref[...] = total * scale
    row_sums(picked_ref, flip_ref, out_ref)


def column_sums(parts_ref, picked_ref, held_refs, contrib_ref, inverse_ref):
    slots, reads, cols = held_refs[0].shape[1:]
    total = parts_ref[0]
    for i in range(1, parts_ref.shape[0]):
        total = total + parts_ref[i]
    inverse_ref[...] = 1.0 / total
    for b in range(inverse_ref.shape[0]):
        held_ref = block_of(held_refs, b)
        left = split(inverse_ref[b : b + 1, :])
        for s in range(0, slots, 2):
            at = b * slots + s
            right = jnp.concatenate([held_ref[s], held_ref[s + 1]], axis=1)
            summed = jnp.sum(dot(left, right), axis=0, keepdims=True)
            contrib_ref[at : at + 1, :] = picked_ref[at : at + 1, :] * summed[:, :cols]
            contrib_ref[at + 1 : at + 2, :] = picked_ref[at + 1 : at + 2, :] * summed[:, cols:]


def column_kernel(info_ref, parts_ref, picked_ref, early_ref, late_ref, out_ref, inverse_ref):
    column_sums(parts_ref, picked_ref, (early_ref, late_ref), out_ref, inverse_ref)
    out_ref[picked_ref.shape[0] :, :] = info_ref[...]


def last_column_kernel(
    order, info_ref, parts_ref, picked_ref, early_ref, late_ref, out_ref, inverse_ref, contrib_ref
):
    column_sums(parts_ref, picked_ref, (early_ref, late_ref), contrib_ref, inverse_ref)
    owners, own_blocks, cols = out_ref.shape
    all_slots = contrib_ref.shape[0]
    block = lax.broadcasted_iota(jnp.int32, (owners * own_blocks, all_slots), 0)
    hot = (block.astype(jnp.float32) == info_ref[0:1, :all_slots]).astype(jnp.float32)
    counts = select_rows(hot, contrib_ref[...])
    for i, owner in enumerate(order):
        out_ref[i] = counts[owner * own_blocks : (owner + 1) * own_blocks, :]


def wanted_kernel(near, all_slots, pieces, *refs):
    given_refs, wanted, outs = refs[:pieces], refs[pieces : pieces + near], refs[pieces + near :]
    rows = all_slots + ID_ROWS
    half = LANES // 2
    lane = lax.broadcasted_iota(jnp.int32, (1, LANES), 1)
    ids, values = [], []
    for ref in given_refs:
        for at in range(0, ref.shape[0], rows):
            ids.append(ref[at + all_slots : at + all_slots + 1, :])
            values.append(ref[at : at + all_slots, :])
    pairs = [
        jnp.where(lane < half, a, pltpu.roll(b, half, 1)) for a, b in zip(ids[::2], ids[1::2])
    ]
    given = terms(jnp.concatenate(values, axis=0))
    for ids_ref, out_ref in zip(wanted, outs):
        column = down(ids_ref[0:1, :])[:all_slots]
        hot = jnp.concatenate([(column == pair).astype(jnp.float32) for pair in pairs], axis=1)
        hot = hot.astype(jnp.bfloat16)
        out_ref[...] = dot(hot, given[0]) + dot(hot, given[1]) + dot(hot, given[2])


def call(kernel, outs, scratch, *operands):
    return pl.pallas_call(
        kernel,
        out_shape=[jax.ShapeDtypeStruct(shape, jnp.float32) for shape in outs],
        in_specs=[VMEM] * len(operands),
        out_specs=[VMEM] * len(outs),
        scratch_shapes=[pltpu.VMEM(shape, jnp.float32) for shape in scratch],
        compiler_params=PARAMS,
    )(*operands)


PARAMS = pltpu.CompilerParams(vmem_limit_bytes=16 * 2**20)


def in_hbm(*arrays):
    return [pltpu.with_memory_space_constraint(x, pltpu.HBM) for x in arrays]


def prepare(own_blocks, early, likelihood, block_ids, slot_valid):
    read_blocks, slots = block_ids.shape
    return pl.pallas_call(
        lambda *refs: prepare_kernel(own_blocks, *refs),
        out_shape=[
            pltpu.VMEM((early,) + likelihood.shape[1:], likelihood.dtype),
            jax.ShapeDtypeStruct((ID_ROWS, LANES), jnp.float32),
        ],
        in_specs=[ANY] * 3,
        out_specs=[VMEM] * 2,
        scratch_shapes=[
            pltpu.VMEM((read_blocks, slots), jnp.int32),
            pltpu.VMEM((read_blocks, slots), jnp.int32),
            pltpu.VMEM((read_blocks, LANES), jnp.float32),
            pltpu.SemaphoreType.DMA((2,)),
            pltpu.SemaphoreType.DMA((early,)),
        ],
        compiler_params=PARAMS,
    )(*in_hbm(likelihood, block_ids, slot_valid))


def flip(after, held, likelihood):
    read_blocks, slots, reads, cols = likelihood.shape
    late = read_blocks - held.shape[0]
    return pl.pallas_call(
        flip_kernel,
        out_shape=[
            pltpu.VMEM((late,) + likelihood.shape[1:], likelihood.dtype),
            pltpu.VMEM((read_blocks, slots // 2, 2 * cols, reads), likelihood.dtype),
        ],
        in_specs=[ANY, VMEM, ANY],
        out_specs=[VMEM] * 2,
        scratch_shapes=[pltpu.SemaphoreType.DMA((late,))],
        compiler_params=PARAMS,
    )(after, held, *in_hbm(likelihood))


def local(likelihood, block_ids, slot_valid, start_weights):
    read_blocks, slots, reads, cols = likelihood.shape
    n = lax.axis_size(ALL)
    chips = lax.axis_size("genome")
    near = radices(n)[0]
    far = n // near
    own_weights = start_weights.reshape(-1, cols)
    own_blocks = own_weights.shape[0]
    all_slots = read_blocks * slots
    total_reads = read_blocks * lax.axis_size("reads") * reads
    scale = n * own_blocks * cols / total_reads

    column = gather_far(own_weights, ALL, CROSSED, GRAY)
    held, info = prepare(own_blocks, read_blocks * 3 // 8, likelihood, block_ids, slot_valid)
    (sent,) = call(join_kernel, [(near_rows(far, own_blocks), cols)], [], *column, info)
    rest, flipped = flip(sent, held, likelihood)
    pieces = [sent] + [swap(sent, ALL, j) for j in GRAY[1:]]
    at = far * own_blocks
    wanted = [info] + [pieces[GRAY[j]][at : at + ID_ROWS] for j in range(1, near)]

    row_shapes = [(chips, read_blocks, reads), (all_slots, cols)]
    inverse = (read_blocks, reads)
    for step in range(ITERS):
        if step == 0:
            row_parts, picked = call(
                lambda *refs: first_row_kernel(near, *refs), row_shapes, [], info, *pieces, flipped
            )
        else:
            row_parts, picked = call(
                lambda *refs: next_row_kernel(near, scale, *refs), row_shapes, [], *parts, flipped
            )
        row_parts = lax.all_to_all(
            row_parts,
            "genome",
            0,
            0,
            tiled=True,
            axis_index_groups=[middle_first(chips, chips // 2 + step)],
        )
        if step + 1 < ITERS:
            (contrib,) = call(
                column_kernel,
                [(all_slots + ID_ROWS, cols)],
                [inverse],
                info,
                row_parts,
                picked,
                held,
                rest,
            )
            given = gather_far(contrib, ALL, (1, 3), range(4))
            sums = call(
                lambda *refs: wanted_kernel(near, all_slots, len(given), *refs),
                [(all_slots, cols)] * near,
                [],
                *given,
                *wanted,
            )
            parts = [sums[0]] + [swap(sums[j], ALL, j) for j in list(range(2, near)) + [1]]
    order = middle_first(n, n // 2 + 3)
    (counts,) = call(
        lambda *refs: last_column_kernel(order, *refs),
        [(n, own_blocks, cols)],
        [inverse, (all_slots, cols)],
        info,
        row_parts,
        picked,
        held,
        rest,
    )
    counts = lax.all_to_all(counts, ALL, 0, 0, tiled=True, axis_index_groups=[order])
    return (jnp.sum(counts, axis=0) * scale).reshape(-1)


def solution(mesh):
    placed = (
        P(("parts", "reads"), "genome", None, None),
        P(("parts", "reads"), "genome"),
        P(("parts", "reads"), "genome"),
        P(("parts", "genome", "reads")),
    )
    return jax.shard_map(
        local,
        mesh=mesh,
        in_specs=placed,
        out_specs=P(("parts", "genome", "reads")),
        check_vma=False,
    )
```

```python
import jax
import jax.numpy as jnp
from jax import lax
from jax.experimental import pallas as pl
from jax.experimental.pallas import tpu as pltpu
from jax.sharding import PartitionSpec as P

ITERS = 2
ALL = ("genome", "reads")
TERMS = 16
ID_ROWS = 8
CROSSED = (1, 2, 3)
LANES = 128
VMEM = pl.BlockSpec(memory_space=pltpu.VMEM)
ANY = pl.BlockSpec(memory_space=pl.ANY)


def radices(n):
    out = []
    while n > 1:
        r = 4 if n % 4 == 0 else 2
        out.append(r)
        n //= r
    return out


def swap(x, axes, k):
    n = lax.axis_size(axes)
    return lax.ppermute(x, axes, [(i, i ^ k) for i in range(n)])


def middle_first(n, k):
    return [i ^ k for i in range(n)]


GRAY = (0, 1, 3, 2)


def position(k, n):
    place = 0
    for r in radices(n):
        n //= r
        digit = k % r
        place = place + (digit ^ (digit >> 1)) * n
        k = k // r
    return place


def gather_far(x, axes, crossed, order):
    parts = [x]
    stride = lax.axis_size(axes)
    for r in radices(stride)[:0:-1]:
        stride //= r
        sent = parts[0] if len(parts) == 1 else jnp.concatenate(parts, axis=0)
        parts = [sent] + [
            swap(sent, axes, j * stride + (j in crossed)) for j in order[1:] if j < r
        ]
    return parts


def dot(a, b, dims=(((1,), (0,)), ((), ()))):
    return lax.dot_general(a, b, dims, preferred_element_type=jnp.float32)


def terms(x):
    hi = x.astype(jnp.bfloat16)
    rest = x - hi.astype(jnp.float32)
    mid = rest.astype(jnp.bfloat16)
    return hi, mid, (rest - mid.astype(jnp.float32)).astype(jnp.bfloat16)


def select_rows(hot, x):
    hi, mid, low = terms(x)
    hot = hot.astype(jnp.bfloat16)
    return dot(hot, hi) + dot(hot, mid) + dot(hot, low)


def split(row):
    x = jnp.broadcast_to(row, (TERMS, row.shape[1]))
    hi = x.astype(jnp.bfloat16).astype(jnp.float32)
    rest = x - hi
    mid = rest.astype(jnp.bfloat16).astype(jnp.float32)
    low = rest - mid
    at = lax.broadcasted_iota(jnp.int32, x.shape, 0)
    out = jnp.where(at == 0, hi, jnp.where(at == 1, mid, jnp.where(at == 2, low, 0.0)))
    return out.astype(jnp.bfloat16)


def down(row):
    return jnp.transpose(jnp.broadcast_to(row, (LANES, LANES)))


def hot_rows(values, count):
    column = down(values)
    blocks = []
    for start in range(0, count, LANES):
        width = min(LANES, count - start)
        lane = lax.broadcasted_iota(jnp.int32, (LANES, width), 1).astype(jnp.float32) + start
        blocks.append((column[:, :width] == lane).astype(jnp.float32))
    return blocks[0] if len(blocks) == 1 else jnp.concatenate(blocks, axis=1)


def prepare_kernel(
    own_blocks,
    lik_ref,
    ids_ref,
    valid_ref,
    held_ref,
    info_ref,
    ids,
    valid,
    wide,
    sems,
    held_sems,
):
    read_blocks, slots = ids.shape
    copies = [
        pltpu.make_async_copy(ids_ref, ids, sems.at[0]),
        pltpu.make_async_copy(valid_ref, valid, sems.at[1]),
    ]
    held = block_copies(lik_ref, held_ref, held_sems, 0)
    for copy in copies + held:
        copy.start()
    for copy in copies:
        copy.wait()
    n = lax.axis_size(ALL)
    near = radices(n)[0]
    far = n // near
    me = lax.axis_index("genome") * lax.axis_size("reads") + lax.axis_index("reads")
    lane = lax.broadcasted_iota(jnp.int32, wide.shape, 1)
    wide[...] = jnp.zeros_like(wide)
    wide[:, :slots] = jnp.where(valid[...] > 0, ids[...], -1).astype(jnp.float32)
    flat = jnp.sum(
        pltpu.roll(wide[...], 0, 1, stride=slots, stride_axis=0), axis=0, keepdims=True
    )
    flat = jnp.where(lane[:1] < read_blocks * slots, flat, -1.0)
    owner = ((flat + 0.5) * (1.0 / own_blocks)).astype(jnp.int32)
    inside = flat.astype(jnp.int32) - owner * own_blocks
    away = owner ^ me
    rest = away // near
    for r in radices(n)[1:]:
        for j in CROSSED:
            away = away ^ jnp.where(rest % r == j, 1, 0)
        rest = rest // r
    place = position(away, n)
    place = (place // far) * near_rows(far, own_blocks) + (place % far) * own_blocks + inside
    place = jnp.where(flat < 0, -1, place).astype(jnp.float32)
    row = lax.broadcasted_iota(jnp.int32, info_ref.shape, 0)
    info_ref[...] = jnp.where(row == 0, flat, jnp.where(row == 1, place, 0.0))
    for copy in held:
        copy.wait()


def join_kernel(*refs):
    out_ref = refs[-1]
    at = 0
    for ref in refs[:-1]:
        out_ref[at : at + ref.shape[0], :] = ref[...]
        at += ref.shape[0]
    if at < out_ref.shape[0]:
        out_ref[at:, :] = jnp.zeros((out_ref.shape[0] - at, out_ref.shape[1]), jnp.float32)


def near_rows(far, own_blocks):
    return -(-(far * own_blocks + ID_ROWS) // 16) * 16


def flip_kernel(after_ref, early_ref, lik_ref, late_ref, out_ref, sems):
    early = early_ref.shape[0]
    copies = block_copies(lik_ref, late_ref, sems, early)
    for copy in copies:
        copy.start()
    for b in range(out_ref.shape[0]):
        if b >= early:
            copies[b - early].wait()
        held_ref = block_of((early_ref, late_ref), b)
        slots, reads, cols = held_ref.shape
        for s in range(slots):
            start = s % 2 * cols
            out_ref[b, s // 2, start : start + cols, :] = jnp.transpose(held_ref[s])


def block_copies(lik_ref, held_ref, sems, start):
    return [
        pltpu.make_async_copy(lik_ref.at[start + b], held_ref.at[b], sems.at[b])
        for b in range(held_ref.shape[0])
    ]


def block_of(held_refs, b):
    early_ref, late_ref = held_refs
    early = early_ref.shape[0]
    return early_ref.at[b] if b < early else late_ref.at[b - early]


def row_sums(picked_ref, flip_ref, out_ref):
    read_blocks, pairs = flip_ref.shape[:2]
    for b in range(read_blocks):
        total = None
        for s in range(pairs):
            at = (b * pairs + s) * 2
            left = jnp.concatenate(
                [split(picked_ref[at : at + 1, :]), split(picked_ref[at + 1 : at + 2, :])], axis=1
            )
            part = dot(left, flip_ref[b, s])
            total = part if total is None else total + part
        row = jnp.sum(total, axis=0, keepdims=True)
        for i in range(out_ref.shape[0]):
            out_ref[i, b : b + 1, :] = row


def first_row_kernel(near, info_ref, *refs):
    pieces, (flip_ref, out_ref, picked_ref) = refs[:near], refs[near:]
    table = jnp.concatenate([piece[...] for piece in pieces], axis=0)
    hot = hot_rows(info_ref[1:2, :], table.shape[0])
    picked_ref[...] = select_rows(hot[: picked_ref.shape[0]], table)
    row_sums(picked_ref, flip_ref, out_ref)


def next_row_kernel(near, scale, *refs):
    parts, (flip_ref, out_ref, picked_ref) = refs[:near], refs[near:]
    total = parts[0][...]
    for part in parts[1:]:
        total = total + part[...]
    picked_ref[...] = total * scale
    row_sums(picked_ref, flip_ref, out_ref)


def column_sums(parts_ref, picked_ref, held_refs, contrib_ref, inverse_ref):
    slots, reads, cols = held_refs[0].shape[1:]
    total = parts_ref[0]
    for i in range(1, parts_ref.shape[0]):
        total = total + parts_ref[i]
    inverse_ref[...] = 1.0 / total
    for b in range(inverse_ref.shape[0]):
        held_ref = block_of(held_refs, b)
        left = split(inverse_ref[b : b + 1, :])
        for s in range(0, slots, 2):
            at = b * slots + s
            right = jnp.concatenate([held_ref[s], held_ref[s + 1]], axis=1)
            summed = jnp.sum(dot(left, right), axis=0, keepdims=True)
            contrib_ref[at : at + 1, :] = picked_ref[at : at + 1, :] * summed[:, :cols]
            contrib_ref[at + 1 : at + 2, :] = picked_ref[at + 1 : at + 2, :] * summed[:, cols:]


def column_kernel(info_ref, parts_ref, picked_ref, early_ref, late_ref, out_ref, inverse_ref):
    column_sums(parts_ref, picked_ref, (early_ref, late_ref), out_ref, inverse_ref)
    out_ref[picked_ref.shape[0] :, :] = info_ref[...]


def last_column_kernel(
    order, info_ref, parts_ref, picked_ref, early_ref, late_ref, out_ref, inverse_ref, contrib_ref
):
    column_sums(parts_ref, picked_ref, (early_ref, late_ref), contrib_ref, inverse_ref)
    owners, own_blocks, cols = out_ref.shape
    all_slots = contrib_ref.shape[0]
    block = lax.broadcasted_iota(jnp.int32, (owners * own_blocks, all_slots), 0)
    hot = (block.astype(jnp.float32) == info_ref[0:1, :all_slots]).astype(jnp.float32)
    counts = select_rows(hot, contrib_ref[...])
    for i, owner in enumerate(order):
        out_ref[i] = counts[owner * own_blocks : (owner + 1) * own_blocks, :]


def wanted_kernel(near, all_slots, pieces, *refs):
    given_refs, wanted, refs = refs[:pieces], refs[pieces : pieces + near], refs[pieces + near :]
    before, outs = refs[:-near], refs[-near:]
    rows = all_slots + ID_ROWS
    half = LANES // 2
    lane = lax.broadcasted_iota(jnp.int32, (1, LANES), 1)
    ids, values = [], []
    for ref in given_refs:
        for at in range(0, ref.shape[0], rows):
            ids.append(ref[at + all_slots : at + all_slots + 1, :])
            values.append(ref[at : at + all_slots, :])
    if len(ids) % 2:
        ids.append(jnp.full_like(ids[0], -2.0))
        values.append(jnp.zeros_like(values[0]))
    pairs = [
        jnp.where(lane < half, a, pltpu.roll(b, half, 1)) for a, b in zip(ids[::2], ids[1::2])
    ]
    columns = [down(ids_ref[0:1, :])[:all_slots] for ids_ref in wanted]
    column = jnp.concatenate(columns, axis=0)
    hot = jnp.concatenate([(column == pair).astype(jnp.float32) for pair in pairs], axis=1)
    sums = select_rows(hot, jnp.concatenate(values, axis=0))
    for j, out_ref in enumerate(outs):
        part = sums[j * all_slots : (j + 1) * all_slots]
        out_ref[...] = part + before[j][...] if before else part


def call(kernel, outs, scratch, *operands):
    return pl.pallas_call(
        kernel,
        out_shape=[jax.ShapeDtypeStruct(shape, jnp.float32) for shape in outs],
        in_specs=[VMEM] * len(operands),
        out_specs=[VMEM] * len(outs),
        scratch_shapes=[pltpu.VMEM(shape, jnp.float32) for shape in scratch],
        compiler_params=PARAMS,
    )(*operands)


PARAMS = pltpu.CompilerParams(vmem_limit_bytes=16 * 2**20)


def in_hbm(*arrays):
    return [pltpu.with_memory_space_constraint(x, pltpu.HBM) for x in arrays]


def prepare(own_blocks, early, likelihood, block_ids, slot_valid):
    read_blocks, slots = block_ids.shape
    return pl.pallas_call(
        lambda *refs: prepare_kernel(own_blocks, *refs),
        out_shape=[
            pltpu.VMEM((early,) + likelihood.shape[1:], likelihood.dtype),
            jax.ShapeDtypeStruct((ID_ROWS, LANES), jnp.float32),
        ],
        in_specs=[ANY] * 3,
        out_specs=[VMEM] * 2,
        scratch_shapes=[
            pltpu.VMEM((read_blocks, slots), jnp.int32),
            pltpu.VMEM((read_blocks, slots), jnp.int32),
            pltpu.VMEM((read_blocks, LANES), jnp.float32),
            pltpu.SemaphoreType.DMA((2,)),
            pltpu.SemaphoreType.DMA((early,)),
        ],
        compiler_params=PARAMS,
    )(*in_hbm(likelihood, block_ids, slot_valid))


def flip(after, held, likelihood):
    read_blocks, slots, reads, cols = likelihood.shape
    late = read_blocks - held.shape[0]
    return pl.pallas_call(
        flip_kernel,
        out_shape=[
            pltpu.VMEM((late,) + likelihood.shape[1:], likelihood.dtype),
            pltpu.VMEM((read_blocks, slots // 2, 2 * cols, reads), likelihood.dtype),
        ],
        in_specs=[ANY, VMEM, ANY],
        out_specs=[VMEM] * 2,
        scratch_shapes=[pltpu.SemaphoreType.DMA((late,))],
        compiler_params=PARAMS,
    )(after, held, *in_hbm(likelihood))


def local(likelihood, block_ids, slot_valid, start_weights):
    read_blocks, slots, reads, cols = likelihood.shape
    n = lax.axis_size(ALL)
    chips = lax.axis_size("genome")
    near = radices(n)[0]
    far = n // near
    own_weights = start_weights.reshape(-1, cols)
    own_blocks = own_weights.shape[0]
    all_slots = read_blocks * slots
    total_reads = read_blocks * lax.axis_size("reads") * reads
    scale = n * own_blocks * cols / total_reads

    column = gather_far(own_weights, ALL, CROSSED, GRAY)
    held, info = prepare(own_blocks, read_blocks * 3 // 8, likelihood, block_ids, slot_valid)
    (sent,) = call(join_kernel, [(near_rows(far, own_blocks), cols)], [], *column, info)
    rest, flipped = flip(sent, held, likelihood)
    pieces = [sent] + [swap(sent, ALL, j) for j in GRAY[1:]]
    at = far * own_blocks
    wanted = [info] + [pieces[GRAY[j]][at : at + ID_ROWS] for j in range(1, near)]

    row_shapes = [(chips, read_blocks, reads), (all_slots, cols)]
    inverse = (read_blocks, reads)
    for step in range(ITERS):
        if step == 0:
            row_parts, picked = call(
                lambda *refs: first_row_kernel(near, *refs), row_shapes, [], info, *pieces, flipped
            )
        else:
            row_parts, picked = call(
                lambda *refs: next_row_kernel(near, scale, *refs), row_shapes, [], *parts, flipped
            )
        row_parts = lax.all_to_all(
            row_parts,
            "genome",
            0,
            0,
            tiled=True,
            axis_index_groups=[middle_first(chips, chips // 2 + step)],
        )
        if step + 1 < ITERS:
            (contrib,) = call(
                column_kernel,
                [(all_slots + ID_ROWS, cols)],
                [inverse],
                info,
                row_parts,
                picked,
                held,
                rest,
            )
            first, last, *others = gather_far(contrib, ALL, (1, 3), range(4))
            sums = []
            for given in ([first] + others, [last]):
                sums = call(
                    lambda *refs: wanted_kernel(near, all_slots, len(given), *refs),
                    [(all_slots, cols)] * near,
                    [],
                    *given,
                    *wanted,
                    *sums,
                )
            parts = [sums[0]] + [swap(sums[j], ALL, j) for j in list(range(2, near)) + [1]]
    order = middle_first(n, n // 2 + 3)
    (counts,) = call(
        lambda *refs: last_column_kernel(order, *refs),
        [(n, own_blocks, cols)],
        [inverse, (all_slots, cols)],
        info,
        row_parts,
        picked,
        held,
        rest,
    )
    counts = lax.all_to_all(counts, ALL, 0, 0, tiled=True, axis_index_groups=[order])
    return (jnp.sum(counts, axis=0) * scale).reshape(-1)


def solution(mesh):
    placed = (
        P(("parts", "reads"), "genome", None, None),
        P(("parts", "reads"), "genome"),
        P(("parts", "reads"), "genome"),
        P(("parts", "genome", "reads")),
    )
    return jax.shard_map(
        local,
        mesh=mesh,
        in_specs=placed,
        out_specs=P(("parts", "genome", "reads")),
        check_vma=False,
    )
```

```python
import jax
import jax.numpy as jnp
from jax import lax
from jax.experimental import pallas as pl
from jax.experimental.pallas import tpu as pltpu
from jax.sharding import PartitionSpec as P

ITERS = 2
ALL = ("genome", "reads")
TERMS = 16
ID_ROWS = 8
CROSSED = (1, 2, 3)
LANES = 128
VMEM = pl.BlockSpec(memory_space=pltpu.VMEM)
ANY = pl.BlockSpec(memory_space=pl.ANY)


def radices(n):
    out = []
    while n > 1:
        r = 4 if n % 4 == 0 else 2
        out.append(r)
        n //= r
    return out


def swap(x, axes, k):
    n = lax.axis_size(axes)
    return lax.ppermute(x, axes, [(i, i ^ k) for i in range(n)])


def middle_first(n, k):
    return [i ^ k for i in range(n)]


GRAY = (0, 1, 3, 2)


def position(k, n):
    place = 0
    for r in radices(n):
        n //= r
        digit = k % r
        place = place + (digit ^ (digit >> 1)) * n
        k = k // r
    return place


def gather_far(x, axes, crossed, order):
    parts = [x]
    stride = lax.axis_size(axes)
    for r in radices(stride)[:0:-1]:
        stride //= r
        sent = parts[0] if len(parts) == 1 else jnp.concatenate(parts, axis=0)
        parts = [sent] + [
            swap(sent, axes, j * stride + (j in crossed)) for j in order[1:] if j < r
        ]
    return parts


def dot(a, b, dims=(((1,), (0,)), ((), ()))):
    return lax.dot_general(a, b, dims, preferred_element_type=jnp.float32)


def terms(x):
    hi = x.astype(jnp.bfloat16)
    rest = x - hi.astype(jnp.float32)
    mid = rest.astype(jnp.bfloat16)
    return hi, mid, (rest - mid.astype(jnp.float32)).astype(jnp.bfloat16)


def select_rows(hot, x):
    hi, mid, low = terms(x)
    hot = hot.astype(jnp.bfloat16)
    return dot(hot, hi) + dot(hot, mid) + dot(hot, low)


def split(row):
    x = jnp.broadcast_to(row, (TERMS, row.shape[1]))
    hi = x.astype(jnp.bfloat16).astype(jnp.float32)
    rest = x - hi
    mid = rest.astype(jnp.bfloat16).astype(jnp.float32)
    low = rest - mid
    at = lax.broadcasted_iota(jnp.int32, x.shape, 0)
    out = jnp.where(at == 0, hi, jnp.where(at == 1, mid, jnp.where(at == 2, low, 0.0)))
    return out.astype(jnp.bfloat16)


def down(row):
    return jnp.transpose(jnp.broadcast_to(row, (LANES, LANES)))


def hot_rows(values, count):
    column = down(values)
    blocks = []
    for start in range(0, count, LANES):
        width = min(LANES, count - start)
        lane = lax.broadcasted_iota(jnp.int32, (LANES, width), 1).astype(jnp.float32) + start
        blocks.append((column[:, :width] == lane).astype(jnp.float32))
    return blocks[0] if len(blocks) == 1 else jnp.concatenate(blocks, axis=1)


def prepare_kernel(
    own_blocks,
    lik_ref,
    ids_ref,
    valid_ref,
    held_ref,
    info_ref,
    ids,
    valid,
    wide,
    sems,
    held_sems,
):
    read_blocks, slots = ids.shape
    copies = [
        pltpu.make_async_copy(ids_ref, ids, sems.at[0]),
        pltpu.make_async_copy(valid_ref, valid, sems.at[1]),
    ]
    held = block_copies(lik_ref, held_ref, held_sems, 0)
    for copy in copies + held:
        copy.start()
    for copy in copies:
        copy.wait()
    n = lax.axis_size(ALL)
    near = radices(n)[0]
    far = n // near
    me = lax.axis_index("genome") * lax.axis_size("reads") + lax.axis_index("reads")
    lane = lax.broadcasted_iota(jnp.int32, wide.shape, 1)
    wide[...] = jnp.zeros_like(wide)
    wide[:, :slots] = jnp.where(valid[...] > 0, ids[...], -1).astype(jnp.float32)
    flat = jnp.sum(
        pltpu.roll(wide[...], 0, 1, stride=slots, stride_axis=0), axis=0, keepdims=True
    )
    flat = jnp.where(lane[:1] < read_blocks * slots, flat, -1.0)
    owner = ((flat + 0.5) * (1.0 / own_blocks)).astype(jnp.int32)
    inside = flat.astype(jnp.int32) - owner * own_blocks
    away = owner ^ me
    rest = away // near
    for r in radices(n)[1:]:
        for j in CROSSED:
            away = away ^ jnp.where(rest % r == j, 1, 0)
        rest = rest // r
    place = position(away, n)
    place = (place // far) * near_rows(far, own_blocks) + (place % far) * own_blocks + inside
    place = jnp.where(flat < 0, -1, place).astype(jnp.float32)
    row = lax.broadcasted_iota(jnp.int32, info_ref.shape, 0)
    info_ref[...] = jnp.where(row == 0, flat, jnp.where(row == 1, place, 0.0))
    for copy in held:
        copy.wait()


def join_kernel(*refs):
    out_ref = refs[-1]
    at = 0
    for ref in refs[:-1]:
        out_ref[at : at + ref.shape[0], :] = ref[...]
        at += ref.shape[0]
    if at < out_ref.shape[0]:
        out_ref[at:, :] = jnp.zeros((out_ref.shape[0] - at, out_ref.shape[1]), jnp.float32)


def near_rows(far, own_blocks):
    return -(-(far * own_blocks + ID_ROWS) // 16) * 16


def flip_kernel(after_ref, early_ref, lik_ref, late_ref, out_ref, sems):
    early = early_ref.shape[0]
    copies = block_copies(lik_ref, late_ref, sems, early)
    for copy in copies:
        copy.start()
    for b in range(out_ref.shape[0]):
        if b >= early:
            copies[b - early].wait()
        held_ref = block_of((early_ref, late_ref), b)
        slots, reads, cols = held_ref.shape
        for s in range(slots):
            start = s % 2 * cols
            out_ref[b, s // 2, start : start + cols, :] = jnp.transpose(held_ref[s])


def block_copies(lik_ref, held_ref, sems, start):
    return [
        pltpu.make_async_copy(lik_ref.at[start + b], held_ref.at[b], sems.at[b])
        for b in range(held_ref.shape[0])
    ]


def block_of(held_refs, b):
    early_ref, late_ref = held_refs
    early = early_ref.shape[0]
    return early_ref.at[b] if b < early else late_ref.at[b - early]


def row_sums(picked_ref, flip_ref, out_ref):
    read_blocks, pairs = flip_ref.shape[:2]
    for b in range(read_blocks):
        total = None
        for s in range(pairs):
            at = (b * pairs + s) * 2
            left = jnp.concatenate(
                [split(picked_ref[at : at + 1, :]), split(picked_ref[at + 1 : at + 2, :])], axis=1
            )
            part = dot(left, flip_ref[b, s])
            total = part if total is None else total + part
        row = jnp.sum(total, axis=0, keepdims=True)
        for i in range(out_ref.shape[0]):
            out_ref[i, b : b + 1, :] = row


def first_row_kernel(near, info_ref, *refs):
    pieces, (flip_ref, out_ref, picked_ref) = refs[:near], refs[near:]
    table = jnp.concatenate([piece[...] for piece in pieces], axis=0)
    hot = hot_rows(info_ref[1:2, :], table.shape[0])
    picked_ref[...] = select_rows(hot[: picked_ref.shape[0]], table)
    row_sums(picked_ref, flip_ref, out_ref)


def next_row_kernel(near, scale, *refs):
    parts, (flip_ref, out_ref, picked_ref) = refs[:near], refs[near:]
    total = parts[0][...]
    for part in parts[1:]:
        total = total + part[...]
    picked_ref[...] = total * scale
    row_sums(picked_ref, flip_ref, out_ref)


def column_sums(parts_ref, picked_ref, held_refs, contrib_ref, inverse_ref):
    slots, reads, cols = held_refs[0].shape[1:]
    total = parts_ref[0]
    for i in range(1, parts_ref.shape[0]):
        total = total + parts_ref[i]
    inverse_ref[...] = 1.0 / total
    for b in range(inverse_ref.shape[0]):
        held_ref = block_of(held_refs, b)
        left = split(inverse_ref[b : b + 1, :])
        for s in range(0, slots, 2):
            at = b * slots + s
            right = jnp.concatenate([held_ref[s], held_ref[s + 1]], axis=1)
            summed = jnp.sum(dot(left, right), axis=0, keepdims=True)
            contrib_ref[at : at + 1, :] = picked_ref[at : at + 1, :] * summed[:, :cols]
            contrib_ref[at + 1 : at + 2, :] = picked_ref[at + 1 : at + 2, :] * summed[:, cols:]


def column_kernel(info_ref, parts_ref, picked_ref, early_ref, late_ref, out_ref, inverse_ref):
    column_sums(parts_ref, picked_ref, (early_ref, late_ref), out_ref, inverse_ref)
    out_ref[picked_ref.shape[0] :, :] = info_ref[...]


def last_column_kernel(
    order, info_ref, parts_ref, picked_ref, early_ref, late_ref, out_ref, inverse_ref, contrib_ref
):
    column_sums(parts_ref, picked_ref, (early_ref, late_ref), contrib_ref, inverse_ref)
    owners, own_blocks, cols = out_ref.shape
    all_slots = contrib_ref.shape[0]
    block = lax.broadcasted_iota(jnp.int32, (owners * own_blocks, all_slots), 0)
    hot = (block.astype(jnp.float32) == info_ref[0:1, :all_slots]).astype(jnp.float32)
    counts = select_rows(hot, contrib_ref[...])
    for i, owner in enumerate(order):
        out_ref[i] = counts[owner * own_blocks : (owner + 1) * own_blocks, :]


def wanted_kernel(near, all_slots, pieces, *refs):
    given_refs, wanted, outs = refs[:pieces], refs[pieces : pieces + near], refs[pieces + near :]
    rows = all_slots + ID_ROWS
    half = LANES // 2
    lane = lax.broadcasted_iota(jnp.int32, (1, LANES), 1)
    ids, values = [], []
    for ref in given_refs:
        for at in range(0, ref.shape[0], rows):
            ids.append(ref[at + all_slots : at + all_slots + 1, :])
            values.append(ref[at : at + all_slots, :])
    pairs = [
        jnp.where(lane < half, a, pltpu.roll(b, half, 1)) for a, b in zip(ids[::2], ids[1::2])
    ]
    given = terms(jnp.concatenate(values, axis=0))
    for ids_ref, out_ref in zip(wanted, outs):
        column = down(ids_ref[0:1, :])[:all_slots]
        hot = jnp.concatenate([(column == pair).astype(jnp.float32) for pair in pairs], axis=1)
        hot = hot.astype(jnp.bfloat16)
        out_ref[...] = dot(hot, given[0]) + dot(hot, given[1]) + dot(hot, given[2])


def call(kernel, outs, scratch, *operands):
    return pl.pallas_call(
        kernel,
        out_shape=[jax.ShapeDtypeStruct(shape, jnp.float32) for shape in outs],
        in_specs=[VMEM] * len(operands),
        out_specs=[VMEM] * len(outs),
        scratch_shapes=[pltpu.VMEM(shape, jnp.float32) for shape in scratch],
        compiler_params=PARAMS,
    )(*operands)


PARAMS = pltpu.CompilerParams(vmem_limit_bytes=16 * 2**20)


def in_hbm(*arrays):
    return [pltpu.with_memory_space_constraint(x, pltpu.HBM) for x in arrays]


def prepare(own_blocks, early, likelihood, block_ids, slot_valid):
    read_blocks, slots = block_ids.shape
    return pl.pallas_call(
        lambda *refs: prepare_kernel(own_blocks, *refs),
        out_shape=[
            pltpu.VMEM((early,) + likelihood.shape[1:], likelihood.dtype),
            jax.ShapeDtypeStruct((ID_ROWS, LANES), jnp.float32),
        ],
        in_specs=[ANY] * 3,
        out_specs=[VMEM] * 2,
        scratch_shapes=[
            pltpu.VMEM((read_blocks, slots), jnp.int32),
            pltpu.VMEM((read_blocks, slots), jnp.int32),
            pltpu.VMEM((read_blocks, LANES), jnp.float32),
            pltpu.SemaphoreType.DMA((2,)),
            pltpu.SemaphoreType.DMA((early,)),
        ],
        compiler_params=PARAMS,
    )(*in_hbm(likelihood, block_ids, slot_valid))


def flip(after, held, likelihood):
    read_blocks, slots, reads, cols = likelihood.shape
    late = read_blocks - held.shape[0]
    return pl.pallas_call(
        flip_kernel,
        out_shape=[
            pltpu.VMEM((late,) + likelihood.shape[1:], likelihood.dtype),
            pltpu.VMEM((read_blocks, slots // 2, 2 * cols, reads), likelihood.dtype),
        ],
        in_specs=[ANY, VMEM, ANY],
        out_specs=[VMEM] * 2,
        scratch_shapes=[pltpu.SemaphoreType.DMA((late,))],
        compiler_params=PARAMS,
    )(after, held, *in_hbm(likelihood))


def local(likelihood, block_ids, slot_valid, start_weights):
    read_blocks, slots, reads, cols = likelihood.shape
    n = lax.axis_size(ALL)
    chips = lax.axis_size("genome")
    near = radices(n)[0]
    far = n // near
    own_weights = start_weights.reshape(-1, cols)
    own_blocks = own_weights.shape[0]
    all_slots = read_blocks * slots
    total_reads = read_blocks * lax.axis_size("reads") * reads
    scale = n * own_blocks * cols / total_reads

    column = gather_far(own_weights, ALL, CROSSED, GRAY)
    held, info = prepare(own_blocks, read_blocks * 3 // 8, likelihood, block_ids, slot_valid)
    (sent,) = call(join_kernel, [(near_rows(far, own_blocks), cols)], [], *column, info)
    rest, flipped = flip(sent, held, likelihood)
    pieces = [sent] + [swap(sent, ALL, j) for j in GRAY[1:]]
    at = far * own_blocks
    wanted = [info] + [pieces[GRAY[j]][at : at + ID_ROWS] for j in range(1, near)]

    row_shapes = [(chips, read_blocks, reads), (all_slots, cols)]
    inverse = (read_blocks, reads)
    for step in range(ITERS):
        if step == 0:
            row_parts, picked = call(
                lambda *refs: first_row_kernel(near, *refs), row_shapes, [], info, *pieces, flipped
            )
        else:
            row_parts, picked = call(
                lambda *refs: next_row_kernel(near, scale, *refs), row_shapes, [], *parts, flipped
            )
        row_parts = lax.all_to_all(
            row_parts,
            "genome",
            0,
            0,
            tiled=True,
            axis_index_groups=[middle_first(chips, chips // 2 + step)],
        )
        if step + 1 < ITERS:
            (contrib,) = call(
                column_kernel,
                [(all_slots + ID_ROWS, cols)],
                [inverse],
                info,
                row_parts,
                picked,
                held,
                rest,
            )
            given = gather_far(contrib, ALL, (1, 2), GRAY)
            sums = call(
                lambda *refs: wanted_kernel(near, all_slots, len(given), *refs),
                [(all_slots, cols)] * near,
                [],
                *given,
                *wanted,
            )
            parts = [sums[0]] + [swap(sums[j], ALL, j) for j in list(range(2, near)) + [1]]
    order = middle_first(n, n // 2 + 3)
    (counts,) = call(
        lambda *refs: last_column_kernel(order, *refs),
        [(n, own_blocks, cols)],
        [inverse, (all_slots, cols)],
        info,
        row_parts,
        picked,
        held,
        rest,
    )
    counts = lax.all_to_all(counts, ALL, 0, 0, tiled=True, axis_index_groups=[order])
    return (jnp.sum(counts, axis=0) * scale).reshape(-1)


def solution(mesh):
    placed = (
        P(("parts", "reads"), "genome", None, None),
        P(("parts", "reads"), "genome"),
        P(("parts", "reads"), "genome"),
        P(("parts", "genome", "reads")),
    )
    return jax.shard_map(
        local,
        mesh=mesh,
        in_specs=placed,
        out_specs=P(("parts", "genome", "reads")),
        check_vma=False,
    )
```

```python
import jax
import jax.numpy as jnp
from jax import lax
from jax.experimental import pallas as pl
from jax.experimental.pallas import tpu as pltpu
from jax.sharding import PartitionSpec as P

ITERS = 2
ALL = ("genome", "reads")
TERMS = 16
ID_ROWS = 8
CROSSED = (1, 2, 3)
LANES = 128
VMEM = pl.BlockSpec(memory_space=pltpu.VMEM)
ANY = pl.BlockSpec(memory_space=pl.ANY)


def radices(n):
    out = []
    while n > 1:
        r = 4 if n % 4 == 0 else 2
        out.append(r)
        n //= r
    return out


def swap(x, axes, k):
    n = lax.axis_size(axes)
    return lax.ppermute(x, axes, [(i, i ^ k) for i in range(n)])


def middle_first(n, k):
    return [i ^ k for i in range(n)]


GRAY = (0, 1, 3, 2)


def position(k, n):
    place = 0
    for r in radices(n):
        n //= r
        digit = k % r
        place = place + (digit ^ (digit >> 1)) * n
        k = k // r
    return place


def gather_far(x, axes, crossed, order):
    parts = [x]
    stride = lax.axis_size(axes)
    for r in radices(stride)[:0:-1]:
        stride //= r
        sent = parts[0] if len(parts) == 1 else jnp.concatenate(parts, axis=0)
        parts = [sent] + [
            swap(sent, axes, j * stride + (j in crossed)) for j in order[1:] if j < r
        ]
    return parts


def dot(a, b, dims=(((1,), (0,)), ((), ()))):
    return lax.dot_general(a, b, dims, preferred_element_type=jnp.float32)


def terms(x):
    hi = x.astype(jnp.bfloat16)
    rest = x - hi.astype(jnp.float32)
    mid = rest.astype(jnp.bfloat16)
    return hi, mid, (rest - mid.astype(jnp.float32)).astype(jnp.bfloat16)


def select_rows(hot, x):
    hi, mid, low = terms(x)
    hot = hot.astype(jnp.bfloat16)
    return dot(hot, hi) + dot(hot, mid) + dot(hot, low)


def split(row):
    x = jnp.broadcast_to(row, (TERMS, row.shape[1]))
    hi = x.astype(jnp.bfloat16).astype(jnp.float32)
    rest = x - hi
    mid = rest.astype(jnp.bfloat16).astype(jnp.float32)
    low = rest - mid
    at = lax.broadcasted_iota(jnp.int32, x.shape, 0)
    out = jnp.where(at == 0, hi, jnp.where(at == 1, mid, jnp.where(at == 2, low, 0.0)))
    return out.astype(jnp.bfloat16)


def down(row):
    return jnp.transpose(jnp.broadcast_to(row, (LANES, LANES)))


def hot_rows(values, count):
    column = down(values)
    blocks = []
    for start in range(0, count, LANES):
        width = min(LANES, count - start)
        lane = lax.broadcasted_iota(jnp.int32, (LANES, width), 1).astype(jnp.float32) + start
        blocks.append((column[:, :width] == lane).astype(jnp.float32))
    return blocks[0] if len(blocks) == 1 else jnp.concatenate(blocks, axis=1)


def prepare_kernel(
    own_blocks,
    lik_ref,
    ids_ref,
    valid_ref,
    held_ref,
    info_ref,
    ids,
    valid,
    wide,
    sems,
    held_sems,
):
    read_blocks, slots = ids.shape
    copies = [
        pltpu.make_async_copy(ids_ref, ids, sems.at[0]),
        pltpu.make_async_copy(valid_ref, valid, sems.at[1]),
    ]
    held = block_copies(lik_ref, held_ref, held_sems, 0)
    for copy in copies + held:
        copy.start()
    for copy in copies:
        copy.wait()
    n = lax.axis_size(ALL)
    near = radices(n)[0]
    far = n // near
    me = lax.axis_index("genome") * lax.axis_size("reads") + lax.axis_index("reads")
    lane = lax.broadcasted_iota(jnp.int32, wide.shape, 1)
    wide[...] = jnp.zeros_like(wide)
    wide[:, :slots] = jnp.where(valid[...] > 0, ids[...], -1).astype(jnp.float32)
    flat = jnp.sum(
        pltpu.roll(wide[...], 0, 1, stride=slots, stride_axis=0), axis=0, keepdims=True
    )
    flat = jnp.where(lane[:1] < read_blocks * slots, flat, -1.0)
    owner = ((flat + 0.5) * (1.0 / own_blocks)).astype(jnp.int32)
    inside = flat.astype(jnp.int32) - owner * own_blocks
    away = owner ^ me
    rest = away // near
    for r in radices(n)[1:]:
        for j in CROSSED:
            away = away ^ jnp.where(rest % r == j, 1, 0)
        rest = rest // r
    place = position(away, n)
    place = (place // far) * near_rows(far, own_blocks) + (place % far) * own_blocks + inside
    place = jnp.where(flat < 0, -1, place).astype(jnp.float32)
    row = lax.broadcasted_iota(jnp.int32, info_ref.shape, 0)
    info_ref[...] = jnp.where(row == 0, flat, jnp.where(row == 1, place, 0.0))
    for copy in held:
        copy.wait()


def join_kernel(*refs):
    out_ref = refs[-1]
    at = 0
    for ref in refs[:-1]:
        out_ref[at : at + ref.shape[0], :] = ref[...]
        at += ref.shape[0]
    if at < out_ref.shape[0]:
        out_ref[at:, :] = jnp.zeros((out_ref.shape[0] - at, out_ref.shape[1]), jnp.float32)


def near_rows(far, own_blocks):
    return -(-(far * own_blocks + ID_ROWS) // 16) * 16


def flip_kernel(after_ref, early_ref, lik_ref, late_ref, out_ref, sems):
    early = early_ref.shape[0]
    copies = block_copies(lik_ref, late_ref, sems, early)
    for copy in copies:
        copy.start()
    for b in range(out_ref.shape[0]):
        if b >= early:
            copies[b - early].wait()
        held_ref = block_of((early_ref, late_ref), b)
        slots, reads, cols = held_ref.shape
        for s in range(slots):
            start = s % 2 * cols
            out_ref[b, s // 2, start : start + cols, :] = jnp.transpose(held_ref[s])


def block_copies(lik_ref, held_ref, sems, start):
    return [
        pltpu.make_async_copy(lik_ref.at[start + b], held_ref.at[b], sems.at[b])
        for b in range(held_ref.shape[0])
    ]


def block_of(held_refs, b):
    early_ref, late_ref = held_refs
    early = early_ref.shape[0]
    return early_ref.at[b] if b < early else late_ref.at[b - early]


def row_sums(picked_ref, flip_ref, out_ref):
    read_blocks, pairs = flip_ref.shape[:2]
    for b in range(read_blocks):
        total = None
        for s in range(pairs):
            at = (b * pairs + s) * 2
            left = jnp.concatenate(
                [split(picked_ref[at : at + 1, :]), split(picked_ref[at + 1 : at + 2, :])], axis=1
            )
            part = dot(left, flip_ref[b, s])
            total = part if total is None else total + part
        row = jnp.sum(total, axis=0, keepdims=True)
        for i in range(out_ref.shape[0]):
            out_ref[i, b : b + 1, :] = row


def first_row_kernel(near, info_ref, *refs):
    pieces, (flip_ref, out_ref, picked_ref) = refs[:near], refs[near:]
    table = jnp.concatenate([piece[...] for piece in pieces], axis=0)
    hot = hot_rows(info_ref[1:2, :], table.shape[0])
    picked_ref[...] = select_rows(hot[: picked_ref.shape[0]], table)
    row_sums(picked_ref, flip_ref, out_ref)


def next_row_kernel(near, scale, *refs):
    parts, (flip_ref, out_ref, picked_ref) = refs[:near], refs[near:]
    total = parts[0][...]
    for part in parts[1:]:
        total = total + part[...]
    picked_ref[...] = total * scale
    row_sums(picked_ref, flip_ref, out_ref)


def column_sums(parts_ref, picked_ref, held_refs, contrib_ref, inverse_ref):
    slots, reads, cols = held_refs[0].shape[1:]
    total = parts_ref[0]
    for i in range(1, parts_ref.shape[0]):
        total = total + parts_ref[i]
    inverse_ref[...] = 1.0 / total
    for b in range(inverse_ref.shape[0]):
        held_ref = block_of(held_refs, b)
        left = split(inverse_ref[b : b + 1, :])
        for s in range(0, slots, 2):
            at = b * slots + s
            right = jnp.concatenate([held_ref[s], held_ref[s + 1]], axis=1)
            summed = jnp.sum(dot(left, right), axis=0, keepdims=True)
            contrib_ref[at : at + 1, :] = picked_ref[at : at + 1, :] * summed[:, :cols]
            contrib_ref[at + 1 : at + 2, :] = picked_ref[at + 1 : at + 2, :] * summed[:, cols:]


def column_kernel(info_ref, parts_ref, picked_ref, early_ref, late_ref, out_ref, inverse_ref):
    column_sums(parts_ref, picked_ref, (early_ref, late_ref), out_ref, inverse_ref)
    out_ref[picked_ref.shape[0] :, :] = info_ref[...]


def last_column_kernel(
    order, info_ref, parts_ref, picked_ref, early_ref, late_ref, out_ref, inverse_ref, contrib_ref
):
    column_sums(parts_ref, picked_ref, (early_ref, late_ref), contrib_ref, inverse_ref)
    owners, own_blocks, cols = out_ref.shape
    all_slots = contrib_ref.shape[0]
    block = lax.broadcasted_iota(jnp.int32, (owners * own_blocks, all_slots), 0)
    hot = (block.astype(jnp.float32) == info_ref[0:1, :all_slots]).astype(jnp.float32)
    counts = select_rows(hot, contrib_ref[...])
    for i, owner in enumerate(order):
        out_ref[i] = counts[owner * own_blocks : (owner + 1) * own_blocks, :]


def wanted_kernel(near, all_slots, pieces, *refs):
    given_refs, wanted, outs = refs[:pieces], refs[pieces : pieces + near], refs[pieces + near :]
    rows = all_slots + ID_ROWS
    half = LANES // 2
    lane = lax.broadcasted_iota(jnp.int32, (1, LANES), 1)
    ids, values = [], []
    for ref in given_refs:
        for at in range(0, ref.shape[0], rows):
            ids.append(ref[at + all_slots : at + all_slots + 1, :])
            values.append(ref[at : at + all_slots, :])
    pairs = [
        jnp.where(lane < half, a, pltpu.roll(b, half, 1)) for a, b in zip(ids[::2], ids[1::2])
    ]
    given = terms(jnp.concatenate(values, axis=0))
    for ids_ref, out_ref in zip(wanted, outs):
        column = down(ids_ref[0:1, :])[:all_slots]
        hot = jnp.concatenate([(column == pair).astype(jnp.float32) for pair in pairs], axis=1)
        hot = hot.astype(jnp.bfloat16)
        out_ref[...] = dot(hot, given[0]) + dot(hot, given[1]) + dot(hot, given[2])


def call(kernel, outs, scratch, *operands):
    return pl.pallas_call(
        kernel,
        out_shape=[jax.ShapeDtypeStruct(shape, jnp.float32) for shape in outs],
        in_specs=[VMEM] * len(operands),
        out_specs=[VMEM] * len(outs),
        scratch_shapes=[pltpu.VMEM(shape, jnp.float32) for shape in scratch],
        compiler_params=PARAMS,
    )(*operands)


PARAMS = pltpu.CompilerParams(vmem_limit_bytes=16 * 2**20)


def in_hbm(*arrays):
    return [pltpu.with_memory_space_constraint(x, pltpu.HBM) for x in arrays]


def prepare(own_blocks, early, likelihood, block_ids, slot_valid):
    read_blocks, slots = block_ids.shape
    return pl.pallas_call(
        lambda *refs: prepare_kernel(own_blocks, *refs),
        out_shape=[
            pltpu.VMEM((early,) + likelihood.shape[1:], likelihood.dtype),
            jax.ShapeDtypeStruct((ID_ROWS, LANES), jnp.float32),
        ],
        in_specs=[ANY] * 3,
        out_specs=[VMEM] * 2,
        scratch_shapes=[
            pltpu.VMEM((read_blocks, slots), jnp.int32),
            pltpu.VMEM((read_blocks, slots), jnp.int32),
            pltpu.VMEM((read_blocks, LANES), jnp.float32),
            pltpu.SemaphoreType.DMA((2,)),
            pltpu.SemaphoreType.DMA((early,)),
        ],
        compiler_params=PARAMS,
    )(*in_hbm(likelihood, block_ids, slot_valid))


def flip(after, held, likelihood):
    read_blocks, slots, reads, cols = likelihood.shape
    late = read_blocks - held.shape[0]
    return pl.pallas_call(
        flip_kernel,
        out_shape=[
            pltpu.VMEM((late,) + likelihood.shape[1:], likelihood.dtype),
            pltpu.VMEM((read_blocks, slots // 2, 2 * cols, reads), likelihood.dtype),
        ],
        in_specs=[ANY, VMEM, ANY],
        out_specs=[VMEM] * 2,
        scratch_shapes=[pltpu.SemaphoreType.DMA((late,))],
        compiler_params=PARAMS,
    )(after, held, *in_hbm(likelihood))


def local(likelihood, block_ids, slot_valid, start_weights):
    read_blocks, slots, reads, cols = likelihood.shape
    n = lax.axis_size(ALL)
    chips = lax.axis_size("genome")
    near = radices(n)[0]
    far = n // near
    own_weights = start_weights.reshape(-1, cols)
    own_blocks = own_weights.shape[0]
    all_slots = read_blocks * slots
    total_reads = read_blocks * lax.axis_size("reads") * reads
    scale = n * own_blocks * cols / total_reads

    column = gather_far(own_weights, ALL, CROSSED, GRAY)
    held, info = prepare(own_blocks, read_blocks // 2, likelihood, block_ids, slot_valid)
    (sent,) = call(join_kernel, [(near_rows(far, own_blocks), cols)], [], *column, info)
    rest, flipped = flip(sent, held, likelihood)
    pieces = [sent] + [swap(sent, ALL, j) for j in GRAY[1:]]
    at = far * own_blocks
    wanted = [info] + [pieces[GRAY[j]][at : at + ID_ROWS] for j in range(1, near)]

    row_shapes = [(chips, read_blocks, reads), (all_slots, cols)]
    inverse = (read_blocks, reads)
    for step in range(ITERS):
        if step == 0:
            row_parts, picked = call(
                lambda *refs: first_row_kernel(near, *refs), row_shapes, [], info, *pieces, flipped
            )
        else:
            row_parts, picked = call(
                lambda *refs: next_row_kernel(near, scale, *refs), row_shapes, [], *parts, flipped
            )
        row_parts = lax.all_to_all(
            row_parts,
            "genome",
            0,
            0,
            tiled=True,
            axis_index_groups=[middle_first(chips, chips // 2 + step)],
        )
        if step + 1 < ITERS:
            (contrib,) = call(
                column_kernel,
                [(all_slots + ID_ROWS, cols)],
                [inverse],
                info,
                row_parts,
                picked,
                held,
                rest,
            )
            given = gather_far(contrib, ALL, (1, 3), range(4))
            sums = call(
                lambda *refs: wanted_kernel(near, all_slots, len(given), *refs),
                [(all_slots, cols)] * near,
                [],
                *given,
                *wanted,
            )
            parts = [sums[0]] + [swap(sums[j], ALL, j) for j in list(range(2, near)) + [1]]
    order = middle_first(n, n // 2 + 3)
    (counts,) = call(
        lambda *refs: last_column_kernel(order, *refs),
        [(n, own_blocks, cols)],
        [inverse, (all_slots, cols)],
        info,
        row_parts,
        picked,
        held,
        rest,
    )
    counts = lax.all_to_all(counts, ALL, 0, 0, tiled=True, axis_index_groups=[order])
    return (jnp.sum(counts, axis=0) * scale).reshape(-1)


def solution(mesh):
    placed = (
        P(("parts", "reads"), "genome", None, None),
        P(("parts", "reads"), "genome"),
        P(("parts", "reads"), "genome"),
        P(("parts", "genome", "reads")),
    )
    return jax.shard_map(
        local,
        mesh=mesh,
        in_specs=placed,
        out_specs=P(("parts", "genome", "reads")),
        check_vma=False,
    )
```

```python
import jax
import jax.numpy as jnp
from jax import lax
from jax.experimental import pallas as pl
from jax.experimental.pallas import tpu as pltpu
from jax.sharding import PartitionSpec as P

ITERS = 2
ALL = ("genome", "reads")
TERMS = 16
ID_ROWS = 8
CROSSED = (1, 2, 3)
LANES = 128
VMEM = pl.BlockSpec(memory_space=pltpu.VMEM)
ANY = pl.BlockSpec(memory_space=pl.ANY)


def radices(n):
    out = []
    while n > 1:
        r = 4 if n % 4 == 0 else 2
        out.append(r)
        n //= r
    return out


def swap(x, axes, k):
    n = lax.axis_size(axes)
    return lax.ppermute(x, axes, [(i, i ^ k) for i in range(n)])


def middle_first(n, k):
    return [i ^ k for i in range(n)]


GRAY = (0, 1, 3, 2)


def position(k, n):
    place = 0
    for r in radices(n):
        n //= r
        digit = k % r
        place = place + (digit ^ (digit >> 1)) * n
        k = k // r
    return place


def gather_far(x, axes, crossed, order):
    parts = [x]
    stride = lax.axis_size(axes)
    for r in radices(stride)[:0:-1]:
        stride //= r
        sent = parts[0] if len(parts) == 1 else jnp.concatenate(parts, axis=0)
        parts = [sent] + [
            swap(sent, axes, j * stride + (j in crossed)) for j in order[1:] if j < r
        ]
    return parts


def dot(a, b, dims=(((1,), (0,)), ((), ()))):
    return lax.dot_general(a, b, dims, preferred_element_type=jnp.float32)


def terms(x):
    hi = x.astype(jnp.bfloat16)
    rest = x - hi.astype(jnp.float32)
    mid = rest.astype(jnp.bfloat16)
    return hi, mid, (rest - mid.astype(jnp.float32)).astype(jnp.bfloat16)


def select_rows(hot, x):
    hi, mid, low = terms(x)
    hot = hot.astype(jnp.bfloat16)
    return dot(hot, hi) + dot(hot, mid) + dot(hot, low)


def split(row):
    x = jnp.broadcast_to(row, (TERMS, row.shape[1]))
    hi = x.astype(jnp.bfloat16).astype(jnp.float32)
    rest = x - hi
    mid = rest.astype(jnp.bfloat16).astype(jnp.float32)
    low = rest - mid
    at = lax.broadcasted_iota(jnp.int32, x.shape, 0)
    out = jnp.where(at == 0, hi, jnp.where(at == 1, mid, jnp.where(at == 2, low, 0.0)))
    return out.astype(jnp.bfloat16)


def down(row):
    return jnp.transpose(jnp.broadcast_to(row, (LANES, LANES)))


def hot_rows(values, count):
    column = down(values)
    blocks = []
    for start in range(0, count, LANES):
        width = min(LANES, count - start)
        lane = lax.broadcasted_iota(jnp.int32, (LANES, width), 1).astype(jnp.float32) + start
        blocks.append((column[:, :width] == lane).astype(jnp.float32))
    return blocks[0] if len(blocks) == 1 else jnp.concatenate(blocks, axis=1)


def prepare_kernel(
    own_blocks,
    lik_ref,
    ids_ref,
    valid_ref,
    held_ref,
    info_ref,
    ids,
    valid,
    wide,
    sems,
    held_sems,
):
    read_blocks, slots = ids.shape
    copies = [
        pltpu.make_async_copy(ids_ref, ids, sems.at[0]),
        pltpu.make_async_copy(valid_ref, valid, sems.at[1]),
    ]
    held = block_copies(lik_ref, held_ref, held_sems, 0)
    for copy in copies + held:
        copy.start()
    for copy in copies:
        copy.wait()
    n = lax.axis_size(ALL)
    near = radices(n)[0]
    far = n // near
    me = lax.axis_index("genome") * lax.axis_size("reads") + lax.axis_index("reads")
    lane = lax.broadcasted_iota(jnp.int32, wide.shape, 1)
    wide[...] = jnp.zeros_like(wide)
    wide[:, :slots] = jnp.where(valid[...] > 0, ids[...], -1).astype(jnp.float32)
    flat = jnp.sum(
        pltpu.roll(wide[...], 0, 1, stride=slots, stride_axis=0), axis=0, keepdims=True
    )
    flat = jnp.where(lane[:1] < read_blocks * slots, flat, -1.0)
    owner = ((flat + 0.5) * (1.0 / own_blocks)).astype(jnp.int32)
    inside = flat.astype(jnp.int32) - owner * own_blocks
    away = owner ^ me
    rest = away // near
    for r in radices(n)[1:]:
        for j in CROSSED:
            away = away ^ jnp.where(rest % r == j, 1, 0)
        rest = rest // r
    place = position(away, n)
    place = (place // far) * near_rows(far, own_blocks) + (place % far) * own_blocks + inside
    place = jnp.where(flat < 0, -1, place).astype(jnp.float32)
    row = lax.broadcasted_iota(jnp.int32, info_ref.shape, 0)
    info_ref[...] = jnp.where(row == 0, flat, jnp.where(row == 1, place, 0.0))
    for copy in held:
        copy.wait()


def join_kernel(*refs):
    out_ref = refs[-1]
    at = 0
    for ref in refs[:-1]:
        out_ref[at : at + ref.shape[0], :] = ref[...]
        at += ref.shape[0]
    if at < out_ref.shape[0]:
        out_ref[at:, :] = jnp.zeros((out_ref.shape[0] - at, out_ref.shape[1]), jnp.float32)


def near_rows(far, own_blocks):
    return -(-(far * own_blocks + ID_ROWS) // 8) * 8


def flip_kernel(after_ref, early_ref, lik_ref, late_ref, out_ref, sems):
    early = early_ref.shape[0]
    copies = block_copies(lik_ref, late_ref, sems, early)
    for copy in copies:
        copy.start()
    for b in range(out_ref.shape[0]):
        if b >= early:
            copies[b - early].wait()
        held_ref = block_of((early_ref, late_ref), b)
        slots, reads, cols = held_ref.shape
        for s in range(slots):
            start = s % 2 * cols
            out_ref[b, s // 2, start : start + cols, :] = jnp.transpose(held_ref[s])


def block_copies(lik_ref, held_ref, sems, start):
    return [
        pltpu.make_async_copy(lik_ref.at[start + b], held_ref.at[b], sems.at[b])
        for b in range(held_ref.shape[0])
    ]


def block_of(held_refs, b):
    early_ref, late_ref = held_refs
    early = early_ref.shape[0]
    return early_ref.at[b] if b < early else late_ref.at[b - early]


def row_sums(picked_ref, flip_ref, out_ref):
    read_blocks, pairs = flip_ref.shape[:2]
    for b in range(read_blocks):
        total = None
        for s in range(pairs):
            at = (b * pairs + s) * 2
            left = jnp.concatenate(
                [split(picked_ref[at : at + 1, :]), split(picked_ref[at + 1 : at + 2, :])], axis=1
            )
            part = dot(left, flip_ref[b, s])
            total = part if total is None else total + part
        row = jnp.sum(total, axis=0, keepdims=True)
        for i in range(out_ref.shape[0]):
            out_ref[i, b : b + 1, :] = row


def first_row_kernel(near, info_ref, *refs):
    pieces, (flip_ref, out_ref, picked_ref) = refs[:near], refs[near:]
    table = jnp.concatenate([piece[...] for piece in pieces], axis=0)
    hot = hot_rows(info_ref[1:2, :], table.shape[0])
    picked_ref[...] = select_rows(hot[: picked_ref.shape[0]], table)
    row_sums(picked_ref, flip_ref, out_ref)


def next_row_kernel(near, scale, *refs):
    parts, (flip_ref, out_ref, picked_ref) = refs[:near], refs[near:]
    total = parts[0][...]
    for part in parts[1:]:
        total = total + part[...]
    picked_ref[...] = total * scale
    row_sums(picked_ref, flip_ref, out_ref)


def column_sums(parts_ref, picked_ref, held_refs, contrib_ref, inverse_ref):
    slots, reads, cols = held_refs[0].shape[1:]
    total = parts_ref[0]
    for i in range(1, parts_ref.shape[0]):
        total = total + parts_ref[i]
    inverse_ref[...] = 1.0 / total
    for b in range(inverse_ref.shape[0]):
        held_ref = block_of(held_refs, b)
        left = split(inverse_ref[b : b + 1, :])
        for s in range(0, slots, 2):
            at = b * slots + s
            right = jnp.concatenate([held_ref[s], held_ref[s + 1]], axis=1)
            summed = jnp.sum(dot(left, right), axis=0, keepdims=True)
            contrib_ref[at : at + 1, :] = picked_ref[at : at + 1, :] * summed[:, :cols]
            contrib_ref[at + 1 : at + 2, :] = picked_ref[at + 1 : at + 2, :] * summed[:, cols:]


def column_kernel(info_ref, parts_ref, picked_ref, early_ref, late_ref, out_ref, inverse_ref):
    column_sums(parts_ref, picked_ref, (early_ref, late_ref), out_ref, inverse_ref)
    out_ref[picked_ref.shape[0] :, :] = info_ref[...]


def last_column_kernel(
    order, info_ref, parts_ref, picked_ref, early_ref, late_ref, out_ref, inverse_ref, contrib_ref
):
    column_sums(parts_ref, picked_ref, (early_ref, late_ref), contrib_ref, inverse_ref)
    owners, own_blocks, cols = out_ref.shape
    all_slots = contrib_ref.shape[0]
    block = lax.broadcasted_iota(jnp.int32, (owners * own_blocks, all_slots), 0)
    hot = (block.astype(jnp.float32) == info_ref[0:1, :all_slots]).astype(jnp.float32)
    counts = select_rows(hot, contrib_ref[...])
    for i, owner in enumerate(order):
        out_ref[i] = counts[owner * own_blocks : (owner + 1) * own_blocks, :]


def wanted_kernel(near, all_slots, pieces, *refs):
    given_refs, wanted, outs = refs[:pieces], refs[pieces : pieces + near], refs[pieces + near :]
    rows = all_slots + ID_ROWS
    half = LANES // 2
    lane = lax.broadcasted_iota(jnp.int32, (1, LANES), 1)
    ids, values = [], []
    for ref in given_refs:
        for at in range(0, ref.shape[0], rows):
            ids.append(ref[at + all_slots : at + all_slots + 1, :])
            values.append(ref[at : at + all_slots, :])
    pairs = [
        jnp.where(lane < half, a, pltpu.roll(b, half, 1)) for a, b in zip(ids[::2], ids[1::2])
    ]
    given = terms(jnp.concatenate(values, axis=0))
    for ids_ref, out_ref in zip(wanted, outs):
        column = down(ids_ref[0:1, :])[:all_slots]
        hot = jnp.concatenate([(column == pair).astype(jnp.float32) for pair in pairs], axis=1)
        hot = hot.astype(jnp.bfloat16)
        out_ref[...] = dot(hot, given[0]) + dot(hot, given[1]) + dot(hot, given[2])


def call(kernel, outs, scratch, *operands):
    return pl.pallas_call(
        kernel,
        out_shape=[jax.ShapeDtypeStruct(shape, jnp.float32) for shape in outs],
        in_specs=[VMEM] * len(operands),
        out_specs=[VMEM] * len(outs),
        scratch_shapes=[pltpu.VMEM(shape, jnp.float32) for shape in scratch],
        compiler_params=PARAMS,
    )(*operands)


PARAMS = pltpu.CompilerParams(vmem_limit_bytes=16 * 2**20)


def in_hbm(*arrays):
    return [pltpu.with_memory_space_constraint(x, pltpu.HBM) for x in arrays]


def prepare(own_blocks, early, likelihood, block_ids, slot_valid):
    read_blocks, slots = block_ids.shape
    return pl.pallas_call(
        lambda *refs: prepare_kernel(own_blocks, *refs),
        out_shape=[
            pltpu.VMEM((early,) + likelihood.shape[1:], likelihood.dtype),
            jax.ShapeDtypeStruct((ID_ROWS, LANES), jnp.float32),
        ],
        in_specs=[ANY] * 3,
        out_specs=[VMEM] * 2,
        scratch_shapes=[
            pltpu.VMEM((read_blocks, slots), jnp.int32),
            pltpu.VMEM((read_blocks, slots), jnp.int32),
            pltpu.VMEM((read_blocks, LANES), jnp.float32),
            pltpu.SemaphoreType.DMA((2,)),
            pltpu.SemaphoreType.DMA((early,)),
        ],
        compiler_params=PARAMS,
    )(*in_hbm(likelihood, block_ids, slot_valid))


def flip(after, held, likelihood):
    read_blocks, slots, reads, cols = likelihood.shape
    late = read_blocks - held.shape[0]
    return pl.pallas_call(
        flip_kernel,
        out_shape=[
            pltpu.VMEM((late,) + likelihood.shape[1:], likelihood.dtype),
            pltpu.VMEM((read_blocks, slots // 2, 2 * cols, reads), likelihood.dtype),
        ],
        in_specs=[ANY, VMEM, ANY],
        out_specs=[VMEM] * 2,
        scratch_shapes=[pltpu.SemaphoreType.DMA((late,))],
        compiler_params=PARAMS,
    )(after, held, *in_hbm(likelihood))


def local(likelihood, block_ids, slot_valid, start_weights):
    read_blocks, slots, reads, cols = likelihood.shape
    n = lax.axis_size(ALL)
    chips = lax.axis_size("genome")
    near = radices(n)[0]
    far = n // near
    own_weights = start_weights.reshape(-1, cols)
    own_blocks = own_weights.shape[0]
    all_slots = read_blocks * slots
    total_reads = read_blocks * lax.axis_size("reads") * reads
    scale = n * own_blocks * cols / total_reads

    column = gather_far(own_weights, ALL, CROSSED, GRAY)
    held, info = prepare(own_blocks, read_blocks * 3 // 8, likelihood, block_ids, slot_valid)
    (sent,) = call(join_kernel, [(near_rows(far, own_blocks), cols)], [], *column, info)
    rest, flipped = flip(sent, held, likelihood)
    pieces = [sent] + [swap(sent, ALL, j) for j in GRAY[1:]]
    at = far * own_blocks
    wanted = [info] + [pieces[GRAY[j]][at : at + ID_ROWS] for j in range(1, near)]

    row_shapes = [(chips, read_blocks, reads), (all_slots, cols)]
    inverse = (read_blocks, reads)
    for step in range(ITERS):
        if step == 0:
            row_parts, picked = call(
                lambda *refs: first_row_kernel(near, *refs), row_shapes, [], info, *pieces, flipped
            )
        else:
            row_parts, picked = call(
                lambda *refs: next_row_kernel(near, scale, *refs), row_shapes, [], *parts, flipped
            )
        row_parts = lax.all_to_all(
            row_parts,
            "genome",
            0,
            0,
            tiled=True,
            axis_index_groups=[middle_first(chips, chips // 2 + step)],
        )
        if step + 1 < ITERS:
            (contrib,) = call(
                column_kernel,
                [(all_slots + ID_ROWS, cols)],
                [inverse],
                info,
                row_parts,
                picked,
                held,
                rest,
            )
            given = gather_far(contrib, ALL, (1, 3), range(4))
            sums = call(
                lambda *refs: wanted_kernel(near, all_slots, len(given), *refs),
                [(all_slots, cols)] * near,
                [],
                *given,
                *wanted,
            )
            parts = [sums[0]] + [swap(sums[j], ALL, j) for j in list(range(2, near)) + [1]]
    order = middle_first(n, n // 2 + 3)
    (counts,) = call(
        lambda *refs: last_column_kernel(order, *refs),
        [(n, own_blocks, cols)],
        [inverse, (all_slots, cols)],
        info,
        row_parts,
        picked,
        held,
        rest,
    )
    counts = lax.all_to_all(counts, ALL, 0, 0, tiled=True, axis_index_groups=[order])
    return (jnp.sum(counts, axis=0) * scale).reshape(-1)


def solution(mesh):
    placed = (
        P(("parts", "reads"), "genome", None, None),
        P(("parts", "reads"), "genome"),
        P(("parts", "reads"), "genome"),
        P(("parts", "genome", "reads")),
    )
    return jax.shard_map(
        local,
        mesh=mesh,
        in_specs=placed,
        out_specs=P(("parts", "genome", "reads")),
        check_vma=False,
    )
```

```python
import jax
import jax.numpy as jnp
from jax import lax
from jax.experimental import pallas as pl
from jax.experimental.pallas import tpu as pltpu
from jax.sharding import PartitionSpec as P

ITERS = 2
ALL = ("genome", "reads")
TERMS = 16
ID_ROWS = 8
CROSSED = (1, 2, 3)
LANES = 128
VMEM = pl.BlockSpec(memory_space=pltpu.VMEM)
ANY = pl.BlockSpec(memory_space=pl.ANY)


def radices(n):
    out = []
    while n > 1:
        r = 4 if n % 4 == 0 else 2
        out.append(r)
        n //= r
    return out


def swap(x, axes, k):
    n = lax.axis_size(axes)
    return lax.ppermute(x, axes, [(i, i ^ k) for i in range(n)])


def middle_first(n, k):
    return [i ^ k for i in range(n)]


GRAY = (0, 1, 3, 2)


def position(k, n):
    place = 0
    for r in radices(n):
        n //= r
        digit = k % r
        place = place + (digit ^ (digit >> 1)) * n
        k = k // r
    return place


def gather_far(x, axes, crossed, order):
    parts = [x]
    stride = lax.axis_size(axes)
    for r in radices(stride)[:0:-1]:
        stride //= r
        sent = parts[0] if len(parts) == 1 else jnp.concatenate(parts, axis=0)
        parts = [sent] + [
            swap(sent, axes, j * stride + (j in crossed)) for j in order[1:] if j < r
        ]
    return parts


def dot(a, b, dims=(((1,), (0,)), ((), ()))):
    return lax.dot_general(a, b, dims, preferred_element_type=jnp.float32)


def terms(x):
    hi = x.astype(jnp.bfloat16)
    return hi, (x - hi.astype(jnp.float32)).astype(jnp.bfloat16)


def select_rows(hot, x):
    hi, low = terms(x)
    hot = hot.astype(jnp.bfloat16)
    return dot(hot, hi) + dot(hot, low)


def split(row):
    x = jnp.broadcast_to(row, (TERMS, row.shape[1]))
    hi = x.astype(jnp.bfloat16).astype(jnp.float32)
    rest = x - hi
    mid = rest.astype(jnp.bfloat16).astype(jnp.float32)
    low = rest - mid
    at = lax.broadcasted_iota(jnp.int32, x.shape, 0)
    out = jnp.where(at == 0, hi, jnp.where(at == 1, mid, jnp.where(at == 2, low, 0.0)))
    return out.astype(jnp.bfloat16)


def down(row):
    return jnp.transpose(jnp.broadcast_to(row, (LANES, LANES)))


def hot_rows(values, count):
    column = down(values)
    blocks = []
    for start in range(0, count, LANES):
        width = min(LANES, count - start)
        lane = lax.broadcasted_iota(jnp.int32, (LANES, width), 1).astype(jnp.float32) + start
        blocks.append((column[:, :width] == lane).astype(jnp.float32))
    return blocks[0] if len(blocks) == 1 else jnp.concatenate(blocks, axis=1)


def prepare_kernel(
    own_blocks,
    lik_ref,
    ids_ref,
    valid_ref,
    held_ref,
    info_ref,
    ids,
    valid,
    wide,
    sems,
    held_sems,
):
    read_blocks, slots = ids.shape
    copies = [
        pltpu.make_async_copy(ids_ref, ids, sems.at[0]),
        pltpu.make_async_copy(valid_ref, valid, sems.at[1]),
    ]
    held = block_copies(lik_ref, held_ref, held_sems, 0)
    for copy in copies + held:
        copy.start()
    for copy in copies:
        copy.wait()
    n = lax.axis_size(ALL)
    near = radices(n)[0]
    far = n // near
    me = lax.axis_index("genome") * lax.axis_size("reads") + lax.axis_index("reads")
    lane = lax.broadcasted_iota(jnp.int32, wide.shape, 1)
    wide[...] = jnp.zeros_like(wide)
    wide[:, :slots] = jnp.where(valid[...] > 0, ids[...], -1).astype(jnp.float32)
    flat = jnp.sum(
        pltpu.roll(wide[...], 0, 1, stride=slots, stride_axis=0), axis=0, keepdims=True
    )
    flat = jnp.where(lane[:1] < read_blocks * slots, flat, -1.0)
    owner = ((flat + 0.5) * (1.0 / own_blocks)).astype(jnp.int32)
    inside = flat.astype(jnp.int32) - owner * own_blocks
    away = owner ^ me
    rest = away // near
    for r in radices(n)[1:]:
        for j in CROSSED:
            away = away ^ jnp.where(rest % r == j, 1, 0)
        rest = rest // r
    place = position(away, n)
    place = (place // far) * near_rows(far, own_blocks) + (place % far) * own_blocks + inside
    place = jnp.where(flat < 0, -1, place).astype(jnp.float32)
    row = lax.broadcasted_iota(jnp.int32, info_ref.shape, 0)
    info_ref[...] = jnp.where(row == 0, flat, jnp.where(row == 1, place, 0.0))
    for copy in held:
        copy.wait()


def join_kernel(*refs):
    out_ref = refs[-1]
    at = 0
    for ref in refs[:-1]:
        out_ref[at : at + ref.shape[0], :] = ref[...]
        at += ref.shape[0]
    if at < out_ref.shape[0]:
        out_ref[at:, :] = jnp.zeros((out_ref.shape[0] - at, out_ref.shape[1]), jnp.float32)


def near_rows(far, own_blocks):
    return -(-(far * own_blocks + ID_ROWS) // 8) * 8


def flip_kernel(after_ref, early_ref, lik_ref, late_ref, out_ref, sems):
    early = early_ref.shape[0]
    copies = block_copies(lik_ref, late_ref, sems, early)
    for copy in copies:
        copy.start()
    for b in range(out_ref.shape[0]):
        if b >= early:
            copies[b - early].wait()
        held_ref = block_of((early_ref, late_ref), b)
        slots, reads, cols = held_ref.shape
        for s in range(slots):
            start = s % 2 * cols
            out_ref[b, s // 2, start : start + cols, :] = jnp.transpose(held_ref[s])


def block_copies(lik_ref, held_ref, sems, start):
    return [
        pltpu.make_async_copy(lik_ref.at[start + b], held_ref.at[b], sems.at[b])
        for b in range(held_ref.shape[0])
    ]


def block_of(held_refs, b):
    early_ref, late_ref = held_refs
    early = early_ref.shape[0]
    return early_ref.at[b] if b < early else late_ref.at[b - early]


def row_sums(picked_ref, flip_ref, out_ref):
    read_blocks, pairs = flip_ref.shape[:2]
    for b in range(read_blocks):
        total = None
        for s in range(pairs):
            at = (b * pairs + s) * 2
            left = jnp.concatenate(
                [split(picked_ref[at : at + 1, :]), split(picked_ref[at + 1 : at + 2, :])], axis=1
            )
            part = dot(left, flip_ref[b, s])
            total = part if total is None else total + part
        row = jnp.sum(total, axis=0, keepdims=True)
        for i in range(out_ref.shape[0]):
            out_ref[i, b : b + 1, :] = row


def first_row_kernel(near, info_ref, *refs):
    pieces, (flip_ref, out_ref, picked_ref) = refs[:near], refs[near:]
    table = jnp.concatenate([piece[...] for piece in pieces], axis=0)
    hot = hot_rows(info_ref[1:2, :], table.shape[0])
    picked_ref[...] = select_rows(hot[: picked_ref.shape[0]], table)
    row_sums(picked_ref, flip_ref, out_ref)


def next_row_kernel(near, scale, *refs):
    parts, (flip_ref, out_ref, picked_ref) = refs[:near], refs[near:]
    total = parts[0][...]
    for part in parts[1:]:
        total = total + part[...]
    picked_ref[...] = total * scale
    row_sums(picked_ref, flip_ref, out_ref)


def column_sums(parts_ref, picked_ref, held_refs, contrib_ref, inverse_ref):
    slots, reads, cols = held_refs[0].shape[1:]
    total = parts_ref[0]
    for i in range(1, parts_ref.shape[0]):
        total = total + parts_ref[i]
    inverse_ref[...] = 1.0 / total
    for b in range(inverse_ref.shape[0]):
        held_ref = block_of(held_refs, b)
        left = split(inverse_ref[b : b + 1, :])
        for s in range(0, slots, 2):
            at = b * slots + s
            right = jnp.concatenate([held_ref[s], held_ref[s + 1]], axis=1)
            summed = jnp.sum(dot(left, right), axis=0, keepdims=True)
            contrib_ref[at : at + 1, :] = picked_ref[at : at + 1, :] * summed[:, :cols]
            contrib_ref[at + 1 : at + 2, :] = picked_ref[at + 1 : at + 2, :] * summed[:, cols:]


def column_kernel(info_ref, parts_ref, picked_ref, early_ref, late_ref, out_ref, inverse_ref):
    column_sums(parts_ref, picked_ref, (early_ref, late_ref), out_ref, inverse_ref)
    out_ref[picked_ref.shape[0] :, :] = info_ref[...]


def last_column_kernel(
    order, info_ref, parts_ref, picked_ref, early_ref, late_ref, out_ref, inverse_ref, contrib_ref
):
    column_sums(parts_ref, picked_ref, (early_ref, late_ref), contrib_ref, inverse_ref)
    owners, own_blocks, cols = out_ref.shape
    all_slots = contrib_ref.shape[0]
    block = lax.broadcasted_iota(jnp.int32, (owners * own_blocks, all_slots), 0)
    hot = (block.astype(jnp.float32) == info_ref[0:1, :all_slots]).astype(jnp.float32)
    counts = select_rows(hot, contrib_ref[...])
    for i, owner in enumerate(order):
        out_ref[i] = counts[owner * own_blocks : (owner + 1) * own_blocks, :]


def wanted_kernel(near, all_slots, pieces, *refs):
    given_refs, wanted, outs = refs[:pieces], refs[pieces : pieces + near], refs[pieces + near :]
    rows = all_slots + ID_ROWS
    half = LANES // 2
    lane = lax.broadcasted_iota(jnp.int32, (1, LANES), 1)
    ids, values = [], []
    for ref in given_refs:
        for at in range(0, ref.shape[0], rows):
            ids.append(ref[at + all_slots : at + all_slots + 1, :])
            values.append(ref[at : at + all_slots, :])
    pairs = [
        jnp.where(lane < half, a, pltpu.roll(b, half, 1)) for a, b in zip(ids[::2], ids[1::2])
    ]
    given = terms(jnp.concatenate(values, axis=0))
    for ids_ref, out_ref in zip(wanted, outs):
        column = down(ids_ref[0:1, :])[:all_slots]
        hot = jnp.concatenate([(column == pair).astype(jnp.float32) for pair in pairs], axis=1)
        hot = hot.astype(jnp.bfloat16)
        out_ref[...] = dot(hot, given[0]) + dot(hot, given[1])


def call(kernel, outs, scratch, *operands):
    return pl.pallas_call(
        kernel,
        out_shape=[jax.ShapeDtypeStruct(shape, jnp.float32) for shape in outs],
        in_specs=[VMEM] * len(operands),
        out_specs=[VMEM] * len(outs),
        scratch_shapes=[pltpu.VMEM(shape, jnp.float32) for shape in scratch],
        compiler_params=PARAMS,
    )(*operands)


PARAMS = pltpu.CompilerParams(vmem_limit_bytes=16 * 2**20)


def in_hbm(*arrays):
    return [pltpu.with_memory_space_constraint(x, pltpu.HBM) for x in arrays]


def prepare(own_blocks, early, likelihood, block_ids, slot_valid):
    read_blocks, slots = block_ids.shape
    return pl.pallas_call(
        lambda *refs: prepare_kernel(own_blocks, *refs),
        out_shape=[
            pltpu.VMEM((early,) + likelihood.shape[1:], likelihood.dtype),
            jax.ShapeDtypeStruct((ID_ROWS, LANES), jnp.float32),
        ],
        in_specs=[ANY] * 3,
        out_specs=[VMEM] * 2,
        scratch_shapes=[
            pltpu.VMEM((read_blocks, slots), jnp.int32),
            pltpu.VMEM((read_blocks, slots), jnp.int32),
            pltpu.VMEM((read_blocks, LANES), jnp.float32),
            pltpu.SemaphoreType.DMA((2,)),
            pltpu.SemaphoreType.DMA((early,)),
        ],
        compiler_params=PARAMS,
    )(*in_hbm(likelihood, block_ids, slot_valid))


def flip(after, held, likelihood):
    read_blocks, slots, reads, cols = likelihood.shape
    late = read_blocks - held.shape[0]
    return pl.pallas_call(
        flip_kernel,
        out_shape=[
            pltpu.VMEM((late,) + likelihood.shape[1:], likelihood.dtype),
            pltpu.VMEM((read_blocks, slots // 2, 2 * cols, reads), likelihood.dtype),
        ],
        in_specs=[ANY, VMEM, ANY],
        out_specs=[VMEM] * 2,
        scratch_shapes=[pltpu.SemaphoreType.DMA((late,))],
        compiler_params=PARAMS,
    )(after, held, *in_hbm(likelihood))


def local(likelihood, block_ids, slot_valid, start_weights):
    read_blocks, slots, reads, cols = likelihood.shape
    n = lax.axis_size(ALL)
    chips = lax.axis_size("genome")
    near = radices(n)[0]
    far = n // near
    own_weights = start_weights.reshape(-1, cols)
    own_blocks = own_weights.shape[0]
    all_slots = read_blocks * slots
    total_reads = read_blocks * lax.axis_size("reads") * reads
    scale = n * own_blocks * cols / total_reads

    column = gather_far(own_weights, ALL, CROSSED, GRAY)
    held, info = prepare(own_blocks, read_blocks * 3 // 8, likelihood, block_ids, slot_valid)
    (sent,) = call(join_kernel, [(near_rows(far, own_blocks), cols)], [], *column, info)
    rest, flipped = flip(sent, held, likelihood)
    pieces = [sent] + [swap(sent, ALL, j) for j in GRAY[1:]]
    at = far * own_blocks
    wanted = [info] + [pieces[GRAY[j]][at : at + ID_ROWS] for j in range(1, near)]

    row_shapes = [(chips, read_blocks, reads), (all_slots, cols)]
    inverse = (read_blocks, reads)
    for step in range(ITERS):
        if step == 0:
            row_parts, picked = call(
                lambda *refs: first_row_kernel(near, *refs), row_shapes, [], info, *pieces, flipped
            )
        else:
            row_parts, picked = call(
                lambda *refs: next_row_kernel(near, scale, *refs), row_shapes, [], *parts, flipped
            )
        row_parts = lax.all_to_all(
            row_parts,
            "genome",
            0,
            0,
            tiled=True,
            axis_index_groups=[middle_first(chips, chips // 2 + step)],
        )
        if step + 1 < ITERS:
            (contrib,) = call(
                column_kernel,
                [(all_slots + ID_ROWS, cols)],
                [inverse],
                info,
                row_parts,
                picked,
                held,
                rest,
            )
            given = gather_far(contrib, ALL, (1, 3), range(4))
            sums = call(
                lambda *refs: wanted_kernel(near, all_slots, len(given), *refs),
                [(all_slots, cols)] * near,
                [],
                *given,
                *wanted,
            )
            parts = [sums[0]] + [swap(sums[j], ALL, j) for j in list(range(2, near)) + [1]]
    order = middle_first(n, n // 2 + 3)
    (counts,) = call(
        lambda *refs: last_column_kernel(order, *refs),
        [(n, own_blocks, cols)],
        [inverse, (all_slots, cols)],
        info,
        row_parts,
        picked,
        held,
        rest,
    )
    counts = lax.all_to_all(counts, ALL, 0, 0, tiled=True, axis_index_groups=[order])
    return (jnp.sum(counts, axis=0) * scale).reshape(-1)


def solution(mesh):
    placed = (
        P(("parts", "reads"), "genome", None, None),
        P(("parts", "reads"), "genome"),
        P(("parts", "reads"), "genome"),
        P(("parts", "genome", "reads")),
    )
    return jax.shard_map(
        local,
        mesh=mesh,
        in_specs=placed,
        out_specs=P(("parts", "genome", "reads")),
        check_vma=False,
    )
```

```python
import jax
import jax.numpy as jnp
from jax import lax
from jax.experimental import pallas as pl
from jax.experimental.pallas import tpu as pltpu
from jax.sharding import PartitionSpec as P

ITERS = 2
ALL = ("genome", "reads")
TERMS = 16
ID_ROWS = 8
CROSSED = (1, 2, 3)
LANES = 128
VMEM = pl.BlockSpec(memory_space=pltpu.VMEM)
ANY = pl.BlockSpec(memory_space=pl.ANY)


def radices(n):
    out = []
    while n > 1:
        r = 4 if n % 4 == 0 else 2
        out.append(r)
        n //= r
    return out


def swap(x, axes, k):
    n = lax.axis_size(axes)
    return lax.ppermute(x, axes, [(i, i ^ k) for i in range(n)])


def middle_first(n, k):
    return [i ^ k for i in range(n)]


GRAY = (0, 1, 3, 2)


def position(k, n):
    place = 0
    for r in radices(n):
        n //= r
        digit = k % r
        place = place + (digit ^ (digit >> 1)) * n
        k = k // r
    return place


def gather_far(x, axes, crossed, order):
    parts = [x]
    stride = lax.axis_size(axes)
    for r in radices(stride)[:0:-1]:
        stride //= r
        sent = parts[0] if len(parts) == 1 else jnp.concatenate(parts, axis=0)
        parts = [sent] + [
            swap(sent, axes, j * stride + (j in crossed)) for j in order[1:] if j < r
        ]
    return parts


def dot(a, b, dims=(((1,), (0,)), ((), ()))):
    return lax.dot_general(a, b, dims, preferred_element_type=jnp.float32)


def terms(x):
    hi = x.astype(jnp.bfloat16)
    return hi, (x - hi.astype(jnp.float32)).astype(jnp.bfloat16)


def select_rows(hot, x):
    hi, low = terms(x)
    hot = hot.astype(jnp.bfloat16)
    return dot(hot, hi) + dot(hot, low)


def split(row):
    x = jnp.broadcast_to(row, (TERMS, row.shape[1]))
    hi = x.astype(jnp.bfloat16).astype(jnp.float32)
    rest = x - hi
    mid = rest.astype(jnp.bfloat16).astype(jnp.float32)
    low = rest - mid
    at = lax.broadcasted_iota(jnp.int32, x.shape, 0)
    out = jnp.where(at == 0, hi, jnp.where(at == 1, mid, jnp.where(at == 2, low, 0.0)))
    return out.astype(jnp.bfloat16)


def down(row):
    return jnp.transpose(jnp.broadcast_to(row, (LANES, LANES)))


def hot_rows(values, count):
    column = down(values)
    blocks = []
    for start in range(0, count, LANES):
        width = min(LANES, count - start)
        lane = lax.broadcasted_iota(jnp.int32, (LANES, width), 1).astype(jnp.float32) + start
        blocks.append((column[:, :width] == lane).astype(jnp.float32))
    return blocks[0] if len(blocks) == 1 else jnp.concatenate(blocks, axis=1)


def prepare_kernel(
    own_blocks,
    lik_ref,
    ids_ref,
    valid_ref,
    held_ref,
    info_ref,
    ids,
    valid,
    wide,
    sems,
    held_sems,
):
    read_blocks, slots = ids.shape
    copies = [
        pltpu.make_async_copy(ids_ref, ids, sems.at[0]),
        pltpu.make_async_copy(valid_ref, valid, sems.at[1]),
    ]
    held = block_copies(lik_ref, held_ref, held_sems, 0)
    for copy in copies + held:
        copy.start()
    for copy in copies:
        copy.wait()
    n = lax.axis_size(ALL)
    near = radices(n)[0]
    far = n // near
    me = lax.axis_index("genome") * lax.axis_size("reads") + lax.axis_index("reads")
    lane = lax.broadcasted_iota(jnp.int32, wide.shape, 1)
    wide[...] = jnp.zeros_like(wide)
    wide[:, :slots] = jnp.where(valid[...] > 0, ids[...], -1).astype(jnp.float32)
    flat = jnp.sum(
        pltpu.roll(wide[...], 0, 1, stride=slots, stride_axis=0), axis=0, keepdims=True
    )
    flat = jnp.where(lane[:1] < read_blocks * slots, flat, -1.0)
    owner = ((flat + 0.5) * (1.0 / own_blocks)).astype(jnp.int32)
    inside = flat.astype(jnp.int32) - owner * own_blocks
    away = owner ^ me
    rest = away // near
    for r in radices(n)[1:]:
        for j in CROSSED:
            away = away ^ jnp.where(rest % r == j, 1, 0)
        rest = rest // r
    place = position(away, n)
    place = (place // far) * near_rows(far, own_blocks) + (place % far) * own_blocks + inside
    place = jnp.where(flat < 0, -1, place).astype(jnp.float32)
    row = lax.broadcasted_iota(jnp.int32, info_ref.shape, 0)
    info_ref[...] = jnp.where(row == 0, flat, jnp.where(row == 1, place, 0.0))
    for copy in held:
        copy.wait()


def join_kernel(*refs):
    out_ref = refs[-1]
    at = 0
    for ref in refs[:-1]:
        out_ref[at : at + ref.shape[0], :] = ref[...]
        at += ref.shape[0]
    if at < out_ref.shape[0]:
        out_ref[at:, :] = jnp.zeros((out_ref.shape[0] - at, out_ref.shape[1]), jnp.float32)


def near_rows(far, own_blocks):
    return -(-(far * own_blocks + ID_ROWS) // 8) * 8


def flip_kernel(after_ref, early_ref, lik_ref, late_ref, out_ref, sems):
    early = early_ref.shape[0]
    copies = block_copies(lik_ref, late_ref, sems, early)
    for copy in copies:
        copy.start()
    for b in range(out_ref.shape[0]):
        if b >= early:
            copies[b - early].wait()
        held_ref = block_of((early_ref, late_ref), b)
        slots, reads, cols = held_ref.shape
        for s in range(slots):
            start = s % 2 * cols
            out_ref[b, s // 2, start : start + cols, :] = jnp.transpose(held_ref[s])


def block_copies(lik_ref, held_ref, sems, start):
    return [
        pltpu.make_async_copy(lik_ref.at[start + b], held_ref.at[b], sems.at[b])
        for b in range(held_ref.shape[0])
    ]


def block_of(held_refs, b):
    early_ref, late_ref = held_refs
    early = early_ref.shape[0]
    return early_ref.at[b] if b < early else late_ref.at[b - early]


def row_sums(picked_ref, flip_ref, out_ref):
    read_blocks, pairs = flip_ref.shape[:2]
    for b in range(read_blocks):
        total = None
        for s in range(pairs):
            at = (b * pairs + s) * 2
            left = jnp.concatenate(
                [split(picked_ref[at : at + 1, :]), split(picked_ref[at + 1 : at + 2, :])], axis=1
            )
            part = dot(left, flip_ref[b, s])
            total = part if total is None else total + part
        row = jnp.sum(total, axis=0, keepdims=True)
        for i in range(out_ref.shape[0]):
            out_ref[i, b : b + 1, :] = row


def first_row_kernel(near, info_ref, *refs):
    pieces, (flip_ref, out_ref, picked_ref) = refs[:near], refs[near:]
    table = jnp.concatenate([piece[...] for piece in pieces], axis=0)
    hot = hot_rows(info_ref[1:2, :], table.shape[0])
    picked_ref[...] = select_rows(hot[: picked_ref.shape[0]], table)
    row_sums(picked_ref, flip_ref, out_ref)


def next_row_kernel(near, scale, *refs):
    parts, (flip_ref, out_ref, picked_ref) = refs[:near], refs[near:]
    total = parts[0][...]
    for part in parts[1:]:
        total = total + part[...]
    picked_ref[...] = total * scale
    row_sums(picked_ref, flip_ref, out_ref)


def column_sums(parts_ref, picked_ref, held_refs, contrib_ref, inverse_ref):
    slots, reads, cols = held_refs[0].shape[1:]
    total = parts_ref[0]
    for i in range(1, parts_ref.shape[0]):
        total = total + parts_ref[i]
    inverse_ref[...] = 1.0 / total
    for b in range(inverse_ref.shape[0]):
        held_ref = block_of(held_refs, b)
        left = split(inverse_ref[b : b + 1, :])
        for s in range(0, slots, 2):
            at = b * slots + s
            right = jnp.concatenate([held_ref[s], held_ref[s + 1]], axis=1)
            summed = jnp.sum(dot(left, right), axis=0, keepdims=True)
            contrib_ref[at : at + 1, :] = picked_ref[at : at + 1, :] * summed[:, :cols]
            contrib_ref[at + 1 : at + 2, :] = picked_ref[at + 1 : at + 2, :] * summed[:, cols:]


def column_kernel(info_ref, parts_ref, picked_ref, early_ref, late_ref, out_ref, inverse_ref):
    column_sums(parts_ref, picked_ref, (early_ref, late_ref), out_ref, inverse_ref)
    out_ref[picked_ref.shape[0] :, :] = info_ref[...]


def last_column_kernel(
    order, info_ref, parts_ref, picked_ref, early_ref, late_ref, out_ref, inverse_ref, contrib_ref
):
    column_sums(parts_ref, picked_ref, (early_ref, late_ref), contrib_ref, inverse_ref)
    owners, own_blocks, cols = out_ref.shape
    all_slots = contrib_ref.shape[0]
    block = lax.broadcasted_iota(jnp.int32, (owners * own_blocks, all_slots), 0)
    hot = (block.astype(jnp.float32) == info_ref[0:1, :all_slots]).astype(jnp.float32)
    counts = select_rows(hot, contrib_ref[...])
    for i, owner in enumerate(order):
        out_ref[i] = counts[owner * own_blocks : (owner + 1) * own_blocks, :]


def wanted_kernel(near, all_slots, pieces, *refs):
    given_refs, wanted, outs = refs[:pieces], refs[pieces : pieces + near], refs[pieces + near :]
    rows = all_slots + ID_ROWS
    half = LANES // 2
    lane = lax.broadcasted_iota(jnp.int32, (1, LANES), 1)
    ids, values = [], []
    for ref in given_refs:
        for at in range(0, ref.shape[0], rows):
            ids.append(ref[at + all_slots : at + all_slots + 1, :])
            values.append(ref[at : at + all_slots, :])
    pairs = [
        jnp.where(lane < half, a, pltpu.roll(b, half, 1)) for a, b in zip(ids[::2], ids[1::2])
    ]
    given = terms(jnp.concatenate(values, axis=0))
    column = jnp.concatenate([down(ids_ref[0:1, :])[:all_slots] for ids_ref in wanted], axis=0)
    hot = jnp.concatenate([(column == pair).astype(jnp.float32) for pair in pairs], axis=1)
    hot = hot.astype(jnp.bfloat16)
    sums = dot(hot, given[0]) + dot(hot, given[1])
    for j, out_ref in enumerate(outs):
        out_ref[...] = sums[j * all_slots : (j + 1) * all_slots]


def call(kernel, outs, scratch, *operands):
    return pl.pallas_call(
        kernel,
        out_shape=[jax.ShapeDtypeStruct(shape, jnp.float32) for shape in outs],
        in_specs=[VMEM] * len(operands),
        out_specs=[VMEM] * len(outs),
        scratch_shapes=[pltpu.VMEM(shape, jnp.float32) for shape in scratch],
        compiler_params=PARAMS,
    )(*operands)


PARAMS = pltpu.CompilerParams(vmem_limit_bytes=16 * 2**20)


def in_hbm(*arrays):
    return [pltpu.with_memory_space_constraint(x, pltpu.HBM) for x in arrays]


def prepare(own_blocks, early, likelihood, block_ids, slot_valid):
    read_blocks, slots = block_ids.shape
    return pl.pallas_call(
        lambda *refs: prepare_kernel(own_blocks, *refs),
        out_shape=[
            pltpu.VMEM((early,) + likelihood.shape[1:], likelihood.dtype),
            jax.ShapeDtypeStruct((ID_ROWS, LANES), jnp.float32),
        ],
        in_specs=[ANY] * 3,
        out_specs=[VMEM] * 2,
        scratch_shapes=[
            pltpu.VMEM((read_blocks, slots), jnp.int32),
            pltpu.VMEM((read_blocks, slots), jnp.int32),
            pltpu.VMEM((read_blocks, LANES), jnp.float32),
            pltpu.SemaphoreType.DMA((2,)),
            pltpu.SemaphoreType.DMA((early,)),
        ],
        compiler_params=PARAMS,
    )(*in_hbm(likelihood, block_ids, slot_valid))


def flip(after, held, likelihood):
    read_blocks, slots, reads, cols = likelihood.shape
    late = read_blocks - held.shape[0]
    return pl.pallas_call(
        flip_kernel,
        out_shape=[
            pltpu.VMEM((late,) + likelihood.shape[1:], likelihood.dtype),
            pltpu.VMEM((read_blocks, slots // 2, 2 * cols, reads), likelihood.dtype),
        ],
        in_specs=[ANY, VMEM, ANY],
        out_specs=[VMEM] * 2,
        scratch_shapes=[pltpu.SemaphoreType.DMA((late,))],
        compiler_params=PARAMS,
    )(after, held, *in_hbm(likelihood))


def local(likelihood, block_ids, slot_valid, start_weights):
    read_blocks, slots, reads, cols = likelihood.shape
    n = lax.axis_size(ALL)
    chips = lax.axis_size("genome")
    near = radices(n)[0]
    far = n // near
    own_weights = start_weights.reshape(-1, cols)
    own_blocks = own_weights.shape[0]
    all_slots = read_blocks * slots
    total_reads = read_blocks * lax.axis_size("reads") * reads
    scale = n * own_blocks * cols / total_reads

    column = gather_far(own_weights, ALL, CROSSED, GRAY)
    held, info = prepare(own_blocks, read_blocks * 3 // 8, likelihood, block_ids, slot_valid)
    (sent,) = call(join_kernel, [(near_rows(far, own_blocks), cols)], [], *column, info)
    rest, flipped = flip(sent, held, likelihood)
    pieces = [sent] + [swap(sent, ALL, j) for j in GRAY[1:]]
    at = far * own_blocks
    wanted = [info] + [pieces[GRAY[j]][at : at + ID_ROWS] for j in range(1, near)]

    row_shapes = [(chips, read_blocks, reads), (all_slots, cols)]
    inverse = (read_blocks, reads)
    for step in range(ITERS):
        if step == 0:
            row_parts, picked = call(
                lambda *refs: first_row_kernel(near, *refs), row_shapes, [], info, *pieces, flipped
            )
        else:
            row_parts, picked = call(
                lambda *refs: next_row_kernel(near, scale, *refs), row_shapes, [], *parts, flipped
            )
        row_parts = lax.all_to_all(
            row_parts,
            "genome",
            0,
            0,
            tiled=True,
            axis_index_groups=[middle_first(chips, chips // 2 + step)],
        )
        if step + 1 < ITERS:
            (contrib,) = call(
                column_kernel,
                [(all_slots + ID_ROWS, cols)],
                [inverse],
                info,
                row_parts,
                picked,
                held,
                rest,
            )
            given = gather_far(contrib, ALL, (1, 3), range(4))
            sums = call(
                lambda *refs: wanted_kernel(near, all_slots, len(given), *refs),
                [(all_slots, cols)] * near,
                [],
                *given,
                *wanted,
            )
            parts = [sums[0]] + [swap(sums[j], ALL, j) for j in list(range(2, near)) + [1]]
    order = middle_first(n, n // 2 + 3)
    (counts,) = call(
        lambda *refs: last_column_kernel(order, *refs),
        [(n, own_blocks, cols)],
        [inverse, (all_slots, cols)],
        info,
        row_parts,
        picked,
        held,
        rest,
    )
    counts = lax.all_to_all(counts, ALL, 0, 0, tiled=True, axis_index_groups=[order])
    return (jnp.sum(counts, axis=0) * scale).reshape(-1)


def solution(mesh):
    placed = (
        P(("parts", "reads"), "genome", None, None),
        P(("parts", "reads"), "genome"),
        P(("parts", "reads"), "genome"),
        P(("parts", "genome", "reads")),
    )
    return jax.shard_map(
        local,
        mesh=mesh,
        in_specs=placed,
        out_specs=P(("parts", "genome", "reads")),
        check_vma=False,
    )
```

```python
import jax
import jax.numpy as jnp
from jax import lax
from jax.experimental import pallas as pl
from jax.experimental.pallas import tpu as pltpu
from jax.sharding import PartitionSpec as P

ITERS = 2
ALL = ("genome", "reads")
TERMS = 16
ID_ROWS = 8
CROSSED = (1, 2, 3)
LANES = 128
VMEM = pl.BlockSpec(memory_space=pltpu.VMEM)
ANY = pl.BlockSpec(memory_space=pl.ANY)


def radices(n):
    out = []
    while n > 1:
        r = 4 if n % 4 == 0 else 2
        out.append(r)
        n //= r
    return out


def swap(x, axes, k):
    n = lax.axis_size(axes)
    return lax.ppermute(x, axes, [(i, i ^ k) for i in range(n)])


def middle_first(n, k):
    return [i ^ k for i in range(n)]


GRAY = (0, 1, 3, 2)


def position(k, n):
    place = 0
    for r in radices(n):
        n //= r
        digit = k % r
        place = place + (digit ^ (digit >> 1)) * n
        k = k // r
    return place


def gather_far(x, axes, crossed, order):
    parts = [x]
    stride = lax.axis_size(axes)
    for r in radices(stride)[:0:-1]:
        stride //= r
        sent = parts[0] if len(parts) == 1 else jnp.concatenate(parts, axis=0)
        parts = [sent] + [
            swap(sent, axes, j * stride + (j in crossed)) for j in order[1:] if j < r
        ]
    return parts


def dot(a, b, dims=(((1,), (0,)), ((), ()))):
    return lax.dot_general(a, b, dims, preferred_element_type=jnp.float32)


def terms(x):
    hi = x.astype(jnp.bfloat16)
    return hi, (x - hi.astype(jnp.float32)).astype(jnp.bfloat16)


def select_rows(hot, x):
    hi, low = terms(x)
    hot = hot.astype(jnp.bfloat16)
    return dot(hot, hi) + dot(hot, low)


def split(row):
    x = jnp.broadcast_to(row, (TERMS, row.shape[1]))
    hi = x.astype(jnp.bfloat16).astype(jnp.float32)
    rest = x - hi
    mid = rest.astype(jnp.bfloat16).astype(jnp.float32)
    low = rest - mid
    at = lax.broadcasted_iota(jnp.int32, x.shape, 0)
    out = jnp.where(at == 0, hi, jnp.where(at == 1, mid, jnp.where(at == 2, low, 0.0)))
    return out.astype(jnp.bfloat16)


def down(row):
    return jnp.transpose(jnp.broadcast_to(row, (LANES, LANES)))


def hot_rows(values, count):
    column = down(values)
    blocks = []
    for start in range(0, count, LANES):
        width = min(LANES, count - start)
        lane = lax.broadcasted_iota(jnp.int32, (LANES, width), 1).astype(jnp.float32) + start
        blocks.append((column[:, :width] == lane).astype(jnp.float32))
    return blocks[0] if len(blocks) == 1 else jnp.concatenate(blocks, axis=1)


def prepare_kernel(
    own_blocks,
    lik_ref,
    ids_ref,
    valid_ref,
    held_ref,
    info_ref,
    ids,
    valid,
    wide,
    sems,
    held_sems,
):
    read_blocks, slots = ids.shape
    copies = [
        pltpu.make_async_copy(ids_ref, ids, sems.at[0]),
        pltpu.make_async_copy(valid_ref, valid, sems.at[1]),
    ]
    held = block_copies(lik_ref, held_ref, held_sems, 0)
    for copy in copies + held:
        copy.start()
    for copy in copies:
        copy.wait()
    n = lax.axis_size(ALL)
    near = radices(n)[0]
    far = n // near
    me = lax.axis_index("genome") * lax.axis_size("reads") + lax.axis_index("reads")
    lane = lax.broadcasted_iota(jnp.int32, wide.shape, 1)
    wide[...] = jnp.zeros_like(wide)
    wide[:, :slots] = jnp.where(valid[...] > 0, ids[...], -1).astype(jnp.float32)
    flat = jnp.sum(
        pltpu.roll(wide[...], 0, 1, stride=slots, stride_axis=0), axis=0, keepdims=True
    )
    flat = jnp.where(lane[:1] < read_blocks * slots, flat, -1.0)
    owner = ((flat + 0.5) * (1.0 / own_blocks)).astype(jnp.int32)
    inside = flat.astype(jnp.int32) - owner * own_blocks
    away = owner ^ me
    rest = away // near
    for r in radices(n)[1:]:
        for j in CROSSED:
            away = away ^ jnp.where(rest % r == j, 1, 0)
        rest = rest // r
    place = position(away, n)
    place = (place // far) * near_rows(far, own_blocks) + (place % far) * own_blocks + inside
    place = jnp.where(flat < 0, -1, place).astype(jnp.float32)
    row = lax.broadcasted_iota(jnp.int32, info_ref.shape, 0)
    info_ref[...] = jnp.where(row == 0, flat, jnp.where(row == 1, place, 0.0))
    for copy in held:
        copy.wait()


def join_kernel(*refs):
    out_ref = refs[-1]
    at = 0
    for ref in refs[:-1]:
        out_ref[at : at + ref.shape[0], :] = ref[...]
        at += ref.shape[0]
    if at < out_ref.shape[0]:
        out_ref[at:, :] = jnp.zeros((out_ref.shape[0] - at, out_ref.shape[1]), jnp.float32)


def near_rows(far, own_blocks):
    return -(-(far * own_blocks + ID_ROWS) // 8) * 8


def flip_kernel(after_ref, early_ref, lik_ref, late_ref, out_ref, sems):
    early = early_ref.shape[0]
    copies = block_copies(lik_ref, late_ref, sems, early)
    for copy in copies:
        copy.start()
    for b in range(out_ref.shape[0]):
        if b >= early:
            copies[b - early].wait()
        held_ref = block_of((early_ref, late_ref), b)
        slots, reads, cols = held_ref.shape
        for s in range(slots):
            start = s % 2 * cols
            out_ref[b, s // 2, start : start + cols, :] = jnp.transpose(held_ref[s])


def block_copies(lik_ref, held_ref, sems, start):
    return [
        pltpu.make_async_copy(lik_ref.at[start + b], held_ref.at[b], sems.at[b])
        for b in range(held_ref.shape[0])
    ]


def block_of(held_refs, b):
    early_ref, late_ref = held_refs
    early = early_ref.shape[0]
    return early_ref.at[b] if b < early else late_ref.at[b - early]


def row_sums(picked_ref, flip_ref, out_ref):
    read_blocks, pairs = flip_ref.shape[:2]
    for b in range(read_blocks):
        total = None
        for s in range(pairs):
            at = (b * pairs + s) * 2
            left = jnp.concatenate(
                [split(picked_ref[at : at + 1, :]), split(picked_ref[at + 1 : at + 2, :])], axis=1
            )
            part = dot(left, flip_ref[b, s])
            total = part if total is None else total + part
        row = jnp.sum(total, axis=0, keepdims=True)
        for i in range(out_ref.shape[0]):
            out_ref[i, b : b + 1, :] = row


def first_row_kernel(near, info_ref, *refs):
    pieces, (flip_ref, out_ref, picked_ref) = refs[:near], refs[near:]
    table = jnp.concatenate([piece[...] for piece in pieces], axis=0)
    hot = hot_rows(info_ref[1:2, :], table.shape[0])
    picked_ref[...] = select_rows(hot[: picked_ref.shape[0]], table)
    row_sums(picked_ref, flip_ref, out_ref)


def next_row_kernel(near, scale, *refs):
    parts, (flip_ref, out_ref, picked_ref) = refs[:near], refs[near:]
    total = parts[0][...]
    for part in parts[1:]:
        total = total + part[...]
    picked_ref[...] = total * scale
    row_sums(picked_ref, flip_ref, out_ref)


def column_sums(parts_ref, picked_ref, held_refs, contrib_ref, inverse_ref):
    slots, reads, cols = held_refs[0].shape[1:]
    total = parts_ref[0]
    for i in range(1, parts_ref.shape[0]):
        total = total + parts_ref[i]
    inverse_ref[...] = 1.0 / total
    for b in range(inverse_ref.shape[0]):
        held_ref = block_of(held_refs, b)
        left = split(inverse_ref[b : b + 1, :])
        for s in range(0, slots, 2):
            at = b * slots + s
            right = jnp.concatenate([held_ref[s], held_ref[s + 1]], axis=1)
            summed = jnp.sum(dot(left, right), axis=0, keepdims=True)
            contrib_ref[at : at + 1, :] = picked_ref[at : at + 1, :] * summed[:, :cols]
            contrib_ref[at + 1 : at + 2, :] = picked_ref[at + 1 : at + 2, :] * summed[:, cols:]


def column_kernel(info_ref, parts_ref, picked_ref, early_ref, late_ref, out_ref, inverse_ref):
    column_sums(parts_ref, picked_ref, (early_ref, late_ref), out_ref, inverse_ref)
    out_ref[picked_ref.shape[0] :, :] = info_ref[...]


def last_column_kernel(
    order, info_ref, parts_ref, picked_ref, early_ref, late_ref, out_ref, inverse_ref, contrib_ref
):
    column_sums(parts_ref, picked_ref, (early_ref, late_ref), contrib_ref, inverse_ref)
    owners, own_blocks, cols = out_ref.shape
    all_slots = contrib_ref.shape[0]
    block = lax.broadcasted_iota(jnp.int32, (owners * own_blocks, all_slots), 0)
    hot = (block.astype(jnp.float32) == info_ref[0:1, :all_slots]).astype(jnp.float32)
    counts = select_rows(hot, contrib_ref[...])
    for i, owner in enumerate(order):
        out_ref[i] = counts[owner * own_blocks : (owner + 1) * own_blocks, :]


def wanted_kernel(near, all_slots, pieces, *refs):
    given_refs, wanted, outs = refs[:pieces], refs[pieces : pieces + near], refs[pieces + near :]
    rows = all_slots + ID_ROWS
    half = LANES // 2
    lane = lax.broadcasted_iota(jnp.int32, (1, LANES), 1)
    ids, values = [], []
    for ref in given_refs:
        for at in range(0, ref.shape[0], rows):
            ids.append(ref[at + all_slots : at + all_slots + 1, :])
            values.append(ref[at : at + all_slots, :])
    pairs = [
        jnp.where(lane < half, a, pltpu.roll(b, half, 1)) for a, b in zip(ids[::2], ids[1::2])
    ]
    given = terms(jnp.concatenate(values, axis=0))
    column = jnp.concatenate([down(ids_ref[0:1, :])[:all_slots] for ids_ref in wanted], axis=0)
    hot = jnp.concatenate([(column == pair).astype(jnp.float32) for pair in pairs], axis=1)
    hot = hot.astype(jnp.bfloat16)
    sums = dot(hot, given[0]) + dot(hot, given[1])
    for j, out_ref in enumerate(outs):
        out_ref[...] = sums[j * all_slots : (j + 1) * all_slots]


def call(kernel, outs, scratch, *operands):
    return pl.pallas_call(
        kernel,
        out_shape=[jax.ShapeDtypeStruct(shape, jnp.float32) for shape in outs],
        in_specs=[VMEM] * len(operands),
        out_specs=[VMEM] * len(outs),
        scratch_shapes=[pltpu.VMEM(shape, jnp.float32) for shape in scratch],
        compiler_params=PARAMS,
    )(*operands)


PARAMS = pltpu.CompilerParams(vmem_limit_bytes=16 * 2**20)


def in_hbm(*arrays):
    return [pltpu.with_memory_space_constraint(x, pltpu.HBM) for x in arrays]


def prepare(own_blocks, early, likelihood, block_ids, slot_valid):
    read_blocks, slots = block_ids.shape
    return pl.pallas_call(
        lambda *refs: prepare_kernel(own_blocks, *refs),
        out_shape=[
            pltpu.VMEM((early,) + likelihood.shape[1:], likelihood.dtype),
            jax.ShapeDtypeStruct((ID_ROWS, LANES), jnp.float32),
        ],
        in_specs=[ANY] * 3,
        out_specs=[VMEM] * 2,
        scratch_shapes=[
            pltpu.VMEM((read_blocks, slots), jnp.int32),
            pltpu.VMEM((read_blocks, slots), jnp.int32),
            pltpu.VMEM((read_blocks, LANES), jnp.float32),
            pltpu.SemaphoreType.DMA((2,)),
            pltpu.SemaphoreType.DMA((early,)),
        ],
        compiler_params=PARAMS,
    )(*in_hbm(likelihood, block_ids, slot_valid))


def flip(after, held, likelihood):
    read_blocks, slots, reads, cols = likelihood.shape
    late = read_blocks - held.shape[0]
    return pl.pallas_call(
        flip_kernel,
        out_shape=[
            pltpu.VMEM((late,) + likelihood.shape[1:], likelihood.dtype),
            pltpu.VMEM((read_blocks, slots // 2, 2 * cols, reads), likelihood.dtype),
        ],
        in_specs=[ANY, VMEM, ANY],
        out_specs=[VMEM] * 2,
        scratch_shapes=[pltpu.SemaphoreType.DMA((late,))],
        compiler_params=PARAMS,
    )(after, held, *in_hbm(likelihood))


def local(likelihood, block_ids, slot_valid, start_weights):
    read_blocks, slots, reads, cols = likelihood.shape
    n = lax.axis_size(ALL)
    chips = lax.axis_size("genome")
    near = radices(n)[0]
    far = n // near
    own_weights = start_weights.reshape(-1, cols)
    own_blocks = own_weights.shape[0]
    all_slots = read_blocks * slots
    total_reads = read_blocks * lax.axis_size("reads") * reads
    scale = n * own_blocks * cols / total_reads

    column = gather_far(own_weights, ALL, CROSSED, GRAY)
    held, info = prepare(own_blocks, read_blocks // 2, likelihood, block_ids, slot_valid)
    (sent,) = call(join_kernel, [(near_rows(far, own_blocks), cols)], [], *column, info)
    rest, flipped = flip(sent, held, likelihood)
    pieces = [sent] + [swap(sent, ALL, j) for j in GRAY[1:]]
    at = far * own_blocks
    wanted = [info] + [pieces[GRAY[j]][at : at + ID_ROWS] for j in range(1, near)]

    row_shapes = [(chips, read_blocks, reads), (all_slots, cols)]
    inverse = (read_blocks, reads)
    for step in range(ITERS):
        if step == 0:
            row_parts, picked = call(
                lambda *refs: first_row_kernel(near, *refs), row_shapes, [], info, *pieces, flipped
            )
        else:
            row_parts, picked = call(
                lambda *refs: next_row_kernel(near, scale, *refs), row_shapes, [], *parts, flipped
            )
        row_parts = lax.all_to_all(
            row_parts,
            "genome",
            0,
            0,
            tiled=True,
            axis_index_groups=[middle_first(chips, chips // 2 + step)],
        )
        if step + 1 < ITERS:
            (contrib,) = call(
                column_kernel,
                [(all_slots + ID_ROWS, cols)],
                [inverse],
                info,
                row_parts,
                picked,
                held,
                rest,
            )
            given = gather_far(contrib, ALL, (1, 3), range(4))
            sums = call(
                lambda *refs: wanted_kernel(near, all_slots, len(given), *refs),
                [(all_slots, cols)] * near,
                [],
                *given,
                *wanted,
            )
            parts = [sums[0]] + [swap(sums[j], ALL, j) for j in list(range(2, near)) + [1]]
    order = middle_first(n, n // 2 + 3)
    (counts,) = call(
        lambda *refs: last_column_kernel(order, *refs),
        [(n, own_blocks, cols)],
        [inverse, (all_slots, cols)],
        info,
        row_parts,
        picked,
        held,
        rest,
    )
    counts = lax.all_to_all(counts, ALL, 0, 0, tiled=True, axis_index_groups=[order])
    return (jnp.sum(counts, axis=0) * scale).reshape(-1)


def solution(mesh):
    placed = (
        P(("parts", "reads"), "genome", None, None),
        P(("parts", "reads"), "genome"),
        P(("parts", "reads"), "genome"),
        P(("parts", "genome", "reads")),
    )
    return jax.shard_map(
        local,
        mesh=mesh,
        in_specs=placed,
        out_specs=P(("parts", "genome", "reads")),
        check_vma=False,
    )
```
